32 devices in a mesh: ctx: 8 (over z, y), tp: 4 (over x, core).
Axes of the slice: x: 2, y: 2, z: 4, core: 2. Of those that a mesh axis runs over, the one named last changes fastest.
Arguments:
- q_input: bfloat16 [1024, 4096], P('ctx', 'tp'), may hold values from -6 to 6
- k_input: bfloat16 [1024, 4096], P('ctx', 'tp'), may hold values from -6 to 6
- v_input: bfloat16 [1024, 4096], P('ctx', 'tp'), may hold values from -6 to 6
- resid: bfloat16 [1024, 4096], P('ctx', 'tp'), may hold values from -18 to 18
- lengths: int32 [8], replicated, may hold values from 1 to 512, 1024 in all
- short_filter: bfloat16 [3, 256, 7], P(None, 'tp'), may hold values from -2 to 2
- long_filter: bfloat16 [256, 128], P('tp'), may hold values from -0.5 to 0.5
- skip: float32 [4096], P('tp'), may hold values from -1 to 1
- gain: float32 [4096], P('tp'), may hold values from 0.1 to 1.9
- cotangent: bfloat16 [1024, 4096], P('ctx', 'tp'), may hold values from -12 to 12
Outputs:
- normed: bfloat16 [1024, 4096], P('ctx', 'tp')
- grad_q: bfloat16 [1024, 4096], P('ctx', 'tp')
- grad_k: bfloat16 [1024, 4096], P('ctx', 'tp')
- grad_v: bfloat16 [1024, 4096], P('ctx', 'tp')
- grad_short: float32 [3, 256, 7], P(None, 'tp')
- grad_long: float32 [256, 128], P('tp')
- grad_skip: float32 [4096], P('tp')
- grad_gain: float32 [4096], P('tp')
The draws below stay inside these ranges and needn't reach their ends.
All inputs are finite; a program needn't handle non-finite values.
Results may differ from the reference program's by a relative error of at most 0.0047.
The reference program's roundings to bfloat16 on the way (of `gated`) count: a program that leaves them out, or rounds other values in their place, can miss the bound.
Values may be sent and summed in bfloat16 or wider, within the bound.
No kernel may reach another device: no remote copies, remote signals or barrier semaphores. Data moves between devices by JAX's collectives and lax.ppermute only.
A program may use at most 128 MiB of HBM per device.

```python
import math
import jax
import jax.numpy as jnp
import numpy as np
from jax import lax

C = 4096
GS = 16
K = 128
KS = 7
GROUPS = 256
TOKENS = 1024
NSEQ = 8
SEQ_MOST = 512


def draw_resid(key, part):
    first, second = jax.random.split(key)
    ramp = jnp.power(3.0, jnp.arange(C, dtype=jnp.float32) / C)
    column = ramp * jnp.exp(jax.random.uniform(second, (C,), jnp.float32) * math.log(10.0))
    base = jax.random.truncated_normal(first, -4.0, 4.0, (TOKENS, C), jnp.float32)
    return (0.15 * base * column[None, :]).astype(jnp.bfloat16)


def draw_cotangent(key, part):
    first = jax.random.fold_in(key, 0)
    ramp = jnp.power(3.0, jnp.arange(TOKENS, dtype=jnp.float32) / TOKENS)
    base = jax.random.truncated_normal(first, -4.0, 4.0, (TOKENS, C), jnp.float32)
    values = base * ramp[:, None]
    return values.astype(jnp.bfloat16)


def shard_levels(stream_key, dims, shards, smallest, largest):
    level, own = 1.0, jax.random.fold_in(stream_key, 6)
    for axis_at, blocks in shards:
        draws = jnp.exp(jax.random.uniform(jax.random.fold_in(own, axis_at), (blocks,), jnp.float32, smallest / len(shards), largest / len(shards)))
        level = level * jnp.repeat(draws, dims[axis_at] // blocks).reshape([-1 if axis == axis_at else 1 for axis in range(len(dims))])
    return level


def length_profile(count, total, limit, lean):
    portions = [(1 << 20) // math.isqrt(grade ** lean) + 1 for grade in range(2, count + 1)]
    surplus, given = total - limit - (count - 1), [1] * (count - 1)
    while surplus > 0:
        free = [i for i in range(count - 1) if given[i] < limit]
        whole, left = sum([portions[i] for i in free]), surplus
        for i in free:
            more = min(limit - given[i], max(1, left * portions[i] // whole), surplus)
            given[i] = given[i] + more
            surplus = surplus - more
    return np.array([limit] + given)


def uneven_parts(own_key, number_of, total, limit, slope):
    if number_of == 2:
        one = jax.random.randint(own_key, (), max(1, total - limit), min(limit, total - 1) + 1)
        return jnp.stack([one, total - one])
    sizes = jnp.asarray(length_profile(number_of, total, limit, slope), jnp.int32)
    couples = (number_of - 1) // 2
    donor, taker = sizes[1:1 + 2 * couples:2], sizes[2:2 + 2 * couples:2]
    slack = jnp.minimum(donor - 1, limit - taker)
    moved = jax.random.randint(jax.random.fold_in(own_key, 1), (couples,), 0, 1 << 20) % (slack + 1)
    sizes = sizes.at[1:1 + 2 * couples:2].set(donor - moved).at[2:2 + 2 * couples:2].set(taker + moved)
    return sizes[jax.random.permutation(jax.random.fold_in(own_key, 2), number_of)]


def noise(own_key, shape, scale, bound, pieces=(), kind=jnp.bfloat16):
    level = shard_levels(own_key, shape, pieces, -0.22, 0.18) if pieces else 1.0
    drawn = jax.random.normal(own_key, shape, jnp.float32) * scale * level
    return jnp.minimum(jnp.maximum(drawn, -bound), bound).astype(kind)


def setup_inputs(seed: int = 0) -> dict:
    seeds = jax.random.split(jax.random.key(seed), 11)
    q_input = noise(seeds[0], (TOKENS, C), 1.0, 6.0, ((0, 8), (1, 4)))
    k_input = noise(seeds[1], (TOKENS, C), 1.0, 6.0, ((0, 8), (1, 4)))
    v_input = noise(seeds[2], (TOKENS, C), 1.0, 6.0, ((0, 8), (1, 4)))
    resid = draw_resid(jax.random.fold_in(seeds[10], 71), 0)
    lengths = uneven_parts(seeds[4], NSEQ, TOKENS, SEQ_MOST, 2).astype(jnp.int32)
    short_filter = noise(seeds[5], (3, GROUPS, KS), KS ** -0.5, 2.0, ((1, 4),))
    long_filter = noise(seeds[6], (GROUPS, K), K ** -0.5, 0.5, ((0, 4),))
    skip = jnp.clip(jax.random.uniform(seeds[7], (C,), jnp.float32, -1.0, 1.0) * shard_levels(seeds[7], (C,), ((0, 4),), -0.4, 0.0), -1.0, 1.0)
    gain = jnp.clip(1.0 + 0.18 * jax.random.normal(seeds[8], (C,), jnp.float32), 0.1, 1.9)
    cotangent = draw_cotangent(jax.random.fold_in(seeds[10], 71), 0)
    return {"q_input": q_input, "k_input": k_input, "v_input": v_input, "resid": resid, "lengths": lengths, "short_filter": short_filter, "long_filter": long_filter, "skip": skip, "gain": gain, "cotangent": cotangent}


EPS = 1e-06
HIGH = lax.Precision.HIGHEST

def positions(lengths, row_ids):
    finish = jnp.cumsum(lengths).astype(jnp.int32)
    starts = finish - lengths
    before = starts[None, :] <= row_ids[:, None]
    begins = lax.optimization_barrier(jnp.max(jnp.where(before, starts[None, :], jnp.zeros_like(starts)[None, :]), axis=1))
    return (row_ids - begins).astype(jnp.int32)

def toeplitz(filters):
    groups, width = filters.shape
    reverse = filters[:, ::-1]
    banded = jnp.broadcast_to(reverse[:, None, :], (groups, width, width))
    banded = jnp.concatenate([banded, jnp.zeros((groups, width, width + 1), filters.dtype)], axis=2)
    flattened = banded.reshape(groups, width * (2 * width + 1))
    flattened = jnp.concatenate([jnp.zeros((groups, 1), filters.dtype), flattened], axis=1)[:, :2 * width * width]
    return flattened.reshape(groups, width, 2 * width)

def diagonals(square):
    groups, width, span = square.shape
    flattened = square.reshape(groups, width * span)
    flattened = jnp.concatenate([flattened[:, 1:], jnp.zeros((groups, width + 1), square.dtype)], axis=1)
    skewed = flattened.reshape(groups, width, span + 1)[:, :, :width]
    return skewed[:, :, ::-1]

def window_mask(row_pos, width):
    lag = jnp.arange(width, dtype=jnp.int32)[:, None] + width - jnp.arange(2 * width, dtype=jnp.int32)[None, :]
    return row_pos[:, None] >= lag

def causal_short(values, weights, pos):
    length, channels = values.shape
    result = jnp.zeros((length, channels), jnp.float32)
    for j in range(KS):
        moved = jnp.concatenate([jnp.zeros((j, channels), values.dtype), values[:length - j]], axis=0)
        result = result + weights[:, j] * moved.astype(jnp.float32) * (pos >= j)[:, None]
    return result

def anticausal_short(grads, weights, pos):
    length, channels = grads.shape
    result = jnp.zeros((length, channels), jnp.float32)
    for j in range(KS):
        masked = grads.astype(jnp.float32) * (pos >= j)[:, None]
        moved = jnp.concatenate([masked[j:], jnp.zeros((j, channels), jnp.float32)], axis=0)
        result = result + weights[:, j] * moved
    return result

def short_grads(grads, values, pos):
    length, channels = values.shape
    columns = []
    for j in range(KS):
        moved = jnp.concatenate([jnp.zeros((j, channels), values.dtype), values[:length - j]], axis=0)
        columns.append(lax.optimization_barrier(jnp.sum(grads.astype(jnp.float32) * moved.astype(jnp.float32) * (pos >= j)[:, None], axis=0)))
    return jnp.stack(columns, axis=1)

def long_forward(gated_groups, matrix, pos):
    groups, members, length = gated_groups.shape
    width = matrix.shape[1]
    padded = jnp.concatenate([jnp.zeros((groups, members, width), gated_groups.dtype), gated_groups], axis=2)

    def one_block(b):
        begin = b * width
        source = lax.dynamic_slice_in_dim(padded, begin, 2 * width, axis=2)
        row_pos = lax.dynamic_slice_in_dim(pos, begin, width)
        masked = matrix * window_mask(row_pos, width).astype(matrix.dtype)[None]
        return jnp.einsum('gcs,gts->gct', source.astype(jnp.float32), masked.astype(jnp.float32), precision=HIGH)
    outs = lax.map(one_block, jnp.arange(length // width, dtype=jnp.int32))
    return jnp.transpose(outs, (1, 2, 0, 3)).reshape(groups, members, length)

def long_backward(grad_groups, gated_groups, matrix, pos):
    groups, members, length = gated_groups.shape
    width = matrix.shape[1]
    padded = jnp.concatenate([jnp.zeros((groups, members, width), gated_groups.dtype), gated_groups], axis=2)

    def step(b, carry):
        accum, filt_grad = carry
        begin = jnp.asarray(b, jnp.int32) * width
        source = lax.dynamic_slice_in_dim(padded, begin, 2 * width, axis=2).astype(jnp.float32)
        row_pos = lax.dynamic_slice_in_dim(pos, begin, width)
        mask_bool = window_mask(row_pos, width)
        masked = (matrix * mask_bool.astype(matrix.dtype)[None]).astype(jnp.float32)
        block_grad = lax.dynamic_slice_in_dim(grad_groups, begin, width, axis=2).astype(jnp.float32)
        contrib = jnp.einsum('gct,gts->gcs', block_grad, masked, precision=HIGH)
        current = lax.dynamic_slice_in_dim(accum, begin, 2 * width, axis=2)
        accum = lax.dynamic_update_slice_in_dim(accum, current + contrib, begin, axis=2)
        cross = jnp.einsum('gct,gcs->gts', block_grad, source, precision=HIGH) * mask_bool.astype(jnp.float32)[None]
        filt_grad = filt_grad + lax.optimization_barrier(jnp.sum(diagonals(cross), axis=1))
        return (accum, filt_grad)
    start_acc = jnp.zeros((groups, members, length + width), jnp.float32)
    start_grad = jnp.zeros((groups, width), jnp.float32)
    accum, filt_grad = lax.fori_loop(0, length // width, step, (start_acc, start_grad))
    return (accum[:, :, width:], filt_grad)

def reference(q_input, k_input, v_input, resid, lengths, short_filter, long_filter, skip, gain, cotangent):
    block_width = math.gcd(C, 512)
    block_count = C // block_width
    block_groups = block_width // GS
    pos = positions(lengths, jnp.arange(TOKENS, dtype=jnp.int32))

    def split(array):
        return jnp.transpose(array.reshape(TOKENS, block_count, block_width), (1, 0, 2))

    def merge(array):
        return jnp.transpose(array, (1, 0, 2)).reshape(TOKENS, C)
    short_blocks = jnp.transpose(short_filter.reshape(3, block_count, block_groups, KS), (1, 0, 2, 3))
    long_blocks = long_filter.reshape(block_count, block_groups, K)
    skip_blocks = skip.reshape(block_count, block_width)
    gain_blocks = gain.reshape(block_count, block_width)

    def expand(taps):
        wide = jnp.broadcast_to(taps.astype(jnp.float32)[:, :, None, :], (3, block_groups, GS, KS))
        return wide.reshape(3, block_width, KS)

    def to_groups(array):
        return array.T.reshape(block_groups, GS, TOKENS)

    def from_groups(array):
        return array.reshape(block_width, TOKENS).T

    def forward(q_blk, k_blk, v_blk, taps, long_taps, skip_blk):
        table = expand(taps)
        q_short = causal_short(q_blk, table[0], pos)
        k_short = causal_short(k_blk, table[1], pos)
        v_short = causal_short(v_blk, table[2], pos)
        gated = (k_short * v_short).astype(jnp.bfloat16)
        matrix = toeplitz(long_taps)
        conv = from_groups(long_forward(to_groups(gated), matrix, pos))
        mixed = conv + skip_blk[None, :] * gated.astype(jnp.float32)
        return (table, q_short, k_short, v_short, gated, matrix, mixed)

    def first_pass(items):
        q_blk, k_blk, v_blk, x_blk, taps, long_taps, skip_blk = items
        outs = forward(q_blk, k_blk, v_blk, taps, long_taps, skip_blk)
        return x_blk.astype(jnp.float32) + outs[1] * outs[6]
    summed = lax.map(first_pass, (split(q_input), split(k_input), split(v_input), split(resid), short_blocks, long_blocks, skip_blocks))
    cot_blocks = split(cotangent)
    squares = lax.optimization_barrier(jnp.sum(summed * summed, axis=(0, 2)))
    inverse = lax.rsqrt(squares / C + EPS)
    mean_mix = lax.optimization_barrier(jnp.sum(gain_blocks[:, None, :] * cot_blocks.astype(jnp.float32) * summed, axis=(0, 2))) / C

    def second_pass(items):
        q_blk, k_blk, v_blk, cot_blk, sum_blk, taps, long_taps, skip_blk, gain_blk = items
        table, q_short, k_short, v_short, gated, matrix, mixed = forward(q_blk, k_blk, v_blk, taps, long_taps, skip_blk)
        normed = (gain_blk * sum_blk * inverse[:, None]).astype(jnp.bfloat16)
        scaled = gain_blk * cot_blk.astype(jnp.float32)
        grad_sum = inverse[:, None] * (scaled - sum_blk * (inverse * inverse * mean_mix)[:, None])
        grad_mixed = (grad_sum * q_short).astype(jnp.bfloat16)
        grad_qs = (grad_sum * mixed).astype(jnp.bfloat16)
        grad_gain = lax.optimization_barrier(jnp.sum(cot_blk.astype(jnp.float32) * sum_blk * inverse[:, None], axis=0))
        grad_conv, grad_long = long_backward(to_groups(grad_mixed), to_groups(gated), matrix, pos)
        grad_gated = skip_blk * grad_mixed.astype(jnp.float32) + from_groups(grad_conv)
        grad_skip = lax.optimization_barrier(jnp.sum(grad_mixed.astype(jnp.float32) * gated.astype(jnp.float32), axis=0))
        grad_ks = (grad_gated * v_short).astype(jnp.bfloat16)
        grad_vs = (grad_gated * k_short).astype(jnp.bfloat16)
        grad_q = anticausal_short(grad_qs, table[0], pos).astype(jnp.bfloat16)
        grad_k = anticausal_short(grad_ks, table[1], pos).astype(jnp.bfloat16)
        grad_v = anticausal_short(grad_vs, table[2], pos).astype(jnp.bfloat16)
        per_channel = jnp.stack([short_grads(grad_qs, q_blk, pos), short_grads(grad_ks, k_blk, pos), short_grads(grad_vs, v_blk, pos)], axis=0)
        grad_short = lax.optimization_barrier(jnp.sum(per_channel.reshape(3, block_groups, GS, KS), axis=2))
        return (normed, grad_q, grad_k, grad_v, grad_short, grad_long, grad_skip, grad_gain)
    results = lax.map(second_pass, (split(q_input), split(k_input), split(v_input), cot_blocks, summed, short_blocks, long_blocks, skip_blocks, gain_blocks))
    grad_short = jnp.transpose(results[4], (1, 0, 2, 3)).reshape(3, GROUPS, KS)
    return (merge(results[0]), merge(results[1]), merge(results[2]), merge(results[3]), grad_short, results[5].reshape(GROUPS, K), results[6].reshape(C), results[7].reshape(C))
```

```python
import functools

import jax
import jax.numpy as jnp
from jax import lax
from jax.experimental import pallas as pl
from jax.experimental.pallas import tpu as pltpu
from jax.sharding import PartitionSpec as P

GS = 16
K = 128
KS = 7
LANES = 128
PER = LANES // GS
RIM = 16
EPS = 1e-06
F32 = jnp.float32
BF16 = jnp.bfloat16


def shifted(x, axis, by):
    count = lax.axis_size(axis)
    pairs = [(i, i + by) for i in range(count) if 0 <= i + by < count]
    return lax.ppermute(x, axis, pairs)


def iota(shape, dim):
    return lax.broadcasted_iota(jnp.int32, shape, dim)


def positions(len_ref, rows):
    begin = jnp.zeros_like(rows)
    start = jnp.int32(0)
    for n in range(len_ref.shape[0]):
        begin = jnp.where(rows >= start, start, begin)
        start = start + len_ref[n]
    return rows - begin


def first_row():
    return lax.axis_index("ctx") * K


def lanes_of(q):
    return pl.ds(pl.multiple_of(q * LANES, LANES), LANES)


def each_chunk(channels, body):
    def step(q, carry):
        body(q)
        return carry

    lax.fori_loop(0, channels // LANES, step, 0)


def as_mask(cond):
    return jnp.where(cond, 1.0, 0.0).astype(BF16)


def extended(rim_ref, which, ref, ls):
    rim = rim_ref[which * RIM : (which + 1) * RIM, ls]
    return jnp.concatenate([rim.astype(F32), ref[:, ls].astype(F32)], axis=0)


def tap_rows(taps_ref, which, ls):
    table = taps_ref[which * 8 : which * 8 + 8, ls]
    return [table[j : j + 1, :] for j in range(KS)]


def causal(ext, taps, pos):
    total = taps[0] * ext[RIM:]
    for j in range(1, KS):
        moved = ext[RIM - j : RIM - j + K]
        total = total + taps[j] * jnp.where(pos >= j, moved, 0.0)
    return total


def group_blocks(mat_ref, q, mask, right):
    left = mat_ref[pl.ds(q * PER, PER)] * mask[None]
    full = jnp.dot(
        left.reshape(PER * K, K), right, preferred_element_type=F32
    ).reshape(PER, K, LANES)
    group = iota((K, LANES), 1) // GS
    out = full[0]
    for g in range(1, PER):
        out = jnp.where(group == g, full[g], out)
    return out


def rims_kernel(q_ref, k_ref, v_ref, out_ref):
    out_ref[0:RIM] = q_ref[...]
    out_ref[RIM : 2 * RIM] = k_ref[...]
    out_ref[2 * RIM :] = v_ref[...]


def tables_kernel(short_ref, long_ref, taps_ref, fwd_ref, bwd_ref, rev_ref, for_ref):
    groups = long_ref.shape[0]
    channels = taps_ref.shape[1]
    spread = as_mask(iota((groups, channels), 1) // GS == iota((groups, channels), 0))
    for i in range(3):
        taps_ref[i * 8 : i * 8 + KS] = lax.dot_general(
            short_ref[i], spread, (((0,), (0,)), ((), ())), preferred_element_type=F32
        )
        taps_ref[i * 8 + KS : i * 8 + 8] = jnp.zeros((8 - KS, channels), F32)
    flip = as_mask((iota((K, K), 0) + iota((K, K), 1)) % K == 0)
    filt = long_ref[...]
    rev_ref[...] = jnp.dot(filt, flip, preferred_element_type=F32)
    for_ref[...] = filt.astype(F32)

    def step(g, carry):
        row = jnp.broadcast_to(rev_ref[pl.ds(g, 1), :], (K, K))
        fwd_ref[g] = pltpu.roll(row, 0, 1, stride=1, stride_axis=0).astype(BF16)
        row = jnp.broadcast_to(for_ref[pl.ds(g, 1), :], (K, K))
        bwd_ref[g] = pltpu.roll(row, 0, 1, stride=1, stride_axis=0).astype(BF16)
        return carry

    lax.fori_loop(0, groups, step, 0)


def gated_kernel(len_ref, k_ref, v_ref, rim_ref, taps_ref, gated_ref):
    pos = positions(len_ref, first_row() + iota((K, LANES), 0))

    def body(q):
        ls = lanes_of(q)
        ks = causal(extended(rim_ref, 1, k_ref, ls), tap_rows(taps_ref, 1, ls), pos)
        vs = causal(extended(rim_ref, 2, v_ref, ls), tap_rows(taps_ref, 2, ls), pos)
        gated_ref[:, ls] = (ks * vs).astype(BF16)

    each_chunk(k_ref.shape[1], body)


def current_kernel(
    len_ref, q_ref, k_ref, v_ref, rim_ref, taps_ref, gated_ref, fwd_ref, skip_ref,
    qs_ref, ks_ref, vs_ref, mixed_ref,
):
    row = iota((K, LANES), 0)
    col = iota((K, LANES), 1)
    pos = positions(len_ref, first_row() + row)
    mask = as_mask((col <= row) & (pos >= row - col))

    def body(q):
        ls = lanes_of(q)
        qs_ref[:, ls] = causal(extended(rim_ref, 0, q_ref, ls), tap_rows(taps_ref, 0, ls), pos)
        ks_ref[:, ls] = causal(extended(rim_ref, 1, k_ref, ls), tap_rows(taps_ref, 1, ls), pos)
        vs_ref[:, ls] = causal(extended(rim_ref, 2, v_ref, ls), tap_rows(taps_ref, 2, ls), pos)
        gated = gated_ref[:, ls]
        conv = group_blocks(fwd_ref, q, mask, gated)
        mixed_ref[:, ls] = conv + skip_ref[:, ls] * gated.astype(F32)

    each_chunk(q_ref.shape[1], body)


def summed_kernel(
    len_ref, before_ref, fwd_ref, part_ref, qs_ref, resid_ref, cot_ref, gain_ref,
    mixed_ref, summed_ref, sums_ref, acc_ref,
):
    row = iota((K, LANES), 0)
    col = iota((K, LANES), 1)
    pos = positions(len_ref, first_row() + row)
    mask = as_mask((col > row) & (pos >= row - col + K))
    acc_ref[...] = jnp.zeros_like(acc_ref)

    def body(q):
        ls = lanes_of(q)
        mixed = part_ref[:, ls] + group_blocks(fwd_ref, q, mask, before_ref[:, ls])
        summed = resid_ref[:, ls].astype(F32) + qs_ref[:, ls] * mixed
        mixed_ref[:, ls] = mixed
        summed_ref[:, ls] = summed
        acc_ref[0] += summed * summed
        acc_ref[1] += gain_ref[:, ls] * cot_ref[:, ls].astype(F32) * summed

    each_chunk(resid_ref.shape[1], body)
    for i in range(2):
        sums_ref[i : i + 1] = jnp.sum(acc_ref[i].T, axis=0, keepdims=True)


def by_row(line):
    return jnp.broadcast_to(line, (K, K)).T


def inverse_of(sums_ref, total):
    return by_row(lax.rsqrt(sums_ref[0:1] / total + EPS))


def grads_kernel(total, summed_ref, mixed_ref, qs_ref, cot_ref, gain_ref, sums_ref, gm_ref, gq_ref):
    inverse = inverse_of(sums_ref, total)
    scale = inverse * inverse * by_row(sums_ref[1:2] / total)

    def body(q):
        ls = lanes_of(q)
        scaled = gain_ref[:, ls] * cot_ref[:, ls].astype(F32)
        grad_sum = inverse * (scaled - summed_ref[:, ls] * scale)
        gm_ref[:, ls] = (grad_sum * qs_ref[:, ls]).astype(BF16)
        gq_ref[:, ls] = (grad_sum * mixed_ref[:, ls]).astype(BF16)

    each_chunk(cot_ref.shape[1], body)


def beside_kernel(
    total, len_ref, summed_ref, cot_ref, gain_ref, sums_ref, gm_ref, gated_ref, before_ref,
    bwd_ref, skip_ref, normed_ref, stats_ref, part_ref,
):
    groups = bwd_ref.shape[0]
    inverse = inverse_of(sums_ref, total)
    row = iota((K, LANES), 0)
    col = iota((K, LANES), 1)
    pos = positions(len_ref, first_row() + col)
    mask = as_mask((col >= row) & (pos >= col - row))
    source = K - 1 - row
    near = (col >= source) & (pos >= col - source)
    far = (col < source) & (pos >= col - source + K)
    flip = as_mask(row + col == K - 1)
    own = [as_mask(col // GS == g) for g in range(PER)]

    def body(q):
        ls = lanes_of(q)
        summed = summed_ref[:, ls]
        normed_ref[:, ls] = (gain_ref[:, ls] * summed * inverse).astype(BF16)
        gm = gm_ref[:, ls]
        gmf = gm.astype(F32)
        gated = gated_ref[:, ls]
        stats_ref[pl.ds(groups + q, 1), :] = jnp.sum(gmf * gated.astype(F32), axis=0, keepdims=True)
        stats_ref[pl.ds(groups + groups // PER + q, 1), :] = jnp.sum(
            cot_ref[:, ls].astype(F32) * summed * inverse, axis=0, keepdims=True
        )
        part_ref[:, ls] = skip_ref[:, ls] * gmf + group_blocks(bwd_ref, q, mask, gm)
        two = jnp.concatenate([before_ref[:, ls], gated], axis=1)
        flipped = jnp.dot(flip, two, preferred_element_type=F32).astype(BF16)
        left = jnp.concatenate([flipped[:, :LANES], flipped[:, LANES:]], axis=0)
        right = jnp.concatenate([gm * own[g] for g in range(PER)], axis=0)
        cross = lax.dot_general(
            left, right, (((1,), (1,)), ((), ())), preferred_element_type=F32
        )
        lines = []
        for g in range(PER):
            gs = slice(g * K, (g + 1) * K)
            square = jnp.where(near, cross[K:, gs], jnp.where(far, cross[:K, gs], 0.0))
            turned = pltpu.roll(square, 1, 1, stride=1, stride_axis=0)
            lines.append(jnp.sum(turned, axis=0, keepdims=True))
        stats_ref[pl.ds(pl.multiple_of(q * PER, PER), PER), :] = jnp.concatenate(lines, axis=0)

    each_chunk(cot_ref.shape[1], body)


def gate_kernel(
    len_ref, part_ref, after_ref, bwd_ref, ks_ref, vs_ref, gq_ref,
    gks_ref, gvs_ref, tails_ref,
):
    row = iota((K, LANES), 0)
    col = iota((K, LANES), 1)
    pos = positions(len_ref, first_row() + K + col)
    mask = as_mask((col < row) & (pos >= col - row + K))

    def body(q):
        ls = lanes_of(q)
        grad = part_ref[:, ls] + group_blocks(bwd_ref, q, mask, after_ref[:, ls])
        gks = (grad * vs_ref[:, ls]).astype(BF16)
        gvs = (grad * ks_ref[:, ls]).astype(BF16)
        gks_ref[:, ls] = gks
        gvs_ref[:, ls] = gvs
        tails_ref[0:RIM, ls] = gq_ref[0:RIM, ls]
        tails_ref[RIM : 2 * RIM, ls] = gks[:RIM]
        tails_ref[2 * RIM :, ls] = gvs[:RIM]

    each_chunk(part_ref.shape[1], body)


def shorts_kernel(
    len_ref, q_ref, k_ref, v_ref, rim_ref, taps_ref, gq_ref, gks_ref, gvs_ref, stats_ref,
    oq_ref, ok_ref, ov_ref, sums_ref, cols_ref,
):
    channels = q_ref.shape[1]
    kept = stats_ref.shape[0]
    pos = positions(len_ref, first_row() + iota((K, LANES), 0))
    pad = jnp.zeros((RIM, LANES), F32)

    def body(q):
        ls = lanes_of(q)
        for i, (x_ref, g_ref, o_ref) in enumerate(
            ((q_ref, gq_ref, oq_ref), (k_ref, gks_ref, ok_ref), (v_ref, gvs_ref, ov_ref))
        ):
            ext = extended(rim_ref, i, x_ref, ls)
            taps = tap_rows(taps_ref, i, ls)
            grad = g_ref[:, ls].astype(F32)
            total = taps[0] * grad
            lines = [jnp.sum(grad * ext[RIM:], axis=0, keepdims=True)]
            for j in range(1, KS):
                held = jnp.where(pos >= j, grad, 0.0)
                lines.append(jnp.sum(held * ext[RIM - j : RIM - j + K], axis=0, keepdims=True))
                total = total + taps[j] * jnp.concatenate([held, pad], axis=0)[j : j + K]
            o_ref[:, ls] = total.astype(BF16)
            lines.append(jnp.zeros((8 - KS, LANES), F32))
            cols_ref[i * 8 : i * 8 + 8, ls] = jnp.concatenate(lines, axis=0)

    each_chunk(channels, body)
    sums_ref[0:kept] = stats_ref[...]
    gather = jnp.where(
        iota((channels, LANES), 0) // GS == iota((channels, LANES), 1), 1.0, 0.0
    )
    sums_ref[kept:] = jnp.dot(
        cols_ref[...], gather, preferred_element_type=F32, precision=lax.Precision.HIGHEST
    )


def ends_kernel(
    len_ref, taps_ref, gq_ref, gks_ref, gvs_ref, tails_ref, sums_ref, aq_ref, ak_ref, av_ref,
    oq_ref, ok_ref, ov_ref, short_ref, long_ref, skip_ref, gain_ref,
):
    groups = long_ref.shape[0]
    rows = groups // PER
    pos = positions(len_ref, first_row() + K - RIM + iota((2 * RIM, LANES), 0))

    def body(q):
        ls = lanes_of(q)
        for i, (g_ref, o_ref) in enumerate(((gq_ref, oq_ref), (gks_ref, ok_ref), (gvs_ref, ov_ref))):
            tail = tails_ref[i * RIM : (i + 1) * RIM, ls].astype(F32)
            ext = jnp.concatenate([g_ref[:, ls].astype(F32), tail], axis=0)
            taps = tap_rows(taps_ref, i, ls)
            total = taps[0] * ext[:RIM]
            for j in range(1, KS):
                held = jnp.where(pos >= j, ext, 0.0)
                total = total + taps[j] * held[j : j + RIM]
            o_ref[:, ls] = total.astype(BF16)

    each_chunk(gq_ref.shape[1], body)
    long_ref[...] = sums_ref[:groups]
    skip_ref[...] = sums_ref[groups : groups + rows]
    gain_ref[...] = sums_ref[groups + rows : groups + 2 * rows]
    turned = jnp.concatenate(
        [sums_ref[groups + 2 * rows :], jnp.zeros((LANES - 24, LANES), F32)], axis=0
    ).T
    for i in range(3):
        short_ref[i] = turned[:groups, i * 8 : i * 8 + KS]


def shards(
    q_input, k_input, v_input, resid, lengths, short_filter, long_filter, skip, gain, cotangent
):
    length, channels = q_input.shape
    groups = channels // GS
    wide = channels * lax.axis_size("tp")
    rows = groups // PER

    def arr(shape, dtype):
        return jax.ShapeDtypeStruct(shape, dtype)

    smem = pl.BlockSpec(memory_space=pltpu.SMEM)
    vmem = pl.BlockSpec(memory_space=pltpu.VMEM)
    params = pltpu.CompilerParams(vmem_limit_bytes=32 * 1024 * 1024)
    full_bf = arr((length, channels), BF16)
    full_f = arr((length, channels), F32)

    def call(kernel, outs, ins, scratch=(), flops=0, moved=0, name=None):
        scalar = ins[0] is lengths
        return pl.pallas_call(
            kernel,
            out_shape=outs,
            in_specs=[smem if (i == 0 and scalar) else vmem for i in range(len(ins))],
            out_specs=[vmem] * len(outs),
            scratch_shapes=scratch,
            compiler_params=params,
            cost_estimate=pl.CostEstimate(flops=flops, bytes_accessed=moved, transcendentals=0),
            name=name,
        )(*ins)

    skip2 = skip.reshape(1, channels)
    gain2 = gain.reshape(1, channels)
    last = pl.BlockSpec((RIM, channels), lambda i: (length // RIM - 1, 0))
    left_rows = pl.pallas_call(
        rims_kernel,
        grid=(1,),
        out_shape=arr((3 * RIM, channels), BF16),
        in_specs=[last] * 3,
        out_specs=pl.BlockSpec((3 * RIM, channels), lambda i: (0, 0)),
        name="rims",
    )(q_input, k_input, v_input)
    rims = shifted(left_rows, "ctx", 1)
    taps, fwd, bwd = call(
        tables_kernel,
        [arr((24, channels), F32), arr((groups, K, K), BF16), arr((groups, K, K), BF16)],
        [short_filter, long_filter],
        [pltpu.VMEM((groups, K), F32), pltpu.VMEM((groups, K), F32)],
        flops=10**9, moved=4 * 10**6, name="tables",
    )
    (gated,) = call(
        gated_kernel, [full_bf], [lengths, k_input, v_input, rims, taps],
        flops=10**8, moved=10**6, name="gated",
    )
    before = shifted(gated, "ctx", 1)
    q_short, k_short, v_short, part = call(
        current_kernel, [full_f] * 4,
        [lengths, q_input, k_input, v_input, rims, taps, gated, fwd, skip2],
        flops=10**9, moved=5 * 10**6, name="current",
    )
    mixed, summed, sums = call(
        summed_kernel, [full_f, full_f, arr((2, K), F32)],
        [lengths, before, fwd, part, q_short, resid, cotangent, gain2],
        [pltpu.VMEM((2, K, LANES), F32)],
        flops=10**9, moved=5 * 10**6, name="summed",
    )
    sums = lax.psum(sums, "tp")
    grad_mixed, grad_qs = call(
        functools.partial(grads_kernel, wide), [full_bf, full_bf],
        [summed, mixed, q_short, cotangent, gain2, sums],
        flops=10**8, moved=2 * 10**6, name="grads",
    )
    after = shifted(grad_mixed, "ctx", -1)
    normed, stats, part = call(
        functools.partial(beside_kernel, wide),
        [full_bf, arr((groups + 2 * rows, LANES), F32), full_f],
        [lengths, summed, cotangent, gain2, sums, grad_mixed, gated, before, bwd, skip2],
        flops=4 * 10**9, moved=5 * 10**6, name="beside",
    )
    grad_ks, grad_vs, tails = call(
        gate_kernel, [full_bf, full_bf, arr((3 * RIM, channels), BF16)],
        [lengths, part, after, bwd, k_short, v_short, grad_qs],
        flops=10**9, moved=5 * 10**6, name="gate",
    )
    tails = shifted(tails, "ctx", -1)
    grad_q, grad_k, grad_v, packed = call(
        shorts_kernel,
        [full_bf, full_bf, full_bf, arr((groups + 2 * rows + 24, LANES), F32)],
        [lengths, q_input, k_input, v_input, rims, taps, grad_qs, grad_ks, grad_vs, stats],
        [pltpu.VMEM((24, channels), F32)],
        flops=10**9, moved=5 * 10**6, name="shorts",
    )
    packed = lax.psum(packed, "ctx")
    whole = lambda *shape: pl.BlockSpec(shape, lambda i: (0,) * len(shape))
    grad_q, grad_k, grad_v, grad_short, grad_long, grad_skip, grad_gain = pl.pallas_call(
        ends_kernel,
        grid=(1,),
        out_shape=[
            full_bf, full_bf, full_bf,
            arr((3, groups, KS), F32), arr((groups, K), F32),
            arr((rows, LANES), F32), arr((rows, LANES), F32),
        ],
        in_specs=[smem, whole(24, channels)] + [last] * 3
        + [whole(3 * RIM, channels), whole(*packed.shape)]
        + [pl.BlockSpec(memory_space=pl.ANY)] * 3,
        out_specs=[last] * 3
        + [whole(3, groups, KS), whole(groups, K), whole(rows, LANES), whole(rows, LANES)],
        input_output_aliases={7: 0, 8: 1, 9: 2},
        name="ends",
    )(lengths, taps, grad_qs, grad_ks, grad_vs, tails, packed, grad_q, grad_k, grad_v)
    return (
        normed, grad_q, grad_k, grad_v, grad_short, grad_long,
        grad_skip.reshape(channels), grad_gain.reshape(channels),
    )


def solution(mesh):
    tiled = P("ctx", "tp")
    return jax.shard_map(
        shards,
        mesh=mesh,
        in_specs=(
            tiled, tiled, tiled, tiled, P(), P(None, "tp", None), P("tp", None), P("tp"), P("tp"),
            tiled,
        ),
        out_specs=(
            tiled, tiled, tiled, tiled, P(None, "tp", None), P("tp", None), P("tp"), P("tp"),
        ),
        check_vma=False,
    )
```

```python
import functools

import jax
import jax.numpy as jnp
from jax import lax
from jax.experimental import pallas as pl
from jax.experimental.pallas import tpu as pltpu
from jax.sharding import PartitionSpec as P

GS = 16
K = 128
KS = 7
LANES = 128
PER = LANES // GS
RIM = 16
EPS = 1e-06
F32 = jnp.float32
BF16 = jnp.bfloat16


def shifted(x, axis, by):
    count = lax.axis_size(axis)
    pairs = [(i, i + by) for i in range(count) if 0 <= i + by < count]
    return lax.ppermute(x, axis, pairs)


def iota(shape, dim):
    return lax.broadcasted_iota(jnp.int32, shape, dim)


def positions(len_ref, rows):
    begin = jnp.zeros_like(rows)
    start = jnp.int32(0)
    for n in range(len_ref.shape[0]):
        begin = jnp.where(rows >= start, start, begin)
        start = start + len_ref[n]
    return rows - begin


def first_row():
    return lax.axis_index("ctx") * K


def lanes_of(q):
    return pl.ds(pl.multiple_of(q * LANES, LANES), LANES)


def each_chunk(channels, body, unroll=2):
    def step(q, carry):
        body(q)
        return carry

    lax.fori_loop(0, channels // LANES, step, 0, unroll=unroll)


def as_mask(cond):
    return jnp.where(cond, 1.0, 0.0).astype(BF16)


def join(*parts):
    return jnp.concatenate(parts, axis=0)


def tap_rows(taps_ref, which, ls):
    table = taps_ref[which * 8 : which * 8 + 8, ls]
    return [table[j : j + 1, :] for j in range(KS)]


def causal(ext, taps, pos):
    rows = ext.shape[0] - RIM
    total = taps[0] * ext[RIM:]
    for j in range(1, KS):
        moved = ext[RIM - j : RIM - j + rows]
        total = total + taps[j] * jnp.where(pos >= j, moved, 0.0)
    return total


def tap_lines(grad, ext, pos):
    lines = [jnp.sum(grad * ext[RIM:], axis=0, keepdims=True)]
    for j in range(1, KS):
        held = jnp.where(pos >= j, grad, 0.0)
        lines.append(jnp.sum(held * ext[RIM - j : RIM - j + K], axis=0, keepdims=True))
    lines.append(jnp.zeros((8 - KS, LANES), F32))
    return join(*lines)


def group_blocks(left, right):
    full = jnp.dot(
        left.reshape(PER * K, left.shape[2]), right, preferred_element_type=F32
    ).reshape(PER, K, LANES)
    group = iota((K, LANES), 1) // GS
    out = full[0]
    for g in range(1, PER):
        out = jnp.where(group == g, full[g], out)
    return out


BULK = K - RIM
Q_LAST, K_LAST, V_LAST, K_FIRST, V_FIRST = (BULK + i * RIM for i in range(5))
SENT = BULK + 5 * RIM


def rim_of(ref, at, ls):
    return ref[at : at + RIM, ls].astype(F32)


def first_kernel(len_ref, short_ref, q_ref, k_ref, v_ref, taps_ref, sent_ref, far_ref):
    groups = short_ref.shape[2]
    channels = taps_ref.shape[1]
    spread = as_mask(iota((groups, channels), 1) // GS == iota((groups, channels), 0))
    for i in range(3):
        taps_ref[i * 8 : i * 8 + KS] = jnp.dot(
            short_ref[i], spread, preferred_element_type=F32
        )
        taps_ref[i * 8 + KS : i * 8 + 8] = jnp.zeros((8 - KS, channels), F32)
    pos = positions(len_ref, first_row() + RIM + iota((BULK, LANES), 0))
    end = slice(K - RIM, K)

    def body(q):
        ls = lanes_of(q)
        ks = causal(k_ref[:, ls].astype(F32), tap_rows(taps_ref, 1, ls), pos)
        vs = causal(v_ref[:, ls].astype(F32), tap_rows(taps_ref, 2, ls), pos)
        sent_ref[:BULK, ls] = (ks * vs).astype(BF16)

    each_chunk(channels, body)
    sent_ref[Q_LAST : Q_LAST + RIM] = q_ref[end]
    sent_ref[K_LAST : K_LAST + RIM] = k_ref[end]
    sent_ref[V_LAST : V_LAST + RIM] = v_ref[end]
    sent_ref[K_FIRST : K_FIRST + RIM] = k_ref[:RIM]
    sent_ref[V_FIRST : V_FIRST + RIM] = v_ref[:RIM]
    far_ref[:RIM] = k_ref[end]
    far_ref[RIM:] = v_ref[end]


def circulant_kernel(turned, long_ref, out_ref, line_ref):
    groups = long_ref.shape[0]
    filt = long_ref[...]
    if turned:
        flip = as_mask((iota((K, K), 0) + iota((K, K), 1)) % K == 0)
        line_ref[...] = jnp.dot(filt, flip, preferred_element_type=F32)
    else:
        line_ref[...] = filt.astype(F32)

    def step(g, carry):
        row = jnp.broadcast_to(line_ref[pl.ds(g, 1), :], (GS, K))
        block = pltpu.roll(row, 0, 1, stride=1, stride_axis=0)
        for i in range(K // GS):
            moved = block if i == 0 else pltpu.roll(block, i * GS, 1)
            out_ref[g, i * GS : (i + 1) * GS] = moved.astype(BF16)
        return carry

    lax.fori_loop(0, groups, step, 0, unroll=8)


def current_kernel(len_ref, q_ref, taps_ref, sent_ref, fwd_ref, skip_ref, qs_ref, part_ref):
    row = iota((K, LANES), 0)
    col = iota((K, LANES), 1)
    pos = positions(len_ref, first_row() + row)
    mask = as_mask((col <= row) & (pos >= row - col))
    top = jnp.zeros((RIM, LANES), BF16)

    def body(q):
        ls = lanes_of(q)
        qs_ref[RIM:, ls] = causal(q_ref[:, ls].astype(F32), tap_rows(taps_ref, 0, ls), pos[RIM:])
        qs_ref[:RIM, ls] = jnp.zeros((RIM, LANES), F32)
        gated = join(top, sent_ref[:BULK, ls])
        left = fwd_ref[pl.ds(q * PER, PER)] * mask[None]
        part_ref[:, ls] = group_blocks(left, gated) + skip_ref[:, ls] * gated.astype(F32)

    each_chunk(q_ref.shape[1], body)


def summed_kernel(
    len_ref, came_ref, far_ref, q_ref, k_ref, v_ref, taps_ref, sent_ref, fwd_ref, bulk_ref,
    part_ref, skip_ref, resid_ref, cot_ref, gain_ref,
    qs_ref, gated_ref, before_ref, mixed_ref, summed_ref, sums_ref, acc_ref,
):
    row = iota((K, LANES), 0)
    col = iota((K, LANES), 1)
    pos = positions(len_ref, first_row() + row)
    far = as_mask((col > row) & (pos >= row - col + K))
    near = as_mask((col <= row) & (col < RIM) & (pos >= row - col))
    pos_top = pos[:RIM]
    pos_far = positions(len_ref, first_row() - K + iota((RIM, LANES), 0))
    rest = jnp.zeros((K - RIM, LANES), BF16)
    acc_ref[...] = jnp.zeros_like(acc_ref)

    def body(q):
        ls = lanes_of(q)
        kt = tap_rows(taps_ref, 1, ls)
        vt = tap_rows(taps_ref, 2, ls)
        k_last = rim_of(came_ref, K_LAST, ls)
        v_last = rim_of(came_ref, V_LAST, ls)
        top = (
            causal(join(k_last, rim_of(k_ref, 0, ls)), kt, pos_top)
            * causal(join(v_last, rim_of(v_ref, 0, ls)), vt, pos_top)
        ).astype(BF16)
        far_top = (
            causal(join(rim_of(far_ref, 0, ls), rim_of(came_ref, K_FIRST, ls)), kt, pos_far)
            * causal(join(rim_of(far_ref, RIM, ls), rim_of(came_ref, V_FIRST, ls)), vt, pos_far)
        ).astype(BF16)
        qs_top = causal(
            join(rim_of(came_ref, Q_LAST, ls), rim_of(q_ref, 0, ls)), tap_rows(taps_ref, 0, ls), pos_top
        )
        before = join(far_top, came_ref[:BULK, ls])
        before_ref[:, ls] = before
        gated_ref[:, ls] = join(top, sent_ref[:BULK, ls])
        qs = join(qs_top, bulk_ref[RIM:, ls])
        qs_ref[:, ls] = qs
        table = fwd_ref[pl.ds(q * PER, PER)]
        left = jnp.concatenate([table * far[None], table * near[None]], axis=2)
        direct = join(skip_ref[:, ls] * top.astype(F32), jnp.zeros((K - RIM, LANES), F32))
        mixed = part_ref[:, ls] + direct + group_blocks(left, join(before, top, rest))
        summed = resid_ref[:, ls].astype(F32) + qs * mixed
        mixed_ref[:, ls] = mixed
        summed_ref[:, ls] = summed
        acc_ref[0] += summed * summed
        acc_ref[1] += gain_ref[:, ls] * cot_ref[:, ls].astype(F32) * summed

    each_chunk(resid_ref.shape[1], body)
    for i in range(2):
        sums_ref[i : i + 1] = jnp.sum(acc_ref[i].T, axis=0, keepdims=True)


def by_row(line):
    return jnp.broadcast_to(line, (K, K)).T


def inverse_of(sums_ref, total):
    return by_row(lax.rsqrt(sums_ref[0:1] / total + EPS))


def grads_kernel(total, summed_ref, mixed_ref, qs_ref, cot_ref, gain_ref, sums_ref, gm_ref, gq_ref):
    inverse = inverse_of(sums_ref, total)
    scale = inverse * inverse * by_row(sums_ref[1:2] / total)

    def body(q):
        ls = lanes_of(q)
        scaled = gain_ref[:, ls] * cot_ref[:, ls].astype(F32)
        grad_sum = inverse * (scaled - summed_ref[:, ls] * scale)
        gm_ref[:, ls] = (grad_sum * qs_ref[:, ls]).astype(BF16)
        gq_ref[:, ls] = (grad_sum * mixed_ref[:, ls]).astype(BF16)

    each_chunk(cot_ref.shape[1], body)


def beside_kernel(
    total, len_ref, summed_ref, cot_ref, gain_ref, sums_ref, gm_ref, gq_ref, gated_ref, before_ref,
    bwd_ref, skip_ref, q_ref, k_ref, v_ref, came_ref, taps_ref,
    normed_ref, stats_ref, part_ref, ks_ref, vs_ref, cols_ref,
):
    groups = bwd_ref.shape[0]
    inverse = inverse_of(sums_ref, total)
    row = iota((K, LANES), 0)
    col = iota((K, LANES), 1)
    pos_row = positions(len_ref, first_row() + row)
    pos = positions(len_ref, first_row() + col)
    mask = as_mask((col >= row) & (pos >= col - row))
    source = K - 1 - row
    near = (col >= source) & (pos >= col - source)
    far = (col < source) & (pos >= col - source + K)
    flip = as_mask(row + col == K - 1)
    own = [as_mask(col // GS == g) for g in range(PER)]

    def body(q):
        ls = lanes_of(q)
        summed = summed_ref[:, ls]
        normed_ref[:, ls] = (gain_ref[:, ls] * summed * inverse).astype(BF16)
        gm = gm_ref[:, ls]
        gmf = gm.astype(F32)
        gated = gated_ref[:, ls]
        stats_ref[pl.ds(groups + q, 1), :] = jnp.sum(gmf * gated.astype(F32), axis=0, keepdims=True)
        stats_ref[pl.ds(groups + groups // PER + q, 1), :] = jnp.sum(
            cot_ref[:, ls].astype(F32) * summed * inverse, axis=0, keepdims=True
        )
        left = bwd_ref[pl.ds(q * PER, PER)] * mask[None]
        part_ref[:, ls] = skip_ref[:, ls] * gmf + group_blocks(left, gm)
        two = jnp.concatenate([before_ref[:, ls], gated], axis=1)
        flipped = jnp.dot(flip, two, preferred_element_type=F32).astype(BF16)
        left = join(flipped[:, :LANES], flipped[:, LANES:])
        right = join(*[gm * own[g] for g in range(PER)])
        cross = lax.dot_general(
            left, right, (((1,), (1,)), ((), ())), preferred_element_type=F32
        )
        lines = []
        for g in range(PER):
            gs = slice(g * K, (g + 1) * K)
            square = jnp.where(near, cross[K:, gs], jnp.where(far, cross[:K, gs], 0.0))
            turned = pltpu.roll(square, 1, 1, stride=1, stride_axis=0)
            lines.append(jnp.sum(turned, axis=0, keepdims=True))
        stats_ref[pl.ds(pl.multiple_of(q * PER, PER), PER), :] = join(*lines)
        k_ext = join(rim_of(came_ref, K_LAST, ls), k_ref[:, ls].astype(F32))
        v_ext = join(rim_of(came_ref, V_LAST, ls), v_ref[:, ls].astype(F32))
        q_ext = join(rim_of(came_ref, Q_LAST, ls), q_ref[:, ls].astype(F32))
        ks_ref[:, ls] = causal(k_ext, tap_rows(taps_ref, 1, ls), pos_row)
        vs_ref[:, ls] = causal(v_ext, tap_rows(taps_ref, 2, ls), pos_row)
        cols_ref[:, ls] = tap_lines(gq_ref[:, ls].astype(F32), q_ext, pos_row)

    each_chunk(cot_ref.shape[1], body, 1)


def gate_kernel(
    len_ref, part_ref, after_ref, bwd_ref, ks_ref, vs_ref, gq_ref, k_ref, v_ref, came_ref,
    stats_ref, qcols_ref, gks_ref, gvs_ref, tails_ref, packed_ref, cols_ref,
):
    channels = part_ref.shape[1]
    kept = stats_ref.shape[0]
    row = iota((K, LANES), 0)
    col = iota((K, LANES), 1)
    pos_row = positions(len_ref, first_row() + row)
    pos = positions(len_ref, first_row() + K + col)
    mask = as_mask((col < row) & (pos >= col - row + K))

    def body(q):
        ls = lanes_of(q)
        left = bwd_ref[pl.ds(q * PER, PER)] * mask[None]
        grad = part_ref[:, ls] + group_blocks(left, after_ref[:, ls])
        gks = (grad * vs_ref[:, ls]).astype(BF16)
        gvs = (grad * ks_ref[:, ls]).astype(BF16)
        gks_ref[:, ls] = gks
        gvs_ref[:, ls] = gvs
        tails_ref[0:RIM, ls] = gq_ref[0:RIM, ls]
        tails_ref[RIM : 2 * RIM, ls] = gks[:RIM]
        tails_ref[2 * RIM :, ls] = gvs[:RIM]
        k_ext = join(rim_of(came_ref, K_LAST, ls), k_ref[:, ls].astype(F32))
        v_ext = join(rim_of(came_ref, V_LAST, ls), v_ref[:, ls].astype(F32))
        cols_ref[0:8, ls] = qcols_ref[:, ls]
        cols_ref[8:16, ls] = tap_lines(gks.astype(F32), k_ext, pos_row)
        cols_ref[16:24, ls] = tap_lines(gvs.astype(F32), v_ext, pos_row)

    each_chunk(channels, body)
    packed_ref[0:kept] = stats_ref[...]
    gather = jnp.where(
        iota((channels, LANES), 0) // GS == iota((channels, LANES), 1), 1.0, 0.0
    )
    packed_ref[kept:] = jnp.dot(
        cols_ref[...], gather, preferred_element_type=F32, precision=lax.Precision.HIGHEST
    )


def mains_kernel(
    len_ref, taps_ref, gq_ref, gks_ref, gvs_ref, tails_ref, oq_ref, ok_ref, ov_ref
):
    pos = positions(len_ref, first_row() + iota((K + RIM, LANES), 0))

    def body(q):
        ls = lanes_of(q)
        for i, (g_ref, o_ref) in enumerate(((gq_ref, oq_ref), (gks_ref, ok_ref), (gvs_ref, ov_ref))):
            ext = join(g_ref[:, ls].astype(F32), rim_of(tails_ref, i * RIM, ls))
            taps = tap_rows(taps_ref, i, ls)
            total = taps[0] * ext[:K]
            for j in range(1, KS):
                held = jnp.where(pos >= j, ext, 0.0)
                total = total + taps[j] * held[j : j + K]
            o_ref[:, ls] = total.astype(BF16)

    each_chunk(gq_ref.shape[1], body)


def unpack_kernel(one_ref, two_ref, short_ref, long_ref, skip_ref, gain_ref):
    groups = long_ref.shape[0]
    rows = groups // PER
    total = one_ref[...] + two_ref[...]
    long_ref[...] = total[:groups]
    skip_ref[...] = total[groups : groups + rows]
    gain_ref[...] = total[groups + rows : groups + 2 * rows]
    for i in range(3):
        at = groups + 2 * rows + i * 8
        short_ref[i] = total[at : at + KS, :groups]


def shards(
    q_input, k_input, v_input, resid, lengths, short_filter, long_filter, skip, gain, cotangent
):
    length, channels = q_input.shape
    groups = channels // GS
    wide = channels * lax.axis_size("tp")
    rows = groups // PER

    def arr(shape, dtype):
        return jax.ShapeDtypeStruct(shape, dtype)

    smem = pl.BlockSpec(memory_space=pltpu.SMEM)
    vmem = pl.BlockSpec(memory_space=pltpu.VMEM)
    full_bf = arr((length, channels), BF16)
    full_f = arr((length, channels), F32)

    def call(name, kernel, outs, ins, scratch=(), flops=10**8, moved=10**6, grant=8):
        scalar = ins[0] is lengths
        return pl.pallas_call(
            kernel,
            out_shape=outs,
            in_specs=[smem if (i == 0 and scalar) else vmem for i in range(len(ins))],
            out_specs=[vmem] * len(outs),
            scratch_shapes=scratch,
            compiler_params=pltpu.CompilerParams(vmem_limit_bytes=grant * 1024 * 1024),
            cost_estimate=pl.CostEstimate(flops=flops, bytes_accessed=moved, transcendentals=0),
            name=name,
        )(*ins)

    skip2 = skip.reshape(1, channels)
    gain2 = gain.reshape(1, channels)
    taps, sent, far = call(
        "first", first_kernel,
        [arr((24, channels), F32), arr((SENT, channels), BF16), arr((2 * RIM, channels), BF16)],
        [lengths, jnp.transpose(short_filter, (0, 2, 1)), q_input, k_input, v_input],
    )
    came = shifted(sent, "ctx", 1)
    came_far = shifted(far, "ctx", 2)

    def circulants(filt, turned):
        return call(
            "circulants", functools.partial(circulant_kernel, turned),
            [arr((groups, K, K), BF16)], [filt], [pltpu.VMEM((groups, K), F32)],
            flops=10**9, moved=4 * 10**6,
        )[0]

    filt, sent = lax.optimization_barrier((long_filter, sent))
    fwd = circulants(filt, True)
    bulk, part = call(
        "current", current_kernel, [full_f] * 2,
        [lengths, q_input, taps, sent, fwd, skip2], flops=10**9, moved=5 * 10**6,
    )
    q_short, gated, before, mixed, summed, sums = call(
        "summed", summed_kernel,
        [full_f, full_bf, full_bf, full_f, full_f, arr((2, K), F32)],
        [
            lengths, came, came_far, q_input, k_input, v_input, taps, sent, fwd, bulk,
            part, skip2, resid, cotangent, gain2,
        ],
        [pltpu.VMEM((2, K, LANES), F32)], flops=10**9, moved=5 * 10**6,
    )
    sums = lax.psum(sums, "tp")
    grad_mixed, grad_qs = call(
        "grads", functools.partial(grads_kernel, wide), [full_bf, full_bf],
        [summed, mixed, q_short, cotangent, gain2, sums],
    )
    after = shifted(grad_mixed, "ctx", -1)
    filt, grad_mixed = lax.optimization_barrier((long_filter, grad_mixed))
    bwd = circulants(filt, False)
    normed, stats, part, k_short, v_short, qcols = call(
        "beside", functools.partial(beside_kernel, wide),
        [
            full_bf, arr((groups + 2 * rows, LANES), F32), full_f, full_f, full_f,
            arr((8, channels), F32),
        ],
        [
            lengths, summed, cotangent, gain2, sums, grad_mixed, grad_qs, gated, before,
            bwd, skip2, q_input, k_input, v_input, came, taps,
        ],
        flops=4 * 10**9, moved=5 * 10**6,
    )
    grad_ks, grad_vs, tails, packed = call(
        "gate", gate_kernel,
        [
            full_bf, full_bf, arr((3 * RIM, channels), BF16),
            arr((groups + 2 * rows + 24, LANES), F32),
        ],
        [
            lengths, part, after, bwd, k_short, v_short, grad_qs, k_input, v_input, came,
            stats, qcols,
        ],
        [pltpu.VMEM((24, channels), F32)], flops=10**9, moved=5 * 10**6,
    )
    tails = shifted(tails, "ctx", -1)
    grad_q, grad_k, grad_v = call(
        "mains", mains_kernel, [full_bf] * 3,
        [lengths, taps, grad_qs, grad_ks, grad_vs, tails], flops=10**9, moved=5 * 10**6,
    )
    count = lax.axis_size("ctx")
    step = 1
    while step < count:
        if step > 1:
            packed = packed + other
        other = lax.ppermute(packed, "ctx", [(i, i ^ step) for i in range(count)])
        step *= 2
    grad_short, grad_long, grad_skip, grad_gain = call(
        "unpack", unpack_kernel,
        [
            arr((3, KS, groups), F32), arr((groups, K), F32),
            arr((rows, LANES), F32), arr((rows, LANES), F32),
        ],
        [packed, other],
    )
    return (
        normed, grad_q, grad_k, grad_v, jnp.transpose(grad_short, (0, 2, 1)), grad_long,
        grad_skip.reshape(channels), grad_gain.reshape(channels),
    )


def solution(mesh):
    tiled = P("ctx", "tp")
    return jax.shard_map(
        shards,
        mesh=mesh,
        in_specs=(
            tiled, tiled, tiled, tiled, P(), P(None, "tp", None), P("tp", None), P("tp"), P("tp"),
            tiled,
        ),
        out_specs=(
            tiled, tiled, tiled, tiled, P(None, "tp", None), P("tp", None), P("tp"), P("tp"),
        ),
        check_vma=False,
    )
```

```python
import functools

import jax
import jax.numpy as jnp
from jax import lax
from jax.experimental import pallas as pl
from jax.experimental.pallas import tpu as pltpu
from jax.sharding import PartitionSpec as P

GS = 16
K = 128
KS = 7
LANES = 128
PER = LANES // GS
RIM = 8
PACK = 16
EPS = 1e-06
F32 = jnp.float32
BF16 = jnp.bfloat16


def shifted(x, axis, by):
    count = lax.axis_size(axis)
    pairs = [(i, i + by) for i in range(count) if 0 <= i + by < count]
    return lax.ppermute(x, axis, pairs)


def iota(shape, dim):
    return lax.broadcasted_iota(jnp.int32, shape, dim)


def positions(len_ref, rows):
    begin = jnp.zeros_like(rows)
    start = jnp.int32(0)
    for n in range(len_ref.shape[0]):
        begin = jnp.where(rows >= start, start, begin)
        start = start + len_ref[n]
    return rows - begin


def first_row():
    return lax.axis_index("ctx") * K


def lanes_of(q):
    return pl.ds(pl.multiple_of(q * LANES, LANES), LANES)


def each_chunk(channels, body, unroll=2):
    def step(q, carry):
        body(q)
        return carry

    lax.fori_loop(0, channels // LANES, step, 0, unroll=unroll)


def as_mask(cond):
    return jnp.where(cond, 1.0, 0.0).astype(BF16)


def join(*parts):
    return jnp.concatenate(parts, axis=0)


def tap_rows(taps_ref, which, ls):
    table = taps_ref[which * 8 : which * 8 + 8, ls]
    return [table[j : j + 1, :] for j in range(KS)]


def causal(ext, taps, pos):
    rows = ext.shape[0] - RIM
    total = taps[0] * ext[RIM:]
    for j in range(1, KS):
        moved = ext[RIM - j : RIM - j + rows]
        total = total + taps[j] * jnp.where(pos >= j, moved, 0.0)
    return total


def tap_lines(grad, ext, pos):
    lines = [jnp.sum(grad * ext[RIM:], axis=0, keepdims=True)]
    for j in range(1, KS):
        held = jnp.where(pos >= j, grad, 0.0)
        lines.append(jnp.sum(held * ext[RIM - j : RIM - j + K], axis=0, keepdims=True))
    lines.append(jnp.zeros((8 - KS, LANES), F32))
    return join(*lines)


def owners():
    lane = iota((K, LANES), 1) // GS
    return [as_mask(lane == g) for g in range(PER)]


def per_group(right, own):
    return join(*[right * mask for mask in own])


def masked(table_ref, q, mask):
    table = table_ref[:, pl.ds(pl.multiple_of(q * PER * K, PER * K), PER * K)]
    return [table[:, g * K : (g + 1) * K] * mask for g in range(PER)]


def product(left, right):
    return jnp.dot(jnp.concatenate(left, axis=1), right, preferred_element_type=F32)


K_FIRST, Q_LAST, K_LAST, V_LAST, V_FIRST, SENT = 0, K, K + 8, K + 16, K + 24, K + 32


def rim_of(ref, at, ls):
    base = at // PACK * PACK
    return ref[base : base + PACK, ls].astype(F32)[at - base : at - base + RIM]


def first_kernel(
    len_hbm, short_hbm, q_hbm, k_hbm, v_hbm, taps_ref, sent_ref, far_ref,
    len_ref, short_ref, q_ref, k_ref, v_ref, sems,
):
    groups = short_ref.shape[2]
    channels = taps_ref.shape[1]
    pairs = (
        (short_hbm, short_ref), (len_hbm, len_ref), (k_hbm, k_ref), (v_hbm, v_ref),
        (q_hbm.at[K - PACK : K], q_ref),
    )
    copies = [pltpu.make_async_copy(a, b, sems.at[i]) for i, (a, b) in enumerate(pairs)]
    for copy in copies:
        copy.start()
    spread = as_mask(iota((groups, channels), 1) // GS == iota((groups, channels), 0))
    copies[0].wait()
    for i in range(3):
        taps_ref[i * 8 : i * 8 + KS] = jnp.dot(
            short_ref[i], spread, preferred_element_type=F32
        )
        taps_ref[i * 8 + KS : i * 8 + 8] = jnp.zeros((8 - KS, channels), F32)
    for copy in copies[1:]:
        copy.wait()
    pos = positions(len_ref, first_row() + RIM + iota((K - RIM, LANES), 0))

    def body(q):
        ls = lanes_of(q)
        kx = k_ref[:, ls].astype(F32)
        vx = v_ref[:, ls].astype(F32)
        ks = causal(kx, tap_rows(taps_ref, 1, ls), pos)
        vs = causal(vx, tap_rows(taps_ref, 2, ls), pos)
        sent_ref[:K, ls] = join(kx[:RIM], ks * vs).astype(BF16)
        q_end = q_ref[:, ls].astype(F32)[PACK - RIM :]
        k_end = kx[K - RIM :]
        v_end = vx[K - RIM :]
        sent_ref[K:, ls] = join(q_end, k_end, v_end, vx[:RIM]).astype(BF16)
        far_ref[:, ls] = join(k_end, v_end).astype(BF16)

    each_chunk(channels, body)


def circulant_kernel(turned, long_ref, out_ref, line_ref):
    groups = long_ref.shape[0]
    filt = long_ref[...]
    if turned:
        flip = as_mask((iota((K, K), 0) + iota((K, K), 1)) % K == 0)
        line_ref[...] = jnp.dot(filt, flip, preferred_element_type=F32)
    else:
        line_ref[...] = filt.astype(F32)

    def step(g, carry):
        row = jnp.broadcast_to(line_ref[pl.ds(g, 1), :], (GS, K))
        block = pltpu.roll(row, 0, 1, stride=1, stride_axis=0)
        for i in range(K // GS):
            moved = block if i == 0 else pltpu.roll(block, i * GS, 1)
            at = pl.ds(pl.multiple_of(g * K, K), K)
            out_ref[i * GS : (i + 1) * GS, at] = moved.astype(BF16)
        return carry

    lax.fori_loop(0, groups, step, 0, unroll=8)


def current_kernel(
    len_ref, q_ref, taps_ref, sent_ref, fwd_ref, skip_ref, qs_ref, part_ref, top_ref
):
    row = iota((K, LANES), 0)
    col = iota((K, LANES), 1)
    pos = positions(len_ref, first_row() + row)
    near = (col <= row) & (pos >= row - col)
    mask = as_mask(near)
    mask_top = as_mask(near & (col < RIM))
    picks = join(*[as_mask((col == row + g * GS) & (row < GS)) for g in range(PER)])
    own = owners()
    top = jnp.zeros((RIM, LANES), F32)

    def body(q):
        ls = lanes_of(q)
        qs_ref[RIM:, ls] = causal(q_ref[:, ls].astype(F32), tap_rows(taps_ref, 0, ls), pos[RIM:])
        qs_ref[:RIM, ls] = top
        gated = join(top, sent_ref[:K, ls].astype(F32)[RIM:])
        rest = product(masked(fwd_ref, q, mask), per_group(gated.astype(BF16), own))
        part_ref[:, ls] = rest + skip_ref[:, ls] * gated
        top_ref[:, ls] = product(masked(fwd_ref, q, mask_top), picks).astype(BF16)

    each_chunk(q_ref.shape[1], body)


def summed_kernel(
    len_ref, came_ref, far_ref, q_ref, k_ref, v_ref, taps_ref, sent_ref, fwd_ref, top_ref,
    bulk_ref, part_ref, skip_ref, resid_ref, cot_ref, gain_ref,
    qs_ref, gated_ref, before_ref, mixed_ref, summed_ref, sums_ref, acc_ref,
):
    row = iota((K, LANES), 0)
    col = iota((K, LANES), 1)
    pos = positions(len_ref, first_row() + row)
    mask = as_mask((col > row) & (pos >= row - col + K))
    pos_top = pos[:RIM]
    pos_far = positions(len_ref, first_row() - K + iota((RIM, LANES), 0))
    own = owners()
    own_top = [
        as_mask((iota((PACK, LANES), 1) // GS == g) & (iota((PACK, LANES), 0) < RIM))
        for g in range(PER)
    ]
    acc_ref[...] = jnp.zeros_like(acc_ref)

    def body(q):
        ls = lanes_of(q)
        kt = tap_rows(taps_ref, 1, ls)
        vt = tap_rows(taps_ref, 2, ls)
        k_last = rim_of(came_ref, K_LAST, ls)
        v_last = rim_of(came_ref, V_LAST, ls)
        top = causal(join(k_last, rim_of(k_ref, 0, ls)), kt, pos_top) * causal(
            join(v_last, rim_of(v_ref, 0, ls)), vt, pos_top
        )
        far_top = causal(
            join(rim_of(far_ref, 0, ls), rim_of(came_ref, K_FIRST, ls)), kt, pos_far
        ) * causal(join(rim_of(far_ref, RIM, ls), rim_of(came_ref, V_FIRST, ls)), vt, pos_far)
        qs_top = causal(
            join(rim_of(came_ref, Q_LAST, ls), rim_of(q_ref, 0, ls)), tap_rows(taps_ref, 0, ls), pos_top
        )
        before = join(far_top, came_ref[:K, ls].astype(F32)[RIM:]).astype(BF16)
        gated = join(top, sent_ref[:K, ls].astype(F32)[RIM:]).astype(BF16)
        before_ref[:, ls] = before
        gated_ref[:, ls] = gated
        qs = join(qs_top, bulk_ref[RIM:, ls])
        qs_ref[:, ls] = qs
        first = gated[:PACK]
        left = masked(fwd_ref, q, mask) + [top_ref[:, ls]]
        right = join(per_group(before, own), per_group(first, own_top))
        direct = skip_ref[:, ls] * first.astype(F32)[:RIM]
        mixed = part_ref[:, ls] + product(left, right)
        mixed = join(mixed[:RIM] + direct, mixed[RIM:])
        summed = resid_ref[:, ls].astype(F32) + qs * mixed
        mixed_ref[:, ls] = mixed
        summed_ref[:, ls] = summed
        acc_ref[0] += summed * summed
        acc_ref[1] += gain_ref[:, ls] * cot_ref[:, ls].astype(F32) * summed

    each_chunk(resid_ref.shape[1], body)
    for i in range(2):
        sums_ref[i : i + 1] = jnp.sum(acc_ref[i].T, axis=0, keepdims=True)


def by_row(line):
    return jnp.broadcast_to(line, (K, K)).T


def inverse_of(sums_ref, total):
    return by_row(lax.rsqrt(sums_ref[0:1] / total + EPS))


def grads_kernel(total, summed_ref, mixed_ref, qs_ref, cot_ref, gain_ref, sums_ref, gm_ref, gq_ref):
    inverse = inverse_of(sums_ref, total)
    scale = inverse * inverse * by_row(sums_ref[1:2] / total)

    def body(q):
        ls = lanes_of(q)
        scaled = gain_ref[:, ls] * cot_ref[:, ls].astype(F32)
        grad_sum = inverse * (scaled - summed_ref[:, ls] * scale)
        gm_ref[:, ls] = (grad_sum * qs_ref[:, ls]).astype(BF16)
        gq_ref[:, ls] = (grad_sum * mixed_ref[:, ls]).astype(BF16)

    each_chunk(cot_ref.shape[1], body)


def beside_kernel(
    total, len_ref, summed_ref, cot_ref, sums_ref, gm_ref, gq_ref, gated_ref, before_ref,
    bwd_ref, skip_ref, q_ref, k_ref, v_ref, came_ref, taps_ref,
    stats_ref, part_ref, ks_ref, vs_ref, cols_ref,
):
    groups = bwd_ref.shape[1] // K
    inverse = inverse_of(sums_ref, total)
    row = iota((K, LANES), 0)
    col = iota((K, LANES), 1)
    pos_row = positions(len_ref, first_row() + row)
    pos = positions(len_ref, first_row() + col)
    mask = as_mask((col >= row) & (pos >= col - row))
    source = K - 1 - row
    near = (col >= source) & (pos >= col - source)
    far = (col < source) & (pos >= col - source + K)
    flip = as_mask(row + col == K - 1)
    own = owners()

    def body(q):
        ls = lanes_of(q)
        summed = summed_ref[:, ls]
        gm = gm_ref[:, ls]
        gmf = gm.astype(F32)
        gated = gated_ref[:, ls]
        stats_ref[pl.ds(groups + q, 1), :] = jnp.sum(gmf * gated.astype(F32), axis=0, keepdims=True)
        stats_ref[pl.ds(groups + groups // PER + q, 1), :] = jnp.sum(
            cot_ref[:, ls].astype(F32) * summed * inverse, axis=0, keepdims=True
        )
        right = per_group(gm, own)
        part_ref[:, ls] = skip_ref[:, ls] * gmf + product(masked(bwd_ref, q, mask), right)
        two = jnp.concatenate([before_ref[:, ls], gated], axis=1)
        flipped = jnp.dot(flip, two, preferred_element_type=F32).astype(BF16)
        left = join(flipped[:, :LANES], flipped[:, LANES:])
        cross = lax.dot_general(
            left, right, (((1,), (1,)), ((), ())), preferred_element_type=F32
        )
        lines = []
        for g in range(PER):
            gs = slice(g * K, (g + 1) * K)
            square = jnp.where(near, cross[K:, gs], jnp.where(far, cross[:K, gs], 0.0))
            turned = pltpu.roll(square, 1, 1, stride=1, stride_axis=0)
            lines.append(jnp.sum(turned, axis=0, keepdims=True))
        stats_ref[pl.ds(pl.multiple_of(q * PER, PER), PER), :] = join(*lines)
        k_ext = join(rim_of(came_ref, K_LAST, ls), k_ref[:, ls].astype(F32))
        v_ext = join(rim_of(came_ref, V_LAST, ls), v_ref[:, ls].astype(F32))
        q_ext = join(rim_of(came_ref, Q_LAST, ls), q_ref[:, ls].astype(F32))
        ks_ref[:, ls] = causal(k_ext, tap_rows(taps_ref, 1, ls), pos_row)
        vs_ref[:, ls] = causal(v_ext, tap_rows(taps_ref, 2, ls), pos_row)
        cols_ref[:, ls] = tap_lines(gq_ref[:, ls].astype(F32), q_ext, pos_row)

    each_chunk(cot_ref.shape[1], body, 1)


def gate_kernel(
    len_ref, part_ref, after_ref, bwd_ref, ks_ref, vs_ref, gq_ref, k_ref, v_ref, came_ref,
    stats_ref, qcols_ref, gks_ref, gvs_ref, tails_ref, packed_ref, cols_ref,
):
    channels = part_ref.shape[1]
    kept = stats_ref.shape[0]
    row = iota((K, LANES), 0)
    col = iota((K, LANES), 1)
    pos_row = positions(len_ref, first_row() + row)
    pos = positions(len_ref, first_row() + K + col)
    mask = as_mask((col < row) & (pos >= col - row + K))
    own = owners()

    def body(q):
        ls = lanes_of(q)
        right = per_group(after_ref[:, ls], own)
        grad = part_ref[:, ls] + product(masked(bwd_ref, q, mask), right)
        gks = (grad * vs_ref[:, ls]).astype(BF16)
        gvs = (grad * ks_ref[:, ls]).astype(BF16)
        gks_ref[:, ls] = gks
        gvs_ref[:, ls] = gvs
        heads = (rim_of(gq_ref, 0, ls), gks.astype(F32)[:RIM], gvs.astype(F32)[:RIM])
        tails_ref[:, ls] = join(*heads, jnp.zeros((RIM, LANES), F32)).astype(BF16)
        k_ext = join(rim_of(came_ref, K_LAST, ls), k_ref[:, ls].astype(F32))
        v_ext = join(rim_of(came_ref, V_LAST, ls), v_ref[:, ls].astype(F32))
        cols_ref[0:8, ls] = qcols_ref[:, ls]
        cols_ref[8:16, ls] = tap_lines(gks.astype(F32), k_ext, pos_row)
        cols_ref[16:24, ls] = tap_lines(gvs.astype(F32), v_ext, pos_row)

    each_chunk(channels, body)
    packed_ref[0:kept] = stats_ref[...]
    gather = jnp.where(
        iota((channels, LANES), 0) // GS == iota((channels, LANES), 1), 1.0, 0.0
    )
    packed_ref[kept:] = jnp.dot(
        cols_ref[...], gather, preferred_element_type=F32, precision=lax.Precision.HIGHEST
    )


def mains_kernel(
    total, len_ref, taps_ref, gq_ref, gks_ref, gvs_ref, tails_ref, summed_ref, gain_ref, sums_ref,
    oq_ref, ok_ref, ov_ref, normed_ref,
):
    pos = positions(len_ref, first_row() + iota((K + RIM, LANES), 0))
    inverse = inverse_of(sums_ref, total)

    def body(q):
        ls = lanes_of(q)
        normed_ref[:, ls] = (gain_ref[:, ls] * summed_ref[:, ls] * inverse).astype(BF16)
        for i, (g_ref, o_ref) in enumerate(((gq_ref, oq_ref), (gks_ref, ok_ref), (gvs_ref, ov_ref))):
            ext = join(g_ref[:, ls].astype(F32), rim_of(tails_ref, i * RIM, ls))
            taps = tap_rows(taps_ref, i, ls)
            grad = taps[0] * ext[:K]
            for j in range(1, KS):
                held = jnp.where(pos >= j, ext, 0.0)
                grad = grad + taps[j] * held[j : j + K]
            o_ref[:, ls] = grad.astype(BF16)

    each_chunk(gq_ref.shape[1], body)


def unpack_kernel(all_ref, short_ref, long_ref, skip_ref, gain_ref):
    groups = long_ref.shape[0]
    rows = groups // PER
    total = lax.fori_loop(
        1, all_ref.shape[0], lambda i, acc: acc + all_ref[i], all_ref[0]
    )
    long_ref[...] = total[:groups]
    skip_ref[...] = total[groups : groups + rows]
    gain_ref[...] = total[groups + rows : groups + 2 * rows]
    for i in range(3):
        at = groups + 2 * rows + i * 8
        short_ref[i] = total[at : at + KS, :groups]


def shards(
    q_input, k_input, v_input, resid, lengths, short_filter, long_filter, skip, gain, cotangent
):
    length, channels = q_input.shape
    groups = channels // GS
    wide = channels * lax.axis_size("tp")
    rows = groups // PER

    def arr(shape, dtype):
        return jax.ShapeDtypeStruct(shape, dtype)

    smem = pl.BlockSpec(memory_space=pltpu.SMEM)
    vmem = pl.BlockSpec(memory_space=pltpu.VMEM)
    far_off = pl.BlockSpec(memory_space=pltpu.HBM)
    full_bf = arr((length, channels), BF16)
    full_f = arr((length, channels), F32)

    def call(name, kernel, outs, ins, scratch=(), flops=10**8, moved=10**6, grant=8, hbm=False):
        scalar = ins[0] is lengths
        return pl.pallas_call(
            kernel,
            out_shape=outs,
            in_specs=[far_off] * len(ins)
            if hbm
            else [smem if (i == 0 and scalar) else vmem for i in range(len(ins))],
            out_specs=[vmem] * len(outs),
            scratch_shapes=scratch,
            compiler_params=pltpu.CompilerParams(vmem_limit_bytes=grant * 1024 * 1024),
            cost_estimate=pl.CostEstimate(flops=flops, bytes_accessed=moved, transcendentals=0),
            name=name,
        )(*ins)

    skip2 = skip.reshape(1, channels)
    gain2 = gain.reshape(1, channels)
    taps, sent, far = call(
        "first", first_kernel,
        [arr((24, channels), F32), arr((SENT, channels), BF16), arr((2 * RIM, channels), BF16)],
        [lengths, jnp.transpose(short_filter, (0, 2, 1)), q_input, k_input, v_input],
        [
            pltpu.SMEM(lengths.shape, jnp.int32), pltpu.VMEM((3, KS, groups), BF16),
            pltpu.VMEM((PACK, channels), BF16), pltpu.VMEM((length, channels), BF16),
            pltpu.VMEM((length, channels), BF16), pltpu.SemaphoreType.DMA((5,)),
        ],
        hbm=True,
    )
    came = shifted(sent, "ctx", 1)
    came_far = shifted(far, "ctx", 2)

    def circulants(filt, turned):
        return call(
            "circulants", functools.partial(circulant_kernel, turned),
            [arr((K, groups * K), BF16)], [filt], [pltpu.VMEM((groups, K), F32)],
            flops=10**9, moved=4 * 10**6,
        )[0]

    filt, sent = lax.optimization_barrier((long_filter, sent))
    fwd = circulants(filt, True)
    bulk, part, top = call(
        "current", current_kernel, [full_f, full_f, full_bf],
        [lengths, q_input, taps, sent, fwd, skip2], flops=10**9, moved=5 * 10**6,
    )
    q_short, gated, before, mixed, summed, sums = call(
        "summed", summed_kernel,
        [full_f, full_bf, full_bf, full_f, full_f, arr((2, K), F32)],
        [
            lengths, came, came_far, q_input, k_input, v_input, taps, sent, fwd, top,
            bulk, part, skip2, resid, cotangent, gain2,
        ],
        [pltpu.VMEM((2, K, LANES), F32)], flops=10**9, moved=5 * 10**6,
    )
    sums = lax.psum(sums, "tp")
    grad_mixed, grad_qs = call(
        "grads", functools.partial(grads_kernel, wide), [full_bf, full_bf],
        [summed, mixed, q_short, cotangent, gain2, sums],
    )
    after = shifted(grad_mixed, "ctx", -1)
    filt, grad_mixed = lax.optimization_barrier((long_filter, grad_mixed))
    bwd = circulants(filt, False)
    stats, part, k_short, v_short, qcols = call(
        "beside", functools.partial(beside_kernel, wide),
        [
            arr((groups + 2 * rows, LANES), F32), full_f, full_f, full_f,
            arr((8, channels), F32),
        ],
        [
            lengths, summed, cotangent, sums, grad_mixed, grad_qs, gated, before, bwd,
            skip2, q_input, k_input, v_input, came, taps,
        ],
        flops=4 * 10**9, moved=5 * 10**6,
    )
    grad_ks, grad_vs, tails, packed = call(
        "gate", gate_kernel,
        [
            full_bf, full_bf, arr((4 * RIM, channels), BF16),
            arr((groups + 2 * rows + 24, LANES), F32),
        ],
        [
            lengths, part, after, bwd, k_short, v_short, grad_qs, k_input, v_input, came,
            stats, qcols,
        ],
        [pltpu.VMEM((24, channels), F32)], flops=10**9, moved=5 * 10**6,
    )
    tails = shifted(tails, "ctx", -1)
    grad_q, grad_k, grad_v, normed = call(
        "mains", functools.partial(mains_kernel, wide), [full_bf] * 4,
        [lengths, taps, grad_qs, grad_ks, grad_vs, tails, summed, gain2, sums], flops=10**9, moved=5 * 10**6,
    )
    packed = lax.all_gather(packed, "ctx")
    grad_short, grad_long, grad_skip, grad_gain = call(
        "unpack", unpack_kernel,
        [
            arr((3, KS, groups), F32), arr((groups, K), F32),
            arr((rows, LANES), F32), arr((rows, LANES), F32),
        ],
        [packed],
    )
    return (
        normed, grad_q, grad_k, grad_v, jnp.transpose(grad_short, (0, 2, 1)), grad_long,
        grad_skip.reshape(channels), grad_gain.reshape(channels),
    )


def solution(mesh):
    tiled = P("ctx", "tp")
    return jax.shard_map(
        shards,
        mesh=mesh,
        in_specs=(
            tiled, tiled, tiled, tiled, P(), P(None, "tp", None), P("tp", None), P("tp"), P("tp"),
            tiled,
        ),
        out_specs=(
            tiled, tiled, tiled, tiled, P(None, "tp", None), P("tp", None), P("tp"), P("tp"),
        ),
        check_vma=False,
    )
```

```python
import functools

import jax
import jax.numpy as jnp
from jax import lax
from jax.experimental import pallas as pl
from jax.experimental.pallas import tpu as pltpu
from jax.sharding import PartitionSpec as P

GS = 16
K = 128
KS = 7
LANES = 128
PER = LANES // GS
RIM = 8
PACK = 16
EPS = 1e-06
F32 = jnp.float32
BF16 = jnp.bfloat16


def shifted(x, axis, by):
    count = lax.axis_size(axis)
    pairs = [(i, i + by) for i in range(count) if 0 <= i + by < count]
    return lax.ppermute(x, axis, pairs)


def iota(shape, dim):
    return lax.broadcasted_iota(jnp.int32, shape, dim)


def positions(len_ref, rows):
    begin = jnp.zeros_like(rows)
    start = jnp.int32(0)
    for n in range(len_ref.shape[0]):
        begin = jnp.where(rows >= start, start, begin)
        start = start + len_ref[n]
    return rows - begin


def first_row():
    return lax.axis_index("ctx") * K


def lanes_of(q):
    return pl.ds(pl.multiple_of(q * LANES, LANES), LANES)


def each_chunk(channels, body, unroll=2):
    def step(q, carry):
        body(q)
        return carry

    lax.fori_loop(0, channels // LANES, step, 0, unroll=unroll)


def as_mask(cond):
    return jnp.where(cond, 1.0, 0.0).astype(BF16)


def join(*parts):
    return jnp.concatenate(parts, axis=0)


def tap_rows(taps_ref, which, ls):
    table = taps_ref[which * 8 : which * 8 + 8, ls]
    return [table[j : j + 1, :] for j in range(KS)]


def causal(ext, taps, pos):
    rows = ext.shape[0] - RIM
    total = taps[0] * ext[RIM:]
    for j in range(1, KS):
        moved = ext[RIM - j : RIM - j + rows]
        total = total + taps[j] * jnp.where(pos >= j, moved, 0.0)
    return total


def tap_lines(grad, ext, pos):
    lines = [jnp.sum(grad * ext[RIM:], axis=0, keepdims=True)]
    for j in range(1, KS):
        held = jnp.where(pos >= j, grad, 0.0)
        lines.append(jnp.sum(held * ext[RIM - j : RIM - j + K], axis=0, keepdims=True))
    lines.append(jnp.zeros((8 - KS, LANES), F32))
    return join(*lines)


def owners():
    lane = iota((K, LANES), 1) // GS
    return [as_mask(lane == g) for g in range(PER)]


def per_group(right, own):
    return join(*[right * mask for mask in own])


def masked(table_ref, q, mask):
    table = table_ref[:, pl.ds(pl.multiple_of(q * PER * K, PER * K), PER * K)]
    return [table[:, g * K : (g + 1) * K] * mask for g in range(PER)]


def product(left, right):
    return jnp.dot(jnp.concatenate(left, axis=1), right, preferred_element_type=F32)


K_FIRST, Q_LAST, K_LAST, V_LAST, V_FIRST, SENT = 0, K, K + 8, K + 16, K + 24, K + 32


def rim_of(ref, at, ls):
    base = at // PACK * PACK
    return ref[base : base + PACK, ls].astype(F32)[at - base : at - base + RIM]


def first_kernel(
    len_hbm, short_hbm, q_hbm, k_hbm, v_hbm, taps_ref, sent_ref, far_ref,
    len_ref, short_ref, q_ref, k_ref, v_ref, sems,
):
    groups = short_ref.shape[2]
    channels = taps_ref.shape[1]
    pairs = (
        (short_hbm, short_ref), (len_hbm, len_ref), (k_hbm, k_ref), (v_hbm, v_ref),
        (q_hbm.at[K - PACK : K], q_ref),
    )
    copies = [pltpu.make_async_copy(a, b, sems.at[i]) for i, (a, b) in enumerate(pairs)]
    for copy in copies:
        copy.start()
    spread = as_mask(iota((groups, channels), 1) // GS == iota((groups, channels), 0))
    copies[0].wait()
    for i in range(3):
        taps_ref[i * 8 : i * 8 + KS] = jnp.dot(
            short_ref[i], spread, preferred_element_type=F32
        )
        taps_ref[i * 8 + KS : i * 8 + 8] = jnp.zeros((8 - KS, channels), F32)
    for copy in copies[1:]:
        copy.wait()
    pos = positions(len_ref, first_row() + RIM + iota((K - RIM, LANES), 0))

    def body(q):
        ls = lanes_of(q)
        kx = k_ref[:, ls].astype(F32)
        vx = v_ref[:, ls].astype(F32)
        ks = causal(kx, tap_rows(taps_ref, 1, ls), pos)
        vs = causal(vx, tap_rows(taps_ref, 2, ls), pos)
        sent_ref[:K, ls] = join(kx[:RIM], ks * vs).astype(BF16)
        q_end = q_ref[:, ls].astype(F32)[PACK - RIM :]
        k_end = kx[K - RIM :]
        v_end = vx[K - RIM :]
        sent_ref[K:, ls] = join(q_end, k_end, v_end, vx[:RIM]).astype(BF16)
        far_ref[:, ls] = join(k_end, v_end).astype(BF16)

    each_chunk(channels, body)


def circulant_kernel(turned, long_ref, out_ref, line_ref):
    groups = long_ref.shape[0]
    filt = long_ref[...]
    if turned:
        flip = as_mask((iota((K, K), 0) + iota((K, K), 1)) % K == 0)
        line_ref[...] = jnp.dot(filt, flip, preferred_element_type=F32)
    else:
        line_ref[...] = filt.astype(F32)

    def step(g, carry):
        row = jnp.broadcast_to(line_ref[pl.ds(g, 1), :], (GS, K))
        block = pltpu.roll(row, 0, 1, stride=1, stride_axis=0)
        for i in range(K // GS):
            moved = block if i == 0 else pltpu.roll(block, i * GS, 1)
            at = pl.ds(pl.multiple_of(g * K, K), K)
            out_ref[i * GS : (i + 1) * GS, at] = moved.astype(BF16)
        return carry

    lax.fori_loop(0, groups, step, 0, unroll=8)


def current_kernel(
    len_ref, q_ref, taps_ref, sent_ref, fwd_ref, skip_ref, qs_ref, part_ref, top_ref
):
    row = iota((K, LANES), 0)
    col = iota((K, LANES), 1)
    pos = positions(len_ref, first_row() + row)
    near = (col <= row) & (pos >= row - col)
    mask = as_mask(near)
    mask_top = as_mask(near & (col < RIM))
    picks = join(*[as_mask((col == row + g * GS) & (row < GS)) for g in range(PER)])
    own = owners()
    top = jnp.zeros((RIM, LANES), F32)

    def body(q):
        ls = lanes_of(q)
        qs_ref[RIM:, ls] = causal(q_ref[:, ls].astype(F32), tap_rows(taps_ref, 0, ls), pos[RIM:])
        qs_ref[:RIM, ls] = top
        gated = join(top, sent_ref[:K, ls].astype(F32)[RIM:])
        rest = product(masked(fwd_ref, q, mask), per_group(gated.astype(BF16), own))
        part_ref[:, ls] = rest + skip_ref[:, ls] * gated
        top_ref[:, ls] = product(masked(fwd_ref, q, mask_top), picks).astype(BF16)

    each_chunk(q_ref.shape[1], body)


def summed_kernel(
    len_ref, came_ref, far_ref, q_ref, k_ref, v_ref, taps_ref, sent_ref, fwd_ref, top_ref,
    bulk_ref, part_ref, skip_ref, resid_ref, cot_ref, gain_ref,
    qs_ref, gated_ref, before_ref, mixed_ref, summed_ref, sums_ref, acc_ref,
):
    row = iota((K, LANES), 0)
    col = iota((K, LANES), 1)
    pos = positions(len_ref, first_row() + row)
    mask = as_mask((col > row) & (pos >= row - col + K))
    pos_top = pos[:RIM]
    pos_far = positions(len_ref, first_row() - K + iota((RIM, LANES), 0))
    own = owners()
    own_top = [
        as_mask((iota((PACK, LANES), 1) // GS == g) & (iota((PACK, LANES), 0) < RIM))
        for g in range(PER)
    ]
    acc_ref[...] = jnp.zeros_like(acc_ref)

    def body(q):
        ls = lanes_of(q)
        kt = tap_rows(taps_ref, 1, ls)
        vt = tap_rows(taps_ref, 2, ls)
        k_last = rim_of(came_ref, K_LAST, ls)
        v_last = rim_of(came_ref, V_LAST, ls)
        top = causal(join(k_last, rim_of(k_ref, 0, ls)), kt, pos_top) * causal(
            join(v_last, rim_of(v_ref, 0, ls)), vt, pos_top
        )
        far_top = causal(
            join(rim_of(far_ref, 0, ls), rim_of(came_ref, K_FIRST, ls)), kt, pos_far
        ) * causal(join(rim_of(far_ref, RIM, ls), rim_of(came_ref, V_FIRST, ls)), vt, pos_far)
        qs_top = causal(
            join(rim_of(came_ref, Q_LAST, ls), rim_of(q_ref, 0, ls)), tap_rows(taps_ref, 0, ls), pos_top
        )
        before = join(far_top, came_ref[:K, ls].astype(F32)[RIM:]).astype(BF16)
        gated = join(top, sent_ref[:K, ls].astype(F32)[RIM:]).astype(BF16)
        before_ref[:, ls] = before
        gated_ref[:, ls] = gated
        qs = join(qs_top, bulk_ref[RIM:, ls])
        qs_ref[:, ls] = qs
        first = gated[:PACK]
        left = masked(fwd_ref, q, mask) + [top_ref[:, ls]]
        right = join(per_group(before, own), per_group(first, own_top))
        direct = skip_ref[:, ls] * first.astype(F32)[:RIM]
        mixed = part_ref[:, ls] + product(left, right)
        mixed = join(mixed[:RIM] + direct, mixed[RIM:])
        summed = resid_ref[:, ls].astype(F32) + qs * mixed
        mixed_ref[:, ls] = mixed
        summed_ref[:, ls] = summed
        acc_ref[0] += summed * summed
        acc_ref[1] += gain_ref[:, ls] * cot_ref[:, ls].astype(F32) * summed

    each_chunk(resid_ref.shape[1], body)
    for i in range(2):
        sums_ref[i : i + 1] = jnp.sum(acc_ref[i].T, axis=0, keepdims=True)


def by_row(line):
    return jnp.broadcast_to(line, (K, K)).T


def inverse_of(sums_ref, total):
    return by_row(lax.rsqrt(sums_ref[0:1] / total + EPS))


def grads_kernel(total, summed_ref, mixed_ref, qs_ref, cot_ref, gain_ref, sums_ref, gm_ref, gq_ref):
    inverse = inverse_of(sums_ref, total)
    scale = inverse * inverse * by_row(sums_ref[1:2] / total)

    def body(q):
        ls = lanes_of(q)
        scaled = gain_ref[:, ls] * cot_ref[:, ls].astype(F32)
        grad_sum = inverse * (scaled - summed_ref[:, ls] * scale)
        gm_ref[:, ls] = (grad_sum * qs_ref[:, ls]).astype(BF16)
        gq_ref[:, ls] = (grad_sum * mixed_ref[:, ls]).astype(BF16)

    each_chunk(cot_ref.shape[1], body)


def beside_kernel(
    total, len_ref, summed_ref, cot_ref, sums_ref, gm_ref, gq_ref, gated_ref, before_ref,
    bwd_ref, skip_ref, q_ref, k_ref, v_ref, came_ref, taps_ref,
    stats_ref, part_ref, ks_ref, vs_ref, cols_ref,
):
    groups = bwd_ref.shape[1] // K
    inverse = inverse_of(sums_ref, total)
    row = iota((K, LANES), 0)
    col = iota((K, LANES), 1)
    pos_row = positions(len_ref, first_row() + row)
    pos = positions(len_ref, first_row() + col)
    mask = as_mask((col >= row) & (pos >= col - row))
    source = K - 1 - row
    near = (col >= source) & (pos >= col - source)
    far = (col < source) & (pos >= col - source + K)
    flip = as_mask(row + col == K - 1)
    own = owners()

    def body(q):
        ls = lanes_of(q)
        summed = summed_ref[:, ls]
        gm = gm_ref[:, ls]
        gmf = gm.astype(F32)
        gated = gated_ref[:, ls]
        stats_ref[pl.ds(groups + q, 1), :] = jnp.sum(gmf * gated.astype(F32), axis=0, keepdims=True)
        stats_ref[pl.ds(groups + groups // PER + q, 1), :] = jnp.sum(
            cot_ref[:, ls].astype(F32) * summed * inverse, axis=0, keepdims=True
        )
        right = per_group(gm, own)
        part_ref[:, ls] = skip_ref[:, ls] * gmf + product(masked(bwd_ref, q, mask), right)
        two = jnp.concatenate([before_ref[:, ls], gated], axis=1)
        flipped = jnp.dot(flip, two, preferred_element_type=F32).astype(BF16)
        left = join(flipped[:, :LANES], flipped[:, LANES:])
        turned = gmf.T.astype(BF16)
        spread = []
        for g in range(PER):
            pieces = [jnp.zeros((GS, K), BF16)] * PER
            pieces[g] = turned[g * GS : (g + 1) * GS]
            spread.append(join(*pieces))
        cross = jnp.dot(left, jnp.concatenate(spread, axis=1), preferred_element_type=F32)
        lines = []
        for g in range(PER):
            gs = slice(g * K, (g + 1) * K)
            square = jnp.where(near, cross[K:, gs], jnp.where(far, cross[:K, gs], 0.0))
            square = pltpu.roll(square, 1, 1, stride=1, stride_axis=0)
            lines.append(jnp.sum(square, axis=0, keepdims=True))
        stats_ref[pl.ds(pl.multiple_of(q * PER, PER), PER), :] = join(*lines)
        k_ext = join(rim_of(came_ref, K_LAST, ls), k_ref[:, ls].astype(F32))
        v_ext = join(rim_of(came_ref, V_LAST, ls), v_ref[:, ls].astype(F32))
        q_ext = join(rim_of(came_ref, Q_LAST, ls), q_ref[:, ls].astype(F32))
        ks_ref[:, ls] = causal(k_ext, tap_rows(taps_ref, 1, ls), pos_row)
        vs_ref[:, ls] = causal(v_ext, tap_rows(taps_ref, 2, ls), pos_row)
        cols_ref[:, ls] = tap_lines(gq_ref[:, ls].astype(F32), q_ext, pos_row)

    each_chunk(cot_ref.shape[1], body, 1)


def gate_kernel(
    len_ref, part_ref, after_ref, bwd_ref, ks_ref, vs_ref, gq_ref, k_ref, v_ref, came_ref,
    stats_ref, qcols_ref, gks_ref, gvs_ref, tails_ref, packed_ref, cols_ref,
):
    channels = part_ref.shape[1]
    kept = stats_ref.shape[0]
    row = iota((K, LANES), 0)
    col = iota((K, LANES), 1)
    pos_row = positions(len_ref, first_row() + row)
    pos = positions(len_ref, first_row() + K + col)
    mask = as_mask((col < row) & (pos >= col - row + K))
    own = owners()

    def body(q):
        ls = lanes_of(q)
        right = per_group(after_ref[:, ls], own)
        grad = part_ref[:, ls] + product(masked(bwd_ref, q, mask), right)
        gks = (grad * vs_ref[:, ls]).astype(BF16)
        gvs = (grad * ks_ref[:, ls]).astype(BF16)
        gks_ref[:, ls] = gks
        gvs_ref[:, ls] = gvs
        heads = (rim_of(gq_ref, 0, ls), gks.astype(F32)[:RIM], gvs.astype(F32)[:RIM])
        tails_ref[:, ls] = join(*heads, jnp.zeros((RIM, LANES), F32)).astype(BF16)
        k_ext = join(rim_of(came_ref, K_LAST, ls), k_ref[:, ls].astype(F32))
        v_ext = join(rim_of(came_ref, V_LAST, ls), v_ref[:, ls].astype(F32))
        cols_ref[0:8, ls] = qcols_ref[:, ls]
        cols_ref[8:16, ls] = tap_lines(gks.astype(F32), k_ext, pos_row)
        cols_ref[16:24, ls] = tap_lines(gvs.astype(F32), v_ext, pos_row)

    each_chunk(channels, body)
    packed_ref[0:kept] = stats_ref[...]
    gather = jnp.where(
        iota((channels, LANES), 0) // GS == iota((channels, LANES), 1), 1.0, 0.0
    )
    packed_ref[kept + 24 :] = jnp.zeros((packed_ref.shape[0] - kept - 24, LANES), F32)
    packed_ref[kept : kept + 24] = jnp.dot(
        cols_ref[...], gather, preferred_element_type=F32, precision=lax.Precision.HIGHEST
    )


def mains_kernel(
    total, len_ref, taps_ref, gq_ref, gks_ref, gvs_ref, tails_ref, summed_ref, gain_ref, sums_ref,
    oq_ref, ok_ref, ov_ref, normed_ref,
):
    pos = positions(len_ref, first_row() + iota((K + RIM, LANES), 0))
    inverse = inverse_of(sums_ref, total)

    def body(q):
        ls = lanes_of(q)
        normed_ref[:, ls] = (gain_ref[:, ls] * summed_ref[:, ls] * inverse).astype(BF16)
        for i, (g_ref, o_ref) in enumerate(((gq_ref, oq_ref), (gks_ref, ok_ref), (gvs_ref, ov_ref))):
            ext = join(g_ref[:, ls].astype(F32), rim_of(tails_ref, i * RIM, ls))
            taps = tap_rows(taps_ref, i, ls)
            grad = taps[0] * ext[:K]
            for j in range(1, KS):
                held = jnp.where(pos >= j, ext, 0.0)
                grad = grad + taps[j] * held[j : j + K]
            o_ref[:, ls] = grad.astype(BF16)

    each_chunk(gq_ref.shape[1], body)


def sum_kernel(all_ref, out_ref):
    count = all_ref.shape[0]
    total = lax.fori_loop(1, count, lambda i, acc: acc + all_ref[i], all_ref[0])
    out_ref[...] = jnp.broadcast_to(total[None], out_ref.shape)


def unpack_kernel(all_ref, short_ref, long_ref, skip_ref, gain_ref):
    groups = long_ref.shape[0]
    rows = groups // PER
    long_ref[...] = all_ref[:groups]
    skip_ref[...] = all_ref[groups : groups + rows]
    gain_ref[...] = all_ref[groups + rows : groups + 2 * rows]
    for i in range(3):
        at = groups + 2 * rows + i * 8
        short_ref[i] = all_ref[at : at + KS, :groups]


def shards(
    q_input, k_input, v_input, resid, lengths, short_filter, long_filter, skip, gain, cotangent
):
    length, channels = q_input.shape
    groups = channels // GS
    wide = channels * lax.axis_size("tp")
    rows = groups // PER
    count = lax.axis_size("ctx")
    piece = -(-(groups + 2 * rows + 24) // (8 * count)) * 8
    packed_rows = piece * count

    def arr(shape, dtype):
        return jax.ShapeDtypeStruct(shape, dtype)

    smem = pl.BlockSpec(memory_space=pltpu.SMEM)
    vmem = pl.BlockSpec(memory_space=pltpu.VMEM)
    far_off = pl.BlockSpec(memory_space=pltpu.HBM)
    full_bf = arr((length, channels), BF16)
    full_f = arr((length, channels), F32)

    def call(name, kernel, outs, ins, scratch=(), flops=10**8, moved=10**6, grant=8, hbm=False):
        scalar = ins[0] is lengths
        return pl.pallas_call(
            kernel,
            out_shape=outs,
            in_specs=[far_off] * len(ins)
            if hbm
            else [smem if (i == 0 and scalar) else vmem for i in range(len(ins))],
            out_specs=[vmem] * len(outs),
            scratch_shapes=scratch,
            compiler_params=pltpu.CompilerParams(vmem_limit_bytes=grant * 1024 * 1024),
            cost_estimate=pl.CostEstimate(flops=flops, bytes_accessed=moved, transcendentals=0),
            name=name,
        )(*ins)

    skip2 = skip.reshape(1, channels)
    gain2 = gain.reshape(1, channels)
    taps, sent, far = call(
        "first", first_kernel,
        [arr((24, channels), F32), arr((SENT, channels), BF16), arr((2 * RIM, channels), BF16)],
        [lengths, jnp.transpose(short_filter, (0, 2, 1)), q_input, k_input, v_input],
        [
            pltpu.SMEM(lengths.shape, jnp.int32), pltpu.VMEM((3, KS, groups), BF16),
            pltpu.VMEM((PACK, channels), BF16), pltpu.VMEM((length, channels), BF16),
            pltpu.VMEM((length, channels), BF16), pltpu.SemaphoreType.DMA((5,)),
        ],
        grant=60,
        hbm=True,
    )
    came = shifted(sent, "ctx", 1)
    came_far = shifted(far, "ctx", 2)

    def circulants(filt, turned):
        return call(
            "circulants", functools.partial(circulant_kernel, turned),
            [arr((K, groups * K), BF16)], [filt], [pltpu.VMEM((groups, K), F32)],
            flops=10**9, moved=4 * 10**6,
        )[0]

    filt, sent = lax.optimization_barrier((long_filter, sent))
    fwd = circulants(filt, True)
    bulk, part, top = call(
        "current", current_kernel, [full_f, full_f, full_bf],
        [lengths, q_input, taps, sent, fwd, skip2], flops=10**9, moved=5 * 10**6,
    )
    q_short, gated, before, mixed, summed, sums = call(
        "summed", summed_kernel,
        [full_f, full_bf, full_bf, full_f, full_f, arr((2, K), F32)],
        [
            lengths, came, came_far, q_input, k_input, v_input, taps, sent, fwd, top,
            bulk, part, skip2, resid, cotangent, gain2,
        ],
        [pltpu.VMEM((2, K, LANES), F32)], flops=10**9, moved=5 * 10**6,
    )
    sums = lax.psum(sums, "tp")
    grad_mixed, grad_qs = call(
        "grads", functools.partial(grads_kernel, wide), [full_bf, full_bf],
        [summed, mixed, q_short, cotangent, gain2, sums],
    )
    after = shifted(grad_mixed, "ctx", -1)
    filt, grad_mixed = lax.optimization_barrier((long_filter, grad_mixed))
    bwd = circulants(filt, False)
    stats, part, k_short, v_short, qcols = call(
        "beside", functools.partial(beside_kernel, wide),
        [
            arr((groups + 2 * rows, LANES), F32), full_f, full_f, full_f,
            arr((8, channels), F32),
        ],
        [
            lengths, summed, cotangent, sums, grad_mixed, grad_qs, gated, before, bwd,
            skip2, q_input, k_input, v_input, came, taps,
        ],
        flops=4 * 10**9, moved=5 * 10**6,
    )
    grad_ks, grad_vs, tails, packed = call(
        "gate", gate_kernel,
        [
            full_bf, full_bf, arr((4 * RIM, channels), BF16),
            arr((packed_rows, LANES), F32),
        ],
        [
            lengths, part, after, bwd, k_short, v_short, grad_qs, k_input, v_input, came,
            stats, qcols,
        ],
        [pltpu.VMEM((24, channels), F32)], flops=10**9, moved=5 * 10**6,
    )
    tails = shifted(tails, "ctx", -1)
    grad_q, grad_k, grad_v, normed = call(
        "mains", functools.partial(mains_kernel, wide), [full_bf] * 4,
        [lengths, taps, grad_qs, grad_ks, grad_vs, tails, summed, gain2, sums], flops=10**9, moved=5 * 10**6,
    )
    parts = lax.all_to_all(packed.reshape(count, piece, LANES), "ctx", 0, 0)
    (spread,) = call("sum_rows", sum_kernel, [arr((count, piece, LANES), F32)], [parts])
    packed = lax.all_to_all(spread, "ctx", 0, 0).reshape(packed_rows, LANES)
    grad_short, grad_long, grad_skip, grad_gain = call(
        "unpack", unpack_kernel,
        [
            arr((3, KS, groups), F32), arr((groups, K), F32),
            arr((rows, LANES), F32), arr((rows, LANES), F32),
        ],
        [packed],
    )
    return (
        normed, grad_q, grad_k, grad_v, jnp.transpose(grad_short, (0, 2, 1)), grad_long,
        grad_skip.reshape(channels), grad_gain.reshape(channels),
    )


def solution(mesh):
    tiled = P("ctx", "tp")
    return jax.shard_map(
        shards,
        mesh=mesh,
        in_specs=(
            tiled, tiled, tiled, tiled, P(), P(None, "tp", None), P("tp", None), P("tp"), P("tp"),
            tiled,
        ),
        out_specs=(
            tiled, tiled, tiled, tiled, P(None, "tp", None), P("tp", None), P("tp"), P("tp"),
        ),
        check_vma=False,
    )
```

```python
import functools

import jax
import jax.numpy as jnp
from jax import lax
from jax.experimental import pallas as pl
from jax.experimental.pallas import tpu as pltpu
from jax.sharding import PartitionSpec as P

GS = 16
K = 128
KS = 7
LANES = 128
PER = LANES // GS
RIM = 8
PACK = 16
EPS = 1e-06
F32 = jnp.float32
BF16 = jnp.bfloat16


def shifted(x, axis, by):
    count = lax.axis_size(axis)
    pairs = [(i, i + by) for i in range(count) if 0 <= i + by < count]
    return lax.ppermute(x, axis, pairs)


def swapped(x, axis, step):
    return lax.ppermute(x, axis, [(i, i ^ step) for i in range(lax.axis_size(axis))])


def iota(shape, dim):
    return lax.broadcasted_iota(jnp.int32, shape, dim)


def positions(len_ref, rows):
    begin = jnp.zeros_like(rows)
    start = jnp.int32(0)
    for n in range(len_ref.shape[0]):
        begin = jnp.where(rows >= start, start, begin)
        start = start + len_ref[n]
    return rows - begin


def first_row():
    return lax.axis_index("ctx") * K


def lanes_of(q):
    return pl.ds(pl.multiple_of(q * LANES, LANES), LANES)


def each_chunk(channels, body, unroll=2):
    def step(q, carry):
        body(q)
        return carry

    lax.fori_loop(0, channels // LANES, step, 0, unroll=unroll)


def as_mask(cond):
    return jnp.where(cond, 1.0, 0.0).astype(BF16)


def join(*parts):
    return jnp.concatenate(parts, axis=0)


def tap_rows(taps_ref, which, ls):
    table = taps_ref[which * 8 : which * 8 + 8, ls]
    return [table[j : j + 1, :] for j in range(KS)]


def causal(ext, taps, pos):
    rows = ext.shape[0] - RIM
    total = taps[0] * ext[RIM:]
    for j in range(1, KS):
        moved = ext[RIM - j : RIM - j + rows]
        total = total + taps[j] * jnp.where(pos >= j, moved, 0.0)
    return total


def tap_lines(grad, ext, pos):
    lines = [jnp.sum(grad * ext[RIM:], axis=0, keepdims=True)]
    for j in range(1, KS):
        held = jnp.where(pos >= j, grad, 0.0)
        lines.append(jnp.sum(held * ext[RIM - j : RIM - j + K], axis=0, keepdims=True))
    lines.append(jnp.zeros((8 - KS, LANES), F32))
    return join(*lines)


def owners():
    lane = iota((K, LANES), 1) // GS
    return [as_mask(lane == g) for g in range(PER)]


def per_group(right, own):
    return join(*[right * mask for mask in own])


def masked(table_ref, q, mask):
    table = table_ref[:, pl.ds(pl.multiple_of(q * PER * K, PER * K), PER * K)]
    return [table[:, g * K : (g + 1) * K] * mask for g in range(PER)]


def product(left, right):
    return jnp.dot(jnp.concatenate(left, axis=1), right, preferred_element_type=F32)


K_FIRST, Q_LAST, K_LAST, V_LAST, V_FIRST, SENT = 0, K, K + 8, K + 16, K + 24, K + 32


def rim_of(ref, at, ls):
    base = at // PACK * PACK
    return ref[base : base + PACK, ls].astype(F32)[at - base : at - base + RIM]


def first_kernel(
    len_hbm, short_hbm, q_hbm, k_hbm, v_hbm, taps_ref, sent_ref, far_ref,
    len_ref, short_ref, q_ref, k_ref, v_ref, sems,
):
    groups = short_ref.shape[2]
    channels = taps_ref.shape[1]
    pairs = (
        (short_hbm, short_ref), (len_hbm, len_ref), (k_hbm, k_ref), (v_hbm, v_ref),
        (q_hbm.at[K - PACK : K], q_ref),
    )
    copies = [pltpu.make_async_copy(a, b, sems.at[i]) for i, (a, b) in enumerate(pairs)]
    for copy in copies:
        copy.start()
    spread = as_mask(iota((groups, channels), 1) // GS == iota((groups, channels), 0))
    copies[0].wait()
    for i in range(3):
        taps_ref[i * 8 : i * 8 + KS] = jnp.dot(
            short_ref[i], spread, preferred_element_type=F32
        )
        taps_ref[i * 8 + KS : i * 8 + 8] = jnp.zeros((8 - KS, channels), F32)
    for copy in copies[1:]:
        copy.wait()
    pos = positions(len_ref, first_row() + RIM + iota((K - RIM, LANES), 0))

    def body(q):
        ls = lanes_of(q)
        kx = k_ref[:, ls].astype(F32)
        vx = v_ref[:, ls].astype(F32)
        ks = causal(kx, tap_rows(taps_ref, 1, ls), pos)
        vs = causal(vx, tap_rows(taps_ref, 2, ls), pos)
        sent_ref[:K, ls] = join(kx[:RIM], ks * vs).astype(BF16)
        q_end = q_ref[:, ls].astype(F32)[PACK - RIM :]
        k_end = kx[K - RIM :]
        v_end = vx[K - RIM :]
        sent_ref[K:, ls] = join(q_end, k_end, v_end, vx[:RIM]).astype(BF16)
        far_ref[:, ls] = join(k_end, v_end).astype(BF16)

    each_chunk(channels, body)


def circulant_kernel(turned, long_ref, out_ref, line_ref):
    groups = long_ref.shape[0]
    filt = long_ref[...]
    if turned:
        flip = as_mask((iota((K, K), 0) + iota((K, K), 1)) % K == 0)
        line_ref[...] = jnp.dot(filt, flip, preferred_element_type=F32)
    else:
        line_ref[...] = filt.astype(F32)

    def step(g, carry):
        row = jnp.broadcast_to(line_ref[pl.ds(g, 1), :], (GS, K))
        block = pltpu.roll(row, 0, 1, stride=1, stride_axis=0)
        for i in range(K // GS):
            moved = block if i == 0 else pltpu.roll(block, i * GS, 1)
            at = pl.ds(pl.multiple_of(g * K, K), K)
            out_ref[i * GS : (i + 1) * GS, at] = moved.astype(BF16)
        return carry

    lax.fori_loop(0, groups, step, 0, unroll=8)


def current_kernel(
    len_ref, q_ref, taps_ref, sent_ref, fwd_ref, skip_ref, qs_ref, part_ref, top_ref
):
    row = iota((K, LANES), 0)
    col = iota((K, LANES), 1)
    pos = positions(len_ref, first_row() + row)
    near = (col <= row) & (pos >= row - col)
    mask = as_mask(near)
    mask_top = as_mask(near & (col < RIM))
    picks = join(*[as_mask((col == row + g * GS) & (row < GS)) for g in range(PER)])
    own = owners()
    top = jnp.zeros((RIM, LANES), F32)

    def body(q):
        ls = lanes_of(q)
        qs_ref[RIM:, ls] = causal(q_ref[:, ls].astype(F32), tap_rows(taps_ref, 0, ls), pos[RIM:])
        qs_ref[:RIM, ls] = top
        gated = join(top, sent_ref[:K, ls].astype(F32)[RIM:])
        rest = product(masked(fwd_ref, q, mask), per_group(gated.astype(BF16), own))
        part_ref[:, ls] = rest + skip_ref[:, ls] * gated
        top_ref[:, ls] = product(masked(fwd_ref, q, mask_top), picks).astype(BF16)

    each_chunk(q_ref.shape[1], body)


def summed_kernel(
    len_ref, came_ref, far_ref, q_ref, k_ref, v_ref, taps_ref, sent_ref, fwd_ref, top_ref,
    bulk_ref, part_ref, skip_ref, resid_ref, cot_ref, gain_ref,
    qs_ref, gated_ref, before_ref, mixed_ref, summed_ref, sums_ref, acc_ref,
):
    row = iota((K, LANES), 0)
    col = iota((K, LANES), 1)
    pos = positions(len_ref, first_row() + row)
    mask = as_mask((col > row) & (pos >= row - col + K))
    pos_top = pos[:RIM]
    pos_far = positions(len_ref, first_row() - K + iota((RIM, LANES), 0))
    own = owners()
    own_top = [
        as_mask((iota((PACK, LANES), 1) // GS == g) & (iota((PACK, LANES), 0) < RIM))
        for g in range(PER)
    ]
    acc_ref[...] = jnp.zeros_like(acc_ref)

    def body(q):
        ls = lanes_of(q)
        kt = tap_rows(taps_ref, 1, ls)
        vt = tap_rows(taps_ref, 2, ls)
        k_last = rim_of(came_ref, K_LAST, ls)
        v_last = rim_of(came_ref, V_LAST, ls)
        top = causal(join(k_last, rim_of(k_ref, 0, ls)), kt, pos_top) * causal(
            join(v_last, rim_of(v_ref, 0, ls)), vt, pos_top
        )
        far_top = causal(
            join(rim_of(far_ref, 0, ls), rim_of(came_ref, K_FIRST, ls)), kt, pos_far
        ) * causal(join(rim_of(far_ref, RIM, ls), rim_of(came_ref, V_FIRST, ls)), vt, pos_far)
        qs_top = causal(
            join(rim_of(came_ref, Q_LAST, ls), rim_of(q_ref, 0, ls)), tap_rows(taps_ref, 0, ls), pos_top
        )
        before = join(far_top, came_ref[:K, ls].astype(F32)[RIM:]).astype(BF16)
        gated = join(top, sent_ref[:K, ls].astype(F32)[RIM:]).astype(BF16)
        before_ref[:, ls] = before
        gated_ref[:, ls] = gated
        qs = join(qs_top, bulk_ref[RIM:, ls])
        qs_ref[:, ls] = qs
        first = gated[:PACK]
        left = masked(fwd_ref, q, mask) + [top_ref[:, ls]]
        right = join(per_group(before, own), per_group(first, own_top))
        direct = skip_ref[:, ls] * first.astype(F32)[:RIM]
        mixed = part_ref[:, ls] + product(left, right)
        mixed = join(mixed[:RIM] + direct, mixed[RIM:])
        summed = resid_ref[:, ls].astype(F32) + qs * mixed
        mixed_ref[:, ls] = mixed
        summed_ref[:, ls] = summed
        acc_ref[0] += summed * summed
        acc_ref[1] += gain_ref[:, ls] * cot_ref[:, ls].astype(F32) * summed

    each_chunk(resid_ref.shape[1], body)
    for i in range(2):
        sums_ref[i : i + 1] = jnp.sum(acc_ref[i].T, axis=0, keepdims=True)


def by_row(line):
    return jnp.broadcast_to(line, (K, K)).T


def inverse_of(sums_ref, total):
    return by_row(lax.rsqrt(sums_ref[0:1] / total + EPS))


def gates_kernel(len_ref, k_ref, v_ref, came_ref, taps_ref, ks_ref, vs_ref):
    pos = positions(len_ref, first_row() + iota((K, LANES), 0))

    def body(q):
        ls = lanes_of(q)
        k_ext = join(rim_of(came_ref, K_LAST, ls), k_ref[:, ls].astype(F32))
        v_ext = join(rim_of(came_ref, V_LAST, ls), v_ref[:, ls].astype(F32))
        ks_ref[:, ls] = causal(k_ext, tap_rows(taps_ref, 1, ls), pos)
        vs_ref[:, ls] = causal(v_ext, tap_rows(taps_ref, 2, ls), pos)

    each_chunk(k_ref.shape[1], body)


def grads_kernel(total, summed_ref, mixed_ref, qs_ref, cot_ref, gain_ref, sums_ref, gm_ref, gq_ref):
    inverse = inverse_of(sums_ref, total)
    scale = inverse * inverse * by_row(sums_ref[1:2] / total)

    def body(q):
        ls = lanes_of(q)
        scaled = gain_ref[:, ls] * cot_ref[:, ls].astype(F32)
        grad_sum = inverse * (scaled - summed_ref[:, ls] * scale)
        gm_ref[:, ls] = (grad_sum * qs_ref[:, ls]).astype(BF16)
        gq_ref[:, ls] = (grad_sum * mixed_ref[:, ls]).astype(BF16)

    each_chunk(cot_ref.shape[1], body)


def beside_kernel(
    total, len_ref, summed_ref, cot_ref, sums_ref, gm_ref, gq_ref, gated_ref, before_ref,
    bwd_ref, skip_ref, q_ref, came_ref, stats_ref, part_ref, cols_ref,
):
    groups = bwd_ref.shape[1] // K
    inverse = inverse_of(sums_ref, total)
    row = iota((K, LANES), 0)
    col = iota((K, LANES), 1)
    pos_row = positions(len_ref, first_row() + row)
    pos = positions(len_ref, first_row() + col)
    mask = as_mask((col >= row) & (pos >= col - row))
    source = K - 1 - row
    near = (col >= source) & (pos >= col - source)
    far = (col < source) & (pos >= col - source + K)
    flip = as_mask(row + col == K - 1)
    own = owners()

    def body(q):
        ls = lanes_of(q)
        summed = summed_ref[:, ls]
        gm = gm_ref[:, ls]
        gmf = gm.astype(F32)
        gated = gated_ref[:, ls]
        stats_ref[pl.ds(groups + q, 1), :] = jnp.sum(gmf * gated.astype(F32), axis=0, keepdims=True)
        stats_ref[pl.ds(groups + groups // PER + q, 1), :] = jnp.sum(
            cot_ref[:, ls].astype(F32) * summed * inverse, axis=0, keepdims=True
        )
        right = per_group(gm, own)
        part_ref[:, ls] = skip_ref[:, ls] * gmf + product(masked(bwd_ref, q, mask), right)
        two = jnp.concatenate([before_ref[:, ls], gated], axis=1)
        flipped = jnp.dot(flip, two, preferred_element_type=F32).astype(BF16)
        left = join(flipped[:, :LANES], flipped[:, LANES:])
        turned = gmf.T.astype(BF16)
        spread = []
        for g in range(PER):
            pieces = [jnp.zeros((GS, K), BF16)] * PER
            pieces[g] = turned[g * GS : (g + 1) * GS]
            spread.append(join(*pieces))
        cross = jnp.dot(left, jnp.concatenate(spread, axis=1), preferred_element_type=F32)
        lines = []
        for g in range(PER):
            gs = slice(g * K, (g + 1) * K)
            square = jnp.where(near, cross[K:, gs], jnp.where(far, cross[:K, gs], 0.0))
            square = pltpu.roll(square, 1, 1, stride=1, stride_axis=0)
            lines.append(jnp.sum(square, axis=0, keepdims=True))
        stats_ref[pl.ds(pl.multiple_of(q * PER, PER), PER), :] = join(*lines)
        q_ext = join(rim_of(came_ref, Q_LAST, ls), q_ref[:, ls].astype(F32))
        cols_ref[:, ls] = tap_lines(gq_ref[:, ls].astype(F32), q_ext, pos_row)

    each_chunk(cot_ref.shape[1], body, 1)


def gate_kernel(
    len_ref, part_ref, after_ref, bwd_ref, ks_ref, vs_ref, gq_ref, k_ref, v_ref, came_ref,
    stats_ref, qcols_ref, gks_ref, gvs_ref, tails_ref, packed_ref, cols_ref,
):
    channels = part_ref.shape[1]
    kept = stats_ref.shape[0]
    row = iota((K, LANES), 0)
    col = iota((K, LANES), 1)
    pos_row = positions(len_ref, first_row() + row)
    pos = positions(len_ref, first_row() + K + col)
    mask = as_mask((col < row) & (pos >= col - row + K))
    own = owners()

    def body(q):
        ls = lanes_of(q)
        right = per_group(after_ref[:, ls], own)
        grad = part_ref[:, ls] + product(masked(bwd_ref, q, mask), right)
        gks = (grad * vs_ref[:, ls]).astype(BF16)
        gvs = (grad * ks_ref[:, ls]).astype(BF16)
        gks_ref[:, ls] = gks
        gvs_ref[:, ls] = gvs
        heads = (rim_of(gq_ref, 0, ls), gks.astype(F32)[:RIM], gvs.astype(F32)[:RIM])
        tails_ref[:, ls] = join(*heads, jnp.zeros((RIM, LANES), F32)).astype(BF16)
        k_ext = join(rim_of(came_ref, K_LAST, ls), k_ref[:, ls].astype(F32))
        v_ext = join(rim_of(came_ref, V_LAST, ls), v_ref[:, ls].astype(F32))
        cols_ref[0:8, ls] = qcols_ref[:, ls]
        cols_ref[8:16, ls] = tap_lines(gks.astype(F32), k_ext, pos_row)
        cols_ref[16:24, ls] = tap_lines(gvs.astype(F32), v_ext, pos_row)

    each_chunk(channels, body)
    packed_ref[0:kept] = stats_ref[...]
    gather = jnp.where(
        iota((channels, LANES), 0) // GS == iota((channels, LANES), 1), 1.0, 0.0
    )
    packed_ref[kept:] = jnp.dot(
        cols_ref[...], gather, preferred_element_type=F32, precision=lax.Precision.HIGHEST
    )


def mains_kernel(
    total, len_ref, taps_ref, gq_ref, gks_ref, gvs_ref, tails_ref, summed_ref, gain_ref, sums_ref,
    oq_ref, ok_ref, ov_ref, normed_ref,
):
    pos = positions(len_ref, first_row() + iota((K + RIM, LANES), 0))
    inverse = inverse_of(sums_ref, total)

    def body(q):
        ls = lanes_of(q)
        normed_ref[:, ls] = (gain_ref[:, ls] * summed_ref[:, ls] * inverse).astype(BF16)
        for i, (g_ref, o_ref) in enumerate(((gq_ref, oq_ref), (gks_ref, ok_ref), (gvs_ref, ov_ref))):
            ext = join(g_ref[:, ls].astype(F32), rim_of(tails_ref, i * RIM, ls))
            taps = tap_rows(taps_ref, i, ls)
            grad = taps[0] * ext[:K]
            for j in range(1, KS):
                held = jnp.where(pos >= j, ext, 0.0)
                grad = grad + taps[j] * held[j : j + K]
            o_ref[:, ls] = grad.astype(BF16)

    each_chunk(gq_ref.shape[1], body)


def unpack_kernel(one_ref, two_ref, short_ref, long_ref, skip_ref, gain_ref):
    groups = long_ref.shape[0]
    rows = groups // PER
    total = one_ref[...] + two_ref[...]
    long_ref[...] = total[:groups]
    skip_ref[...] = total[groups : groups + rows]
    gain_ref[...] = total[groups + rows : groups + 2 * rows]
    for i in range(3):
        at = groups + 2 * rows + i * 8
        short_ref[i] = total[at : at + KS, :groups]


def shards(
    q_input, k_input, v_input, resid, lengths, short_filter, long_filter, skip, gain, cotangent
):
    length, channels = q_input.shape
    groups = channels // GS
    wide = channels * lax.axis_size("tp")
    rows = groups // PER
    packed_rows = groups + 2 * rows + 24

    def arr(shape, dtype):
        return jax.ShapeDtypeStruct(shape, dtype)

    smem = pl.BlockSpec(memory_space=pltpu.SMEM)
    vmem = pl.BlockSpec(memory_space=pltpu.VMEM)
    far_off = pl.BlockSpec(memory_space=pltpu.HBM)
    full_bf = arr((length, channels), BF16)
    full_f = arr((length, channels), F32)

    def call(name, kernel, outs, ins, scratch=(), flops=10**8, moved=10**6, grant=8, hbm=False):
        scalar = ins[0] is lengths
        return pl.pallas_call(
            kernel,
            out_shape=outs,
            in_specs=[far_off] * len(ins)
            if hbm
            else [smem if (i == 0 and scalar) else vmem for i in range(len(ins))],
            out_specs=[vmem] * len(outs),
            scratch_shapes=scratch,
            compiler_params=pltpu.CompilerParams(vmem_limit_bytes=grant * 1024 * 1024),
            cost_estimate=pl.CostEstimate(flops=flops, bytes_accessed=moved, transcendentals=0),
            name=name,
        )(*ins)

    skip2 = skip.reshape(1, channels)
    gain2 = gain.reshape(1, channels)
    taps, sent, far = call(
        "first", first_kernel,
        [arr((24, channels), F32), arr((SENT, channels), BF16), arr((2 * RIM, channels), BF16)],
        [lengths, jnp.transpose(short_filter, (0, 2, 1)), q_input, k_input, v_input],
        [
            pltpu.SMEM(lengths.shape, jnp.int32), pltpu.VMEM((3, KS, groups), BF16),
            pltpu.VMEM((PACK, channels), BF16), pltpu.VMEM((length, channels), BF16),
            pltpu.VMEM((length, channels), BF16), pltpu.SemaphoreType.DMA((5,)),
        ],
        grant=60,
        hbm=True,
    )
    came = shifted(sent, "ctx", 1)
    came_far = shifted(far, "ctx", 2)

    def circulants(filt, turned):
        return call(
            "circulants", functools.partial(circulant_kernel, turned),
            [arr((K, groups * K), BF16)], [filt], [pltpu.VMEM((groups, K), F32)],
            flops=10**9, moved=4 * 10**6,
        )[0]

    filt, sent = lax.optimization_barrier((long_filter, sent))
    fwd = circulants(filt, True)
    bulk, part, top = call(
        "current", current_kernel, [full_f, full_f, full_bf],
        [lengths, q_input, taps, sent, fwd, skip2], flops=10**9, moved=5 * 10**6,
    )
    q_short, gated, before, mixed, summed, sums = call(
        "summed", summed_kernel,
        [full_f, full_bf, full_bf, full_f, full_f, arr((2, K), F32)],
        [
            lengths, came, came_far, q_input, k_input, v_input, taps, sent, fwd, top,
            bulk, part, skip2, resid, cotangent, gain2,
        ],
        [pltpu.VMEM((2, K, LANES), F32)], flops=10**9, moved=5 * 10**6,
    )
    own_sums = sums
    step = 1
    while step < lax.axis_size("tp"):
        sums = sums + swapped(sums, "tp", step)
        step *= 2
    filt, came, _ = lax.optimization_barrier((long_filter, came, own_sums))
    bwd = circulants(filt, False)
    k_short, v_short = call(
        "gates", gates_kernel, [full_f] * 2, [lengths, k_input, v_input, came, taps],
        flops=10**8, moved=2 * 10**6,
    )
    sums, bwd, k_short, v_short = lax.optimization_barrier((sums, bwd, k_short, v_short))
    grad_mixed, grad_qs = call(
        "grads", functools.partial(grads_kernel, wide), [full_bf, full_bf],
        [summed, mixed, q_short, cotangent, gain2, sums],
    )
    after = shifted(grad_mixed, "ctx", -1)
    stats, part, qcols = call(
        "beside", functools.partial(beside_kernel, wide),
        [
            arr((groups + 2 * rows, LANES), F32), full_f, arr((8, channels), F32),
        ],
        [
            lengths, summed, cotangent, sums, grad_mixed, grad_qs, gated, before, bwd,
            skip2, q_input, came,
        ],
        flops=4 * 10**9, moved=5 * 10**6,
    )
    grad_ks, grad_vs, tails, packed = call(
        "gate", gate_kernel,
        [
            full_bf, full_bf, arr((4 * RIM, channels), BF16),
            arr((packed_rows, LANES), F32),
        ],
        [
            lengths, part, after, bwd, k_short, v_short, grad_qs, k_input, v_input, came,
            stats, qcols,
        ],
        [pltpu.VMEM((24, channels), F32)], flops=10**9, moved=5 * 10**6,
    )
    tails = shifted(tails, "ctx", -1)
    grad_q, grad_k, grad_v, normed = call(
        "mains", functools.partial(mains_kernel, wide), [full_bf] * 4,
        [lengths, taps, grad_qs, grad_ks, grad_vs, tails, summed, gain2, sums], flops=10**9, moved=5 * 10**6,
    )
    outs = (grad_q, grad_k, grad_v, normed)
    count = lax.axis_size("ctx")
    step = 1
    while 2 * step < count:
        packed = packed + swapped(packed, "ctx", step)
        step *= 2
    packed, *outs = lax.optimization_barrier((packed, *outs))
    grad_q, grad_k, grad_v, normed = outs
    other = swapped(packed, "ctx", step)
    grad_short, grad_long, grad_skip, grad_gain = call(
        "unpack", unpack_kernel,
        [
            arr((3, KS, groups), F32), arr((groups, K), F32),
            arr((rows, LANES), F32), arr((rows, LANES), F32),
        ],
        [packed, other],
    )
    return (
        normed, grad_q, grad_k, grad_v, jnp.transpose(grad_short, (0, 2, 1)), grad_long,
        grad_skip.reshape(channels), grad_gain.reshape(channels),
    )


def solution(mesh):
    tiled = P("ctx", "tp")
    return jax.shard_map(
        shards,
        mesh=mesh,
        in_specs=(
            tiled, tiled, tiled, tiled, P(), P(None, "tp", None), P("tp", None), P("tp"), P("tp"),
            tiled,
        ),
        out_specs=(
            tiled, tiled, tiled, tiled, P(None, "tp", None), P("tp", None), P("tp"), P("tp"),
        ),
        check_vma=False,
    )
```

```python
import functools

import jax
import jax.numpy as jnp
from jax import lax
from jax.experimental import pallas as pl
from jax.experimental.pallas import tpu as pltpu
from jax.sharding import PartitionSpec as P

GS = 16
K = 128
KS = 7
LANES = 128
PER = LANES // GS
RIM = 8
PACK = 16
EPS = 1e-06
F32 = jnp.float32
BF16 = jnp.bfloat16


def shifted(x, axis, by):
    count = lax.axis_size(axis)
    return lax.ppermute(x, axis, [(i, (i + by) % count) for i in range(count)])


def swapped(x, axis, step):
    return lax.ppermute(x, axis, [(i, i ^ step) for i in range(lax.axis_size(axis))])


def iota(shape, dim):
    return lax.broadcasted_iota(jnp.int32, shape, dim)


def positions(len_ref, rows):
    begin = jnp.zeros_like(rows)
    start = jnp.int32(0)
    for n in range(len_ref.shape[0]):
        begin = jnp.where(rows >= start, start, begin)
        start = start + len_ref[n]
    return jnp.where(rows < start, rows - begin, -1)


def first_row():
    return lax.axis_index("ctx") * K


def lanes_of(q):
    return pl.ds(pl.multiple_of(q * LANES, LANES), LANES)


def each_chunk(channels, body, unroll=2):
    def step(q, carry):
        body(q)
        return carry

    lax.fori_loop(0, channels // LANES, step, 0, unroll=unroll)


def as_mask(cond):
    return jnp.where(cond, 1.0, 0.0).astype(BF16)


def join(*parts):
    return jnp.concatenate(parts, axis=0)


def tap_rows(taps_ref, which, ls):
    table = taps_ref[which * 8 : which * 8 + 8, ls]
    return [table[j : j + 1, :] for j in range(KS)]


def causal(ext, taps, pos):
    rows = ext.shape[0] - RIM
    total = taps[0] * ext[RIM:]
    for j in range(1, KS):
        moved = ext[RIM - j : RIM - j + rows]
        total = total + taps[j] * jnp.where(pos >= j, moved, 0.0)
    return total


def tap_lines(grad, ext, pos):
    lines = [jnp.sum(grad * ext[RIM:], axis=0, keepdims=True)]
    for j in range(1, KS):
        held = jnp.where(pos >= j, grad, 0.0)
        lines.append(jnp.sum(held * ext[RIM - j : RIM - j + K], axis=0, keepdims=True))
    lines.append(jnp.zeros((8 - KS, LANES), F32))
    return join(*lines)


def owners():
    lane = iota((K, LANES), 1) // GS
    return [as_mask(lane == g) for g in range(PER)]


def per_group(right, own):
    return join(*[right * mask for mask in own])


def masked(table_ref, q, mask):
    table = table_ref[:, pl.ds(pl.multiple_of(q * PER * K, PER * K), PER * K)]
    return [table[:, g * K : (g + 1) * K] * mask for g in range(PER)]


def product(left, right):
    return jnp.dot(jnp.concatenate(left, axis=1), right, preferred_element_type=F32)


K_FIRST, Q_LAST, K_LAST, V_LAST, V_FIRST, SENT = 0, K, K + 8, K + 16, K + 24, K + 32


def rim_of(ref, at, ls):
    base = at // PACK * PACK
    return ref[base : base + PACK, ls].astype(F32)[at - base : at - base + RIM]


def first_kernel(
    len_hbm, short_hbm, q_hbm, k_hbm, v_hbm, taps_ref, sent_ref, far_ref,
    len_ref, short_ref, q_ref, k_ref, v_ref, sems,
):
    groups = short_ref.shape[2]
    channels = taps_ref.shape[1]
    pairs = (
        (short_hbm, short_ref), (len_hbm, len_ref), (k_hbm, k_ref), (v_hbm, v_ref),
        (q_hbm.at[K - PACK : K], q_ref),
    )
    copies = [pltpu.make_async_copy(a, b, sems.at[i]) for i, (a, b) in enumerate(pairs)]
    for copy in copies:
        copy.start()
    spread = as_mask(iota((groups, channels), 1) // GS == iota((groups, channels), 0))
    copies[0].wait()
    for i in range(3):
        taps_ref[i * 8 : i * 8 + KS] = jnp.dot(
            short_ref[i], spread, preferred_element_type=F32
        )
        taps_ref[i * 8 + KS : i * 8 + 8] = jnp.zeros((8 - KS, channels), F32)
    for copy in copies[1:]:
        copy.wait()
    pos = positions(len_ref, first_row() + RIM + iota((K - RIM, LANES), 0))

    def body(q):
        ls = lanes_of(q)
        kx = k_ref[:, ls].astype(F32)
        vx = v_ref[:, ls].astype(F32)
        ks = causal(kx, tap_rows(taps_ref, 1, ls), pos)
        vs = causal(vx, tap_rows(taps_ref, 2, ls), pos)
        sent_ref[:K, ls] = join(kx[:RIM], ks * vs).astype(BF16)
        q_end = q_ref[:, ls].astype(F32)[PACK - RIM :]
        k_end = kx[K - RIM :]
        v_end = vx[K - RIM :]
        sent_ref[K:, ls] = join(q_end, k_end, v_end, vx[:RIM]).astype(BF16)
        far_ref[:, ls] = join(k_end, v_end).astype(BF16)

    each_chunk(channels, body)


def circulant_kernel(turned, long_ref, out_ref, line_ref):
    groups = long_ref.shape[0]
    filt = long_ref[...]
    if turned:
        flip = as_mask((iota((K, K), 0) + iota((K, K), 1)) % K == 0)
        line_ref[...] = jnp.dot(filt, flip, preferred_element_type=F32)
    else:
        line_ref[...] = filt.astype(F32)

    def step(g, carry):
        row = jnp.broadcast_to(line_ref[pl.ds(g, 1), :], (GS, K))
        block = pltpu.roll(row, 0, 1, stride=1, stride_axis=0)
        for i in range(K // GS):
            moved = block if i == 0 else pltpu.roll(block, i * GS, 1)
            at = pl.ds(pl.multiple_of(g * K, K), K)
            out_ref[i * GS : (i + 1) * GS, at] = moved.astype(BF16)
        return carry

    lax.fori_loop(0, groups, step, 0, unroll=8)


def current_kernel(
    len_ref, q_ref, taps_ref, sent_ref, fwd_ref, skip_ref, qs_ref, part_ref, top_ref
):
    row = iota((K, LANES), 0)
    col = iota((K, LANES), 1)
    pos = positions(len_ref, first_row() + row)
    near = (col <= row) & (pos >= row - col)
    mask = as_mask(near)
    mask_top = as_mask(near & (col < RIM))
    picks = join(*[as_mask((col == row + g * GS) & (row < GS)) for g in range(PER)])
    own = owners()
    top = jnp.zeros((RIM, LANES), F32)

    def body(q):
        ls = lanes_of(q)
        qs_ref[RIM:, ls] = causal(q_ref[:, ls].astype(F32), tap_rows(taps_ref, 0, ls), pos[RIM:])
        qs_ref[:RIM, ls] = top
        gated = join(top, sent_ref[:K, ls].astype(F32)[RIM:])
        rest = product(masked(fwd_ref, q, mask), per_group(gated.astype(BF16), own))
        part_ref[:, ls] = rest + skip_ref[:, ls] * gated
        top_ref[:, ls] = product(masked(fwd_ref, q, mask_top), picks).astype(BF16)

    each_chunk(q_ref.shape[1], body)


def summed_kernel(
    len_ref, came_ref, far_ref, q_ref, k_ref, v_ref, taps_ref, sent_ref, fwd_ref, top_ref,
    bulk_ref, part_ref, skip_ref, resid_ref, cot_ref, gain_ref,
    qs_ref, gated_ref, before_ref, mixed_ref, summed_ref, sums_ref, acc_ref,
):
    row = iota((K, LANES), 0)
    col = iota((K, LANES), 1)
    pos = positions(len_ref, first_row() + row)
    mask = as_mask((col > row) & (pos >= row - col + K))
    pos_top = pos[:RIM]
    pos_far = positions(len_ref, first_row() - K + iota((RIM, LANES), 0))
    own = owners()
    own_top = [
        as_mask((iota((PACK, LANES), 1) // GS == g) & (iota((PACK, LANES), 0) < RIM))
        for g in range(PER)
    ]
    acc_ref[...] = jnp.zeros_like(acc_ref)

    def body(q):
        ls = lanes_of(q)
        kt = tap_rows(taps_ref, 1, ls)
        vt = tap_rows(taps_ref, 2, ls)
        k_last = rim_of(came_ref, K_LAST, ls)
        v_last = rim_of(came_ref, V_LAST, ls)
        top = causal(join(k_last, rim_of(k_ref, 0, ls)), kt, pos_top) * causal(
            join(v_last, rim_of(v_ref, 0, ls)), vt, pos_top
        )
        far_top = causal(
            join(rim_of(far_ref, 0, ls), rim_of(came_ref, K_FIRST, ls)), kt, pos_far
        ) * causal(join(rim_of(far_ref, RIM, ls), rim_of(came_ref, V_FIRST, ls)), vt, pos_far)
        qs_top = causal(
            join(rim_of(came_ref, Q_LAST, ls), rim_of(q_ref, 0, ls)), tap_rows(taps_ref, 0, ls), pos_top
        )
        before = join(far_top, came_ref[:K, ls].astype(F32)[RIM:]).astype(BF16)
        gated = join(top, sent_ref[:K, ls].astype(F32)[RIM:]).astype(BF16)
        before_ref[:, ls] = before
        gated_ref[:, ls] = gated
        qs = join(qs_top, bulk_ref[RIM:, ls])
        qs_ref[:, ls] = qs
        first = gated[:PACK]
        left = masked(fwd_ref, q, mask) + [top_ref[:, ls]]
        right = join(per_group(before, own), per_group(first, own_top))
        direct = skip_ref[:, ls] * first.astype(F32)[:RIM]
        mixed = part_ref[:, ls] + product(left, right)
        mixed = join(mixed[:RIM] + direct, mixed[RIM:])
        summed = resid_ref[:, ls].astype(F32) + qs * mixed
        mixed_ref[:, ls] = mixed
        summed_ref[:, ls] = summed
        acc_ref[0] += summed * summed
        acc_ref[1] += gain_ref[:, ls] * cot_ref[:, ls].astype(F32) * summed

    each_chunk(resid_ref.shape[1], body)
    for i in range(2):
        sums_ref[i : i + 1] = jnp.sum(acc_ref[i].T, axis=0, keepdims=True)


def by_row(line):
    return jnp.broadcast_to(line, (K, K)).T


def inverse_of(sums_ref, total):
    return by_row(lax.rsqrt(sums_ref[0:1] / total + EPS))


def gates_kernel(len_ref, k_ref, v_ref, came_ref, taps_ref, ks_ref, vs_ref):
    pos = positions(len_ref, first_row() + iota((K, LANES), 0))

    def body(q):
        ls = lanes_of(q)
        k_ext = join(rim_of(came_ref, K_LAST, ls), k_ref[:, ls].astype(F32))
        v_ext = join(rim_of(came_ref, V_LAST, ls), v_ref[:, ls].astype(F32))
        ks_ref[:, ls] = causal(k_ext, tap_rows(taps_ref, 1, ls), pos)
        vs_ref[:, ls] = causal(v_ext, tap_rows(taps_ref, 2, ls), pos)

    each_chunk(k_ref.shape[1], body)


def grads_kernel(total, summed_ref, mixed_ref, qs_ref, cot_ref, gain_ref, sums_ref, gm_ref, gq_ref):
    inverse = inverse_of(sums_ref, total)
    scale = inverse * inverse * by_row(sums_ref[1:2] / total)

    def body(q):
        ls = lanes_of(q)
        scaled = gain_ref[:, ls] * cot_ref[:, ls].astype(F32)
        grad_sum = inverse * (scaled - summed_ref[:, ls] * scale)
        gm_ref[:, ls] = (grad_sum * qs_ref[:, ls]).astype(BF16)
        gq_ref[:, ls] = (grad_sum * mixed_ref[:, ls]).astype(BF16)

    each_chunk(cot_ref.shape[1], body)


def beside_kernel(
    total, len_ref, summed_ref, cot_ref, sums_ref, gm_ref, gq_ref, gated_ref, before_ref,
    bwd_ref, skip_ref, q_ref, came_ref, stats_ref, part_ref, cols_ref,
):
    groups = bwd_ref.shape[1] // K
    inverse = inverse_of(sums_ref, total)
    row = iota((K, LANES), 0)
    col = iota((K, LANES), 1)
    pos_row = positions(len_ref, first_row() + row)
    pos = positions(len_ref, first_row() + col)
    mask = as_mask((col >= row) & (pos >= col - row))
    source = K - 1 - row
    near = (col >= source) & (pos >= col - source)
    far = (col < source) & (pos >= col - source + K)
    flip = as_mask(row + col == K - 1)
    own = owners()

    def body(q):
        ls = lanes_of(q)
        summed = summed_ref[:, ls]
        gm = gm_ref[:, ls]
        gmf = gm.astype(F32)
        gated = gated_ref[:, ls]
        stats_ref[pl.ds(groups + q, 1), :] = jnp.sum(gmf * gated.astype(F32), axis=0, keepdims=True)
        stats_ref[pl.ds(groups + groups // PER + q, 1), :] = jnp.sum(
            cot_ref[:, ls].astype(F32) * summed * inverse, axis=0, keepdims=True
        )
        right = per_group(gm, own)
        part_ref[:, ls] = skip_ref[:, ls] * gmf + product(masked(bwd_ref, q, mask), right)
        two = jnp.concatenate([before_ref[:, ls], gated], axis=1)
        flipped = jnp.dot(flip, two, preferred_element_type=F32).astype(BF16)
        left = join(flipped[:, :LANES], flipped[:, LANES:])
        turned = gmf.T.astype(BF16)
        spread = []
        for g in range(PER):
            pieces = [jnp.zeros((GS, K), BF16)] * PER
            pieces[g] = turned[g * GS : (g + 1) * GS]
            spread.append(join(*pieces))
        cross = jnp.dot(left, jnp.concatenate(spread, axis=1), preferred_element_type=F32)
        lines = []
        for g in range(PER):
            gs = slice(g * K, (g + 1) * K)
            square = jnp.where(near, cross[K:, gs], jnp.where(far, cross[:K, gs], 0.0))
            square = pltpu.roll(square, 1, 1, stride=1, stride_axis=0)
            lines.append(jnp.sum(square, axis=0, keepdims=True))
        stats_ref[pl.ds(pl.multiple_of(q * PER, PER), PER), :] = join(*lines)
        q_ext = join(rim_of(came_ref, Q_LAST, ls), q_ref[:, ls].astype(F32))
        cols_ref[:, ls] = tap_lines(gq_ref[:, ls].astype(F32), q_ext, pos_row)

    each_chunk(cot_ref.shape[1], body, 1)


def gate_kernel(
    len_ref, part_ref, after_ref, bwd_ref, ks_ref, vs_ref, gq_ref, k_ref, v_ref, came_ref,
    stats_ref, qcols_ref, gks_ref, gvs_ref, tails_ref, packed_ref, cols_ref,
):
    channels = part_ref.shape[1]
    kept = stats_ref.shape[0]
    row = iota((K, LANES), 0)
    col = iota((K, LANES), 1)
    pos_row = positions(len_ref, first_row() + row)
    pos = positions(len_ref, first_row() + K + col)
    mask = as_mask((col < row) & (pos >= col - row + K))
    own = owners()

    def body(q):
        ls = lanes_of(q)
        right = per_group(after_ref[:, ls], own)
        grad = part_ref[:, ls] + product(masked(bwd_ref, q, mask), right)
        gks = (grad * vs_ref[:, ls]).astype(BF16)
        gvs = (grad * ks_ref[:, ls]).astype(BF16)
        gks_ref[:, ls] = gks
        gvs_ref[:, ls] = gvs
        heads = (rim_of(gq_ref, 0, ls), gks.astype(F32)[:RIM], gvs.astype(F32)[:RIM])
        tails_ref[:, ls] = join(*heads, jnp.zeros((RIM, LANES), F32)).astype(BF16)
        k_ext = join(rim_of(came_ref, K_LAST, ls), k_ref[:, ls].astype(F32))
        v_ext = join(rim_of(came_ref, V_LAST, ls), v_ref[:, ls].astype(F32))
        cols_ref[0:8, ls] = qcols_ref[:, ls]
        cols_ref[8:16, ls] = tap_lines(gks.astype(F32), k_ext, pos_row)
        cols_ref[16:24, ls] = tap_lines(gvs.astype(F32), v_ext, pos_row)

    each_chunk(channels, body)
    packed_ref[0:kept] = stats_ref[...]
    gather = jnp.where(
        iota((channels, LANES), 0) // GS == iota((channels, LANES), 1), 1.0, 0.0
    )
    packed_ref[kept:] = jnp.dot(
        cols_ref[...], gather, preferred_element_type=F32, precision=lax.Precision.HIGHEST
    )


def mains_kernel(
    total, len_ref, taps_ref, gq_ref, gks_ref, gvs_ref, tails_ref, summed_ref, gain_ref, sums_ref,
    oq_ref, ok_ref, ov_ref, normed_ref,
):
    pos = positions(len_ref, first_row() + iota((K + RIM, LANES), 0))
    inverse = inverse_of(sums_ref, total)

    def body(q):
        ls = lanes_of(q)
        normed_ref[:, ls] = (gain_ref[:, ls] * summed_ref[:, ls] * inverse).astype(BF16)
        for i, (g_ref, o_ref) in enumerate(((gq_ref, oq_ref), (gks_ref, ok_ref), (gvs_ref, ov_ref))):
            ext = join(g_ref[:, ls].astype(F32), rim_of(tails_ref, i * RIM, ls))
            taps = tap_rows(taps_ref, i, ls)
            grad = taps[0] * ext[:K]
            for j in range(1, KS):
                held = jnp.where(pos >= j, ext, 0.0)
                grad = grad + taps[j] * held[j : j + K]
            o_ref[:, ls] = grad.astype(BF16)

    each_chunk(gq_ref.shape[1], body)


def unpack_kernel(one_ref, two_ref, short_ref, long_ref, skip_ref, gain_ref):
    groups = long_ref.shape[0]
    rows = groups // PER
    total = one_ref[...] + two_ref[...]
    long_ref[...] = total[:groups]
    skip_ref[...] = total[groups : groups + rows]
    gain_ref[...] = total[groups + rows : groups + 2 * rows]
    for i in range(3):
        at = groups + 2 * rows + i * 8
        short_ref[i] = total[at : at + KS, :groups]


def shards(
    q_input, k_input, v_input, resid, lengths, short_filter, long_filter, skip, gain, cotangent
):
    length, channels = q_input.shape
    groups = channels // GS
    wide = channels * lax.axis_size("tp")
    rows = groups // PER
    packed_rows = groups + 2 * rows + 24

    def arr(shape, dtype):
        return jax.ShapeDtypeStruct(shape, dtype)

    smem = pl.BlockSpec(memory_space=pltpu.SMEM)
    vmem = pl.BlockSpec(memory_space=pltpu.VMEM)
    far_off = pl.BlockSpec(memory_space=pltpu.HBM)
    full_bf = arr((length, channels), BF16)
    full_f = arr((length, channels), F32)

    def call(name, kernel, outs, ins, scratch=(), flops=10**8, moved=10**6, grant=8, hbm=False):
        scalar = ins[0] is lengths
        return pl.pallas_call(
            kernel,
            out_shape=outs,
            in_specs=[far_off] * len(ins)
            if hbm
            else [smem if (i == 0 and scalar) else vmem for i in range(len(ins))],
            out_specs=[vmem] * len(outs),
            scratch_shapes=scratch,
            compiler_params=pltpu.CompilerParams(vmem_limit_bytes=grant * 1024 * 1024),
            cost_estimate=pl.CostEstimate(flops=flops, bytes_accessed=moved, transcendentals=0),
            name=name,
        )(*ins)

    skip2 = skip.reshape(1, channels)
    gain2 = gain.reshape(1, channels)
    taps, sent, far = call(
        "first", first_kernel,
        [arr((24, channels), F32), arr((SENT, channels), BF16), arr((2 * RIM, channels), BF16)],
        [lengths, jnp.transpose(short_filter, (0, 2, 1)), q_input, k_input, v_input],
        [
            pltpu.SMEM(lengths.shape, jnp.int32), pltpu.VMEM((3, KS, groups), BF16),
            pltpu.VMEM((PACK, channels), BF16), pltpu.VMEM((length, channels), BF16),
            pltpu.VMEM((length, channels), BF16), pltpu.SemaphoreType.DMA((5,)),
        ],
        grant=60,
        hbm=True,
    )
    came = shifted(sent, "ctx", 1)
    came_far = shifted(far, "ctx", 2)

    def circulants(filt, turned):
        return call(
            "circulants", functools.partial(circulant_kernel, turned),
            [arr((K, groups * K), BF16)], [filt], [pltpu.VMEM((groups, K), F32)],
            flops=10**9, moved=4 * 10**6,
        )[0]

    filt, sent = lax.optimization_barrier((long_filter, sent))
    fwd = circulants(filt, True)
    bulk, part, top = call(
        "current", current_kernel, [full_f, full_f, full_bf],
        [lengths, q_input, taps, sent, fwd, skip2], flops=10**9, moved=5 * 10**6,
    )
    q_short, gated, before, mixed, summed, sums = call(
        "summed", summed_kernel,
        [full_f, full_bf, full_bf, full_f, full_f, arr((2, K), F32)],
        [
            lengths, came, came_far, q_input, k_input, v_input, taps, sent, fwd, top,
            bulk, part, skip2, resid, cotangent, gain2,
        ],
        [pltpu.VMEM((2, K, LANES), F32)], flops=10**9, moved=5 * 10**6,
    )
    own_sums = sums
    step = 1
    while step < lax.axis_size("tp"):
        sums = sums + swapped(sums, "tp", step)
        step *= 2
    filt, came, _ = lax.optimization_barrier((long_filter, came, own_sums))
    bwd = circulants(filt, False)
    k_short, v_short = call(
        "gates", gates_kernel, [full_f] * 2, [lengths, k_input, v_input, came, taps],
        flops=10**8, moved=2 * 10**6,
    )
    sums, bwd, k_short, v_short = lax.optimization_barrier((sums, bwd, k_short, v_short))
    grad_mixed, grad_qs = call(
        "grads", functools.partial(grads_kernel, wide), [full_bf, full_bf],
        [summed, mixed, q_short, cotangent, gain2, sums],
    )
    after = shifted(grad_mixed, "ctx", -1)
    stats, part, qcols = call(
        "beside", functools.partial(beside_kernel, wide),
        [
            arr((groups + 2 * rows, LANES), F32), full_f, arr((8, channels), F32),
        ],
        [
            lengths, summed, cotangent, sums, grad_mixed, grad_qs, gated, before, bwd,
            skip2, q_input, came,
        ],
        flops=4 * 10**9, moved=5 * 10**6,
    )
    grad_ks, grad_vs, tails, packed = call(
        "gate", gate_kernel,
        [
            full_bf, full_bf, arr((4 * RIM, channels), BF16),
            arr((packed_rows, LANES), F32),
        ],
        [
            lengths, part, after, bwd, k_short, v_short, grad_qs, k_input, v_input, came,
            stats, qcols,
        ],
        [pltpu.VMEM((24, channels), F32)], flops=10**9, moved=5 * 10**6,
    )
    tails = shifted(tails, "ctx", -1)
    grad_q, grad_k, grad_v, normed = call(
        "mains", functools.partial(mains_kernel, wide), [full_bf] * 4,
        [lengths, taps, grad_qs, grad_ks, grad_vs, tails, summed, gain2, sums], flops=10**9, moved=5 * 10**6,
    )
    outs = (grad_q, grad_k, grad_v, normed)
    count = lax.axis_size("ctx")
    step = 1
    while 2 * step < count:
        packed = packed + swapped(packed, "ctx", step)
        step *= 2
    packed, *outs = lax.optimization_barrier((packed, *outs))
    grad_q, grad_k, grad_v, normed = outs
    other = swapped(packed, "ctx", step)
    grad_short, grad_long, grad_skip, grad_gain = call(
        "unpack", unpack_kernel,
        [
            arr((3, KS, groups), F32), arr((groups, K), F32),
            arr((rows, LANES), F32), arr((rows, LANES), F32),
        ],
        [packed, other],
    )
    return (
        normed, grad_q, grad_k, grad_v, jnp.transpose(grad_short, (0, 2, 1)), grad_long,
        grad_skip.reshape(channels), grad_gain.reshape(channels),
    )


def solution(mesh):
    tiled = P("ctx", "tp")
    return jax.shard_map(
        shards,
        mesh=mesh,
        in_specs=(
            tiled, tiled, tiled, tiled, P(), P(None, "tp", None), P("tp", None), P("tp"), P("tp"),
            tiled,
        ),
        out_specs=(
            tiled, tiled, tiled, tiled, P(None, "tp", None), P("tp", None), P("tp"), P("tp"),
        ),
        check_vma=False,
    )
```

```python
import functools

import jax
import jax.numpy as jnp
from jax import lax
from jax.experimental import pallas as pl
from jax.experimental.pallas import tpu as pltpu
from jax.sharding import PartitionSpec as P

GS = 16
K = 128
KS = 7
LANES = 128
PER = LANES // GS
RIM = 8
PACK = 16
EPS = 1e-06
F32 = jnp.float32
BF16 = jnp.bfloat16


def shifted(x, axis, by):
    count = lax.axis_size(axis)
    return lax.ppermute(x, axis, [(i, (i + by) % count) for i in range(count)])


def swapped(x, axis, step):
    return lax.ppermute(x, axis, [(i, i ^ step) for i in range(lax.axis_size(axis))])


def iota(shape, dim):
    return lax.broadcasted_iota(jnp.int32, shape, dim)


def positions(len_ref, rows):
    begin = jnp.zeros_like(rows)
    start = jnp.int32(0)
    for n in range(len_ref.shape[0]):
        begin = jnp.where(rows >= start, start, begin)
        start = start + len_ref[n]
    return jnp.where(rows < start, rows - begin, -1)


def first_row():
    return lax.axis_index("ctx") * K


def lanes_of(q):
    return pl.ds(pl.multiple_of(q * LANES, LANES), LANES)


def each_chunk(channels, body, unroll=2):
    def step(q, carry):
        body(q)
        return carry

    lax.fori_loop(0, channels // LANES, step, 0, unroll=unroll)


def as_mask(cond):
    return jnp.where(cond, 1.0, 0.0).astype(BF16)


def join(*parts):
    return jnp.concatenate(parts, axis=0)


def tap_rows(taps_ref, which, ls):
    table = taps_ref[which * 8 : which * 8 + 8, ls]
    return [table[j : j + 1, :] for j in range(KS)]


def causal(ext, taps, pos):
    rows = ext.shape[0] - RIM
    total = taps[0] * ext[RIM:]
    for j in range(1, KS):
        moved = ext[RIM - j : RIM - j + rows]
        total = total + taps[j] * jnp.where(pos >= j, moved, 0.0)
    return total


def tap_lines(grad, ext, pos):
    lines = [jnp.sum(grad * ext[RIM:], axis=0, keepdims=True)]
    for j in range(1, KS):
        held = jnp.where(pos >= j, grad, 0.0)
        lines.append(jnp.sum(held * ext[RIM - j : RIM - j + K], axis=0, keepdims=True))
    lines.append(jnp.zeros((8 - KS, LANES), F32))
    return join(*lines)


def owners():
    lane = iota((K, LANES), 1) // GS
    return [as_mask(lane == g) for g in range(PER)]


def per_group(right, own):
    return join(*[right * mask for mask in own])


def masked(table_ref, q, mask):
    table = table_ref[:, pl.ds(pl.multiple_of(q * PER * K, PER * K), PER * K)]
    return [table[:, g * K : (g + 1) * K] * mask for g in range(PER)]


def product(left, right):
    return jnp.dot(jnp.concatenate(left, axis=1), right, preferred_element_type=F32)


K_FIRST, Q_LAST, K_LAST, V_LAST, V_FIRST, SENT = 0, K, K + 8, K + 16, K + 24, K + 32


def rim_of(ref, at, ls):
    base = at // PACK * PACK
    return ref[base : base + PACK, ls].astype(F32)[at - base : at - base + RIM]


def first_kernel(
    len_hbm, short_hbm, q_hbm, k_hbm, v_hbm, taps_ref, sent_ref, far_ref,
    len_ref, short_ref, q_ref, k_ref, v_ref, sems,
):
    groups = short_ref.shape[2]
    channels = taps_ref.shape[1]
    pairs = (
        (short_hbm, short_ref), (len_hbm, len_ref), (k_hbm, k_ref), (v_hbm, v_ref),
        (q_hbm.at[K - PACK : K], q_ref),
    )
    copies = [pltpu.make_async_copy(a, b, sems.at[i]) for i, (a, b) in enumerate(pairs)]
    for copy in copies:
        copy.start()
    spread = as_mask(iota((groups, channels), 1) // GS == iota((groups, channels), 0))
    copies[0].wait()
    for i in range(3):
        taps_ref[i * 8 : i * 8 + KS] = jnp.dot(
            short_ref[i], spread, preferred_element_type=F32
        )
        taps_ref[i * 8 + KS : i * 8 + 8] = jnp.zeros((8 - KS, channels), F32)
    for copy in copies[1:]:
        copy.wait()
    pos = positions(len_ref, first_row() + RIM + iota((K - RIM, LANES), 0))

    def body(q):
        ls = lanes_of(q)
        kx = k_ref[:, ls].astype(F32)
        vx = v_ref[:, ls].astype(F32)
        ks = causal(kx, tap_rows(taps_ref, 1, ls), pos)
        vs = causal(vx, tap_rows(taps_ref, 2, ls), pos)
        sent_ref[:K, ls] = join(kx[:RIM], ks * vs).astype(BF16)
        q_end = q_ref[:, ls].astype(F32)[PACK - RIM :]
        k_end = kx[K - RIM :]
        v_end = vx[K - RIM :]
        sent_ref[K:, ls] = join(q_end, k_end, v_end, vx[:RIM]).astype(BF16)
        far_ref[:, ls] = join(k_end, v_end).astype(BF16)

    each_chunk(channels, body)


def circulant_kernel(turned, long_ref, out_ref, line_ref):
    groups = long_ref.shape[0]
    filt = long_ref[...]
    if turned:
        flip = as_mask((iota((K, K), 0) + iota((K, K), 1)) % K == 0)
        line_ref[...] = jnp.dot(filt, flip, preferred_element_type=F32)
    else:
        line_ref[...] = filt.astype(F32)

    def step(g, carry):
        row = jnp.broadcast_to(line_ref[pl.ds(g, 1), :], (GS, K))
        block = pltpu.roll(row, 0, 1, stride=1, stride_axis=0)
        for i in range(K // GS):
            moved = block if i == 0 else pltpu.roll(block, i * GS, 1)
            at = pl.ds(pl.multiple_of(g * K, K), K)
            out_ref[i * GS : (i + 1) * GS, at] = moved.astype(BF16)
        return carry

    lax.fori_loop(0, groups, step, 0, unroll=8)


def current_kernel(
    len_ref, q_ref, taps_ref, sent_ref, fwd_ref, skip_ref, qs_ref, part_ref, top_ref
):
    row = iota((K, LANES), 0)
    col = iota((K, LANES), 1)
    pos = positions(len_ref, first_row() + row)
    near = (col <= row) & (pos >= row - col)
    mask = as_mask(near)
    mask_top = as_mask(near & (col < RIM))
    picks = join(*[as_mask((col == row + g * GS) & (row < GS)) for g in range(PER)])
    own = owners()
    top = jnp.zeros((RIM, LANES), F32)

    def body(q):
        ls = lanes_of(q)
        qs_ref[RIM:, ls] = causal(q_ref[:, ls].astype(F32), tap_rows(taps_ref, 0, ls), pos[RIM:])
        qs_ref[:RIM, ls] = top
        gated = join(top, sent_ref[:K, ls].astype(F32)[RIM:])
        rest = product(masked(fwd_ref, q, mask), per_group(gated.astype(BF16), own))
        part_ref[:, ls] = rest + skip_ref[:, ls] * gated
        top_ref[:, ls] = product(masked(fwd_ref, q, mask_top), picks).astype(BF16)

    each_chunk(q_ref.shape[1], body)


def summed_kernel(
    len_ref, came_ref, far_ref, q_ref, k_ref, v_ref, taps_ref, sent_ref, fwd_ref, top_ref,
    bulk_ref, part_ref, skip_ref, resid_ref, cot_ref, gain_ref,
    qs_ref, gated_ref, before_ref, mixed_ref, summed_ref, sums_ref, acc_ref,
):
    row = iota((K, LANES), 0)
    col = iota((K, LANES), 1)
    pos = positions(len_ref, first_row() + row)
    mask = as_mask((col > row) & (pos >= row - col + K))
    pos_top = pos[:RIM]
    pos_far = positions(len_ref, first_row() - K + iota((RIM, LANES), 0))
    own = owners()
    own_top = [
        as_mask((iota((PACK, LANES), 1) // GS == g) & (iota((PACK, LANES), 0) < RIM))
        for g in range(PER)
    ]
    acc_ref[...] = jnp.zeros_like(acc_ref)

    def body(q):
        ls = lanes_of(q)
        kt = tap_rows(taps_ref, 1, ls)
        vt = tap_rows(taps_ref, 2, ls)
        k_last = rim_of(came_ref, K_LAST, ls)
        v_last = rim_of(came_ref, V_LAST, ls)
        top = causal(join(k_last, rim_of(k_ref, 0, ls)), kt, pos_top) * causal(
            join(v_last, rim_of(v_ref, 0, ls)), vt, pos_top
        )
        far_top = causal(
            join(rim_of(far_ref, 0, ls), rim_of(came_ref, K_FIRST, ls)), kt, pos_far
        ) * causal(join(rim_of(far_ref, RIM, ls), rim_of(came_ref, V_FIRST, ls)), vt, pos_far)
        qs_top = causal(
            join(rim_of(came_ref, Q_LAST, ls), rim_of(q_ref, 0, ls)), tap_rows(taps_ref, 0, ls), pos_top
        )
        before = join(far_top, came_ref[:K, ls].astype(F32)[RIM:]).astype(BF16)
        gated = join(top, sent_ref[:K, ls].astype(F32)[RIM:]).astype(BF16)
        before_ref[:, ls] = before
        gated_ref[:, ls] = gated
        qs = join(qs_top, bulk_ref[RIM:, ls])
        qs_ref[:, ls] = qs
        first = gated[:PACK]
        left = masked(fwd_ref, q, mask) + [top_ref[:, ls]]
        right = join(per_group(before, own), per_group(first, own_top))
        direct = skip_ref[:, ls] * first.astype(F32)[:RIM]
        mixed = part_ref[:, ls] + product(left, right)
        mixed = join(mixed[:RIM] + direct, mixed[RIM:])
        summed = resid_ref[:, ls].astype(F32) + qs * mixed
        mixed_ref[:, ls] = mixed
        summed_ref[:, ls] = summed
        acc_ref[0] += summed * summed
        acc_ref[1] += gain_ref[:, ls] * cot_ref[:, ls].astype(F32) * summed

    each_chunk(resid_ref.shape[1], body)
    for i in range(2):
        sums_ref[i : i + 1] = jnp.sum(acc_ref[i].T, axis=0, keepdims=True)


def group_sums(cols):
    count, channels = cols.shape
    gather = as_mask(iota((channels, LANES), 0) // GS == iota((channels, LANES), 1))
    high = cols.astype(BF16)
    rest = cols - high.astype(F32)
    mid = rest.astype(BF16)
    low = (rest - mid.astype(F32)).astype(BF16)
    parts = join(high.astype(F32), mid.astype(F32), low.astype(F32)).astype(BF16)
    sums = jnp.dot(parts, gather, preferred_element_type=F32)
    return sums[:count] + sums[count : 2 * count] + sums[2 * count :]


def by_row(line):
    return jnp.broadcast_to(line, (K, K)).T


def inverse_of(sums_ref, total):
    return by_row(lax.rsqrt(sums_ref[0:1] / total + EPS))


def gates_kernel(len_ref, k_ref, v_ref, came_ref, taps_ref, ks_ref, vs_ref):
    pos = positions(len_ref, first_row() + iota((K, LANES), 0))

    def body(q):
        ls = lanes_of(q)
        k_ext = join(rim_of(came_ref, K_LAST, ls), k_ref[:, ls].astype(F32))
        v_ext = join(rim_of(came_ref, V_LAST, ls), v_ref[:, ls].astype(F32))
        ks_ref[:, ls] = causal(k_ext, tap_rows(taps_ref, 1, ls), pos)
        vs_ref[:, ls] = causal(v_ext, tap_rows(taps_ref, 2, ls), pos)

    each_chunk(k_ref.shape[1], body)


def grads_kernel(total, summed_ref, mixed_ref, qs_ref, cot_ref, gain_ref, sums_ref, gm_ref, gq_ref, head_ref):
    inverse = inverse_of(sums_ref, total)
    scale = inverse * inverse * by_row(sums_ref[1:2] / total)

    def body(q):
        ls = lanes_of(q)
        scaled = gain_ref[:, ls] * cot_ref[:, ls].astype(F32)
        grad_sum = inverse * (scaled - summed_ref[:, ls] * scale)
        gm_ref[:, ls] = (grad_sum * qs_ref[:, ls]).astype(BF16)
        gq = (grad_sum * mixed_ref[:, ls]).astype(BF16)
        gq_ref[:, ls] = gq
        head_ref[:, ls] = gq[:PACK]

    each_chunk(cot_ref.shape[1], body)


def beside_kernel(
    total, len_ref, summed_ref, cot_ref, sums_ref, gm_ref, gq_ref, gated_ref, before_ref,
    bwd_ref, skip_ref, q_ref, came_ref, stats_ref, part_ref, cols_ref,
):
    groups = bwd_ref.shape[1] // K
    inverse = inverse_of(sums_ref, total)
    row = iota((K, LANES), 0)
    col = iota((K, LANES), 1)
    pos_row = positions(len_ref, first_row() + row)
    pos = positions(len_ref, first_row() + col)
    mask = as_mask((col >= row) & (pos >= col - row))
    source = K - 1 - row
    near = (col >= source) & (pos >= col - source)
    far = (col < source) & (pos >= col - source + K)
    flip = as_mask(row + col == K - 1)
    own = owners()

    def body(q):
        ls = lanes_of(q)
        summed = summed_ref[:, ls]
        gm = gm_ref[:, ls]
        gmf = gm.astype(F32)
        gated = gated_ref[:, ls]
        stats_ref[pl.ds(groups + q, 1), :] = jnp.sum(gmf * gated.astype(F32), axis=0, keepdims=True)
        stats_ref[pl.ds(groups + groups // PER + q, 1), :] = jnp.sum(
            cot_ref[:, ls].astype(F32) * summed * inverse, axis=0, keepdims=True
        )
        right = per_group(gm, own)
        part_ref[:, ls] = skip_ref[:, ls] * gmf + product(masked(bwd_ref, q, mask), right)
        two = jnp.concatenate([before_ref[:, ls], gated], axis=1)
        flipped = jnp.dot(flip, two, preferred_element_type=F32).astype(BF16)
        left = join(flipped[:, :LANES], flipped[:, LANES:])
        turned = gmf.T.astype(BF16)
        spread = []
        for g in range(PER):
            pieces = [jnp.zeros((GS, K), BF16)] * PER
            pieces[g] = turned[g * GS : (g + 1) * GS]
            spread.append(join(*pieces))
        cross = jnp.dot(left, jnp.concatenate(spread, axis=1), preferred_element_type=F32)
        lines = []
        for g in range(PER):
            gs = slice(g * K, (g + 1) * K)
            square = jnp.where(near, cross[K:, gs], jnp.where(far, cross[:K, gs], 0.0))
            square = pltpu.roll(square, 1, 1, stride=1, stride_axis=0)
            lines.append(jnp.sum(square, axis=0, keepdims=True))
        stats_ref[pl.ds(pl.multiple_of(q * PER, PER), PER), :] = join(*lines)
        q_ext = join(rim_of(came_ref, Q_LAST, ls), q_ref[:, ls].astype(F32))
        cols_ref[:, ls] = tap_lines(gq_ref[:, ls].astype(F32), q_ext, pos_row)

    each_chunk(cot_ref.shape[1], body, 1)
    stats_ref[groups + 2 * (groups // PER) :] = group_sums(cols_ref[...])


def gate_kernel(
    len_ref, part_ref, after_ref, bwd_ref, ks_ref, vs_ref, k_ref, v_ref, came_ref,
    gks_ref, gvs_ref, tails_ref, short_ref, cols_ref,
):
    channels = part_ref.shape[1]
    row = iota((K, LANES), 0)
    col = iota((K, LANES), 1)
    pos_row = positions(len_ref, first_row() + row)
    pos = positions(len_ref, first_row() + K + col)
    mask = as_mask((col < row) & (pos >= col - row + K))
    own = owners()

    def body(q):
        ls = lanes_of(q)
        right = per_group(after_ref[:, ls], own)
        grad = part_ref[:, ls] + product(masked(bwd_ref, q, mask), right)
        gks = (grad * vs_ref[:, ls]).astype(BF16)
        gvs = (grad * ks_ref[:, ls]).astype(BF16)
        gks_ref[:, ls] = gks
        gvs_ref[:, ls] = gvs
        tails_ref[:, ls] = join(gks.astype(F32)[:RIM], gvs.astype(F32)[:RIM]).astype(BF16)
        k_ext = join(rim_of(came_ref, K_LAST, ls), k_ref[:, ls].astype(F32))
        v_ext = join(rim_of(came_ref, V_LAST, ls), v_ref[:, ls].astype(F32))
        cols_ref[:8, ls] = tap_lines(gks.astype(F32), k_ext, pos_row)
        cols_ref[8:, ls] = tap_lines(gvs.astype(F32), v_ext, pos_row)

    each_chunk(channels, body)
    short_ref[...] = group_sums(cols_ref[...])


def back_short(which, at, pos, ls, taps_ref, grad_ref, tail_ref):
    ext = join(grad_ref[:, ls].astype(F32), rim_of(tail_ref, at, ls))
    taps = tap_rows(taps_ref, which, ls)
    grad = taps[0] * ext[:K]
    for j in range(1, KS):
        held = jnp.where(pos >= j, ext, 0.0)
        grad = grad + taps[j] * held[j : j + K]
    return grad.astype(BF16)


def main_kernel(which, at, len_ref, taps_ref, grad_ref, tail_ref, out_ref):
    pos = positions(len_ref, first_row() + iota((K + RIM, LANES), 0))

    def body(q):
        ls = lanes_of(q)
        out_ref[:, ls] = back_short(which, at, pos, ls, taps_ref, grad_ref, tail_ref)

    each_chunk(grad_ref.shape[1], body)


def main_q_kernel(
    total, len_ref, taps_ref, grad_ref, tail_ref, summed_ref, gain_ref, sums_ref, out_ref, normed_ref
):
    inverse = inverse_of(sums_ref, total)
    pos = positions(len_ref, first_row() + iota((K + RIM, LANES), 0))

    def body(q):
        ls = lanes_of(q)
        out_ref[:, ls] = back_short(0, 0, pos, ls, taps_ref, grad_ref, tail_ref)
        normed_ref[:, ls] = (gain_ref[:, ls] * summed_ref[:, ls] * inverse).astype(BF16)

    each_chunk(grad_ref.shape[1], body)


def unpack_kernel(
    stats_ref, stats2_ref, last_ref, last2_ref, short_ref, long_ref, skip_ref, gain_ref
):
    groups = long_ref.shape[0]
    rows = groups // PER
    stats = stats_ref[...] + stats2_ref[...]
    last = last_ref[...] + last2_ref[...]
    long_ref[...] = stats[:groups]
    skip_ref[...] = stats[groups : groups + rows]
    gain_ref[...] = stats[groups + rows : groups + 2 * rows]
    short_ref[0] = stats[groups + 2 * rows :][:KS, :groups]
    short_ref[1] = last[:KS, :groups]
    short_ref[2] = last[8 : 8 + KS, :groups]


def shards(
    q_input, k_input, v_input, resid, lengths, short_filter, long_filter, skip, gain, cotangent
):
    length, channels = q_input.shape
    groups = channels // GS
    wide = channels * lax.axis_size("tp")
    rows = groups // PER

    def arr(shape, dtype):
        return jax.ShapeDtypeStruct(shape, dtype)

    smem = pl.BlockSpec(memory_space=pltpu.SMEM)
    vmem = pl.BlockSpec(memory_space=pltpu.VMEM)
    far_off = pl.BlockSpec(memory_space=pltpu.HBM)
    full_bf = arr((length, channels), BF16)
    full_f = arr((length, channels), F32)

    def call(name, kernel, outs, ins, scratch=(), flops=10**8, moved=10**6, grant=8, hbm=False):
        scalar = ins[0] is lengths
        return pl.pallas_call(
            kernel,
            out_shape=outs,
            in_specs=[far_off] * len(ins)
            if hbm
            else [smem if (i == 0 and scalar) else vmem for i in range(len(ins))],
            out_specs=[vmem] * len(outs),
            scratch_shapes=scratch,
            compiler_params=pltpu.CompilerParams(vmem_limit_bytes=grant * 1024 * 1024),
            cost_estimate=pl.CostEstimate(flops=flops, bytes_accessed=moved, transcendentals=0),
            name=name,
        )(*ins)

    skip2 = skip.reshape(1, channels)
    gain2 = gain.reshape(1, channels)
    taps, sent, far = call(
        "first", first_kernel,
        [arr((24, channels), F32), arr((SENT, channels), BF16), arr((2 * RIM, channels), BF16)],
        [lengths, jnp.transpose(short_filter, (0, 2, 1)), q_input, k_input, v_input],
        [
            pltpu.SMEM(lengths.shape, jnp.int32), pltpu.VMEM((3, KS, groups), BF16),
            pltpu.VMEM((PACK, channels), BF16), pltpu.VMEM((length, channels), BF16),
            pltpu.VMEM((length, channels), BF16), pltpu.SemaphoreType.DMA((5,)),
        ],
        grant=60,
        hbm=True,
    )
    came = shifted(sent, "ctx", 1)
    came_far = shifted(far, "ctx", 2)

    def circulants(filt, turned):
        return call(
            "circulants", functools.partial(circulant_kernel, turned),
            [arr((K, groups * K), BF16)], [filt], [pltpu.VMEM((groups, K), F32)],
            flops=10**9, moved=4 * 10**6,
        )[0]

    filt, sent = lax.optimization_barrier((long_filter, sent))
    fwd = circulants(filt, True)
    bulk, part, top = call(
        "current", current_kernel, [full_f, full_f, full_bf],
        [lengths, q_input, taps, sent, fwd, skip2], flops=10**9, moved=5 * 10**6,
    )
    q_short, gated, before, mixed, summed, sums = call(
        "summed", summed_kernel,
        [full_f, full_bf, full_bf, full_f, full_f, arr((2, K), F32)],
        [
            lengths, came, came_far, q_input, k_input, v_input, taps, sent, fwd, top,
            bulk, part, skip2, resid, cotangent, gain2,
        ],
        [pltpu.VMEM((2, K, LANES), F32)], flops=10**9, moved=5 * 10**6,
    )
    own_sums = sums
    step = 1
    while step < lax.axis_size("tp"):
        sums = sums + swapped(sums, "tp", step)
        step *= 2
    filt, came, _ = lax.optimization_barrier((long_filter, came, own_sums))
    bwd = circulants(filt, False)
    k_short, v_short = call(
        "gates", gates_kernel, [full_f] * 2, [lengths, k_input, v_input, came, taps],
        flops=10**8, moved=2 * 10**6,
    )
    sums, bwd, k_short, v_short = lax.optimization_barrier((sums, bwd, k_short, v_short))
    grad_mixed, grad_qs, head = call(
        "grads", functools.partial(grads_kernel, wide),
        [full_bf, full_bf, arr((PACK, channels), BF16)],
        [summed, mixed, q_short, cotangent, gain2, sums],
    )
    after = shifted(grad_mixed, "ctx", -1)
    tails_q = shifted(head, "ctx", -1)
    stats, part = call(
        "beside", functools.partial(beside_kernel, wide),
        [
            arr((groups + 2 * rows + 8, LANES), F32), full_f,
        ],
        [
            lengths, summed, cotangent, sums, grad_mixed, grad_qs, gated, before, bwd,
            skip2, q_input, came,
        ],
        [pltpu.VMEM((8, channels), F32)],
        flops=4 * 10**9, moved=5 * 10**6,
    )
    count = lax.axis_size("ctx")
    steps = [1 << i for i in range(count.bit_length() - 1)]
    others = swapped(stats, "ctx", steps[0])
    grad_ks, grad_vs, tails, last = call(
        "gate", gate_kernel,
        [full_bf, full_bf, arr((2 * RIM, channels), BF16), arr((16, LANES), F32)],
        [lengths, part, after, bwd, k_short, v_short, k_input, v_input, came],
        [pltpu.VMEM((16, channels), F32)], flops=10**9, moved=5 * 10**6,
    )
    others, last = lax.optimization_barrier((others, last))
    outs = []
    for i, step in enumerate(steps):
        if i:
            last, *outs = lax.optimization_barrier((last + other, *outs))
        other = swapped(last, "ctx", step)
        if i == 0:
            stats = stats + others
            others = swapped(stats, "ctx", steps[1])
            tails = shifted(tails, "ctx", -1)
            outs += call(
                "main_q", functools.partial(main_q_kernel, wide), [full_bf] * 2,
                [lengths, taps, grad_qs, tails_q, summed, gain2, sums],
            )
        if i == 1:
            outs += call(
                "main_k", functools.partial(main_kernel, 1, 0), [full_bf],
                [lengths, taps, grad_ks, tails],
            )
        if i == 2:
            outs += call(
                "main_v", functools.partial(main_kernel, 2, RIM), [full_bf],
                [lengths, taps, grad_vs, tails],
            )
        if 0 < i < len(steps) - 1:
            others, *outs = lax.optimization_barrier((others, *outs))
            stats = stats + others
            others = swapped(stats, "ctx", steps[i + 1])
    grad_q, normed, grad_k, grad_v = outs
    grad_short, grad_long, grad_skip, grad_gain = call(
        "unpack", unpack_kernel,
        [
            arr((3, KS, groups), F32), arr((groups, K), F32),
            arr((rows, LANES), F32), arr((rows, LANES), F32),
        ],
        [stats, others, last, other],
    )
    return (
        normed, grad_q, grad_k, grad_v, jnp.transpose(grad_short, (0, 2, 1)), grad_long,
        grad_skip.reshape(channels), grad_gain.reshape(channels),
    )


def solution(mesh):
    tiled = P("ctx", "tp")
    return jax.shard_map(
        shards,
        mesh=mesh,
        in_specs=(
            tiled, tiled, tiled, tiled, P(), P(None, "tp", None), P("tp", None), P("tp"), P("tp"),
            tiled,
        ),
        out_specs=(
            tiled, tiled, tiled, tiled, P(None, "tp", None), P("tp", None), P("tp"), P("tp"),
        ),
        check_vma=False,
    )
```

```python
import functools

import jax
import jax.numpy as jnp
from jax import lax
from jax.experimental import pallas as pl
from jax.experimental.pallas import tpu as pltpu
from jax.sharding import PartitionSpec as P

GS = 16
K = 128
KS = 7
LANES = 128
PER = LANES // GS
RIM = 8
PACK = 16
EPS = 1e-06
F32 = jnp.float32
BF16 = jnp.bfloat16


def shifted(x, axis, by):
    count = lax.axis_size(axis)
    return lax.ppermute(x, axis, [(i, (i + by) % count) for i in range(count)])


def swapped(x, axis, step):
    return lax.ppermute(x, axis, [(i, i ^ step) for i in range(lax.axis_size(axis))])


def iota(shape, dim):
    return lax.broadcasted_iota(jnp.int32, shape, dim)


def positions(len_ref, rows):
    begin = jnp.zeros_like(rows)
    start = jnp.int32(0)
    for n in range(len_ref.shape[0]):
        begin = jnp.where(rows >= start, start, begin)
        start = start + len_ref[n]
    return jnp.where(rows < start, rows - begin, -1)


def first_row():
    return lax.axis_index("ctx") * K


def lanes_of(q):
    return pl.ds(pl.multiple_of(q * LANES, LANES), LANES)


def each_chunk(channels, body, unroll=2):
    def step(q, carry):
        body(q)
        return carry

    lax.fori_loop(0, channels // LANES, step, 0, unroll=unroll)


def as_mask(cond):
    return jnp.where(cond, 1.0, 0.0).astype(BF16)


def join(*parts):
    return jnp.concatenate(parts, axis=0)


def tap_rows(taps_ref, which, ls):
    table = taps_ref[which * 8 : which * 8 + 8, ls]
    return [table[j : j + 1, :] for j in range(KS)]


def causal(ext, taps, pos):
    rows = ext.shape[0] - RIM
    total = taps[0] * ext[RIM:]
    for j in range(1, KS):
        moved = ext[RIM - j : RIM - j + rows]
        total = total + taps[j] * jnp.where(pos >= j, moved, 0.0)
    return total


def tap_lines(grad, ext, pos):
    lines = [jnp.sum(grad * ext[RIM:], axis=0, keepdims=True)]
    for j in range(1, KS):
        held = jnp.where(pos >= j, grad, 0.0)
        lines.append(jnp.sum(held * ext[RIM - j : RIM - j + K], axis=0, keepdims=True))
    lines.append(jnp.zeros((8 - KS, LANES), F32))
    return join(*lines)


def owners():
    lane = iota((K, LANES), 1) // GS
    return [as_mask(lane == g) for g in range(PER)]


def per_group(right, own):
    return join(*[right * mask for mask in own])


def masked(table_ref, q, mask):
    table = table_ref[:, pl.ds(pl.multiple_of(q * PER * K, PER * K), PER * K)]
    return [table[:, g * K : (g + 1) * K] * mask for g in range(PER)]


def product(left, right):
    return jnp.dot(jnp.concatenate(left, axis=1), right, preferred_element_type=F32)


K_FIRST, Q_LAST, K_LAST, V_LAST, V_FIRST, SENT = 0, K, K + 8, K + 16, K + 24, K + 32


def rim_of(ref, at, ls):
    base = at // PACK * PACK
    return ref[base : base + PACK, ls].astype(F32)[at - base : at - base + RIM]


def first_kernel(
    len_hbm, short_hbm, q_hbm, k_hbm, v_hbm, taps_ref, sent_ref, far_ref,
    len_ref, short_ref, q_ref, k_ref, v_ref, sems,
):
    groups = short_ref.shape[2]
    channels = taps_ref.shape[1]
    pairs = (
        (short_hbm, short_ref), (len_hbm, len_ref), (k_hbm, k_ref), (v_hbm, v_ref),
        (q_hbm.at[K - PACK : K], q_ref),
    )
    copies = [pltpu.make_async_copy(a, b, sems.at[i]) for i, (a, b) in enumerate(pairs)]
    for copy in copies:
        copy.start()
    spread = as_mask(iota((groups, channels), 1) // GS == iota((groups, channels), 0))
    copies[0].wait()
    for i in range(3):
        taps_ref[i * 8 : i * 8 + KS] = jnp.dot(
            short_ref[i], spread, preferred_element_type=F32
        )
        taps_ref[i * 8 + KS : i * 8 + 8] = jnp.zeros((8 - KS, channels), F32)
    for copy in copies[1:]:
        copy.wait()
    pos = positions(len_ref, first_row() + RIM + iota((K - RIM, LANES), 0))

    def body(q):
        ls = lanes_of(q)
        kx = k_ref[:, ls].astype(F32)
        vx = v_ref[:, ls].astype(F32)
        ks = causal(kx, tap_rows(taps_ref, 1, ls), pos)
        vs = causal(vx, tap_rows(taps_ref, 2, ls), pos)
        sent_ref[:K, ls] = join(kx[:RIM], ks * vs).astype(BF16)
        q_end = q_ref[:, ls].astype(F32)[PACK - RIM :]
        k_end = kx[K - RIM :]
        v_end = vx[K - RIM :]
        sent_ref[K:, ls] = join(q_end, k_end, v_end, vx[:RIM]).astype(BF16)
        far_ref[:, ls] = join(k_end, v_end).astype(BF16)

    each_chunk(channels, body)


def circulant_kernel(turned, long_ref, out_ref, line_ref):
    groups = long_ref.shape[0]
    filt = long_ref[...]
    if turned:
        flip = as_mask((iota((K, K), 0) + iota((K, K), 1)) % K == 0)
        line_ref[...] = jnp.dot(filt, flip, preferred_element_type=F32)
    else:
        line_ref[...] = filt.astype(F32)

    def step(g, carry):
        row = jnp.broadcast_to(line_ref[pl.ds(g, 1), :], (GS, K))
        block = pltpu.roll(row, 0, 1, stride=1, stride_axis=0)
        for i in range(K // GS):
            moved = block if i == 0 else pltpu.roll(block, i * GS, 1)
            at = pl.ds(pl.multiple_of(g * K, K), K)
            out_ref[i * GS : (i + 1) * GS, at] = moved.astype(BF16)
        return carry

    lax.fori_loop(0, groups, step, 0, unroll=8)


def current_kernel(
    len_ref, q_ref, taps_ref, sent_ref, fwd_ref, skip_ref, qs_ref, part_ref, top_ref
):
    row = iota((K, LANES), 0)
    col = iota((K, LANES), 1)
    pos = positions(len_ref, first_row() + row)
    near = (col <= row) & (pos >= row - col)
    mask = as_mask(near)
    mask_top = as_mask(near & (col < RIM))
    picks = join(*[as_mask((col == row + g * GS) & (row < GS)) for g in range(PER)])
    own = owners()
    top = jnp.zeros((RIM, LANES), F32)

    def body(q):
        ls = lanes_of(q)
        qs_ref[RIM:, ls] = causal(q_ref[:, ls].astype(F32), tap_rows(taps_ref, 0, ls), pos[RIM:])
        qs_ref[:RIM, ls] = top
        gated = join(top, sent_ref[:K, ls].astype(F32)[RIM:])
        rest = product(masked(fwd_ref, q, mask), per_group(gated.astype(BF16), own))
        part_ref[:, ls] = rest + skip_ref[:, ls] * gated
        top_ref[:, ls] = product(masked(fwd_ref, q, mask_top), picks).astype(BF16)

    each_chunk(q_ref.shape[1], body)


def summed_kernel(
    len_ref, came_ref, far_ref, q_ref, k_ref, v_ref, taps_ref, sent_ref, fwd_ref, top_ref,
    bulk_ref, part_ref, skip_ref, resid_ref, cot_ref, gain_ref,
    qs_ref, gated_ref, before_ref, mixed_ref, summed_ref, sums_ref, acc_ref,
):
    row = iota((K, LANES), 0)
    col = iota((K, LANES), 1)
    pos = positions(len_ref, first_row() + row)
    mask = as_mask((col > row) & (pos >= row - col + K))
    pos_top = pos[:RIM]
    pos_far = positions(len_ref, first_row() - K + iota((RIM, LANES), 0))
    own = owners()
    own_top = [
        as_mask((iota((PACK, LANES), 1) // GS == g) & (iota((PACK, LANES), 0) < RIM))
        for g in range(PER)
    ]
    acc_ref[...] = jnp.zeros_like(acc_ref)

    def body(q):
        ls = lanes_of(q)
        kt = tap_rows(taps_ref, 1, ls)
        vt = tap_rows(taps_ref, 2, ls)
        k_last = rim_of(came_ref, K_LAST, ls)
        v_last = rim_of(came_ref, V_LAST, ls)
        top = causal(join(k_last, rim_of(k_ref, 0, ls)), kt, pos_top) * causal(
            join(v_last, rim_of(v_ref, 0, ls)), vt, pos_top
        )
        far_top = causal(
            join(rim_of(far_ref, 0, ls), rim_of(came_ref, K_FIRST, ls)), kt, pos_far
        ) * causal(join(rim_of(far_ref, RIM, ls), rim_of(came_ref, V_FIRST, ls)), vt, pos_far)
        qs_top = causal(
            join(rim_of(came_ref, Q_LAST, ls), rim_of(q_ref, 0, ls)), tap_rows(taps_ref, 0, ls), pos_top
        )
        before = join(far_top, came_ref[:K, ls].astype(F32)[RIM:]).astype(BF16)
        gated = join(top, sent_ref[:K, ls].astype(F32)[RIM:]).astype(BF16)
        before_ref[:, ls] = before
        gated_ref[:, ls] = gated
        qs = join(qs_top, bulk_ref[RIM:, ls])
        qs_ref[:, ls] = qs
        first = gated[:PACK]
        left = masked(fwd_ref, q, mask) + [top_ref[:, ls]]
        right = join(per_group(before, own), per_group(first, own_top))
        direct = skip_ref[:, ls] * first.astype(F32)[:RIM]
        mixed = part_ref[:, ls] + product(left, right)
        mixed = join(mixed[:RIM] + direct, mixed[RIM:])
        summed = resid_ref[:, ls].astype(F32) + qs * mixed
        mixed_ref[:, ls] = mixed
        summed_ref[:, ls] = summed
        acc_ref[0] += summed * summed
        acc_ref[1] += gain_ref[:, ls] * cot_ref[:, ls].astype(F32) * summed

    each_chunk(resid_ref.shape[1], body)
    for i in range(2):
        sums_ref[i : i + 1] = jnp.sum(acc_ref[i].T, axis=0, keepdims=True)


def group_sums(cols):
    count, channels = cols.shape
    gather = as_mask(iota((channels, LANES), 0) // GS == iota((channels, LANES), 1))
    high = cols.astype(BF16)
    rest = cols - high.astype(F32)
    mid = rest.astype(BF16)
    low = (rest - mid.astype(F32)).astype(BF16)
    parts = join(high.astype(F32), mid.astype(F32), low.astype(F32)).astype(BF16)
    sums = jnp.dot(parts, gather, preferred_element_type=F32)
    return sums[:count] + sums[count : 2 * count] + sums[2 * count :]


def by_row(line):
    return jnp.broadcast_to(line, (K, K)).T


def inverse_of(sums_ref, total):
    return by_row(lax.rsqrt(sums_ref[0:1] / total + EPS))


def gates_kernel(len_ref, k_ref, v_ref, came_ref, taps_ref, ks_ref, vs_ref):
    pos = positions(len_ref, first_row() + iota((K, LANES), 0))

    def body(q):
        ls = lanes_of(q)
        k_ext = join(rim_of(came_ref, K_LAST, ls), k_ref[:, ls].astype(F32))
        v_ext = join(rim_of(came_ref, V_LAST, ls), v_ref[:, ls].astype(F32))
        ks_ref[:, ls] = causal(k_ext, tap_rows(taps_ref, 1, ls), pos)
        vs_ref[:, ls] = causal(v_ext, tap_rows(taps_ref, 2, ls), pos)

    each_chunk(k_ref.shape[1], body)


def grads_kernel(total, summed_ref, mixed_ref, qs_ref, cot_ref, gain_ref, sums_ref, gm_ref, gq_ref, head_ref):
    inverse = inverse_of(sums_ref, total)
    scale = inverse * inverse * by_row(sums_ref[1:2] / total)

    def body(q):
        ls = lanes_of(q)
        scaled = gain_ref[:, ls] * cot_ref[:, ls].astype(F32)
        grad_sum = inverse * (scaled - summed_ref[:, ls] * scale)
        gm_ref[:, ls] = (grad_sum * qs_ref[:, ls]).astype(BF16)
        gq = (grad_sum * mixed_ref[:, ls]).astype(BF16)
        gq_ref[:, ls] = gq
        head_ref[:, ls] = gq[:PACK]

    each_chunk(cot_ref.shape[1], body)


def beside_kernel(
    total, len_ref, summed_ref, cot_ref, sums_ref, gm_ref, gq_ref, gated_ref, before_ref,
    bwd_ref, skip_ref, q_ref, came_ref, stats_ref, part_ref, cols_ref,
):
    groups = bwd_ref.shape[1] // K
    inverse = inverse_of(sums_ref, total)
    row = iota((K, LANES), 0)
    col = iota((K, LANES), 1)
    pos_row = positions(len_ref, first_row() + row)
    pos = positions(len_ref, first_row() + col)
    mask = as_mask((col >= row) & (pos >= col - row))
    source = K - 1 - row
    near = (col >= source) & (pos >= col - source)
    far = (col < source) & (pos >= col - source + K)
    flip = as_mask(row + col == K - 1)
    own = owners()

    def body(q):
        ls = lanes_of(q)
        summed = summed_ref[:, ls]
        gm = gm_ref[:, ls]
        gmf = gm.astype(F32)
        gated = gated_ref[:, ls]
        stats_ref[pl.ds(groups + q, 1), :] = jnp.sum(gmf * gated.astype(F32), axis=0, keepdims=True)
        stats_ref[pl.ds(groups + groups // PER + q, 1), :] = jnp.sum(
            cot_ref[:, ls].astype(F32) * summed * inverse, axis=0, keepdims=True
        )
        right = per_group(gm, own)
        part_ref[:, ls] = skip_ref[:, ls] * gmf + product(masked(bwd_ref, q, mask), right)
        two = jnp.concatenate([before_ref[:, ls], gated], axis=1)
        flipped = jnp.dot(flip, two, preferred_element_type=F32).astype(BF16)
        left = join(flipped[:, :LANES], flipped[:, LANES:])
        turned = gmf.T.astype(BF16)
        spread = []
        for g in range(PER):
            pieces = [jnp.zeros((GS, K), BF16)] * PER
            pieces[g] = turned[g * GS : (g + 1) * GS]
            spread.append(join(*pieces))
        cross = jnp.dot(left, jnp.concatenate(spread, axis=1), preferred_element_type=F32)
        lines = []
        for g in range(PER):
            gs = slice(g * K, (g + 1) * K)
            square = jnp.where(near, cross[K:, gs], jnp.where(far, cross[:K, gs], 0.0))
            square = pltpu.roll(square, 1, 1, stride=1, stride_axis=0)
            lines.append(jnp.sum(square, axis=0, keepdims=True))
        stats_ref[pl.ds(pl.multiple_of(q * PER, PER), PER), :] = join(*lines)
        q_ext = join(rim_of(came_ref, Q_LAST, ls), q_ref[:, ls].astype(F32))
        cols_ref[:, ls] = tap_lines(gq_ref[:, ls].astype(F32), q_ext, pos_row)

    each_chunk(cot_ref.shape[1], body, 1)
    stats_ref[groups + 2 * (groups // PER) :] = group_sums(cols_ref[...])


def gate_kernel(
    len_ref, part_ref, after_ref, bwd_ref, ks_ref, vs_ref, k_ref, v_ref, came_ref,
    gks_ref, gvs_ref, tails_ref, short_ref, cols_ref,
):
    channels = part_ref.shape[1]
    row = iota((K, LANES), 0)
    col = iota((K, LANES), 1)
    pos_row = positions(len_ref, first_row() + row)
    pos = positions(len_ref, first_row() + K + col)
    mask = as_mask((col < row) & (pos >= col - row + K))
    own = owners()

    def body(q):
        ls = lanes_of(q)
        right = per_group(after_ref[:, ls], own)
        grad = part_ref[:, ls] + product(masked(bwd_ref, q, mask), right)
        gks = (grad * vs_ref[:, ls]).astype(BF16)
        gvs = (grad * ks_ref[:, ls]).astype(BF16)
        gks_ref[:, ls] = gks
        gvs_ref[:, ls] = gvs
        tails_ref[:, ls] = join(gks.astype(F32)[:RIM], gvs.astype(F32)[:RIM]).astype(BF16)
        k_ext = join(rim_of(came_ref, K_LAST, ls), k_ref[:, ls].astype(F32))
        v_ext = join(rim_of(came_ref, V_LAST, ls), v_ref[:, ls].astype(F32))
        cols_ref[:8, ls] = tap_lines(gks.astype(F32), k_ext, pos_row)
        cols_ref[8:, ls] = tap_lines(gvs.astype(F32), v_ext, pos_row)

    each_chunk(channels, body)
    short_ref[...] = group_sums(cols_ref[...])


def back_short(which, at, pos, ls, taps_ref, grad_ref, tail_ref):
    ext = join(grad_ref[:, ls].astype(F32), rim_of(tail_ref, at, ls))
    taps = tap_rows(taps_ref, which, ls)
    grad = taps[0] * ext[:K]
    for j in range(1, KS):
        held = jnp.where(pos >= j, ext, 0.0)
        grad = grad + taps[j] * held[j : j + K]
    return grad.astype(BF16)


def main_kv_kernel(len_ref, taps_ref, gks_ref, gvs_ref, tail_ref, ok_ref, ov_ref):
    pos = positions(len_ref, first_row() + iota((K + RIM, LANES), 0))

    def body(q):
        ls = lanes_of(q)
        ok_ref[:, ls] = back_short(1, 0, pos, ls, taps_ref, gks_ref, tail_ref)
        ov_ref[:, ls] = back_short(2, RIM, pos, ls, taps_ref, gvs_ref, tail_ref)

    each_chunk(gks_ref.shape[1], body)


def main_q_kernel(
    total, len_ref, taps_ref, grad_ref, tail_ref, summed_ref, gain_ref, sums_ref, out_ref, normed_ref
):
    inverse = inverse_of(sums_ref, total)
    pos = positions(len_ref, first_row() + iota((K + RIM, LANES), 0))

    def body(q):
        ls = lanes_of(q)
        out_ref[:, ls] = back_short(0, 0, pos, ls, taps_ref, grad_ref, tail_ref)
        normed_ref[:, ls] = (gain_ref[:, ls] * summed_ref[:, ls] * inverse).astype(BF16)

    each_chunk(grad_ref.shape[1], body)


def unpack_kernel(
    stats_ref, stats2_ref, last_ref, last2_ref, short_ref, long_ref, skip_ref, gain_ref
):
    groups = long_ref.shape[0]
    rows = groups // PER
    stats = stats_ref[...] + stats2_ref[...]
    last = last_ref[...] + last2_ref[...]
    long_ref[...] = stats[:groups]
    skip_ref[...] = stats[groups : groups + rows]
    gain_ref[...] = stats[groups + rows : groups + 2 * rows]
    short_ref[0] = stats[groups + 2 * rows :][:KS, :groups]
    short_ref[1] = last[:KS, :groups]
    short_ref[2] = last[8 : 8 + KS, :groups]


def shards(
    q_input, k_input, v_input, resid, lengths, short_filter, long_filter, skip, gain, cotangent
):
    length, channels = q_input.shape
    groups = channels // GS
    wide = channels * lax.axis_size("tp")
    rows = groups // PER

    def arr(shape, dtype):
        return jax.ShapeDtypeStruct(shape, dtype)

    smem = pl.BlockSpec(memory_space=pltpu.SMEM)
    vmem = pl.BlockSpec(memory_space=pltpu.VMEM)
    far_off = pl.BlockSpec(memory_space=pltpu.HBM)
    full_bf = arr((length, channels), BF16)
    full_f = arr((length, channels), F32)

    def call(name, kernel, outs, ins, scratch=(), flops=10**8, moved=10**6, grant=8, hbm=False):
        scalar = ins[0] is lengths
        return pl.pallas_call(
            kernel,
            out_shape=outs,
            in_specs=[far_off] * len(ins)
            if hbm
            else [smem if (i == 0 and scalar) else vmem for i in range(len(ins))],
            out_specs=[vmem] * len(outs),
            scratch_shapes=scratch,
            compiler_params=pltpu.CompilerParams(vmem_limit_bytes=grant * 1024 * 1024),
            cost_estimate=pl.CostEstimate(flops=flops, bytes_accessed=moved, transcendentals=0),
            name=name,
        )(*ins)

    skip2 = skip.reshape(1, channels)
    gain2 = gain.reshape(1, channels)
    taps, sent, far = call(
        "first", first_kernel,
        [arr((24, channels), F32), arr((SENT, channels), BF16), arr((2 * RIM, channels), BF16)],
        [lengths, jnp.transpose(short_filter, (0, 2, 1)), q_input, k_input, v_input],
        [
            pltpu.SMEM(lengths.shape, jnp.int32), pltpu.VMEM((3, KS, groups), BF16),
            pltpu.VMEM((PACK, channels), BF16), pltpu.VMEM((length, channels), BF16),
            pltpu.VMEM((length, channels), BF16), pltpu.SemaphoreType.DMA((5,)),
        ],
        grant=60,
        hbm=True,
    )
    came = shifted(sent, "ctx", 1)
    came_far = shifted(far, "ctx", 2)

    def circulants(filt, turned):
        return call(
            "circulants", functools.partial(circulant_kernel, turned),
            [arr((K, groups * K), BF16)], [filt], [pltpu.VMEM((groups, K), F32)],
            flops=10**9, moved=4 * 10**6,
        )[0]

    filt, sent = lax.optimization_barrier((long_filter, sent))
    fwd = circulants(filt, True)
    bulk, part, top = call(
        "current", current_kernel, [full_f, full_f, full_bf],
        [lengths, q_input, taps, sent, fwd, skip2], flops=10**9, moved=5 * 10**6,
    )
    q_short, gated, before, mixed, summed, sums = call(
        "summed", summed_kernel,
        [full_f, full_bf, full_bf, full_f, full_f, arr((2, K), F32)],
        [
            lengths, came, came_far, q_input, k_input, v_input, taps, sent, fwd, top,
            bulk, part, skip2, resid, cotangent, gain2,
        ],
        [pltpu.VMEM((2, K, LANES), F32)], flops=10**9, moved=5 * 10**6,
    )
    own_sums = sums
    step = 1
    while step < lax.axis_size("tp"):
        sums = sums + swapped(sums, "tp", step)
        step *= 2
    filt, came, _ = lax.optimization_barrier((long_filter, came, own_sums))
    bwd = circulants(filt, False)
    k_short, v_short = call(
        "gates", gates_kernel, [full_f] * 2, [lengths, k_input, v_input, came, taps],
        flops=10**8, moved=2 * 10**6,
    )
    sums, bwd, k_short, v_short = lax.optimization_barrier((sums, bwd, k_short, v_short))
    grad_mixed, grad_qs, head = call(
        "grads", functools.partial(grads_kernel, wide),
        [full_bf, full_bf, arr((PACK, channels), BF16)],
        [summed, mixed, q_short, cotangent, gain2, sums],
    )
    after = shifted(grad_mixed, "ctx", -1)
    tails_q = shifted(head, "ctx", -1)
    stats, part = call(
        "beside", functools.partial(beside_kernel, wide),
        [
            arr((groups + 2 * rows + 8, LANES), F32), full_f,
        ],
        [
            lengths, summed, cotangent, sums, grad_mixed, grad_qs, gated, before, bwd,
            skip2, q_input, came,
        ],
        [pltpu.VMEM((8, channels), F32)],
        flops=4 * 10**9, moved=5 * 10**6,
    )
    count = lax.axis_size("ctx")
    steps = [1 << i for i in range(count.bit_length() - 1)]
    others = swapped(stats, "ctx", steps[0])
    grad_ks, grad_vs, tails, last = call(
        "gate", gate_kernel,
        [full_bf, full_bf, arr((2 * RIM, channels), BF16), arr((16, LANES), F32)],
        [lengths, part, after, bwd, k_short, v_short, k_input, v_input, came],
        [pltpu.VMEM((16, channels), F32)], flops=10**9, moved=5 * 10**6,
    )
    others, last = lax.optimization_barrier((others, last))
    for i, step in enumerate(steps):
        other = swapped(last, "ctx", step)
        if i == 0:
            stats = stats + others
            others = swapped(stats, "ctx", steps[1])
            tails = shifted(tails, "ctx", -1)
            grad_q, normed = call(
                "main_q", functools.partial(main_q_kernel, wide), [full_bf] * 2,
                [lengths, taps, grad_qs, tails_q, summed, gain2, sums],
            )
            last, grad_q, normed = lax.optimization_barrier((last + other, grad_q, normed))
        elif i < len(steps) - 1:
            last, stats, tails = lax.optimization_barrier((last + other, stats + others, tails))
            others = swapped(stats, "ctx", steps[i + 1])
    grad_ks, grad_vs, last = lax.optimization_barrier((grad_ks, grad_vs, last))
    grad_k, grad_v = call(
        "main_kv", main_kv_kernel, [full_bf] * 2, [lengths, taps, grad_ks, grad_vs, tails]
    )
    grad_short, grad_long, grad_skip, grad_gain = call(
        "unpack", unpack_kernel,
        [
            arr((3, KS, groups), F32), arr((groups, K), F32),
            arr((rows, LANES), F32), arr((rows, LANES), F32),
        ],
        [stats, others, last, other],
    )
    return (
        normed, grad_q, grad_k, grad_v, jnp.transpose(grad_short, (0, 2, 1)), grad_long,
        grad_skip.reshape(channels), grad_gain.reshape(channels),
    )


def solution(mesh):
    tiled = P("ctx", "tp")
    return jax.shard_map(
        shards,
        mesh=mesh,
        in_specs=(
            tiled, tiled, tiled, tiled, P(), P(None, "tp", None), P("tp", None), P("tp"), P("tp"),
            tiled,
        ),
        out_specs=(
            tiled, tiled, tiled, tiled, P(None, "tp", None), P("tp", None), P("tp"), P("tp"),
        ),
        check_vma=False,
    )
```

```python
import functools

import jax
import jax.numpy as jnp
from jax import lax
from jax.experimental import pallas as pl
from jax.experimental.pallas import tpu as pltpu
from jax.sharding import PartitionSpec as P

GS = 16
K = 128
KS = 7
LANES = 128
PER = LANES // GS
RIM = 8
PACK = 16
EPS = 1e-06
F32 = jnp.float32
BF16 = jnp.bfloat16


def shifted(x, axis, by):
    count = lax.axis_size(axis)
    return lax.ppermute(x, axis, [(i, (i + by) % count) for i in range(count)])


def swapped(x, axis, step):
    return lax.ppermute(x, axis, [(i, i ^ step) for i in range(lax.axis_size(axis))])


def iota(shape, dim):
    return lax.broadcasted_iota(jnp.int32, shape, dim)


def positions(len_ref, rows):
    begin = jnp.zeros_like(rows)
    start = jnp.int32(0)
    for n in range(len_ref.shape[0]):
        begin = jnp.where(rows >= start, start, begin)
        start = start + len_ref[n]
    return jnp.where(rows < start, rows - begin, -1)


def first_row():
    return lax.axis_index("ctx") * K


def lanes_of(q):
    return pl.ds(pl.multiple_of(q * LANES, LANES), LANES)


def each_chunk(channels, body, unroll=2):
    def step(q, carry):
        body(q)
        return carry

    lax.fori_loop(0, channels // LANES, step, 0, unroll=unroll)


def each_part(part, channels, body, unroll=2):
    count = channels // LANES // 2

    def step(q, carry):
        body(part * count + q, lanes_of(part * count + q), lanes_of(q))
        return carry

    lax.fori_loop(0, count, step, 0, unroll=unroll)


def as_mask(cond):
    return jnp.where(cond, 1.0, 0.0).astype(BF16)


def join(*parts):
    return jnp.concatenate(parts, axis=0)


def tap_rows(taps_ref, which, ls):
    table = taps_ref[which * 8 : which * 8 + 8, ls]
    return [table[j : j + 1, :] for j in range(KS)]


def causal(ext, taps, pos):
    rows = ext.shape[0] - RIM
    total = taps[0] * ext[RIM:]
    for j in range(1, KS):
        moved = ext[RIM - j : RIM - j + rows]
        total = total + taps[j] * jnp.where(pos >= j, moved, 0.0)
    return total


def tap_lines(grad, ext, pos):
    lines = [jnp.sum(grad * ext[RIM:], axis=0, keepdims=True)]
    for j in range(1, KS):
        held = jnp.where(pos >= j, grad, 0.0)
        lines.append(jnp.sum(held * ext[RIM - j : RIM - j + K], axis=0, keepdims=True))
    lines.append(jnp.zeros((8 - KS, LANES), F32))
    return join(*lines)


def owners():
    lane = iota((K, LANES), 1) // GS
    return [as_mask(lane == g) for g in range(PER)]


def per_group(right, own):
    return join(*[right * mask for mask in own])


def masked(table_ref, q, mask):
    table = table_ref[:, pl.ds(pl.multiple_of(q * PER * K, PER * K), PER * K)]
    return [table[:, g * K : (g + 1) * K] * mask for g in range(PER)]


def product(left, right):
    return jnp.dot(jnp.concatenate(left, axis=1), right, preferred_element_type=F32)


K_FIRST, Q_LAST, K_LAST, V_LAST, V_FIRST, SENT = 0, K, K + 8, K + 16, K + 24, K + 32


def rim_of(ref, at, ls):
    base = at // PACK * PACK
    return ref[base : base + PACK, ls].astype(F32)[at - base : at - base + RIM]


def load_all(pairs, sems):
    copies = [pltpu.make_async_copy(a, b, sems.at[i]) for i, (a, b) in enumerate(pairs)]
    for copy in copies:
        copy.start()
    return copies


def send_part(part, channels, len_ref, q_ref, k_ref, v_ref, taps_ref, taps_part, sent_ref):
    pos = positions(len_ref, first_row() + RIM + iota((K - RIM, LANES), 0))

    def body(q, ls, hs):
        at = hs if taps_part else ls
        kx = k_ref[:, hs].astype(F32)
        vx = v_ref[:, hs].astype(F32)
        ks = causal(kx, tap_rows(taps_ref, 1, at), pos)
        vs = causal(vx, tap_rows(taps_ref, 2, at), pos)
        sent_ref[:K, hs] = join(kx[:RIM], ks * vs).astype(BF16)
        q_end = q_ref[:, hs].astype(F32)[PACK - RIM :]
        sent_ref[K:, hs] = join(q_end, kx[K - RIM :], vx[K - RIM :], vx[:RIM]).astype(BF16)

    each_part(part, channels, body)


def first_kernel(
    len_hbm, short_hbm, q_hbm, k_hbm, v_hbm, taps_ref, sent_ref,
    len_ref, short_ref, q_ref, k_ref, v_ref, sems,
):
    groups = short_ref.shape[2]
    channels = taps_ref.shape[1]
    part = slice(0, channels // 2)
    copies = load_all(
        (
            (short_hbm, short_ref), (len_hbm, len_ref), (k_hbm.at[:, part], k_ref),
            (v_hbm.at[:, part], v_ref), (q_hbm.at[K - PACK : K, part], q_ref),
        ),
        sems,
    )
    spread = as_mask(iota((groups, channels), 1) // GS == iota((groups, channels), 0))
    copies[0].wait()
    for i in range(3):
        taps_ref[i * 8 : i * 8 + KS] = jnp.dot(
            short_ref[i], spread, preferred_element_type=F32
        )
        taps_ref[i * 8 + KS : i * 8 + 8] = jnp.zeros((8 - KS, channels), F32)
    for copy in copies[1:]:
        copy.wait()
    send_part(0, channels, len_ref, q_ref, k_ref, v_ref, taps_ref, False, sent_ref)


def second_kernel(
    len_hbm, taps_hbm, q_hbm, k_hbm, v_hbm, sent_ref, far_ref,
    len_ref, taps_ref, q_ref, k_ref, v_ref, k_end, v_end, sems,
):
    channels = far_ref.shape[1]
    part = slice(channels // 2, channels)
    end = slice(K - PACK, K)
    copies = load_all(
        (
            (taps_hbm.at[:, part], taps_ref), (len_hbm, len_ref), (k_hbm.at[:, part], k_ref),
            (v_hbm.at[:, part], v_ref), (q_hbm.at[end, part], q_ref),
            (k_hbm.at[end], k_end), (v_hbm.at[end], v_end),
        ),
        sems,
    )
    for copy in copies:
        copy.wait()
    send_part(1, channels, len_ref, q_ref, k_ref, v_ref, taps_ref, True, sent_ref)
    k_rows = k_end[...].astype(F32)[PACK - RIM :]
    v_rows = v_end[...].astype(F32)[PACK - RIM :]
    far_ref[...] = join(k_rows, v_rows).astype(BF16)


def circulant_kernel(turned, long_ref, out_ref, line_ref):
    groups = long_ref.shape[0]
    filt = long_ref[...]
    if turned:
        flip = as_mask((iota((K, K), 0) + iota((K, K), 1)) % K == 0)
        line_ref[...] = jnp.dot(filt, flip, preferred_element_type=F32)
    else:
        line_ref[...] = filt.astype(F32)

    def step(g, carry):
        row = jnp.broadcast_to(line_ref[pl.ds(g, 1), :], (GS, K))
        block = pltpu.roll(row, 0, 1, stride=1, stride_axis=0)
        for i in range(K // GS):
            moved = block if i == 0 else pltpu.roll(block, i * GS, 1)
            at = pl.ds(pl.multiple_of(g * K, K), K)
            out_ref[i * GS : (i + 1) * GS, at] = moved.astype(BF16)
        return carry

    lax.fori_loop(0, groups, step, 0, unroll=8)


def current_kernel(
    len_ref, q_ref, k_ref, v_ref, taps_ref, sent0_ref, sent1_ref, fwd_ref, skip_ref,
    qs_ref, ks_ref, vs_ref, part_ref, top_ref,
):
    row = iota((K, LANES), 0)
    col = iota((K, LANES), 1)
    pos = positions(len_ref, first_row() + row)
    near = (col <= row) & (pos >= row - col)
    mask = as_mask(near)
    mask_top = as_mask(near & (col < RIM))
    picks = join(*[as_mask((col == row + g * GS) & (row < GS)) for g in range(PER)])
    own = owners()
    top = jnp.zeros((RIM, LANES), F32)

    def body(sent_ref, q, ls, hs):
        for i, (x_ref, o_ref) in enumerate(((q_ref, qs_ref), (k_ref, ks_ref), (v_ref, vs_ref))):
            short = causal(x_ref[:, ls].astype(F32), tap_rows(taps_ref, i, ls), pos[RIM:])
            o_ref[:, ls] = join(top, short)
        gated = join(top, sent_ref[:K, hs].astype(F32)[RIM:])
        rest = product(masked(fwd_ref, q, mask), per_group(gated.astype(BF16), own))
        part_ref[:, ls] = rest + skip_ref[:, ls] * gated
        top_ref[:, ls] = product(masked(fwd_ref, q, mask_top), picks).astype(BF16)

    for part, sent_ref in enumerate((sent0_ref, sent1_ref)):
        each_part(part, q_ref.shape[1], functools.partial(body, sent_ref))


def summed_kernel(
    part, len_ref, came_ref, far_ref, q_ref, k_ref, v_ref, taps_ref, sent_ref, fwd_ref, top_ref,
    qbulk_ref, kbulk_ref, vbulk_ref, part_ref, skip_ref, resid_ref, cot_ref, gain_ref, so_far_ref,
    qs_ref, ks_ref, vs_ref, gated_ref, before_ref, mixed_ref, summed_ref, sums_ref, acc_ref,
):
    row = iota((K, LANES), 0)
    col = iota((K, LANES), 1)
    pos = positions(len_ref, first_row() + row)
    mask = as_mask((col > row) & (pos >= row - col + K))
    pos_top = pos[:RIM]
    pos_far = positions(len_ref, first_row() - K + iota((RIM, LANES), 0))
    own = owners()
    own_top = [
        as_mask((iota((PACK, LANES), 1) // GS == g) & (iota((PACK, LANES), 0) < RIM))
        for g in range(PER)
    ]
    acc_ref[...] = jnp.zeros_like(acc_ref)

    def body(q, ls, hs):
        kt = tap_rows(taps_ref, 1, ls)
        vt = tap_rows(taps_ref, 2, ls)
        k_last = rim_of(came_ref, K_LAST, hs)
        v_last = rim_of(came_ref, V_LAST, hs)
        ks_top = causal(join(k_last, rim_of(k_ref, 0, ls)), kt, pos_top)
        vs_top = causal(join(v_last, rim_of(v_ref, 0, ls)), vt, pos_top)
        ks_ref[:, hs] = join(ks_top, kbulk_ref[RIM:, ls])
        vs_ref[:, hs] = join(vs_top, vbulk_ref[RIM:, ls])
        far_top = causal(
            join(rim_of(far_ref, 0, ls), rim_of(came_ref, K_FIRST, hs)), kt, pos_far
        ) * causal(join(rim_of(far_ref, RIM, ls), rim_of(came_ref, V_FIRST, hs)), vt, pos_far)
        qs_top = causal(
            join(rim_of(came_ref, Q_LAST, hs), rim_of(q_ref, 0, ls)), tap_rows(taps_ref, 0, ls), pos_top
        )
        before = join(far_top, came_ref[:K, hs].astype(F32)[RIM:]).astype(BF16)
        gated = join(ks_top * vs_top, sent_ref[:K, hs].astype(F32)[RIM:]).astype(BF16)
        before_ref[:, hs] = before
        gated_ref[:, hs] = gated
        qs = join(qs_top, qbulk_ref[RIM:, ls])
        qs_ref[:, hs] = qs
        first = gated[:PACK]
        left = masked(fwd_ref, q, mask) + [top_ref[:, ls]]
        right = join(per_group(before, own), per_group(first, own_top))
        direct = skip_ref[:, ls] * first.astype(F32)[:RIM]
        mixed = part_ref[:, ls] + product(left, right)
        mixed = join(mixed[:RIM] + direct, mixed[RIM:])
        summed = resid_ref[:, ls].astype(F32) + qs * mixed
        mixed_ref[:, hs] = mixed
        summed_ref[:, hs] = summed
        acc_ref[0] += summed * summed
        acc_ref[1] += gain_ref[:, ls] * cot_ref[:, ls].astype(F32) * summed

    each_part(part, resid_ref.shape[1], body)
    for i in range(2):
        own_sum = jnp.sum(acc_ref[i].T, axis=0, keepdims=True)
        sums_ref[i : i + 1] = own_sum + so_far_ref[i : i + 1]


def group_sums(cols):
    count, channels = cols.shape
    gather = as_mask(iota((channels, LANES), 0) // GS == iota((channels, LANES), 1))
    high = cols.astype(BF16)
    rest = cols - high.astype(F32)
    mid = rest.astype(BF16)
    low = (rest - mid.astype(F32)).astype(BF16)
    parts = join(high.astype(F32), mid.astype(F32), low.astype(F32)).astype(BF16)
    sums = jnp.dot(parts, gather, preferred_element_type=F32)
    return sums[:count] + sums[count : 2 * count] + sums[2 * count :]


def by_row(line):
    return jnp.broadcast_to(line, (K, K)).T


def inverse_of(sums_ref, total):
    return by_row(lax.rsqrt(sums_ref[0:1] / total + EPS))


def grads_kernel(
    total, part, summed_ref, mixed_ref, qs_ref, cot_ref, gain_ref, sums_ref, gm_ref, gq_ref
):
    inverse = inverse_of(sums_ref, total)
    scale = inverse * inverse * by_row(sums_ref[1:2] / total)

    def body(q, ls, hs):
        scaled = gain_ref[:, ls] * cot_ref[:, ls].astype(F32)
        grad_sum = inverse * (scaled - summed_ref[:, hs] * scale)
        gm_ref[:, hs] = (grad_sum * qs_ref[:, hs]).astype(BF16)
        gq_ref[:, hs] = (grad_sum * mixed_ref[:, hs]).astype(BF16)

    each_part(part, cot_ref.shape[1], body)


def beside_kernel(
    total, len_ref, cot_ref, sums_ref, bwd_ref, skip_ref, q_ref, *refs
):
    halves = refs[:6], refs[6:12]
    stats_ref, part_ref, cols_ref = refs[12:]
    groups = bwd_ref.shape[1] // K
    inverse = inverse_of(sums_ref, total)
    row = iota((K, LANES), 0)
    col = iota((K, LANES), 1)
    pos_row = positions(len_ref, first_row() + row)
    pos = positions(len_ref, first_row() + col)
    mask = as_mask((col >= row) & (pos >= col - row))
    source = K - 1 - row
    near = (col >= source) & (pos >= col - source)
    far = (col < source) & (pos >= col - source + K)
    flip = as_mask(row + col == K - 1)
    own = owners()

    def body(half, q, ls, hs):
        summed_ref, gm_ref, gq_ref, gated_ref, before_ref, came_ref = half
        summed = summed_ref[:, hs]
        gm = gm_ref[:, hs]
        gmf = gm.astype(F32)
        gated = gated_ref[:, hs]
        stats_ref[pl.ds(groups + q, 1), :] = jnp.sum(gmf * gated.astype(F32), axis=0, keepdims=True)
        stats_ref[pl.ds(groups + groups // PER + q, 1), :] = jnp.sum(
            cot_ref[:, ls].astype(F32) * summed * inverse, axis=0, keepdims=True
        )
        right = per_group(gm, own)
        part_ref[:, ls] = skip_ref[:, ls] * gmf + product(masked(bwd_ref, q, mask), right)
        two = jnp.concatenate([before_ref[:, hs], gated], axis=1)
        flipped = jnp.dot(flip, two, preferred_element_type=F32).astype(BF16)
        left = join(flipped[:, :LANES], flipped[:, LANES:])
        turned = gmf.T.astype(BF16)
        spread = []
        for g in range(PER):
            pieces = [jnp.zeros((GS, K), BF16)] * PER
            pieces[g] = turned[g * GS : (g + 1) * GS]
            spread.append(join(*pieces))
        cross = jnp.dot(left, jnp.concatenate(spread, axis=1), preferred_element_type=F32)
        lines = []
        for g in range(PER):
            gs = slice(g * K, (g + 1) * K)
            square = jnp.where(near, cross[K:, gs], jnp.where(far, cross[:K, gs], 0.0))
            square = pltpu.roll(square, 1, 1, stride=1, stride_axis=0)
            lines.append(jnp.sum(square, axis=0, keepdims=True))
        stats_ref[pl.ds(pl.multiple_of(q * PER, PER), PER), :] = join(*lines)
        q_ext = join(rim_of(came_ref, Q_LAST, hs), q_ref[:, ls].astype(F32))
        cols_ref[:, ls] = tap_lines(gq_ref[:, hs].astype(F32), q_ext, pos_row)

    for part, half in enumerate(halves):
        each_part(part, cot_ref.shape[1], functools.partial(body, half), 1)


def gate_kernel(
    part, len_ref, part_ref, bwd_ref, k_ref, v_ref, after_ref, ks_ref, vs_ref, gq_ref, came_ref, *refs
):
    if part:
        stats_ref, qcols_ref, cols0_ref, tails0_ref = refs[:4]
        gks_ref, gvs_ref, tails_ref, packed_ref, cols_ref = refs[4:]
    else:
        gks_ref, gvs_ref, tails_ref, cols_ref = refs
    channels = part_ref.shape[1]
    row = iota((K, LANES), 0)
    col = iota((K, LANES), 1)
    pos_row = positions(len_ref, first_row() + row)
    pos = positions(len_ref, first_row() + K + col)
    mask = as_mask((col < row) & (pos >= col - row + K))
    own = owners()

    def body(q, ls, hs):
        right = per_group(after_ref[:, hs], own)
        grad = part_ref[:, ls] + product(masked(bwd_ref, q, mask), right)
        gks = (grad * vs_ref[:, hs]).astype(BF16)
        gvs = (grad * ks_ref[:, hs]).astype(BF16)
        gks_ref[:, hs] = gks
        gvs_ref[:, hs] = gvs
        heads = (rim_of(gq_ref, 0, hs), gks.astype(F32)[:RIM], gvs.astype(F32)[:RIM])
        at = ls if part else hs
        tails_ref[:, at] = join(*heads, jnp.zeros((RIM, LANES), F32)).astype(BF16)
        k_ext = join(rim_of(came_ref, K_LAST, hs), k_ref[:, ls].astype(F32))
        v_ext = join(rim_of(came_ref, V_LAST, hs), v_ref[:, ls].astype(F32))
        base = 8 if part else 0
        cols_ref[base : base + 8, at] = tap_lines(gks.astype(F32), k_ext, pos_row)
        cols_ref[base + 8 : base + 16, at] = tap_lines(gvs.astype(F32), v_ext, pos_row)

    each_part(part, channels, body)
    if part:
        half = channels // 2
        kept = stats_ref.shape[0]
        tails_ref[:, :half] = tails0_ref[...]
        cols_ref[8:, :half] = cols0_ref[...]
        cols_ref[:8] = qcols_ref[...]
        packed_ref[0:kept] = stats_ref[...]
        packed_ref[kept:] = group_sums(cols_ref[...])


def mains_kernel(total, len_ref, taps_ref, tails_ref, gain_ref, sums_ref, *refs):
    halves = refs[:4], refs[4:8]
    normed_ref, *out_refs = refs[8:]
    pos = positions(len_ref, first_row() + iota((K + RIM, LANES), 0))
    inverse = inverse_of(sums_ref, total)

    def body(half, q, ls, hs):
        normed_ref[:, ls] = (gain_ref[:, ls] * half[0][:, hs] * inverse).astype(BF16)
        for i, (g_ref, o_ref) in enumerate(zip(half[1:], out_refs)):
            ext = join(g_ref[:, hs].astype(F32), rim_of(tails_ref, i * RIM, ls))
            taps = tap_rows(taps_ref, i, ls)
            grad = taps[0] * ext[:K]
            for j in range(1, KS):
                held = jnp.where(pos >= j, ext, 0.0)
                grad = grad + taps[j] * held[j : j + K]
            o_ref[:, ls] = grad.astype(BF16)

    for part, half in enumerate(halves):
        each_part(part, gain_ref.shape[1], functools.partial(body, half))


def unpack_kernel(one_ref, two_ref, short_ref, long_ref, skip_ref, gain_ref):
    groups = long_ref.shape[0]
    rows = groups // PER
    total = one_ref[...] + two_ref[...]
    long_ref[...] = total[:groups]
    skip_ref[...] = total[groups : groups + rows]
    gain_ref[...] = total[groups + rows : groups + 2 * rows]
    for i in range(3):
        at = groups + 2 * rows + i * 8
        short_ref[i] = total[at : at + KS, :groups]


def shards(
    q_input, k_input, v_input, resid, lengths, short_filter, long_filter, skip, gain, cotangent
):
    length, channels = q_input.shape
    groups = channels // GS
    wide = channels * lax.axis_size("tp")
    rows = groups // PER

    def arr(shape, dtype):
        return jax.ShapeDtypeStruct(shape, dtype)

    smem = pl.BlockSpec(memory_space=pltpu.SMEM)
    vmem = pl.BlockSpec(memory_space=pltpu.VMEM)
    far_off = pl.BlockSpec(memory_space=pltpu.HBM)
    full_bf = arr((length, channels), BF16)
    full_f = arr((length, channels), F32)

    def call(name, kernel, outs, ins, scratch=(), flops=10**8, moved=10**6, grant=8, hbm=False):
        scalar = ins[0] is lengths
        return pl.pallas_call(
            kernel,
            out_shape=outs,
            in_specs=[far_off] * len(ins)
            if hbm
            else [smem if (i == 0 and scalar) else vmem for i in range(len(ins))],
            out_specs=[vmem] * len(outs),
            scratch_shapes=scratch,
            compiler_params=pltpu.CompilerParams(vmem_limit_bytes=grant * 1024 * 1024),
            cost_estimate=pl.CostEstimate(flops=flops, bytes_accessed=moved, transcendentals=0),
            name=name,
        )(*ins)

    skip2 = skip.reshape(1, channels)
    gain2 = gain.reshape(1, channels)
    half_bf = arr((length, channels // 2), BF16)
    half_f = arr((length, channels // 2), F32)
    sent_half = arr((SENT, channels // 2), BF16)
    loads = [
        pltpu.VMEM((PACK, channels // 2), BF16), pltpu.VMEM((length, channels // 2), BF16),
        pltpu.VMEM((length, channels // 2), BF16),
    ]
    taps, sent0 = call(
        "first", first_kernel, [arr((24, channels), F32), sent_half],
        [lengths, jnp.transpose(short_filter, (0, 2, 1)), q_input, k_input, v_input],
        [pltpu.SMEM(lengths.shape, jnp.int32), pltpu.VMEM((3, KS, groups), BF16)]
        + loads + [pltpu.SemaphoreType.DMA((5,))],
        grant=60, hbm=True,
    )
    came0 = shifted(sent0, "ctx", 1)
    sent1, far = call(
        "second", second_kernel, [sent_half, arr((2 * RIM, channels), BF16)],
        [lengths, taps, q_input, k_input, v_input],
        [pltpu.SMEM(lengths.shape, jnp.int32), pltpu.VMEM((24, channels // 2), F32)]
        + loads + [pltpu.VMEM((PACK, channels), BF16)] * 2 + [pltpu.SemaphoreType.DMA((7,))],
        flops=10**9, moved=5 * 10**6, grant=60, hbm=True,
    )
    came1 = shifted(sent1, "ctx", 1)
    came_far = shifted(far, "ctx", 2)
    sent, came = (sent0, sent1), (came0, came1)

    def circulants(filt, turned):
        return call(
            "circulants", functools.partial(circulant_kernel, turned),
            [arr((K, groups * K), BF16)], [filt], [pltpu.VMEM((groups, K), F32)],
            flops=10**3, moved=10**3,
        )[0]

    filt, filt2, sent = lax.optimization_barrier((long_filter, long_filter, sent))
    fwd = circulants(filt, True)
    qbulk, kbulk, vbulk, part, top = call(
        "current", current_kernel, [full_f] * 4 + [full_bf],
        [lengths, q_input, k_input, v_input, taps, *sent, fwd, skip2],
        flops=10**3, moved=10**3,
    )
    bwd = circulants(filt2, False)
    made = []
    sums = jnp.zeros((2, K), F32)
    for i in range(2):
        *some, sums = call(
            "summed", functools.partial(summed_kernel, i),
            [half_f] * 3 + [half_bf] * 2 + [half_f] * 2 + [arr((2, K), F32)],
            [
                lengths, came[i], came_far, q_input, k_input, v_input, taps, sent[i], fwd, top,
                qbulk, kbulk, vbulk, part, skip2, resid, cotangent, gain2, sums,
            ],
            [pltpu.VMEM((2, K, LANES), F32)], flops=10**9, moved=5 * 10**6,
        )
        made.append(some)
    q_short, k_short, v_short, gated, before, mixed, summed = zip(*made)
    sums, bwd = lax.optimization_barrier((sums, bwd))
    step = 1
    while step < lax.axis_size("tp"):
        sums = sums + swapped(sums, "tp", step)
        step *= 2
    grads = [
        call(
            "grads", functools.partial(grads_kernel, wide, i), [half_bf, half_bf],
            [summed[i], mixed[i], q_short[i], cotangent, gain2, sums],
        )
        for i in range(2)
    ]
    after = [shifted(grads[i][0], "ctx", -1) for i in range(2)]
    pairs = [
        (summed[i], *grads[i], gated[i], before[i], came[i]) for i in range(2)
    ]
    stats, part, qcols = call(
        "beside", functools.partial(beside_kernel, wide),
        [arr((groups + 2 * rows, LANES), F32), full_f, arr((8, channels), F32)],
        [lengths, cotangent, sums, bwd, skip2, q_input, *pairs[0], *pairs[1]],
        flops=4 * 10**9, moved=5 * 10**6,
    )
    half_cols = arr((16, channels // 2), F32)
    grad_ks0, grad_vs0, tails, cols = call(
        "gate", functools.partial(gate_kernel, 0),
        [half_bf, half_bf, arr((4 * RIM, channels // 2), BF16), half_cols],
        [
            lengths, part, bwd, k_input, v_input, after[0], k_short[0], v_short[0], grads[0][1],
            came[0],
        ],
        flops=10**9, moved=5 * 10**6,
    )
    grad_ks1, grad_vs1, tails, packed = call(
        "gate", functools.partial(gate_kernel, 1),
        [
            half_bf, half_bf, arr((4 * RIM, channels), BF16),
            arr((groups + 2 * rows + 24, LANES), F32),
        ],
        [
            lengths, part, bwd, k_input, v_input, after[1], k_short[1], v_short[1], grads[1][1],
            came[1], stats, qcols, cols, tails,
        ],
        [pltpu.VMEM((24, channels), F32)], flops=10**9, moved=5 * 10**6,
    )
    tails = shifted(tails, "ctx", -1)
    normed, grad_q, grad_k, grad_v = call(
        "mains", functools.partial(mains_kernel, wide), [full_bf] * 4,
        [
            lengths, taps, tails, gain2, sums, summed[0], grads[0][1], grad_ks0, grad_vs0,
            summed[1], grads[1][1], grad_ks1, grad_vs1,
        ],
        flops=10**9, moved=5 * 10**6,
    )
    outs = (grad_q, grad_k, grad_v, normed)
    count = lax.axis_size("ctx")
    step = 1
    while 2 * step < count:
        packed = packed + swapped(packed, "ctx", step)
        step *= 2
    packed, *outs = lax.optimization_barrier((packed, *outs))
    grad_q, grad_k, grad_v, normed = outs
    other = swapped(packed, "ctx", step)
    grad_short, grad_long, grad_skip, grad_gain = call(
        "unpack", unpack_kernel,
        [
            arr((3, KS, groups), F32), arr((groups, K), F32),
            arr((rows, LANES), F32), arr((rows, LANES), F32),
        ],
        [packed, other],
    )
    return (
        normed, grad_q, grad_k, grad_v, jnp.transpose(grad_short, (0, 2, 1)), grad_long,
        grad_skip.reshape(channels), grad_gain.reshape(channels),
    )


def solution(mesh):
    tiled = P("ctx", "tp")
    return jax.shard_map(
        shards,
        mesh=mesh,
        in_specs=(
            tiled, tiled, tiled, tiled, P(), P(None, "tp", None), P("tp", None), P("tp"), P("tp"),
            tiled,
        ),
        out_specs=(
            tiled, tiled, tiled, tiled, P(None, "tp", None), P("tp", None), P("tp"), P("tp"),
        ),
        check_vma=False,
    )
```

```python
import functools

import jax
import jax.numpy as jnp
from jax import lax
from jax.experimental import pallas as pl
from jax.experimental.pallas import tpu as pltpu
from jax.sharding import PartitionSpec as P

GS = 16
K = 128
KS = 7
LANES = 128
PER = LANES // GS
RIM = 8
PACK = 16
EPS = 1e-06
F32 = jnp.float32
BF16 = jnp.bfloat16


def shifted(x, axis, by, wrap=True):
    count = lax.axis_size(axis)
    pairs = [(i, (i + by) % count) for i in range(count)]
    return lax.ppermute(x, axis, [p for p in pairs if wrap or p[1] - p[0] == by])


def swapped(x, axis, step):
    return lax.ppermute(x, axis, [(i, i ^ step) for i in range(lax.axis_size(axis))])


def iota(shape, dim):
    return lax.broadcasted_iota(jnp.int32, shape, dim)


def positions(len_ref, rows):
    begin = jnp.zeros_like(rows)
    start = jnp.int32(0)
    for n in range(len_ref.shape[0]):
        begin = jnp.where(rows >= start, start, begin)
        start = start + len_ref[n]
    return jnp.where(rows < start, rows - begin, -1)


def first_row():
    return lax.axis_index("ctx") * K


def lanes_of(q):
    return pl.ds(pl.multiple_of(q * LANES, LANES), LANES)


def each_chunk(channels, body, unroll=4):
    def step(q, carry):
        body(q)
        return carry

    lax.fori_loop(0, channels // LANES, step, 0, unroll=unroll)


def as_mask(cond):
    return jnp.where(cond, 1.0, 0.0).astype(BF16)


def join(*parts):
    return jnp.concatenate(parts, axis=0)


def tap_rows(taps_ref, which, ls):
    table = taps_ref[which * 8 : which * 8 + 8, ls]
    return [table[j : j + 1, :] for j in range(KS)]


def causal(ext, taps, pos):
    rows = ext.shape[0] - RIM
    total = taps[0] * ext[RIM:]
    for j in range(1, KS):
        moved = ext[RIM - j : RIM - j + rows]
        total = total + taps[j] * jnp.where(pos >= j, moved, 0.0)
    return total


def tap_lines(grad, ext, pos):
    lines = [jnp.sum(grad * ext[RIM:], axis=0, keepdims=True)]
    for j in range(1, KS):
        held = jnp.where(pos >= j, grad, 0.0)
        lines.append(jnp.sum(held * ext[RIM - j : RIM - j + K], axis=0, keepdims=True))
    lines.append(jnp.zeros((8 - KS, LANES), F32))
    return join(*lines)


def owners():
    lane = iota((K, LANES), 1) // GS
    return [as_mask(lane == g) for g in range(PER)]


def per_group(right, own):
    return join(*[right * mask for mask in own])


def masked(table_ref, q, mask):
    table = table_ref[:, pl.ds(pl.multiple_of(q * PER * K, PER * K), PER * K)]
    return [table[:, g * K : (g + 1) * K] * mask for g in range(PER)]


def product(left, right):
    return jnp.dot(jnp.concatenate(left, axis=1), right, preferred_element_type=F32)


K_FIRST, Q_LAST, K_LAST, V_LAST, V_FIRST, SENT = 0, K, K + 8, K + 16, K + 24, K + 32


def rim_of(ref, at, ls):
    base = at // PACK * PACK
    return ref[base : base + PACK, ls].astype(F32)[at - base : at - base + RIM]


def first_kernel(
    len_hbm, short_hbm, q_hbm, k_hbm, v_hbm, taps_ref, sent_ref, far_ref,
    len_ref, short_ref, q_ref, k_ref, v_ref, sems,
):
    groups = short_ref.shape[2]
    channels = taps_ref.shape[1]
    pairs = (
        (short_hbm, short_ref), (len_hbm, len_ref), (k_hbm, k_ref), (v_hbm, v_ref),
        (q_hbm.at[K - PACK : K], q_ref),
    )
    copies = [pltpu.make_async_copy(a, b, sems.at[i]) for i, (a, b) in enumerate(pairs)]
    for copy in copies:
        copy.start()
    spread = as_mask(iota((groups, channels), 1) // GS == iota((groups, channels), 0))
    copies[0].wait()
    for i in range(3):
        taps_ref[i * 8 : i * 8 + KS] = jnp.dot(
            short_ref[i], spread, preferred_element_type=F32
        )
        taps_ref[i * 8 + KS : i * 8 + 8] = jnp.zeros((8 - KS, channels), F32)
    for copy in copies[1:]:
        copy.wait()
    pos = positions(len_ref, first_row() + RIM + iota((K - RIM, LANES), 0))

    def body(q):
        ls = lanes_of(q)
        kx = k_ref[:, ls].astype(F32)
        vx = v_ref[:, ls].astype(F32)
        ks = causal(kx, tap_rows(taps_ref, 1, ls), pos)
        vs = causal(vx, tap_rows(taps_ref, 2, ls), pos)
        sent_ref[:K, ls] = join(kx[:RIM], ks * vs).astype(BF16)
        q_end = q_ref[:, ls].astype(F32)[PACK - RIM :]
        k_end = kx[K - RIM :]
        v_end = vx[K - RIM :]
        sent_ref[K:, ls] = join(q_end, k_end, v_end, vx[:RIM]).astype(BF16)
        far_ref[:, ls] = join(k_end, v_end).astype(BF16)

    each_chunk(channels, body)


def circulant_kernel(turned, long_ref, out_ref, line_ref):
    groups = long_ref.shape[0]
    filt = long_ref[...]
    if turned:
        flip = as_mask((iota((K, K), 0) + iota((K, K), 1)) % K == 0)
        line_ref[...] = jnp.dot(filt, flip, preferred_element_type=F32)
    else:
        line_ref[...] = filt.astype(F32)

    def step(g, carry):
        row = jnp.broadcast_to(line_ref[pl.ds(g, 1), :], (GS, K))
        block = pltpu.roll(row, 0, 1, stride=1, stride_axis=0)
        for i in range(K // GS):
            moved = block if i == 0 else pltpu.roll(block, i * GS, 1)
            at = pl.ds(pl.multiple_of(g * K, K), K)
            out_ref[i * GS : (i + 1) * GS, at] = moved.astype(BF16)
        return carry

    lax.fori_loop(0, groups, step, 0, unroll=8)


def current_kernel(
    len_ref, q_ref, taps_ref, sent_ref, fwd_ref, skip_ref, qs_ref, part_ref, top_ref
):
    row = iota((K, LANES), 0)
    col = iota((K, LANES), 1)
    pos = positions(len_ref, first_row() + row)
    near = (col <= row) & (pos >= row - col)
    mask = as_mask(near)
    mask_top = as_mask(near & (col < RIM))
    picks = join(*[as_mask((col == row + g * GS) & (row < GS)) for g in range(PER)])
    own = owners()
    top = jnp.zeros((RIM, LANES), F32)

    def body(q):
        ls = lanes_of(q)
        qs_ref[RIM:, ls] = causal(q_ref[:, ls].astype(F32), tap_rows(taps_ref, 0, ls), pos[RIM:])
        qs_ref[:RIM, ls] = top
        gated = join(top, sent_ref[:K, ls].astype(F32)[RIM:])
        rest = product(masked(fwd_ref, q, mask), per_group(gated.astype(BF16), own))
        part_ref[:, ls] = rest + skip_ref[:, ls] * gated
        top_ref[:, ls] = product(masked(fwd_ref, q, mask_top), picks).astype(BF16)

    each_chunk(q_ref.shape[1], body)


def summed_kernel(
    len_ref, came_ref, far_ref, q_ref, k_ref, v_ref, taps_ref, sent_ref, fwd_ref, top_ref,
    bulk_ref, part_ref, skip_ref, resid_ref, cot_ref, gain_ref,
    qs_ref, gated_ref, before_ref, mixed_ref, summed_ref, sums_ref, acc_ref,
):
    row = iota((K, LANES), 0)
    col = iota((K, LANES), 1)
    pos = positions(len_ref, first_row() + row)
    mask = as_mask((col > row) & (pos >= row - col + K))
    pos_top = pos[:RIM]
    pos_far = positions(len_ref, first_row() - K + iota((RIM, LANES), 0))
    own = owners()
    own_top = [
        as_mask((iota((PACK, LANES), 1) // GS == g) & (iota((PACK, LANES), 0) < RIM))
        for g in range(PER)
    ]
    acc_ref[...] = jnp.zeros_like(acc_ref)

    def body(q):
        ls = lanes_of(q)
        kt = tap_rows(taps_ref, 1, ls)
        vt = tap_rows(taps_ref, 2, ls)
        k_last = rim_of(came_ref, K_LAST, ls)
        v_last = rim_of(came_ref, V_LAST, ls)
        top = causal(join(k_last, rim_of(k_ref, 0, ls)), kt, pos_top) * causal(
            join(v_last, rim_of(v_ref, 0, ls)), vt, pos_top
        )
        far_top = causal(
            join(rim_of(far_ref, 0, ls), rim_of(came_ref, K_FIRST, ls)), kt, pos_far
        ) * causal(join(rim_of(far_ref, RIM, ls), rim_of(came_ref, V_FIRST, ls)), vt, pos_far)
        qs_top = causal(
            join(rim_of(came_ref, Q_LAST, ls), rim_of(q_ref, 0, ls)), tap_rows(taps_ref, 0, ls), pos_top
        )
        before = join(far_top, came_ref[:K, ls].astype(F32)[RIM:]).astype(BF16)
        gated = join(top, sent_ref[:K, ls].astype(F32)[RIM:]).astype(BF16)
        before_ref[:, ls] = before
        gated_ref[:, ls] = gated
        qs = join(qs_top, bulk_ref[RIM:, ls])
        qs_ref[:, ls] = qs
        first = gated[:PACK]
        left = masked(fwd_ref, q, mask) + [top_ref[:, ls]]
        right = join(per_group(before, own), per_group(first, own_top))
        direct = skip_ref[:, ls] * first.astype(F32)[:RIM]
        mixed = part_ref[:, ls] + product(left, right)
        mixed = join(mixed[:RIM] + direct, mixed[RIM:])
        summed = resid_ref[:, ls].astype(F32) + qs * mixed
        mixed_ref[:, ls] = mixed
        summed_ref[:, ls] = summed
        acc_ref[0] += summed * summed
        acc_ref[1] += gain_ref[:, ls] * cot_ref[:, ls].astype(F32) * summed

    each_chunk(resid_ref.shape[1], body)
    for i in range(2):
        sums_ref[i : i + 1] = jnp.sum(acc_ref[i].T, axis=0, keepdims=True)


def group_sums(cols):
    count, channels = cols.shape
    gather = as_mask(iota((channels, LANES), 0) // GS == iota((channels, LANES), 1))
    high = cols.astype(BF16)
    rest = cols - high.astype(F32)
    mid = rest.astype(BF16)
    low = (rest - mid.astype(F32)).astype(BF16)
    parts = join(high.astype(F32), mid.astype(F32), low.astype(F32)).astype(BF16)
    sums = jnp.dot(parts, gather, preferred_element_type=F32)
    return sums[:count] + sums[count : 2 * count] + sums[2 * count :]


def by_row(line):
    return jnp.broadcast_to(line, (K, K)).T


def inverse_of(sums_ref, total):
    return by_row(lax.rsqrt(sums_ref[0:1] / total + EPS))


def gates_kernel(len_ref, k_ref, v_ref, came_ref, taps_ref, ks_ref, vs_ref):
    pos = positions(len_ref, first_row() + iota((K, LANES), 0))

    def body(q):
        ls = lanes_of(q)
        k_ext = join(rim_of(came_ref, K_LAST, ls), k_ref[:, ls].astype(F32))
        v_ext = join(rim_of(came_ref, V_LAST, ls), v_ref[:, ls].astype(F32))
        ks_ref[:, ls] = causal(k_ext, tap_rows(taps_ref, 1, ls), pos)
        vs_ref[:, ls] = causal(v_ext, tap_rows(taps_ref, 2, ls), pos)

    each_chunk(k_ref.shape[1], body)


def grads_kernel(total, summed_ref, mixed_ref, qs_ref, cot_ref, gain_ref, sums_ref, gm_ref, gq_ref):
    inverse = inverse_of(sums_ref, total)
    scale = inverse * inverse * by_row(sums_ref[1:2] / total)

    def body(q):
        ls = lanes_of(q)
        scaled = gain_ref[:, ls] * cot_ref[:, ls].astype(F32)
        grad_sum = inverse * (scaled - summed_ref[:, ls] * scale)
        gm_ref[:, ls] = (grad_sum * qs_ref[:, ls]).astype(BF16)
        gq_ref[:, ls] = (grad_sum * mixed_ref[:, ls]).astype(BF16)

    each_chunk(cot_ref.shape[1], body)


def beside_kernel(
    total, len_ref, summed_ref, cot_ref, sums_ref, gm_ref, gq_ref, gated_ref, before_ref,
    bwd_ref, skip_ref, q_ref, came_ref, stats_ref, part_ref, cols_ref,
):
    groups = bwd_ref.shape[1] // K
    inverse = inverse_of(sums_ref, total)
    row = iota((K, LANES), 0)
    col = iota((K, LANES), 1)
    pos_row = positions(len_ref, first_row() + row)
    pos = positions(len_ref, first_row() + col)
    mask = as_mask((col >= row) & (pos >= col - row))
    source = K - 1 - row
    near = (col >= source) & (pos >= col - source)
    far = (col < source) & (pos >= col - source + K)
    flip = as_mask(row + col == K - 1)
    own = owners()

    def body(q):
        ls = lanes_of(q)
        summed = summed_ref[:, ls]
        gm = gm_ref[:, ls]
        gmf = gm.astype(F32)
        gated = gated_ref[:, ls]
        stats_ref[pl.ds(groups + q, 1), :] = jnp.sum(gmf * gated.astype(F32), axis=0, keepdims=True)
        stats_ref[pl.ds(groups + groups // PER + q, 1), :] = jnp.sum(
            cot_ref[:, ls].astype(F32) * summed * inverse, axis=0, keepdims=True
        )
        right = per_group(gm, own)
        part_ref[:, ls] = skip_ref[:, ls] * gmf + product(masked(bwd_ref, q, mask), right)
        two = jnp.concatenate([before_ref[:, ls], gated], axis=1)
        flipped = jnp.dot(flip, two, preferred_element_type=F32).astype(BF16)
        left = join(flipped[:, :LANES], flipped[:, LANES:])
        turned = gmf.T.astype(BF16)
        spread = []
        for g in range(PER):
            pieces = [jnp.zeros((GS, K), BF16)] * PER
            pieces[g] = turned[g * GS : (g + 1) * GS]
            spread.append(join(*pieces))
        cross = jnp.dot(left, jnp.concatenate(spread, axis=1), preferred_element_type=F32)
        lines = []
        for g in range(PER):
            gs = slice(g * K, (g + 1) * K)
            square = jnp.where(near, cross[K:, gs], jnp.where(far, cross[:K, gs], 0.0))
            square = pltpu.roll(square, 1, 1, stride=1, stride_axis=0)
            lines.append(jnp.sum(square, axis=0, keepdims=True))
        stats_ref[pl.ds(pl.multiple_of(q * PER, PER), PER), :] = join(*lines)
        q_ext = join(rim_of(came_ref, Q_LAST, ls), q_ref[:, ls].astype(F32))
        cols_ref[:, ls] = tap_lines(gq_ref[:, ls].astype(F32), q_ext, pos_row)

    each_chunk(cot_ref.shape[1], body, 2)


def gate_kernel(
    len_ref, part_ref, after_ref, bwd_ref, ks_ref, vs_ref, gq_ref, k_ref, v_ref, came_ref,
    stats_ref, qcols_ref, gks_ref, gvs_ref, tails_ref, packed_ref, cols_ref,
):
    channels = part_ref.shape[1]
    kept = stats_ref.shape[0]
    row = iota((K, LANES), 0)
    col = iota((K, LANES), 1)
    pos_row = positions(len_ref, first_row() + row)
    pos = positions(len_ref, first_row() + K + col)
    mask = as_mask((col < row) & (pos >= col - row + K))
    own = owners()

    def body(q):
        ls = lanes_of(q)
        right = per_group(after_ref[:, ls], own)
        grad = part_ref[:, ls] + product(masked(bwd_ref, q, mask), right)
        gks = (grad * vs_ref[:, ls]).astype(BF16)
        gvs = (grad * ks_ref[:, ls]).astype(BF16)
        gks_ref[:, ls] = gks
        gvs_ref[:, ls] = gvs
        heads = (rim_of(gq_ref, 0, ls), gks.astype(F32)[:RIM], gvs.astype(F32)[:RIM])
        tails_ref[:, ls] = join(*heads, jnp.zeros((RIM, LANES), F32)).astype(BF16)
        k_ext = join(rim_of(came_ref, K_LAST, ls), k_ref[:, ls].astype(F32))
        v_ext = join(rim_of(came_ref, V_LAST, ls), v_ref[:, ls].astype(F32))
        cols_ref[0:8, ls] = qcols_ref[:, ls]
        cols_ref[8:16, ls] = tap_lines(gks.astype(F32), k_ext, pos_row)
        cols_ref[16:24, ls] = tap_lines(gvs.astype(F32), v_ext, pos_row)

    each_chunk(channels, body)
    packed_ref[0:kept] = stats_ref[...]
    packed_ref[kept:] = group_sums(cols_ref[...])


def mains_kernel(
    total, len_ref, taps_ref, gq_ref, gks_ref, gvs_ref, tails_ref, summed_ref, gain_ref, sums_ref,
    oq_ref, ok_ref, ov_ref, normed_ref,
):
    pos = positions(len_ref, first_row() + iota((K + RIM, LANES), 0))
    inverse = inverse_of(sums_ref, total)

    def body(q):
        ls = lanes_of(q)
        normed_ref[:, ls] = (gain_ref[:, ls] * summed_ref[:, ls] * inverse).astype(BF16)
        for i, (g_ref, o_ref) in enumerate(((gq_ref, oq_ref), (gks_ref, ok_ref), (gvs_ref, ov_ref))):
            ext = join(g_ref[:, ls].astype(F32), rim_of(tails_ref, i * RIM, ls))
            taps = tap_rows(taps_ref, i, ls)
            grad = taps[0] * ext[:K]
            for j in range(1, KS):
                held = jnp.where(pos >= j, ext, 0.0)
                grad = grad + taps[j] * held[j : j + K]
            o_ref[:, ls] = grad.astype(BF16)

    each_chunk(gq_ref.shape[1], body)


def unpack_kernel(one_ref, two_ref, short_ref, long_ref, skip_ref, gain_ref):
    groups = long_ref.shape[0]
    rows = groups // PER
    total = one_ref[...] + two_ref[...]
    long_ref[...] = total[:groups]
    skip_ref[...] = total[groups : groups + rows]
    gain_ref[...] = total[groups + rows : groups + 2 * rows]
    for i in range(3):
        at = groups + 2 * rows + i * 8
        short_ref[i] = total[at : at + KS, :groups]


def shards(
    q_input, k_input, v_input, resid, lengths, short_filter, long_filter, skip, gain, cotangent
):
    length, channels = q_input.shape
    groups = channels // GS
    wide = channels * lax.axis_size("tp")
    rows = groups // PER
    packed_rows = groups + 2 * rows + 24

    def arr(shape, dtype):
        return jax.ShapeDtypeStruct(shape, dtype)

    smem = pl.BlockSpec(memory_space=pltpu.SMEM)
    vmem = pl.BlockSpec(memory_space=pltpu.VMEM)
    far_off = pl.BlockSpec(memory_space=pltpu.HBM)
    full_bf = arr((length, channels), BF16)
    full_f = arr((length, channels), F32)

    def call(name, kernel, outs, ins, scratch=(), flops=10**8, moved=10**6, grant=8, hbm=False):
        scalar = ins[0] is lengths
        return pl.pallas_call(
            kernel,
            out_shape=outs,
            in_specs=[far_off] * len(ins)
            if hbm
            else [smem if (i == 0 and scalar) else vmem for i in range(len(ins))],
            out_specs=[vmem] * len(outs),
            scratch_shapes=scratch,
            compiler_params=pltpu.CompilerParams(vmem_limit_bytes=grant * 1024 * 1024),
            cost_estimate=pl.CostEstimate(flops=flops, bytes_accessed=moved, transcendentals=0),
            name=name,
        )(*ins)

    skip2 = skip.reshape(1, channels)
    gain2 = gain.reshape(1, channels)
    taps, sent, far = call(
        "first", first_kernel,
        [arr((24, channels), F32), arr((SENT, channels), BF16), arr((2 * RIM, channels), BF16)],
        [lengths, jnp.transpose(short_filter, (0, 2, 1)), q_input, k_input, v_input],
        [
            pltpu.SMEM(lengths.shape, jnp.int32), pltpu.VMEM((3, KS, groups), BF16),
            pltpu.VMEM((PACK, channels), BF16), pltpu.VMEM((length, channels), BF16),
            pltpu.VMEM((length, channels), BF16), pltpu.SemaphoreType.DMA((5,)),
        ],
        grant=60,
        hbm=True,
    )
    came = shifted(sent, "ctx", 1)
    came_far = shifted(far, "ctx", 2)

    def circulants(filt, turned):
        return call(
            "circulants", functools.partial(circulant_kernel, turned),
            [arr((K, groups * K), BF16)], [filt], [pltpu.VMEM((groups, K), F32)],
            flops=10**9, moved=4 * 10**6,
        )[0]

    filt, filt2, sent = lax.optimization_barrier((long_filter, long_filter, sent))
    fwd = circulants(filt, True)
    bulk, part, top = call(
        "current", current_kernel, [full_f, full_f, full_bf],
        [lengths, q_input, taps, sent, fwd, skip2], flops=10**9, moved=5 * 10**6,
    )
    bwd = circulants(filt2, False)
    came, bwd = lax.optimization_barrier((came, bwd))
    q_short, gated, before, mixed, summed, sums = call(
        "summed", summed_kernel,
        [full_f, full_bf, full_bf, full_f, full_f, arr((2, K), F32)],
        [
            lengths, came, came_far, q_input, k_input, v_input, taps, sent, fwd, top,
            bulk, part, skip2, resid, cotangent, gain2,
        ],
        [pltpu.VMEM((2, K, LANES), F32)], flops=10**9, moved=5 * 10**6,
    )
    own_sums = sums
    step = 1
    while step < lax.axis_size("tp"):
        sums = sums + swapped(sums, "tp", step)
        step *= 2
    came, _ = lax.optimization_barrier((came, own_sums))
    k_short, v_short = call(
        "gates", gates_kernel, [full_f] * 2, [lengths, k_input, v_input, came, taps],
        flops=10**8, moved=2 * 10**6,
    )
    sums, k_short, v_short = lax.optimization_barrier((sums, k_short, v_short))
    grad_mixed, grad_qs = call(
        "grads", functools.partial(grads_kernel, wide), [full_bf, full_bf],
        [summed, mixed, q_short, cotangent, gain2, sums],
    )
    after = shifted(grad_mixed, "ctx", -1, wrap=False)
    stats, part, qcols = call(
        "beside", functools.partial(beside_kernel, wide),
        [
            arr((groups + 2 * rows, LANES), F32), full_f, arr((8, channels), F32),
        ],
        [
            lengths, summed, cotangent, sums, grad_mixed, grad_qs, gated, before, bwd,
            skip2, q_input, came,
        ],
        flops=4 * 10**9, moved=5 * 10**6,
    )
    grad_ks, grad_vs, tails, packed = call(
        "gate", gate_kernel,
        [
            full_bf, full_bf, arr((4 * RIM, channels), BF16),
            arr((packed_rows, LANES), F32),
        ],
        [
            lengths, part, after, bwd, k_short, v_short, grad_qs, k_input, v_input, came,
            stats, qcols,
        ],
        [pltpu.VMEM((24, channels), F32)], flops=10**9, moved=5 * 10**6,
    )
    tails = shifted(tails, "ctx", -1)
    grad_q, grad_k, grad_v, normed = call(
        "mains", functools.partial(mains_kernel, wide), [full_bf] * 4,
        [lengths, taps, grad_qs, grad_ks, grad_vs, tails, summed, gain2, sums], flops=10**9, moved=5 * 10**6,
    )
    outs = (grad_q, grad_k, grad_v, normed)
    count = lax.axis_size("ctx")
    step = 1
    while 2 * step < count:
        packed = packed + swapped(packed, "ctx", step)
        step *= 2
    packed, *outs = lax.optimization_barrier((packed, *outs))
    grad_q, grad_k, grad_v, normed = outs
    other = swapped(packed, "ctx", step)
    grad_short, grad_long, grad_skip, grad_gain = call(
        "unpack", unpack_kernel,
        [
            arr((3, KS, groups), F32), arr((groups, K), F32),
            arr((rows, LANES), F32), arr((rows, LANES), F32),
        ],
        [packed, other],
    )
    return (
        normed, grad_q, grad_k, grad_v, jnp.transpose(grad_short, (0, 2, 1)), grad_long,
        grad_skip.reshape(channels), grad_gain.reshape(channels),
    )


def solution(mesh):
    tiled = P("ctx", "tp")
    return jax.shard_map(
        shards,
        mesh=mesh,
        in_specs=(
            tiled, tiled, tiled, tiled, P(), P(None, "tp", None), P("tp", None), P("tp"), P("tp"),
            tiled,
        ),
        out_specs=(
            tiled, tiled, tiled, tiled, P(None, "tp", None), P("tp", None), P("tp"), P("tp"),
        ),
        check_vma=False,
    )
```

```python
import functools

import jax
import jax.numpy as jnp
from jax import lax
from jax.experimental import pallas as pl
from jax.experimental.pallas import tpu as pltpu
from jax.sharding import PartitionSpec as P

GS = 16
K = 128
KS = 7
LANES = 128
PER = LANES // GS
RIM = 8
PACK = 16
EPS = 1e-06
F32 = jnp.float32
BF16 = jnp.bfloat16


def shifted(x, axis, by, wrap=True):
    count = lax.axis_size(axis)
    pairs = [(i, (i + by) % count) for i in range(count)]
    return lax.ppermute(x, axis, [p for p in pairs if wrap or p[1] - p[0] == by])


def swapped(x, axis, step):
    return lax.ppermute(x, axis, [(i, i ^ step) for i in range(lax.axis_size(axis))])


def iota(shape, dim):
    return lax.broadcasted_iota(jnp.int32, shape, dim)


def positions(len_ref, rows):
    begin = jnp.zeros_like(rows)
    start = jnp.int32(0)
    for n in range(len_ref.shape[0]):
        begin = jnp.where(rows >= start, start, begin)
        start = start + len_ref[n]
    return jnp.where(rows < start, rows - begin, -1)


def first_row():
    return lax.axis_index("ctx") * K


def lanes_of(q):
    return pl.ds(pl.multiple_of(q * LANES, LANES), LANES)


def each_chunk(channels, body, unroll=4):
    def step(q, carry):
        body(q)
        return carry

    lax.fori_loop(0, channels // LANES, step, 0, unroll=unroll)


def as_mask(cond):
    return jnp.where(cond, 1.0, 0.0).astype(BF16)


def join(*parts):
    return jnp.concatenate(parts, axis=0)


def tap_rows(taps_ref, which, ls):
    table = taps_ref[which * 8 : which * 8 + 8, ls]
    return [table[j : j + 1, :] for j in range(KS)]


def causal(ext, taps, pos):
    rows = ext.shape[0] - RIM
    total = taps[0] * ext[RIM:]
    for j in range(1, KS):
        moved = ext[RIM - j : RIM - j + rows]
        total = total + taps[j] * jnp.where(pos >= j, moved, 0.0)
    return total


def tap_lines(grad, ext, pos):
    lines = [jnp.sum(grad * ext[RIM:], axis=0, keepdims=True)]
    for j in range(1, KS):
        held = jnp.where(pos >= j, grad, 0.0)
        lines.append(jnp.sum(held * ext[RIM - j : RIM - j + K], axis=0, keepdims=True))
    lines.append(jnp.zeros((8 - KS, LANES), F32))
    return join(*lines)


def owners():
    lane = iota((K, LANES), 1) // GS
    return [as_mask(lane == g) for g in range(PER)]


def per_group(right, own):
    return join(*[right * mask for mask in own])


def masked(table_ref, q, mask):
    table = table_ref[:, pl.ds(pl.multiple_of(q * PER * K, PER * K), PER * K)]
    return [table[:, g * K : (g + 1) * K] * mask for g in range(PER)]


def product(left, right):
    return jnp.dot(jnp.concatenate(left, axis=1), right, preferred_element_type=F32)


K_FIRST, Q_LAST, K_LAST, V_LAST, V_FIRST, SENT = 0, K, K + 8, K + 16, K + 24, K + 32


def rim_of(ref, at, ls):
    base = at // PACK * PACK
    return ref[base : base + PACK, ls].astype(F32)[at - base : at - base + RIM]


def first_kernel(
    len_hbm, short_hbm, q_hbm, k_hbm, v_hbm, taps_ref, sent_ref, far_ref,
    len_ref, short_ref, q_ref, k_ref, v_ref, sems,
):
    groups = short_ref.shape[2]
    channels = taps_ref.shape[1]
    pairs = (
        (short_hbm, short_ref), (len_hbm, len_ref), (k_hbm, k_ref), (v_hbm, v_ref),
        (q_hbm.at[K - PACK : K], q_ref),
    )
    copies = [pltpu.make_async_copy(a, b, sems.at[i]) for i, (a, b) in enumerate(pairs)]
    for copy in copies:
        copy.start()
    spread = as_mask(iota((groups, channels), 1) // GS == iota((groups, channels), 0))
    copies[0].wait()
    for i in range(3):
        taps_ref[i * 8 : i * 8 + KS] = jnp.dot(
            short_ref[i], spread, preferred_element_type=F32
        )
        taps_ref[i * 8 + KS : i * 8 + 8] = jnp.zeros((8 - KS, channels), F32)
    for copy in copies[1:]:
        copy.wait()
    pos = positions(len_ref, first_row() + RIM + iota((K - RIM, LANES), 0))

    def body(q):
        ls = lanes_of(q)
        kx = k_ref[:, ls].astype(F32)
        vx = v_ref[:, ls].astype(F32)
        ks = causal(kx, tap_rows(taps_ref, 1, ls), pos)
        vs = causal(vx, tap_rows(taps_ref, 2, ls), pos)
        sent_ref[:K, ls] = join(kx[:RIM], ks * vs).astype(BF16)
        q_end = q_ref[:, ls].astype(F32)[PACK - RIM :]
        k_end = kx[K - RIM :]
        v_end = vx[K - RIM :]
        sent_ref[K:, ls] = join(q_end, k_end, v_end, vx[:RIM]).astype(BF16)
        far_ref[:, ls] = join(k_end, v_end).astype(BF16)

    each_chunk(channels, body)


def circulant_kernel(turned, long_ref, out_ref, line_ref):
    groups = long_ref.shape[0]
    filt = long_ref[...]
    if turned:
        flip = as_mask((iota((K, K), 0) + iota((K, K), 1)) % K == 0)
        line_ref[...] = jnp.dot(filt, flip, preferred_element_type=F32)
    else:
        line_ref[...] = filt.astype(F32)

    def step(g, carry):
        row = jnp.broadcast_to(line_ref[pl.ds(g, 1), :], (GS, K))
        block = pltpu.roll(row, 0, 1, stride=1, stride_axis=0)
        for i in range(K // GS):
            moved = block if i == 0 else pltpu.roll(block, i * GS, 1)
            at = pl.ds(pl.multiple_of(g * K, K), K)
            out_ref[i * GS : (i + 1) * GS, at] = moved.astype(BF16)
        return carry

    lax.fori_loop(0, groups, step, 0, unroll=8)


def current_kernel(
    len_ref, q_ref, taps_ref, sent_ref, fwd_ref, skip_ref, qs_ref, part_ref, top_ref
):
    row = iota((K, LANES), 0)
    col = iota((K, LANES), 1)
    pos = positions(len_ref, first_row() + row)
    near = (col <= row) & (pos >= row - col)
    mask = as_mask(near)
    mask_top = as_mask(near & (col < RIM))
    picks = join(*[as_mask((col == row + g * GS) & (row < GS)) for g in range(PER)])
    own = owners()
    top = jnp.zeros((RIM, LANES), F32)

    def body(q):
        ls = lanes_of(q)
        qs_ref[RIM:, ls] = causal(q_ref[:, ls].astype(F32), tap_rows(taps_ref, 0, ls), pos[RIM:])
        qs_ref[:RIM, ls] = top
        gated = join(top, sent_ref[:K, ls].astype(F32)[RIM:])
        rest = product(masked(fwd_ref, q, mask), per_group(gated.astype(BF16), own))
        part_ref[:, ls] = rest + skip_ref[:, ls] * gated
        top_ref[:, ls] = product(masked(fwd_ref, q, mask_top), picks).astype(BF16)

    each_chunk(q_ref.shape[1], body)


def summed_kernel(
    len_ref, came_ref, far_ref, q_ref, k_ref, v_ref, taps_ref, sent_ref, fwd_ref, top_ref,
    bulk_ref, part_ref, skip_ref, resid_ref, cot_ref, gain_ref,
    qs_ref, gated_ref, before_ref, mixed_ref, summed_ref, sums_ref, acc_ref,
):
    row = iota((K, LANES), 0)
    col = iota((K, LANES), 1)
    pos = positions(len_ref, first_row() + row)
    mask = as_mask((col > row) & (pos >= row - col + K))
    pos_top = pos[:RIM]
    pos_far = positions(len_ref, first_row() - K + iota((RIM, LANES), 0))
    own = owners()
    own_top = [
        as_mask((iota((PACK, LANES), 1) // GS == g) & (iota((PACK, LANES), 0) < RIM))
        for g in range(PER)
    ]
    acc_ref[...] = jnp.zeros_like(acc_ref)

    def body(q):
        ls = lanes_of(q)
        kt = tap_rows(taps_ref, 1, ls)
        vt = tap_rows(taps_ref, 2, ls)
        k_last = rim_of(came_ref, K_LAST, ls)
        v_last = rim_of(came_ref, V_LAST, ls)
        top = causal(join(k_last, rim_of(k_ref, 0, ls)), kt, pos_top) * causal(
            join(v_last, rim_of(v_ref, 0, ls)), vt, pos_top
        )
        far_top = causal(
            join(rim_of(far_ref, 0, ls), rim_of(came_ref, K_FIRST, ls)), kt, pos_far
        ) * causal(join(rim_of(far_ref, RIM, ls), rim_of(came_ref, V_FIRST, ls)), vt, pos_far)
        qs_top = causal(
            join(rim_of(came_ref, Q_LAST, ls), rim_of(q_ref, 0, ls)), tap_rows(taps_ref, 0, ls), pos_top
        )
        before = join(far_top, came_ref[:K, ls].astype(F32)[RIM:]).astype(BF16)
        gated = join(top, sent_ref[:K, ls].astype(F32)[RIM:]).astype(BF16)
        before_ref[:, ls] = before
        gated_ref[:, ls] = gated
        qs = join(qs_top, bulk_ref[RIM:, ls])
        qs_ref[:, ls] = qs
        first = gated[:PACK]
        left = masked(fwd_ref, q, mask) + [top_ref[:, ls]]
        right = join(per_group(before, own), per_group(first, own_top))
        direct = skip_ref[:, ls] * first.astype(F32)[:RIM]
        mixed = part_ref[:, ls] + product(left, right)
        mixed = join(mixed[:RIM] + direct, mixed[RIM:])
        summed = resid_ref[:, ls].astype(F32) + qs * mixed
        mixed_ref[:, ls] = mixed
        summed_ref[:, ls] = summed
        acc_ref[0] += summed * summed
        acc_ref[1] += gain_ref[:, ls] * cot_ref[:, ls].astype(F32) * summed

    each_chunk(resid_ref.shape[1], body)
    for i in range(2):
        sums_ref[i : i + 1] = jnp.sum(acc_ref[i].T, axis=0, keepdims=True)


def group_sums(cols):
    count, channels = cols.shape
    gather = as_mask(iota((channels, LANES), 0) // GS == iota((channels, LANES), 1))
    high = cols.astype(BF16)
    rest = cols - high.astype(F32)
    mid = rest.astype(BF16)
    low = (rest - mid.astype(F32)).astype(BF16)
    parts = join(high.astype(F32), mid.astype(F32), low.astype(F32)).astype(BF16)
    sums = jnp.dot(parts, gather, preferred_element_type=F32)
    return sums[:count] + sums[count : 2 * count] + sums[2 * count :]


def by_row(line):
    return jnp.broadcast_to(line, (K, K)).T


def inverse_of(sums_ref, total):
    return by_row(lax.rsqrt(sums_ref[0:1] / total + EPS))


def grads_kernel(total, summed_ref, mixed_ref, qs_ref, cot_ref, gain_ref, sums_ref, gm_ref, gq_ref):
    inverse = inverse_of(sums_ref, total)
    scale = inverse * inverse * by_row(sums_ref[1:2] / total)

    def body(q):
        ls = lanes_of(q)
        scaled = gain_ref[:, ls] * cot_ref[:, ls].astype(F32)
        grad_sum = inverse * (scaled - summed_ref[:, ls] * scale)
        gm_ref[:, ls] = (grad_sum * qs_ref[:, ls]).astype(BF16)
        gq_ref[:, ls] = (grad_sum * mixed_ref[:, ls]).astype(BF16)

    each_chunk(cot_ref.shape[1], body)


def beside_kernel(
    total, len_ref, summed_ref, cot_ref, sums_ref, gm_ref, gq_ref, gated_ref, before_ref,
    bwd_ref, skip_ref, q_ref, k_ref, v_ref, came_ref, taps_ref,
    stats_ref, part_ref, cols_ref, ks_ref, vs_ref,
):
    groups = bwd_ref.shape[1] // K
    inverse = inverse_of(sums_ref, total)
    row = iota((K, LANES), 0)
    col = iota((K, LANES), 1)
    pos_row = positions(len_ref, first_row() + row)
    pos = positions(len_ref, first_row() + col)
    mask = as_mask((col >= row) & (pos >= col - row))
    source = K - 1 - row
    near = (col >= source) & (pos >= col - source)
    far = (col < source) & (pos >= col - source + K)
    flip = as_mask(row + col == K - 1)
    own = owners()

    def body(q):
        ls = lanes_of(q)
        summed = summed_ref[:, ls]
        gm = gm_ref[:, ls]
        gmf = gm.astype(F32)
        gated = gated_ref[:, ls]
        stats_ref[pl.ds(groups + q, 1), :] = jnp.sum(gmf * gated.astype(F32), axis=0, keepdims=True)
        stats_ref[pl.ds(groups + groups // PER + q, 1), :] = jnp.sum(
            cot_ref[:, ls].astype(F32) * summed * inverse, axis=0, keepdims=True
        )
        right = per_group(gm, own)
        part_ref[:, ls] = skip_ref[:, ls] * gmf + product(masked(bwd_ref, q, mask), right)
        two = jnp.concatenate([before_ref[:, ls], gated], axis=1)
        flipped = jnp.dot(flip, two, preferred_element_type=F32).astype(BF16)
        left = join(flipped[:, :LANES], flipped[:, LANES:])
        turned = gmf.T.astype(BF16)
        spread = []
        for g in range(PER):
            pieces = [jnp.zeros((GS, K), BF16)] * PER
            pieces[g] = turned[g * GS : (g + 1) * GS]
            spread.append(join(*pieces))
        cross = jnp.dot(left, jnp.concatenate(spread, axis=1), preferred_element_type=F32)
        lines = []
        for g in range(PER):
            gs = slice(g * K, (g + 1) * K)
            square = jnp.where(near, cross[K:, gs], jnp.where(far, cross[:K, gs], 0.0))
            square = pltpu.roll(square, 1, 1, stride=1, stride_axis=0)
            lines.append(jnp.sum(square, axis=0, keepdims=True))
        stats_ref[pl.ds(pl.multiple_of(q * PER, PER), PER), :] = join(*lines)
        q_ext = join(rim_of(came_ref, Q_LAST, ls), q_ref[:, ls].astype(F32))
        cols_ref[:, ls] = tap_lines(gq_ref[:, ls].astype(F32), q_ext, pos_row)
        k_ext = join(rim_of(came_ref, K_LAST, ls), k_ref[:, ls].astype(F32))
        v_ext = join(rim_of(came_ref, V_LAST, ls), v_ref[:, ls].astype(F32))
        ks_ref[:, ls] = causal(k_ext, tap_rows(taps_ref, 1, ls), pos_row)
        vs_ref[:, ls] = causal(v_ext, tap_rows(taps_ref, 2, ls), pos_row)

    each_chunk(cot_ref.shape[1], body, 2)


def gate_kernel(
    len_ref, part_ref, after_ref, bwd_ref, ks_ref, vs_ref, gq_ref, k_ref, v_ref, came_ref,
    stats_ref, qcols_ref, gks_ref, gvs_ref, tails_ref, packed_ref, cols_ref,
):
    channels = part_ref.shape[1]
    kept = stats_ref.shape[0]
    row = iota((K, LANES), 0)
    col = iota((K, LANES), 1)
    pos_row = positions(len_ref, first_row() + row)
    pos = positions(len_ref, first_row() + K + col)
    mask = as_mask((col < row) & (pos >= col - row + K))
    own = owners()

    def body(q):
        ls = lanes_of(q)
        right = per_group(after_ref[:, ls], own)
        grad = part_ref[:, ls] + product(masked(bwd_ref, q, mask), right)
        gks = (grad * vs_ref[:, ls]).astype(BF16)
        gvs = (grad * ks_ref[:, ls]).astype(BF16)
        gks_ref[:, ls] = gks
        gvs_ref[:, ls] = gvs
        heads = (rim_of(gq_ref, 0, ls), gks.astype(F32)[:RIM], gvs.astype(F32)[:RIM])
        tails_ref[:, ls] = join(*heads, jnp.zeros((RIM, LANES), F32)).astype(BF16)
        k_ext = join(rim_of(came_ref, K_LAST, ls), k_ref[:, ls].astype(F32))
        v_ext = join(rim_of(came_ref, V_LAST, ls), v_ref[:, ls].astype(F32))
        cols_ref[0:8, ls] = qcols_ref[:, ls]
        cols_ref[8:16, ls] = tap_lines(gks.astype(F32), k_ext, pos_row)
        cols_ref[16:24, ls] = tap_lines(gvs.astype(F32), v_ext, pos_row)

    each_chunk(channels, body)
    packed_ref[0:kept] = stats_ref[...]
    packed_ref[kept:] = group_sums(cols_ref[...])


def back_short(which, pos, ls, taps_ref, grad_ref, tails_ref):
    ext = join(grad_ref[:, ls].astype(F32), rim_of(tails_ref, which * RIM, ls))
    taps = tap_rows(taps_ref, which, ls)
    grad = taps[0] * ext[:K]
    for j in range(1, KS):
        held = jnp.where(pos >= j, ext, 0.0)
        grad = grad + taps[j] * held[j : j + K]
    return grad.astype(BF16)


def main_qk_kernel(len_ref, taps_ref, tails_ref, gq_ref, gks_ref, oq_ref, ok_ref):
    pos = positions(len_ref, first_row() + iota((K + RIM, LANES), 0))

    def body(q):
        ls = lanes_of(q)
        oq_ref[:, ls] = back_short(0, pos, ls, taps_ref, gq_ref, tails_ref)
        ok_ref[:, ls] = back_short(1, pos, ls, taps_ref, gks_ref, tails_ref)

    each_chunk(gq_ref.shape[1], body)


def main_v_kernel(
    total, len_ref, taps_ref, tails_ref, gvs_ref, summed_ref, gain_ref, sums_ref, ov_ref, normed_ref
):
    pos = positions(len_ref, first_row() + iota((K + RIM, LANES), 0))
    inverse = inverse_of(sums_ref, total)

    def body(q):
        ls = lanes_of(q)
        normed_ref[:, ls] = (gain_ref[:, ls] * summed_ref[:, ls] * inverse).astype(BF16)
        ov_ref[:, ls] = back_short(2, pos, ls, taps_ref, gvs_ref, tails_ref)

    each_chunk(gvs_ref.shape[1], body)


def unpack_kernel(one_ref, two_ref, short_ref, long_ref, skip_ref, gain_ref):
    groups = long_ref.shape[0]
    rows = groups // PER
    total = one_ref[...] + two_ref[...]
    long_ref[...] = total[:groups]
    skip_ref[...] = total[groups : groups + rows]
    gain_ref[...] = total[groups + rows : groups + 2 * rows]
    for i in range(3):
        at = groups + 2 * rows + i * 8
        short_ref[i] = total[at : at + KS, :groups]


def shards(
    q_input, k_input, v_input, resid, lengths, short_filter, long_filter, skip, gain, cotangent
):
    length, channels = q_input.shape
    groups = channels // GS
    wide = channels * lax.axis_size("tp")
    rows = groups // PER
    packed_rows = groups + 2 * rows + 24

    def arr(shape, dtype):
        return jax.ShapeDtypeStruct(shape, dtype)

    smem = pl.BlockSpec(memory_space=pltpu.SMEM)
    vmem = pl.BlockSpec(memory_space=pltpu.VMEM)
    far_off = pl.BlockSpec(memory_space=pltpu.HBM)
    full_bf = arr((length, channels), BF16)
    full_f = arr((length, channels), F32)

    def call(name, kernel, outs, ins, scratch=(), flops=10**8, moved=10**6, grant=8, hbm=False):
        scalar = ins[0] is lengths
        return pl.pallas_call(
            kernel,
            out_shape=outs,
            in_specs=[far_off] * len(ins)
            if hbm
            else [smem if (i == 0 and scalar) else vmem for i in range(len(ins))],
            out_specs=[vmem] * len(outs),
            scratch_shapes=scratch,
            compiler_params=pltpu.CompilerParams(vmem_limit_bytes=grant * 1024 * 1024),
            cost_estimate=pl.CostEstimate(flops=flops, bytes_accessed=moved, transcendentals=0),
            name=name,
        )(*ins)

    skip2 = skip.reshape(1, channels)
    gain2 = gain.reshape(1, channels)
    taps, sent, far = call(
        "first", first_kernel,
        [arr((24, channels), F32), arr((SENT, channels), BF16), arr((2 * RIM, channels), BF16)],
        [lengths, jnp.transpose(short_filter, (0, 2, 1)), q_input, k_input, v_input],
        [
            pltpu.SMEM(lengths.shape, jnp.int32), pltpu.VMEM((3, KS, groups), BF16),
            pltpu.VMEM((PACK, channels), BF16), pltpu.VMEM((length, channels), BF16),
            pltpu.VMEM((length, channels), BF16), pltpu.SemaphoreType.DMA((5,)),
        ],
        grant=60,
        hbm=True,
    )
    came = shifted(sent, "ctx", 1)
    came_far = shifted(far, "ctx", 2)

    def circulants(filt, turned):
        return call(
            "circulants", functools.partial(circulant_kernel, turned),
            [arr((K, groups * K), BF16)], [filt], [pltpu.VMEM((groups, K), F32)],
            flops=10**9, moved=4 * 10**6,
        )[0]

    filt, filt2, sent = lax.optimization_barrier((long_filter, long_filter, sent))
    fwd = circulants(filt, True)
    bulk, part, top = call(
        "current", current_kernel, [full_f, full_f, full_bf],
        [lengths, q_input, taps, sent, fwd, skip2], flops=10**9, moved=5 * 10**6,
    )
    bwd = circulants(filt2, False)
    came, bwd = lax.optimization_barrier((came, bwd))
    q_short, gated, before, mixed, summed, sums = call(
        "summed", summed_kernel,
        [full_f, full_bf, full_bf, full_f, full_f, arr((2, K), F32)],
        [
            lengths, came, came_far, q_input, k_input, v_input, taps, sent, fwd, top,
            bulk, part, skip2, resid, cotangent, gain2,
        ],
        [pltpu.VMEM((2, K, LANES), F32)], flops=10**9, moved=5 * 10**6,
    )
    step = 1
    while step < lax.axis_size("tp"):
        sums = sums + swapped(sums, "tp", step)
        step *= 2
    grad_mixed, grad_qs = call(
        "grads", functools.partial(grads_kernel, wide), [full_bf, full_bf],
        [summed, mixed, q_short, cotangent, gain2, sums],
    )
    after = shifted(grad_mixed, "ctx", -1, wrap=False)
    stats, part, qcols, k_short, v_short = call(
        "beside", functools.partial(beside_kernel, wide),
        [
            arr((groups + 2 * rows, LANES), F32), full_f, arr((8, channels), F32),
            full_f, full_f,
        ],
        [
            lengths, summed, cotangent, sums, grad_mixed, grad_qs, gated, before, bwd,
            skip2, q_input, k_input, v_input, came, taps,
        ],
        flops=4 * 10**9, moved=5 * 10**6,
    )
    grad_ks, grad_vs, tails, packed = call(
        "gate", gate_kernel,
        [
            full_bf, full_bf, arr((4 * RIM, channels), BF16),
            arr((packed_rows, LANES), F32),
        ],
        [
            lengths, part, after, bwd, k_short, v_short, grad_qs, k_input, v_input, came,
            stats, qcols,
        ],
        [pltpu.VMEM((24, channels), F32)], flops=10**9, moved=5 * 10**6,
    )
    tails = shifted(tails, "ctx", -1)
    grad_q, grad_k = call(
        "main_qk", main_qk_kernel, [full_bf] * 2, [lengths, taps, tails, grad_qs, grad_ks],
        flops=10**9, moved=5 * 10**6,
    )
    count = lax.axis_size("ctx")
    step = 1
    while 2 * step < count:
        packed = packed + swapped(packed, "ctx", step)
        step *= 2
    packed, grad_q, grad_k, grad_vs = lax.optimization_barrier((packed, grad_q, grad_k, grad_vs))
    grad_v, normed = call(
        "main_v", functools.partial(main_v_kernel, wide), [full_bf] * 2,
        [lengths, taps, tails, grad_vs, summed, gain2, sums], flops=10**9, moved=5 * 10**6,
    )
    other = swapped(packed, "ctx", step)
    grad_short, grad_long, grad_skip, grad_gain = call(
        "unpack", unpack_kernel,
        [
            arr((3, KS, groups), F32), arr((groups, K), F32),
            arr((rows, LANES), F32), arr((rows, LANES), F32),
        ],
        [packed, other],
    )
    return (
        normed, grad_q, grad_k, grad_v, jnp.transpose(grad_short, (0, 2, 1)), grad_long,
        grad_skip.reshape(channels), grad_gain.reshape(channels),
    )


def solution(mesh):
    tiled = P("ctx", "tp")
    return jax.shard_map(
        shards,
        mesh=mesh,
        in_specs=(
            tiled, tiled, tiled, tiled, P(), P(None, "tp", None), P("tp", None), P("tp"), P("tp"),
            tiled,
        ),
        out_specs=(
            tiled, tiled, tiled, tiled, P(None, "tp", None), P("tp", None), P("tp"), P("tp"),
        ),
        check_vma=False,
    )
```

```python
import functools

import jax
import jax.numpy as jnp
from jax import lax
from jax.experimental import pallas as pl
from jax.experimental.pallas import tpu as pltpu
from jax.sharding import PartitionSpec as P

GS = 16
K = 128
KS = 7
LANES = 128
PER = LANES // GS
RIM = 8
PACK = 16
EPS = 1e-06
F32 = jnp.float32
BF16 = jnp.bfloat16


def shifted(x, axis, by, wrap=True):
    count = lax.axis_size(axis)
    pairs = [(i, (i + by) % count) for i in range(count)]
    return lax.ppermute(x, axis, [p for p in pairs if wrap or p[1] - p[0] == by])


def swapped(x, axis, step):
    return lax.ppermute(x, axis, [(i, i ^ step) for i in range(lax.axis_size(axis))])


def iota(shape, dim):
    return lax.broadcasted_iota(jnp.int32, shape, dim)


def positions(len_ref, rows):
    begin = jnp.zeros_like(rows)
    start = jnp.int32(0)
    for n in range(len_ref.shape[0]):
        begin = jnp.where(rows >= start, start, begin)
        start = start + len_ref[n]
    return jnp.where(rows < start, rows - begin, -1)


def first_row():
    return lax.axis_index("ctx") * K


def lanes_of(q):
    return pl.ds(pl.multiple_of(q * LANES, LANES), LANES)


def each_chunk(channels, body, unroll=4):
    def step(q, carry):
        body(q)
        return carry

    lax.fori_loop(0, channels // LANES, step, 0, unroll=unroll)


def as_mask(cond):
    return jnp.where(cond, 1.0, 0.0).astype(BF16)


def join(*parts):
    return jnp.concatenate(parts, axis=0)


def tap_rows(taps_ref, which, ls):
    table = taps_ref[which * 8 : which * 8 + 8, ls]
    return [table[j : j + 1, :] for j in range(KS)]


def follows(len_ref, start, count):
    pos = positions(len_ref, start + iota((count, LANES), 0))
    return jnp.where(pos >= 1, 1.0, 0.0)


def moved_on(x, after):
    return pltpu.roll(x, 1, 0) * after


def causal(ext, taps, after):
    total = taps[0] * ext[RIM:]
    for j in range(1, KS):
        ext = moved_on(ext, after)
        total = total + taps[j] * ext[RIM:]
    return total


def tap_lines(grad, ext, after):
    lines = [jnp.sum(grad * ext[RIM:], axis=0, keepdims=True)]
    for j in range(1, KS):
        ext = moved_on(ext, after)
        lines.append(jnp.sum(grad * ext[RIM:], axis=0, keepdims=True))
    lines.append(jnp.zeros((8 - KS, LANES), F32))
    return join(*lines)


def owners():
    lane = iota((K, LANES), 1) // GS
    return [as_mask(lane == g) for g in range(PER)]


def per_group(right, own):
    return join(*[right * mask for mask in own])


def masked(table_ref, q, mask):
    table = table_ref[:, pl.ds(pl.multiple_of(q * PER * K, PER * K), PER * K)]
    return [table[:, g * K : (g + 1) * K] * mask for g in range(PER)]


def product(left, right):
    return jnp.dot(jnp.concatenate(left, axis=1), right, preferred_element_type=F32)


K_FIRST, Q_LAST, K_LAST, V_LAST, V_FIRST, SENT = 0, K, K + 8, K + 16, K + 24, K + 32


def rim_of(ref, at, ls):
    base = at // PACK * PACK
    return ref[base : base + PACK, ls].astype(F32)[at - base : at - base + RIM]


def first_kernel(
    len_hbm, short_hbm, q_hbm, k_hbm, v_hbm, taps_ref, sent_ref, far_ref,
    len_ref, short_ref, q_ref, k_ref, v_ref, sems,
):
    groups = short_ref.shape[2]
    channels = taps_ref.shape[1]
    pairs = (
        (short_hbm, short_ref), (len_hbm, len_ref), (k_hbm, k_ref), (v_hbm, v_ref),
        (q_hbm.at[K - PACK : K], q_ref),
    )
    copies = [pltpu.make_async_copy(a, b, sems.at[i]) for i, (a, b) in enumerate(pairs)]
    for copy in copies:
        copy.start()
    spread = as_mask(iota((groups, channels), 1) // GS == iota((groups, channels), 0))
    copies[0].wait()
    for i in range(3):
        taps_ref[i * 8 : i * 8 + KS] = jnp.dot(
            short_ref[i], spread, preferred_element_type=F32
        )
        taps_ref[i * 8 + KS : i * 8 + 8] = jnp.zeros((8 - KS, channels), F32)
    for copy in copies[1:]:
        copy.wait()
    after = follows(len_ref, first_row(), K)

    def body(q):
        ls = lanes_of(q)
        kx = k_ref[:, ls].astype(F32)
        vx = v_ref[:, ls].astype(F32)
        ks = causal(kx, tap_rows(taps_ref, 1, ls), after)
        vs = causal(vx, tap_rows(taps_ref, 2, ls), after)
        sent_ref[:K, ls] = join(kx[:RIM], ks * vs).astype(BF16)
        q_end = q_ref[:, ls].astype(F32)[PACK - RIM :]
        k_end = kx[K - RIM :]
        v_end = vx[K - RIM :]
        sent_ref[K:, ls] = join(q_end, k_end, v_end, vx[:RIM]).astype(BF16)
        far_ref[:, ls] = join(k_end, v_end).astype(BF16)

    each_chunk(channels, body)


def circulant_kernel(turned, long_ref, out_ref, line_ref):
    groups = long_ref.shape[0]
    filt = long_ref[...]
    if turned:
        flip = as_mask((iota((K, K), 0) + iota((K, K), 1)) % K == 0)
        line_ref[...] = jnp.dot(filt, flip, preferred_element_type=F32)
    else:
        line_ref[...] = filt.astype(F32)

    def step(g, carry):
        row = jnp.broadcast_to(line_ref[pl.ds(g, 1), :], (GS, K))
        block = pltpu.roll(row, 0, 1, stride=1, stride_axis=0)
        for i in range(K // GS):
            moved = block if i == 0 else pltpu.roll(block, i * GS, 1)
            at = pl.ds(pl.multiple_of(g * K, K), K)
            out_ref[i * GS : (i + 1) * GS, at] = moved.astype(BF16)
        return carry

    lax.fori_loop(0, groups, step, 0, unroll=8)


def current_kernel(
    len_ref, q_ref, taps_ref, sent_ref, fwd_ref, skip_ref, qs_ref, part_ref, top_ref
):
    row = iota((K, LANES), 0)
    col = iota((K, LANES), 1)
    pos = positions(len_ref, first_row() + row)
    near = (col <= row) & (pos >= row - col)
    mask = as_mask(near)
    mask_top = as_mask(near & (col < RIM))
    picks = join(*[as_mask((col == row + g * GS) & (row < GS)) for g in range(PER)])
    own = owners()
    top = jnp.zeros((RIM, LANES), F32)
    after = follows(len_ref, first_row(), K)

    def body(q):
        ls = lanes_of(q)
        qs_ref[RIM:, ls] = causal(q_ref[:, ls].astype(F32), tap_rows(taps_ref, 0, ls), after)
        qs_ref[:RIM, ls] = top
        gated = join(top, sent_ref[:K, ls].astype(F32)[RIM:])
        rest = product(masked(fwd_ref, q, mask), per_group(gated.astype(BF16), own))
        part_ref[:, ls] = rest + skip_ref[:, ls] * gated
        top_ref[:, ls] = product(masked(fwd_ref, q, mask_top), picks).astype(BF16)

    each_chunk(q_ref.shape[1], body)


def summed_kernel(
    len_ref, came_ref, far_ref, q_ref, k_ref, v_ref, taps_ref, sent_ref, fwd_ref, top_ref,
    bulk_ref, part_ref, skip_ref, resid_ref, cot_ref, gain_ref,
    qs_ref, gated_ref, before_ref, mixed_ref, summed_ref, sums_ref, acc_ref,
):
    row = iota((K, LANES), 0)
    col = iota((K, LANES), 1)
    pos = positions(len_ref, first_row() + row)
    mask = as_mask((col > row) & (pos >= row - col + K))
    after = follows(len_ref, first_row() - RIM, 2 * RIM)
    after_far = follows(len_ref, first_row() - K - RIM, 2 * RIM)
    own = owners()
    own_top = [
        as_mask((iota((PACK, LANES), 1) // GS == g) & (iota((PACK, LANES), 0) < RIM))
        for g in range(PER)
    ]
    acc_ref[...] = jnp.zeros_like(acc_ref)

    def body(q):
        ls = lanes_of(q)
        kt = tap_rows(taps_ref, 1, ls)
        vt = tap_rows(taps_ref, 2, ls)
        k_last = rim_of(came_ref, K_LAST, ls)
        v_last = rim_of(came_ref, V_LAST, ls)
        top = causal(join(k_last, rim_of(k_ref, 0, ls)), kt, after) * causal(
            join(v_last, rim_of(v_ref, 0, ls)), vt, after
        )
        far_top = causal(
            join(rim_of(far_ref, 0, ls), rim_of(came_ref, K_FIRST, ls)), kt, after_far
        ) * causal(join(rim_of(far_ref, RIM, ls), rim_of(came_ref, V_FIRST, ls)), vt, after_far)
        qs_top = causal(
            join(rim_of(came_ref, Q_LAST, ls), rim_of(q_ref, 0, ls)), tap_rows(taps_ref, 0, ls), after
        )
        before = join(far_top, came_ref[:K, ls].astype(F32)[RIM:]).astype(BF16)
        gated = join(top, sent_ref[:K, ls].astype(F32)[RIM:]).astype(BF16)
        before_ref[:, ls] = before
        gated_ref[:, ls] = gated
        qs = join(qs_top, bulk_ref[RIM:, ls])
        qs_ref[:, ls] = qs
        first = gated[:PACK]
        left = masked(fwd_ref, q, mask) + [top_ref[:, ls]]
        right = join(per_group(before, own), per_group(first, own_top))
        direct = skip_ref[:, ls] * first.astype(F32)[:RIM]
        mixed = part_ref[:, ls] + product(left, right)
        mixed = join(mixed[:RIM] + direct, mixed[RIM:])
        summed = resid_ref[:, ls].astype(F32) + qs * mixed
        mixed_ref[:, ls] = mixed
        summed_ref[:, ls] = summed
        acc_ref[0] += summed * summed
        acc_ref[1] += gain_ref[:, ls] * cot_ref[:, ls].astype(F32) * summed

    each_chunk(resid_ref.shape[1], body)
    for i in range(2):
        sums_ref[i : i + 1] = jnp.sum(acc_ref[i].T, axis=0, keepdims=True)


def group_sums(cols):
    count, channels = cols.shape
    gather = as_mask(iota((channels, LANES), 0) // GS == iota((channels, LANES), 1))
    high = cols.astype(BF16)
    rest = cols - high.astype(F32)
    mid = rest.astype(BF16)
    low = (rest - mid.astype(F32)).astype(BF16)
    parts = join(high.astype(F32), mid.astype(F32), low.astype(F32)).astype(BF16)
    sums = jnp.dot(parts, gather, preferred_element_type=F32)
    return sums[:count] + sums[count : 2 * count] + sums[2 * count :]


def by_row(line):
    return jnp.broadcast_to(line, (K, K)).T


def inverse_of(sums_ref, total):
    return by_row(lax.rsqrt(sums_ref[0:1] / total + EPS))


def gates_kernel(len_ref, k_ref, v_ref, came_ref, taps_ref, ks_ref, vs_ref):
    after = follows(len_ref, first_row() - RIM, K + RIM)

    def body(q):
        ls = lanes_of(q)
        k_ext = join(rim_of(came_ref, K_LAST, ls), k_ref[:, ls].astype(F32))
        v_ext = join(rim_of(came_ref, V_LAST, ls), v_ref[:, ls].astype(F32))
        ks_ref[:, ls] = causal(k_ext, tap_rows(taps_ref, 1, ls), after)
        vs_ref[:, ls] = causal(v_ext, tap_rows(taps_ref, 2, ls), after)

    each_chunk(k_ref.shape[1], body)


def grads_kernel(total, summed_ref, mixed_ref, qs_ref, cot_ref, gain_ref, sums_ref, gm_ref, gq_ref):
    inverse = inverse_of(sums_ref, total)
    scale = inverse * inverse * by_row(sums_ref[1:2] / total)

    def body(q):
        ls = lanes_of(q)
        scaled = gain_ref[:, ls] * cot_ref[:, ls].astype(F32)
        grad_sum = inverse * (scaled - summed_ref[:, ls] * scale)
        gm_ref[:, ls] = (grad_sum * qs_ref[:, ls]).astype(BF16)
        gq_ref[:, ls] = (grad_sum * mixed_ref[:, ls]).astype(BF16)

    each_chunk(cot_ref.shape[1], body)


def beside_kernel(
    total, len_ref, summed_ref, cot_ref, sums_ref, gm_ref, gq_ref, gated_ref, before_ref,
    bwd_ref, skip_ref, q_ref, came_ref, stats_ref, part_ref, cols_ref,
):
    groups = bwd_ref.shape[1] // K
    inverse = inverse_of(sums_ref, total)
    row = iota((K, LANES), 0)
    col = iota((K, LANES), 1)
    after = follows(len_ref, first_row() - RIM, K + RIM)
    pos = positions(len_ref, first_row() + col)
    mask = as_mask((col >= row) & (pos >= col - row))
    source = K - 1 - row
    near = (col >= source) & (pos >= col - source)
    far = (col < source) & (pos >= col - source + K)
    flip = as_mask(row + col == K - 1)
    own = owners()

    def body(q):
        ls = lanes_of(q)
        summed = summed_ref[:, ls]
        gm = gm_ref[:, ls]
        gmf = gm.astype(F32)
        gated = gated_ref[:, ls]
        stats_ref[pl.ds(groups + q, 1), :] = jnp.sum(gmf * gated.astype(F32), axis=0, keepdims=True)
        stats_ref[pl.ds(groups + groups // PER + q, 1), :] = jnp.sum(
            cot_ref[:, ls].astype(F32) * summed * inverse, axis=0, keepdims=True
        )
        right = per_group(gm, own)
        part_ref[:, ls] = skip_ref[:, ls] * gmf + product(masked(bwd_ref, q, mask), right)
        two = jnp.concatenate([before_ref[:, ls], gated], axis=1)
        flipped = jnp.dot(flip, two, preferred_element_type=F32).astype(BF16)
        left = join(flipped[:, :LANES], flipped[:, LANES:])
        turned = gmf.T.astype(BF16)
        spread = []
        for g in range(PER):
            pieces = [jnp.zeros((GS, K), BF16)] * PER
            pieces[g] = turned[g * GS : (g + 1) * GS]
            spread.append(join(*pieces))
        cross = jnp.dot(left, jnp.concatenate(spread, axis=1), preferred_element_type=F32)
        lines = []
        for g in range(PER):
            gs = slice(g * K, (g + 1) * K)
            square = jnp.where(near, cross[K:, gs], jnp.where(far, cross[:K, gs], 0.0))
            square = pltpu.roll(square, 1, 1, stride=1, stride_axis=0)
            lines.append(jnp.sum(square, axis=0, keepdims=True))
        stats_ref[pl.ds(pl.multiple_of(q * PER, PER), PER), :] = join(*lines)
        q_ext = join(rim_of(came_ref, Q_LAST, ls), q_ref[:, ls].astype(F32))
        cols_ref[:, ls] = tap_lines(gq_ref[:, ls].astype(F32), q_ext, after)

    each_chunk(cot_ref.shape[1], body, 2)


def gate_kernel(
    len_ref, part_ref, after_ref, bwd_ref, ks_ref, vs_ref, gq_ref, k_ref, v_ref, came_ref,
    stats_ref, qcols_ref, gks_ref, gvs_ref, tails_ref, packed_ref, cols_ref,
):
    channels = part_ref.shape[1]
    kept = stats_ref.shape[0]
    row = iota((K, LANES), 0)
    col = iota((K, LANES), 1)
    after = follows(len_ref, first_row() - RIM, K + RIM)
    pos = positions(len_ref, first_row() + K + col)
    mask = as_mask((col < row) & (pos >= col - row + K))
    own = owners()

    def body(q):
        ls = lanes_of(q)
        right = per_group(after_ref[:, ls], own)
        grad = part_ref[:, ls] + product(masked(bwd_ref, q, mask), right)
        gks = (grad * vs_ref[:, ls]).astype(BF16)
        gvs = (grad * ks_ref[:, ls]).astype(BF16)
        gks_ref[:, ls] = gks
        gvs_ref[:, ls] = gvs
        heads = (rim_of(gq_ref, 0, ls), gks.astype(F32)[:RIM], gvs.astype(F32)[:RIM])
        tails_ref[:, ls] = join(*heads, jnp.zeros((RIM, LANES), F32)).astype(BF16)
        k_ext = join(rim_of(came_ref, K_LAST, ls), k_ref[:, ls].astype(F32))
        v_ext = join(rim_of(came_ref, V_LAST, ls), v_ref[:, ls].astype(F32))
        cols_ref[0:8, ls] = qcols_ref[:, ls]
        cols_ref[8:16, ls] = tap_lines(gks.astype(F32), k_ext, after)
        cols_ref[16:24, ls] = tap_lines(gvs.astype(F32), v_ext, after)

    each_chunk(channels, body)
    packed_ref[0:kept] = stats_ref[...]
    packed_ref[kept:] = group_sums(cols_ref[...])


def back_short(which, after, ls, taps_ref, grad_ref, tails_ref):
    ext = join(grad_ref[:, ls].astype(F32), rim_of(tails_ref, which * RIM, ls))
    taps = tap_rows(taps_ref, which, ls)
    grad = taps[0] * ext[:K]
    for j in range(1, KS):
        ext = pltpu.roll(ext * after, K + RIM - 1, 0)
        grad = grad + taps[j] * ext[:K]
    return grad.astype(BF16)


def main_qk_kernel(len_ref, taps_ref, tails_ref, gq_ref, gks_ref, oq_ref, ok_ref):
    after = follows(len_ref, first_row(), K + RIM)

    def body(q):
        ls = lanes_of(q)
        oq_ref[:, ls] = back_short(0, after, ls, taps_ref, gq_ref, tails_ref)
        ok_ref[:, ls] = back_short(1, after, ls, taps_ref, gks_ref, tails_ref)

    each_chunk(gq_ref.shape[1], body)


def main_v_kernel(
    total, len_ref, taps_ref, tails_ref, gvs_ref, summed_ref, gain_ref, sums_ref, ov_ref, normed_ref
):
    after = follows(len_ref, first_row(), K + RIM)
    inverse = inverse_of(sums_ref, total)

    def body(q):
        ls = lanes_of(q)
        normed_ref[:, ls] = (gain_ref[:, ls] * summed_ref[:, ls] * inverse).astype(BF16)
        ov_ref[:, ls] = back_short(2, after, ls, taps_ref, gvs_ref, tails_ref)

    each_chunk(gvs_ref.shape[1], body)


def unpack_kernel(one_ref, two_ref, short_ref, long_ref, skip_ref, gain_ref):
    groups = long_ref.shape[0]
    rows = groups // PER
    total = one_ref[...] + two_ref[...]
    long_ref[...] = total[:groups]
    skip_ref[...] = total[groups : groups + rows]
    gain_ref[...] = total[groups + rows : groups + 2 * rows]
    for i in range(3):
        at = groups + 2 * rows + i * 8
        short_ref[i] = total[at : at + KS, :groups]


def shards(
    q_input, k_input, v_input, resid, lengths, short_filter, long_filter, skip, gain, cotangent
):
    length, channels = q_input.shape
    groups = channels // GS
    wide = channels * lax.axis_size("tp")
    rows = groups // PER
    packed_rows = groups + 2 * rows + 24

    def arr(shape, dtype):
        return jax.ShapeDtypeStruct(shape, dtype)

    smem = pl.BlockSpec(memory_space=pltpu.SMEM)
    vmem = pl.BlockSpec(memory_space=pltpu.VMEM)
    far_off = pl.BlockSpec(memory_space=pltpu.HBM)
    full_bf = arr((length, channels), BF16)
    full_f = arr((length, channels), F32)

    def call(name, kernel, outs, ins, scratch=(), flops=10**8, moved=10**6, grant=8, hbm=False):
        scalar = ins[0] is lengths
        return pl.pallas_call(
            kernel,
            out_shape=outs,
            in_specs=[far_off] * len(ins)
            if hbm
            else [smem if (i == 0 and scalar) else vmem for i in range(len(ins))],
            out_specs=[vmem] * len(outs),
            scratch_shapes=scratch,
            compiler_params=pltpu.CompilerParams(vmem_limit_bytes=grant * 1024 * 1024),
            cost_estimate=pl.CostEstimate(flops=flops, bytes_accessed=moved, transcendentals=0),
            name=name,
        )(*ins)

    skip2 = skip.reshape(1, channels)
    gain2 = gain.reshape(1, channels)
    taps, sent, far = call(
        "first", first_kernel,
        [arr((24, channels), F32), arr((SENT, channels), BF16), arr((2 * RIM, channels), BF16)],
        [lengths, jnp.transpose(short_filter, (0, 2, 1)), q_input, k_input, v_input],
        [
            pltpu.SMEM(lengths.shape, jnp.int32), pltpu.VMEM((3, KS, groups), BF16),
            pltpu.VMEM((PACK, channels), BF16), pltpu.VMEM((length, channels), BF16),
            pltpu.VMEM((length, channels), BF16), pltpu.SemaphoreType.DMA((5,)),
        ],
        grant=60,
        hbm=True,
    )
    came = shifted(sent, "ctx", 1)
    came_far = shifted(far, "ctx", 2)

    def circulants(filt, turned):
        return call(
            "circulants", functools.partial(circulant_kernel, turned),
            [arr((K, groups * K), BF16)], [filt], [pltpu.VMEM((groups, K), F32)],
            flops=10**9, moved=4 * 10**6,
        )[0]

    filt, filt2, sent = lax.optimization_barrier((long_filter, long_filter, sent))
    fwd = circulants(filt, True)
    bulk, part, top = call(
        "current", current_kernel, [full_f, full_f, full_bf],
        [lengths, q_input, taps, sent, fwd, skip2], flops=10**9, moved=5 * 10**6,
    )
    bwd = circulants(filt2, False)
    came, bwd = lax.optimization_barrier((came, bwd))
    q_short, gated, before, mixed, summed, sums = call(
        "summed", summed_kernel,
        [full_f, full_bf, full_bf, full_f, full_f, arr((2, K), F32)],
        [
            lengths, came, came_far, q_input, k_input, v_input, taps, sent, fwd, top,
            bulk, part, skip2, resid, cotangent, gain2,
        ],
        [pltpu.VMEM((2, K, LANES), F32)], flops=10**9, moved=5 * 10**6,
    )
    own_sums = sums
    step = 1
    while step < lax.axis_size("tp"):
        sums = sums + swapped(sums, "tp", step)
        step *= 2
    came, _ = lax.optimization_barrier((came, own_sums))
    k_short, v_short = call(
        "gates", gates_kernel, [full_f] * 2, [lengths, k_input, v_input, came, taps],
        flops=10**8, moved=2 * 10**6,
    )
    sums, k_short, v_short = lax.optimization_barrier((sums, k_short, v_short))
    grad_mixed, grad_qs = call(
        "grads", functools.partial(grads_kernel, wide), [full_bf, full_bf],
        [summed, mixed, q_short, cotangent, gain2, sums],
    )
    after = shifted(grad_mixed, "ctx", -1, wrap=False)
    stats, part, qcols = call(
        "beside", functools.partial(beside_kernel, wide),
        [
            arr((groups + 2 * rows, LANES), F32), full_f, arr((8, channels), F32),
        ],
        [
            lengths, summed, cotangent, sums, grad_mixed, grad_qs, gated, before, bwd,
            skip2, q_input, came,
        ],
        flops=4 * 10**9, moved=5 * 10**6,
    )
    grad_ks, grad_vs, tails, packed = call(
        "gate", gate_kernel,
        [
            full_bf, full_bf, arr((4 * RIM, channels), BF16),
            arr((packed_rows, LANES), F32),
        ],
        [
            lengths, part, after, bwd, k_short, v_short, grad_qs, k_input, v_input, came,
            stats, qcols,
        ],
        [pltpu.VMEM((24, channels), F32)], flops=10**9, moved=5 * 10**6,
    )
    tails = shifted(tails, "ctx", -1)
    grad_q, grad_k = call(
        "main_qk", main_qk_kernel, [full_bf] * 2, [lengths, taps, tails, grad_qs, grad_ks],
        flops=10**9, moved=5 * 10**6,
    )
    count = lax.axis_size("ctx")
    step = 1
    while 2 * step < count:
        packed = packed + swapped(packed, "ctx", step)
        step *= 2
    packed, grad_q, grad_k, grad_vs = lax.optimization_barrier((packed, grad_q, grad_k, grad_vs))
    grad_v, normed = call(
        "main_v", functools.partial(main_v_kernel, wide), [full_bf] * 2,
        [lengths, taps, tails, grad_vs, summed, gain2, sums], flops=10**9, moved=5 * 10**6,
    )
    other = swapped(packed, "ctx", step)
    grad_short, grad_long, grad_skip, grad_gain = call(
        "unpack", unpack_kernel,
        [
            arr((3, KS, groups), F32), arr((groups, K), F32),
            arr((rows, LANES), F32), arr((rows, LANES), F32),
        ],
        [packed, other],
    )
    return (
        normed, grad_q, grad_k, grad_v, jnp.transpose(grad_short, (0, 2, 1)), grad_long,
        grad_skip.reshape(channels), grad_gain.reshape(channels),
    )


def solution(mesh):
    tiled = P("ctx", "tp")
    return jax.shard_map(
        shards,
        mesh=mesh,
        in_specs=(
            tiled, tiled, tiled, tiled, P(), P(None, "tp", None), P("tp", None), P("tp"), P("tp"),
            tiled,
        ),
        out_specs=(
            tiled, tiled, tiled, tiled, P(None, "tp", None), P("tp", None), P("tp"), P("tp"),
        ),
        check_vma=False,
    )
```

```python
import functools

import jax
import jax.numpy as jnp
from jax import lax
from jax.experimental import pallas as pl
from jax.experimental.pallas import tpu as pltpu
from jax.sharding import PartitionSpec as P

GS = 16
K = 128
KS = 7
LANES = 128
PER = LANES // GS
RIM = 8
PACK = 16
EPS = 1e-06
F32 = jnp.float32
BF16 = jnp.bfloat16


def shifted(x, axis, by, wrap=True):
    count = lax.axis_size(axis)
    pairs = [(i, (i + by) % count) for i in range(count)]
    return lax.ppermute(x, axis, [p for p in pairs if wrap or p[1] - p[0] == by])


def swapped(x, axis, step):
    return lax.ppermute(x, axis, [(i, i ^ step) for i in range(lax.axis_size(axis))])


def iota(shape, dim):
    return lax.broadcasted_iota(jnp.int32, shape, dim)


def positions(len_ref, rows):
    begin = jnp.zeros_like(rows)
    start = jnp.int32(0)
    for n in range(len_ref.shape[0]):
        begin = jnp.where(rows >= start, start, begin)
        start = start + len_ref[n]
    return jnp.where(rows < start, rows - begin, -1)


def first_row():
    return lax.axis_index("ctx") * K


def lanes_of(q):
    return pl.ds(pl.multiple_of(q * LANES, LANES), LANES)


def each_chunk(channels, body, unroll=4):
    def step(q, carry):
        body(q)
        return carry

    lax.fori_loop(0, channels // LANES, step, 0, unroll=unroll)


def as_mask(cond):
    return jnp.where(cond, 1.0, 0.0).astype(BF16)


def join(*parts):
    return jnp.concatenate(parts, axis=0)


def tap_rows(taps_ref, which, ls):
    table = taps_ref[which * 8 : which * 8 + 8, ls]
    return [table[j : j + 1, :] for j in range(KS)]


def follows(len_ref, start, count):
    pos = positions(len_ref, start + iota((count, LANES), 0))
    return jnp.where(pos >= 1, 1.0, 0.0)


def moved_on(x, after):
    return pltpu.roll(x, 1, 0) * after


def causal(ext, taps, after):
    total = taps[0] * ext[RIM:]
    for j in range(1, KS):
        ext = moved_on(ext, after)
        total = total + taps[j] * ext[RIM:]
    return total


def tap_lines(grad, ext, after):
    lines = [jnp.sum(grad * ext[RIM:], axis=0, keepdims=True)]
    for j in range(1, KS):
        ext = moved_on(ext, after)
        lines.append(jnp.sum(grad * ext[RIM:], axis=0, keepdims=True))
    lines.append(jnp.zeros((8 - KS, LANES), F32))
    return join(*lines)


def owners():
    lane = iota((K, LANES), 1) // GS
    return [as_mask(lane == g) for g in range(PER)]


def per_group(right, own):
    return join(*[right * mask for mask in own])


def masked(table_ref, q, mask):
    table = table_ref[:, pl.ds(pl.multiple_of(q * PER * K, PER * K), PER * K)]
    return [table[:, g * K : (g + 1) * K] * mask for g in range(PER)]


def product(left, right):
    return jnp.dot(jnp.concatenate(left, axis=1), right, preferred_element_type=F32)


K_FIRST, Q_LAST, K_LAST, V_LAST, V_FIRST, SENT = 0, K, K + 8, K + 16, K + 24, K + 32


def rim_of(ref, at, ls):
    base = at // PACK * PACK
    return ref[base : base + PACK, ls].astype(F32)[at - base : at - base + RIM]


def first_kernel(
    len_hbm, short_hbm, q_hbm, k_hbm, v_hbm, taps_ref, sent_ref, far_ref,
    len_ref, short_ref, q_ref, k_ref, v_ref, sems,
):
    groups = short_ref.shape[2]
    channels = taps_ref.shape[1]
    pairs = (
        (short_hbm, short_ref), (len_hbm, len_ref), (k_hbm, k_ref), (v_hbm, v_ref),
        (q_hbm.at[K - PACK : K], q_ref),
    )
    copies = [pltpu.make_async_copy(a, b, sems.at[i]) for i, (a, b) in enumerate(pairs)]
    for copy in copies:
        copy.start()
    spread = as_mask(iota((groups, channels), 1) // GS == iota((groups, channels), 0))
    copies[0].wait()
    for i in range(3):
        taps_ref[i * 8 : i * 8 + KS] = jnp.dot(
            short_ref[i], spread, preferred_element_type=F32
        )
        taps_ref[i * 8 + KS : i * 8 + 8] = jnp.zeros((8 - KS, channels), F32)
    for copy in copies[1:]:
        copy.wait()
    after = follows(len_ref, first_row(), K)

    def body(q):
        ls = lanes_of(q)
        kx = k_ref[:, ls].astype(F32)
        vx = v_ref[:, ls].astype(F32)
        ks = causal(kx, tap_rows(taps_ref, 1, ls), after)
        vs = causal(vx, tap_rows(taps_ref, 2, ls), after)
        sent_ref[:K, ls] = join(kx[:RIM], ks * vs).astype(BF16)
        q_end = q_ref[:, ls].astype(F32)[PACK - RIM :]
        k_end = kx[K - RIM :]
        v_end = vx[K - RIM :]
        sent_ref[K:, ls] = join(q_end, k_end, v_end, vx[:RIM]).astype(BF16)
        far_ref[:, ls] = join(k_end, v_end).astype(BF16)

    each_chunk(channels, body)


def circulant_kernel(turned, long_ref, out_ref, line_ref):
    groups = long_ref.shape[0]
    filt = long_ref[...]
    if turned:
        flip = as_mask((iota((K, K), 0) + iota((K, K), 1)) % K == 0)
        line_ref[...] = jnp.dot(filt, flip, preferred_element_type=F32)
    else:
        line_ref[...] = filt.astype(F32)

    def step(g, carry):
        row = jnp.broadcast_to(line_ref[pl.ds(g, 1), :], (GS, K))
        block = pltpu.roll(row, 0, 1, stride=1, stride_axis=0)
        for i in range(K // GS):
            moved = block if i == 0 else pltpu.roll(block, i * GS, 1)
            at = pl.ds(pl.multiple_of(g * K, K), K)
            out_ref[i * GS : (i + 1) * GS, at] = moved.astype(BF16)
        return carry

    lax.fori_loop(0, groups, step, 0, unroll=8)


def current_kernel(
    len_ref, q_ref, taps_ref, sent_ref, fwd_ref, skip_ref, qs_ref, part_ref, top_ref
):
    row = iota((K, LANES), 0)
    col = iota((K, LANES), 1)
    pos = positions(len_ref, first_row() + row)
    near = (col <= row) & (pos >= row - col)
    mask = as_mask(near)
    mask_top = as_mask(near & (col < RIM))
    picks = join(*[as_mask((col == row + g * GS) & (row < GS)) for g in range(PER)])
    own = owners()
    top = jnp.zeros((RIM, LANES), F32)
    after = follows(len_ref, first_row(), K)

    def body(q):
        ls = lanes_of(q)
        qs_ref[RIM:, ls] = causal(q_ref[:, ls].astype(F32), tap_rows(taps_ref, 0, ls), after)
        qs_ref[:RIM, ls] = top
        gated = join(top, sent_ref[:K, ls].astype(F32)[RIM:])
        rest = product(masked(fwd_ref, q, mask), per_group(gated.astype(BF16), own))
        part_ref[:, ls] = rest + skip_ref[:, ls] * gated
        top_ref[:, ls] = product(masked(fwd_ref, q, mask_top), picks).astype(BF16)

    each_chunk(q_ref.shape[1], body)


def summed_kernel(
    len_ref, came_ref, far_ref, q_ref, k_ref, v_ref, taps_ref, sent_ref, fwd_ref, top_ref,
    bulk_ref, part_ref, skip_ref, resid_ref, cot_ref, gain_ref,
    qs_ref, gated_ref, before_ref, mixed_ref, summed_ref, sums_ref, acc_ref,
):
    row = iota((K, LANES), 0)
    col = iota((K, LANES), 1)
    pos = positions(len_ref, first_row() + row)
    mask = as_mask((col > row) & (pos >= row - col + K))
    after = follows(len_ref, first_row() - RIM, 2 * RIM)
    after_far = follows(len_ref, first_row() - K - RIM, 2 * RIM)
    own = owners()
    own_top = [
        as_mask((iota((PACK, LANES), 1) // GS == g) & (iota((PACK, LANES), 0) < RIM))
        for g in range(PER)
    ]
    acc_ref[...] = jnp.zeros_like(acc_ref)

    def body(q):
        ls = lanes_of(q)
        kt = tap_rows(taps_ref, 1, ls)
        vt = tap_rows(taps_ref, 2, ls)
        k_last = rim_of(came_ref, K_LAST, ls)
        v_last = rim_of(came_ref, V_LAST, ls)
        top = causal(join(k_last, rim_of(k_ref, 0, ls)), kt, after) * causal(
            join(v_last, rim_of(v_ref, 0, ls)), vt, after
        )
        far_top = causal(
            join(rim_of(far_ref, 0, ls), rim_of(came_ref, K_FIRST, ls)), kt, after_far
        ) * causal(join(rim_of(far_ref, RIM, ls), rim_of(came_ref, V_FIRST, ls)), vt, after_far)
        qs_top = causal(
            join(rim_of(came_ref, Q_LAST, ls), rim_of(q_ref, 0, ls)), tap_rows(taps_ref, 0, ls), after
        )
        before = join(far_top, came_ref[:K, ls].astype(F32)[RIM:]).astype(BF16)
        gated = join(top, sent_ref[:K, ls].astype(F32)[RIM:]).astype(BF16)
        before_ref[:, ls] = before
        gated_ref[:, ls] = gated
        qs = join(qs_top, bulk_ref[RIM:, ls])
        qs_ref[:, ls] = qs
        first = gated[:PACK]
        left = masked(fwd_ref, q, mask) + [top_ref[:, ls]]
        right = join(per_group(before, own), per_group(first, own_top))
        direct = skip_ref[:, ls] * first.astype(F32)[:RIM]
        mixed = part_ref[:, ls] + product(left, right)
        mixed = join(mixed[:RIM] + direct, mixed[RIM:])
        summed = resid_ref[:, ls].astype(F32) + qs * mixed
        mixed_ref[:, ls] = mixed
        summed_ref[:, ls] = summed
        acc_ref[0] += summed * summed
        acc_ref[1] += gain_ref[:, ls] * cot_ref[:, ls].astype(F32) * summed

    each_chunk(resid_ref.shape[1], body)
    for i in range(2):
        sums_ref[i : i + 1] = jnp.sum(acc_ref[i].T, axis=0, keepdims=True)


def group_sums(cols):
    count, channels = cols.shape
    gather = as_mask(iota((channels, LANES), 0) // GS == iota((channels, LANES), 1))
    high = cols.astype(BF16)
    rest = cols - high.astype(F32)
    mid = rest.astype(BF16)
    low = (rest - mid.astype(F32)).astype(BF16)
    parts = join(high.astype(F32), mid.astype(F32), low.astype(F32)).astype(BF16)
    sums = jnp.dot(parts, gather, preferred_element_type=F32)
    return sums[:count] + sums[count : 2 * count] + sums[2 * count :]


def by_row(line):
    return jnp.broadcast_to(line, (K, K)).T


def inverse_of(sums_ref, total):
    return by_row(lax.rsqrt(sums_ref[0:1] / total + EPS))


def gates_kernel(len_ref, k_ref, v_ref, came_ref, taps_ref, ks_ref, vs_ref):
    after = follows(len_ref, first_row() - RIM, K + RIM)

    def body(q):
        ls = lanes_of(q)
        k_ext = join(rim_of(came_ref, K_LAST, ls), k_ref[:, ls].astype(F32))
        v_ext = join(rim_of(came_ref, V_LAST, ls), v_ref[:, ls].astype(F32))
        ks_ref[:, ls] = causal(k_ext, tap_rows(taps_ref, 1, ls), after)
        vs_ref[:, ls] = causal(v_ext, tap_rows(taps_ref, 2, ls), after)

    each_chunk(k_ref.shape[1], body)


def grads_kernel(total, summed_ref, mixed_ref, qs_ref, cot_ref, gain_ref, sums_ref, gm_ref, gq_ref):
    inverse = inverse_of(sums_ref, total)
    scale = inverse * inverse * by_row(sums_ref[1:2] / total)

    def body(q):
        ls = lanes_of(q)
        scaled = gain_ref[:, ls] * cot_ref[:, ls].astype(F32)
        grad_sum = inverse * (scaled - summed_ref[:, ls] * scale)
        gm_ref[:, ls] = (grad_sum * qs_ref[:, ls]).astype(BF16)
        gq_ref[:, ls] = (grad_sum * mixed_ref[:, ls]).astype(BF16)

    each_chunk(cot_ref.shape[1], body)


def beside_kernel(
    total, len_ref, summed_ref, cot_ref, sums_ref, gm_ref, gq_ref, gated_ref, before_ref,
    bwd_ref, skip_ref, q_ref, came_ref, stats_ref, part_ref, cols_ref,
):
    groups = bwd_ref.shape[1] // K
    inverse = inverse_of(sums_ref, total)
    row = iota((K, LANES), 0)
    col = iota((K, LANES), 1)
    after = follows(len_ref, first_row() - RIM, K + RIM)
    pos = positions(len_ref, first_row() + col)
    mask = as_mask((col >= row) & (pos >= col - row))
    source = K - 1 - row
    near = (col >= source) & (pos >= col - source)
    far = (col < source) & (pos >= col - source + K)
    flip = as_mask(row + col == K - 1)
    own = owners()

    def body(q):
        ls = lanes_of(q)
        summed = summed_ref[:, ls]
        gm = gm_ref[:, ls]
        gmf = gm.astype(F32)
        gated = gated_ref[:, ls]
        stats_ref[pl.ds(groups + q, 1), :] = jnp.sum(gmf * gated.astype(F32), axis=0, keepdims=True)
        stats_ref[pl.ds(groups + groups // PER + q, 1), :] = jnp.sum(
            cot_ref[:, ls].astype(F32) * summed * inverse, axis=0, keepdims=True
        )
        right = per_group(gm, own)
        part_ref[:, ls] = skip_ref[:, ls] * gmf + product(masked(bwd_ref, q, mask), right)
        two = jnp.concatenate([before_ref[:, ls], gated], axis=1)
        flipped = jnp.dot(flip, two, preferred_element_type=F32).astype(BF16)
        left = join(flipped[:, :LANES], flipped[:, LANES:])
        turned = gmf.T.astype(BF16)
        spread = []
        for g in range(PER):
            pieces = [jnp.zeros((GS, K), BF16)] * PER
            pieces[g] = turned[g * GS : (g + 1) * GS]
            spread.append(join(*pieces))
        cross = jnp.dot(left, jnp.concatenate(spread, axis=1), preferred_element_type=F32)
        lines = []
        for g in range(PER):
            gs = slice(g * K, (g + 1) * K)
            square = jnp.where(near, cross[K:, gs], jnp.where(far, cross[:K, gs], 0.0))
            square = pltpu.roll(square, 1, 1, stride=1, stride_axis=0)
            lines.append(jnp.sum(square, axis=0, keepdims=True))
        stats_ref[pl.ds(pl.multiple_of(q * PER, PER), PER), :] = join(*lines)
        q_ext = join(rim_of(came_ref, Q_LAST, ls), q_ref[:, ls].astype(F32))
        cols_ref[:, ls] = tap_lines(gq_ref[:, ls].astype(F32), q_ext, after)

    each_chunk(cot_ref.shape[1], body, 4)


def gate_kernel(
    len_ref, part_ref, after_ref, bwd_ref, ks_ref, vs_ref, gq_ref, k_ref, v_ref, came_ref,
    stats_ref, qcols_ref, gks_ref, gvs_ref, tails_ref, packed_ref, cols_ref,
):
    channels = part_ref.shape[1]
    kept = stats_ref.shape[0]
    row = iota((K, LANES), 0)
    col = iota((K, LANES), 1)
    after = follows(len_ref, first_row() - RIM, K + RIM)
    pos = positions(len_ref, first_row() + K + col)
    mask = as_mask((col < row) & (pos >= col - row + K))
    own = owners()

    def body(q):
        ls = lanes_of(q)
        right = per_group(after_ref[:, ls], own)
        grad = part_ref[:, ls] + product(masked(bwd_ref, q, mask), right)
        gks = (grad * vs_ref[:, ls]).astype(BF16)
        gvs = (grad * ks_ref[:, ls]).astype(BF16)
        gks_ref[:, ls] = gks
        gvs_ref[:, ls] = gvs
        heads = (rim_of(gq_ref, 0, ls), gks.astype(F32)[:RIM], gvs.astype(F32)[:RIM])
        tails_ref[:, ls] = join(*heads, jnp.zeros((RIM, LANES), F32)).astype(BF16)
        k_ext = join(rim_of(came_ref, K_LAST, ls), k_ref[:, ls].astype(F32))
        v_ext = join(rim_of(came_ref, V_LAST, ls), v_ref[:, ls].astype(F32))
        cols_ref[0:8, ls] = qcols_ref[:, ls]
        cols_ref[8:16, ls] = tap_lines(gks.astype(F32), k_ext, after)
        cols_ref[16:24, ls] = tap_lines(gvs.astype(F32), v_ext, after)

    each_chunk(channels, body)
    packed_ref[0:kept] = stats_ref[...]
    packed_ref[kept:] = group_sums(cols_ref[...])


def back_short(which, after, ls, taps_ref, grad_ref, tails_ref):
    ext = join(grad_ref[:, ls].astype(F32), rim_of(tails_ref, which * RIM, ls))
    taps = tap_rows(taps_ref, which, ls)
    grad = taps[0] * ext[:K]
    for j in range(1, KS):
        ext = pltpu.roll(ext * after, K + RIM - 1, 0)
        grad = grad + taps[j] * ext[:K]
    return grad.astype(BF16)


def mains_kernel(len_ref, taps_ref, tails_ref, gq_ref, gks_ref, gvs_ref, oq_ref, ok_ref, ov_ref):
    after = follows(len_ref, first_row(), K + RIM)

    def body(q):
        ls = lanes_of(q)
        oq_ref[:, ls] = back_short(0, after, ls, taps_ref, gq_ref, tails_ref)
        ok_ref[:, ls] = back_short(1, after, ls, taps_ref, gks_ref, tails_ref)
        ov_ref[:, ls] = back_short(2, after, ls, taps_ref, gvs_ref, tails_ref)

    each_chunk(gq_ref.shape[1], body)


def normed_kernel(total, summed_ref, gain_ref, sums_ref, normed_ref):
    inverse = inverse_of(sums_ref, total)

    def body(q):
        ls = lanes_of(q)
        normed_ref[:, ls] = (gain_ref[:, ls] * summed_ref[:, ls] * inverse).astype(BF16)

    each_chunk(summed_ref.shape[1], body)


def unpack_kernel(one_ref, two_ref, short_ref, long_ref, skip_ref, gain_ref):
    groups = long_ref.shape[0]
    rows = groups // PER
    total = one_ref[...] + two_ref[...]
    long_ref[...] = total[:groups]
    skip_ref[...] = total[groups : groups + rows]
    gain_ref[...] = total[groups + rows : groups + 2 * rows]
    for i in range(3):
        at = groups + 2 * rows + i * 8
        short_ref[i] = total[at : at + KS, :groups]


def shards(
    q_input, k_input, v_input, resid, lengths, short_filter, long_filter, skip, gain, cotangent
):
    length, channels = q_input.shape
    groups = channels // GS
    wide = channels * lax.axis_size("tp")
    rows = groups // PER
    packed_rows = groups + 2 * rows + 24

    def arr(shape, dtype):
        return jax.ShapeDtypeStruct(shape, dtype)

    smem = pl.BlockSpec(memory_space=pltpu.SMEM)
    vmem = pl.BlockSpec(memory_space=pltpu.VMEM)
    far_off = pl.BlockSpec(memory_space=pltpu.HBM)
    full_bf = arr((length, channels), BF16)
    full_f = arr((length, channels), F32)

    def call(name, kernel, outs, ins, scratch=(), flops=10**8, moved=10**6, grant=8, hbm=False):
        scalar = ins[0] is lengths
        return pl.pallas_call(
            kernel,
            out_shape=outs,
            in_specs=[far_off] * len(ins)
            if hbm
            else [smem if (i == 0 and scalar) else vmem for i in range(len(ins))],
            out_specs=[vmem] * len(outs),
            scratch_shapes=scratch,
            compiler_params=pltpu.CompilerParams(vmem_limit_bytes=grant * 1024 * 1024),
            cost_estimate=pl.CostEstimate(flops=flops, bytes_accessed=moved, transcendentals=0),
            name=name,
        )(*ins)

    skip2 = skip.reshape(1, channels)
    gain2 = gain.reshape(1, channels)
    taps, sent, far = call(
        "first", first_kernel,
        [arr((24, channels), F32), arr((SENT, channels), BF16), arr((2 * RIM, channels), BF16)],
        [lengths, jnp.transpose(short_filter, (0, 2, 1)), q_input, k_input, v_input],
        [
            pltpu.SMEM(lengths.shape, jnp.int32), pltpu.VMEM((3, KS, groups), BF16),
            pltpu.VMEM((PACK, channels), BF16), pltpu.VMEM((length, channels), BF16),
            pltpu.VMEM((length, channels), BF16), pltpu.SemaphoreType.DMA((5,)),
        ],
        grant=60,
        hbm=True,
    )
    came = shifted(sent, "ctx", 1)
    came_far = shifted(far, "ctx", 2)

    def circulants(filt, turned):
        return call(
            "circulants", functools.partial(circulant_kernel, turned),
            [arr((K, groups * K), BF16)], [filt], [pltpu.VMEM((groups, K), F32)],
            flops=10**9, moved=4 * 10**6,
        )[0]

    filt, filt2, sent = lax.optimization_barrier((long_filter, long_filter, sent))
    fwd = circulants(filt, True)
    bulk, part, top = call(
        "current", current_kernel, [full_f, full_f, full_bf],
        [lengths, q_input, taps, sent, fwd, skip2], flops=10**9, moved=5 * 10**6,
    )
    bwd = circulants(filt2, False)
    came, bwd = lax.optimization_barrier((came, bwd))
    q_short, gated, before, mixed, summed, sums = call(
        "summed", summed_kernel,
        [full_f, full_bf, full_bf, full_f, full_f, arr((2, K), F32)],
        [
            lengths, came, came_far, q_input, k_input, v_input, taps, sent, fwd, top,
            bulk, part, skip2, resid, cotangent, gain2,
        ],
        [pltpu.VMEM((2, K, LANES), F32)], flops=10**9, moved=5 * 10**6,
    )
    own_sums = sums
    step = 1
    while step < lax.axis_size("tp"):
        sums = sums + swapped(sums, "tp", step)
        step *= 2
    came, _ = lax.optimization_barrier((came, own_sums))
    k_short, v_short = call(
        "gates", gates_kernel, [full_f] * 2, [lengths, k_input, v_input, came, taps],
        flops=10**8, moved=2 * 10**6,
    )
    sums, k_short, v_short = lax.optimization_barrier((sums, k_short, v_short))
    grad_mixed, grad_qs = call(
        "grads", functools.partial(grads_kernel, wide), [full_bf, full_bf],
        [summed, mixed, q_short, cotangent, gain2, sums],
    )
    after = shifted(grad_mixed, "ctx", -1, wrap=False)
    stats, part, qcols = call(
        "beside", functools.partial(beside_kernel, wide),
        [
            arr((groups + 2 * rows, LANES), F32), full_f, arr((8, channels), F32),
        ],
        [
            lengths, summed, cotangent, sums, grad_mixed, grad_qs, gated, before, bwd,
            skip2, q_input, came,
        ],
        flops=4 * 10**9, moved=5 * 10**6,
    )
    grad_ks, grad_vs, tails, packed = call(
        "gate", gate_kernel,
        [
            full_bf, full_bf, arr((4 * RIM, channels), BF16),
            arr((packed_rows, LANES), F32),
        ],
        [
            lengths, part, after, bwd, k_short, v_short, grad_qs, k_input, v_input, came,
            stats, qcols,
        ],
        [pltpu.VMEM((24, channels), F32)], flops=10**9, moved=5 * 10**6,
    )
    count = lax.axis_size("ctx")
    packed, summed = lax.optimization_barrier((packed, summed))
    packed = packed + swapped(packed, "ctx", 1)
    (normed,) = call(
        "normed", functools.partial(normed_kernel, wide), [full_bf], [summed, gain2, sums],
        flops=10**9, moved=5 * 10**6,
    )
    normed, tails, packed = lax.optimization_barrier((normed, tails, packed))
    tails = shifted(tails, "ctx", -1)
    step = 2
    while 2 * step < count:
        packed = packed + swapped(packed, "ctx", step)
        step *= 2
    packed, tails = lax.optimization_barrier((packed, tails))
    other = swapped(packed, "ctx", step)
    grad_q, grad_k, grad_v = call(
        "mains", mains_kernel, [full_bf] * 3,
        [lengths, taps, tails, grad_qs, grad_ks, grad_vs], flops=10**9, moved=5 * 10**6,
    )
    grad_short, grad_long, grad_skip, grad_gain = call(
        "unpack", unpack_kernel,
        [
            arr((3, KS, groups), F32), arr((groups, K), F32),
            arr((rows, LANES), F32), arr((rows, LANES), F32),
        ],
        [packed, other],
    )
    return (
        normed, grad_q, grad_k, grad_v, jnp.transpose(grad_short, (0, 2, 1)), grad_long,
        grad_skip.reshape(channels), grad_gain.reshape(channels),
    )


def solution(mesh):
    tiled = P("ctx", "tp")
    return jax.shard_map(
        shards,
        mesh=mesh,
        in_specs=(
            tiled, tiled, tiled, tiled, P(), P(None, "tp", None), P("tp", None), P("tp"), P("tp"),
            tiled,
        ),
        out_specs=(
            tiled, tiled, tiled, tiled, P(None, "tp", None), P("tp", None), P("tp"), P("tp"),
        ),
        check_vma=False,
    )
```

```python
import functools

import jax
import jax.numpy as jnp
from jax import lax
from jax.experimental import pallas as pl
from jax.experimental.pallas import tpu as pltpu
from jax.sharding import PartitionSpec as P

GS = 16
K = 128
KS = 7
LANES = 128
PER = LANES // GS
RIM = 8
PACK = 16
EPS = 1e-06
F32 = jnp.float32
BF16 = jnp.bfloat16


def shifted(x, axis, by, wrap=True):
    count = lax.axis_size(axis)
    pairs = [(i, (i + by) % count) for i in range(count)]
    return lax.ppermute(x, axis, [p for p in pairs if wrap or p[1] - p[0] == by])


def swapped(x, axis, step):
    return lax.ppermute(x, axis, [(i, i ^ step) for i in range(lax.axis_size(axis))])


def iota(shape, dim):
    return lax.broadcasted_iota(jnp.int32, shape, dim)


def positions(len_ref, rows):
    begin = jnp.zeros_like(rows)
    start = jnp.int32(0)
    for n in range(len_ref.shape[0]):
        begin = jnp.where(rows >= start, start, begin)
        start = start + len_ref[n]
    return jnp.where(rows < start, rows - begin, -1)


def first_row():
    return lax.axis_index("ctx") * K


def lanes_of(q):
    return pl.ds(pl.multiple_of(q * LANES, LANES), LANES)


def each_chunk(channels, body, unroll=4):
    def step(q, carry):
        body(q)
        return carry

    lax.fori_loop(0, channels // LANES, step, 0, unroll=unroll)


def as_mask(cond):
    return jnp.where(cond, 1.0, 0.0).astype(BF16)


def join(*parts):
    return jnp.concatenate(parts, axis=0)


def tap_rows(taps_ref, which, ls):
    table = taps_ref[which * 8 : which * 8 + 8, ls]
    return [table[j : j + 1, :] for j in range(KS)]


def follows(len_ref, start, count):
    pos = positions(len_ref, start + iota((count, LANES), 0))
    return jnp.where(pos >= 1, 1.0, 0.0)


def moved_on(x, after):
    return pltpu.roll(x, 1, 0) * after


def causal(ext, taps, after):
    total = taps[0] * ext[RIM:]
    for j in range(1, KS):
        ext = moved_on(ext, after)
        total = total + taps[j] * ext[RIM:]
    return total


def tap_lines(grad, ext, after):
    lines = [jnp.sum(grad * ext[RIM:], axis=0, keepdims=True)]
    for j in range(1, KS):
        ext = moved_on(ext, after)
        lines.append(jnp.sum(grad * ext[RIM:], axis=0, keepdims=True))
    lines.append(jnp.zeros((8 - KS, LANES), F32))
    return join(*lines)


def owners():
    lane = iota((K, LANES), 1) // GS
    return [as_mask(lane == g) for g in range(PER)]


def per_group(right, own):
    return join(*[right * mask for mask in own])


def masked(table_ref, q, mask):
    table = table_ref[:, pl.ds(pl.multiple_of(q * PER * K, PER * K), PER * K)]
    return [table[:, g * K : (g + 1) * K] * mask for g in range(PER)]


def product(left, right):
    return jnp.dot(jnp.concatenate(left, axis=1), right, preferred_element_type=F32)


K_FIRST, Q_LAST, K_LAST, V_LAST, V_FIRST, SENT = 0, K, K + 8, K + 16, K + 24, K + 32


def rim_of(ref, at, ls):
    base = at // PACK * PACK
    return ref[base : base + PACK, ls].astype(F32)[at - base : at - base + RIM]


def first_kernel(
    len_hbm, short_hbm, q_hbm, k_hbm, v_hbm, taps_ref, sent_ref, far_ref,
    len_ref, short_ref, q_ref, k_ref, v_ref, sems,
):
    groups = short_ref.shape[2]
    channels = taps_ref.shape[1]
    pairs = (
        (short_hbm, short_ref), (len_hbm, len_ref), (k_hbm, k_ref), (v_hbm, v_ref),
        (q_hbm.at[K - PACK : K], q_ref),
    )
    copies = [pltpu.make_async_copy(a, b, sems.at[i]) for i, (a, b) in enumerate(pairs)]
    for copy in copies:
        copy.start()
    spread = as_mask(iota((groups, channels), 1) // GS == iota((groups, channels), 0))
    copies[0].wait()
    for i in range(3):
        taps_ref[i * 8 : i * 8 + KS] = jnp.dot(
            short_ref[i], spread, preferred_element_type=F32
        )
        taps_ref[i * 8 + KS : i * 8 + 8] = jnp.zeros((8 - KS, channels), F32)
    for copy in copies[1:]:
        copy.wait()
    after = follows(len_ref, first_row(), K)

    def body(q):
        ls = lanes_of(q)
        kx = k_ref[:, ls].astype(F32)
        vx = v_ref[:, ls].astype(F32)
        ks = causal(kx, tap_rows(taps_ref, 1, ls), after)
        vs = causal(vx, tap_rows(taps_ref, 2, ls), after)
        sent_ref[:K, ls] = join(kx[:RIM], ks * vs).astype(BF16)
        q_end = q_ref[:, ls].astype(F32)[PACK - RIM :]
        k_end = kx[K - RIM :]
        v_end = vx[K - RIM :]
        sent_ref[K:, ls] = join(q_end, k_end, v_end, vx[:RIM]).astype(BF16)
        far_ref[:, ls] = join(k_end, v_end).astype(BF16)

    each_chunk(channels, body)


def circulant_kernel(turned, long_ref, out_ref, line_ref):
    groups = long_ref.shape[0]
    filt = long_ref[...]
    if turned:
        flip = as_mask((iota((K, K), 0) + iota((K, K), 1)) % K == 0)
        line_ref[...] = jnp.dot(filt, flip, preferred_element_type=F32)
    else:
        line_ref[...] = filt.astype(F32)

    def step(g, carry):
        row = jnp.broadcast_to(line_ref[pl.ds(g, 1), :], (GS, K))
        block = pltpu.roll(row, 0, 1, stride=1, stride_axis=0)
        for i in range(K // GS):
            moved = block if i == 0 else pltpu.roll(block, i * GS, 1)
            at = pl.ds(pl.multiple_of(g * K, K), K)
            out_ref[i * GS : (i + 1) * GS, at] = moved.astype(BF16)
        return carry

    lax.fori_loop(0, groups, step, 0, unroll=8)


def current_kernel(
    len_ref, q_ref, taps_ref, sent_ref, fwd_ref, skip_ref, qs_ref, part_ref, top_ref
):
    row = iota((K, LANES), 0)
    col = iota((K, LANES), 1)
    pos = positions(len_ref, first_row() + row)
    near = (col <= row) & (pos >= row - col)
    mask = as_mask(near)
    mask_top = as_mask(near & (col < RIM))
    picks = join(*[as_mask((col == row + g * GS) & (row < GS)) for g in range(PER)])
    own = owners()
    top = jnp.zeros((RIM, LANES), F32)
    after = follows(len_ref, first_row(), K)

    def body(q):
        ls = lanes_of(q)
        qs_ref[RIM:, ls] = causal(q_ref[:, ls].astype(F32), tap_rows(taps_ref, 0, ls), after)
        qs_ref[:RIM, ls] = top
        gated = join(top, sent_ref[:K, ls].astype(F32)[RIM:])
        rest = product(masked(fwd_ref, q, mask), per_group(gated.astype(BF16), own))
        part_ref[:, ls] = rest + skip_ref[:, ls] * gated
        top_ref[:, ls] = product(masked(fwd_ref, q, mask_top), picks).astype(BF16)

    each_chunk(q_ref.shape[1], body)


def summed_kernel(
    len_ref, came_ref, far_ref, q_ref, k_ref, v_ref, taps_ref, sent_ref, fwd_ref, top_ref,
    bulk_ref, part_ref, skip_ref, resid_ref, cot_ref, gain_ref,
    qs_ref, gated_ref, before_ref, mixed_ref, summed_ref, sums_ref, acc_ref,
):
    row = iota((K, LANES), 0)
    col = iota((K, LANES), 1)
    pos = positions(len_ref, first_row() + row)
    mask = as_mask((col > row) & (pos >= row - col + K))
    after = follows(len_ref, first_row() - RIM, 2 * RIM)
    after_far = follows(len_ref, first_row() - K - RIM, 2 * RIM)
    own = owners()
    own_top = [
        as_mask((iota((PACK, LANES), 1) // GS == g) & (iota((PACK, LANES), 0) < RIM))
        for g in range(PER)
    ]
    acc_ref[...] = jnp.zeros_like(acc_ref)

    def body(q):
        ls = lanes_of(q)
        kt = tap_rows(taps_ref, 1, ls)
        vt = tap_rows(taps_ref, 2, ls)
        k_last = rim_of(came_ref, K_LAST, ls)
        v_last = rim_of(came_ref, V_LAST, ls)
        top = causal(join(k_last, rim_of(k_ref, 0, ls)), kt, after) * causal(
            join(v_last, rim_of(v_ref, 0, ls)), vt, after
        )
        far_top = causal(
            join(rim_of(far_ref, 0, ls), rim_of(came_ref, K_FIRST, ls)), kt, after_far
        ) * causal(join(rim_of(far_ref, RIM, ls), rim_of(came_ref, V_FIRST, ls)), vt, after_far)
        qs_top = causal(
            join(rim_of(came_ref, Q_LAST, ls), rim_of(q_ref, 0, ls)), tap_rows(taps_ref, 0, ls), after
        )
        before = join(far_top, came_ref[:K, ls].astype(F32)[RIM:]).astype(BF16)
        gated = join(top, sent_ref[:K, ls].astype(F32)[RIM:]).astype(BF16)
        before_ref[:, ls] = before
        gated_ref[:, ls] = gated
        qs = join(qs_top, bulk_ref[RIM:, ls])
        qs_ref[:, ls] = qs
        first = gated[:PACK]
        left = masked(fwd_ref, q, mask) + [top_ref[:, ls]]
        right = join(per_group(before, own), per_group(first, own_top))
        direct = skip_ref[:, ls] * first.astype(F32)[:RIM]
        mixed = part_ref[:, ls] + product(left, right)
        mixed = join(mixed[:RIM] + direct, mixed[RIM:])
        summed = resid_ref[:, ls].astype(F32) + qs * mixed
        mixed_ref[:, ls] = mixed
        summed_ref[:, ls] = summed
        acc_ref[0] += summed * summed
        acc_ref[1] += gain_ref[:, ls] * cot_ref[:, ls].astype(F32) * summed

    each_chunk(resid_ref.shape[1], body)
    for i in range(2):
        sums_ref[i : i + 1] = jnp.sum(acc_ref[i].T, axis=0, keepdims=True)


def group_sums(cols):
    count, channels = cols.shape
    gather = as_mask(iota((channels, LANES), 0) // GS == iota((channels, LANES), 1))
    high = cols.astype(BF16)
    rest = cols - high.astype(F32)
    mid = rest.astype(BF16)
    low = (rest - mid.astype(F32)).astype(BF16)
    parts = join(high.astype(F32), mid.astype(F32), low.astype(F32)).astype(BF16)
    sums = jnp.dot(parts, gather, preferred_element_type=F32)
    return sums[:count] + sums[count : 2 * count] + sums[2 * count :]


def by_row(line):
    return jnp.broadcast_to(line, (K, K)).T


def inverse_of(sums_ref, total):
    return by_row(lax.rsqrt(sums_ref[0:1] / total + EPS))


def gates_kernel(len_ref, k_ref, v_ref, came_ref, taps_ref, ks_ref, vs_ref):
    after = follows(len_ref, first_row() - RIM, K + RIM)

    def body(q):
        ls = lanes_of(q)
        k_ext = join(rim_of(came_ref, K_LAST, ls), k_ref[:, ls].astype(F32))
        v_ext = join(rim_of(came_ref, V_LAST, ls), v_ref[:, ls].astype(F32))
        ks_ref[:, ls] = causal(k_ext, tap_rows(taps_ref, 1, ls), after)
        vs_ref[:, ls] = causal(v_ext, tap_rows(taps_ref, 2, ls), after)

    each_chunk(k_ref.shape[1], body)


def grads_kernel(total, summed_ref, mixed_ref, qs_ref, cot_ref, gain_ref, sums_ref, gm_ref, gq_ref):
    inverse = inverse_of(sums_ref, total)
    scale = inverse * inverse * by_row(sums_ref[1:2] / total)

    def body(q):
        ls = lanes_of(q)
        scaled = gain_ref[:, ls] * cot_ref[:, ls].astype(F32)
        grad_sum = inverse * (scaled - summed_ref[:, ls] * scale)
        gm_ref[:, ls] = (grad_sum * qs_ref[:, ls]).astype(BF16)
        gq_ref[:, ls] = (grad_sum * mixed_ref[:, ls]).astype(BF16)

    each_chunk(cot_ref.shape[1], body)


def beside_kernel(
    total, len_ref, summed_ref, cot_ref, sums_ref, gm_ref, gq_ref, gated_ref, before_ref,
    bwd_ref, skip_ref, q_ref, came_ref, stats_ref, part_ref, cols_ref,
):
    groups = bwd_ref.shape[1] // K
    inverse = inverse_of(sums_ref, total)
    row = iota((K, LANES), 0)
    col = iota((K, LANES), 1)
    after = follows(len_ref, first_row() - RIM, K + RIM)
    pos = positions(len_ref, first_row() + col)
    mask = as_mask((col >= row) & (pos >= col - row))
    source = K - 1 - row
    near = (col >= source) & (pos >= col - source)
    far = (col < source) & (pos >= col - source + K)
    flip = as_mask(row + col == K - 1)
    own = owners()

    def body(q):
        ls = lanes_of(q)
        summed = summed_ref[:, ls]
        gm = gm_ref[:, ls]
        gmf = gm.astype(F32)
        gated = gated_ref[:, ls]
        stats_ref[pl.ds(groups + q, 1), :] = jnp.sum(gmf * gated.astype(F32), axis=0, keepdims=True)
        stats_ref[pl.ds(groups + groups // PER + q, 1), :] = jnp.sum(
            cot_ref[:, ls].astype(F32) * summed * inverse, axis=0, keepdims=True
        )
        right = per_group(gm, own)
        part_ref[:, ls] = skip_ref[:, ls] * gmf + product(masked(bwd_ref, q, mask), right)
        two = jnp.concatenate([before_ref[:, ls], gated], axis=1)
        flipped = jnp.dot(flip, two, preferred_element_type=F32).astype(BF16)
        left = join(flipped[:, :LANES], flipped[:, LANES:])
        turned = gmf.T.astype(BF16)
        spread = []
        for g in range(PER):
            pieces = [jnp.zeros((GS, K), BF16)] * PER
            pieces[g] = turned[g * GS : (g + 1) * GS]
            spread.append(join(*pieces))
        cross = jnp.dot(left, jnp.concatenate(spread, axis=1), preferred_element_type=F32)
        lines = []
        for g in range(PER):
            gs = slice(g * K, (g + 1) * K)
            square = jnp.where(near, cross[K:, gs], jnp.where(far, cross[:K, gs], 0.0))
            square = pltpu.roll(square, 1, 1, stride=1, stride_axis=0)
            lines.append(jnp.sum(square, axis=0, keepdims=True))
        stats_ref[pl.ds(pl.multiple_of(q * PER, PER), PER), :] = join(*lines)
        q_ext = join(rim_of(came_ref, Q_LAST, ls), q_ref[:, ls].astype(F32))
        cols_ref[:, ls] = tap_lines(gq_ref[:, ls].astype(F32), q_ext, after)

    each_chunk(cot_ref.shape[1], body, 4)


def gate_kernel(
    len_ref, part_ref, after_ref, bwd_ref, ks_ref, vs_ref, gq_ref, k_ref, v_ref, came_ref,
    stats_ref, qcols_ref, gks_ref, gvs_ref, tails_ref, packed_ref, cols_ref,
):
    channels = part_ref.shape[1]
    kept = stats_ref.shape[0]
    row = iota((K, LANES), 0)
    col = iota((K, LANES), 1)
    after = follows(len_ref, first_row() - RIM, K + RIM)
    pos = positions(len_ref, first_row() + K + col)
    mask = as_mask((col < row) & (pos >= col - row + K))
    own = owners()

    def body(q):
        ls = lanes_of(q)
        right = per_group(after_ref[:, ls], own)
        grad = part_ref[:, ls] + product(masked(bwd_ref, q, mask), right)
        gks = (grad * vs_ref[:, ls]).astype(BF16)
        gvs = (grad * ks_ref[:, ls]).astype(BF16)
        gks_ref[:, ls] = gks
        gvs_ref[:, ls] = gvs
        heads = (rim_of(gq_ref, 0, ls), gks.astype(F32)[:RIM], gvs.astype(F32)[:RIM])
        tails_ref[:, ls] = join(*heads, jnp.zeros((RIM, LANES), F32)).astype(BF16)
        k_ext = join(rim_of(came_ref, K_LAST, ls), k_ref[:, ls].astype(F32))
        v_ext = join(rim_of(came_ref, V_LAST, ls), v_ref[:, ls].astype(F32))
        cols_ref[0:8, ls] = qcols_ref[:, ls]
        cols_ref[8:16, ls] = tap_lines(gks.astype(F32), k_ext, after)
        cols_ref[16:24, ls] = tap_lines(gvs.astype(F32), v_ext, after)

    each_chunk(channels, body)
    packed_ref[0:kept] = stats_ref[...]
    packed_ref[kept:] = group_sums(cols_ref[...])


def back_short(which, after, ls, taps_ref, grad_ref, tails_ref):
    ext = join(grad_ref[:, ls].astype(F32), rim_of(tails_ref, which * RIM, ls))
    taps = tap_rows(taps_ref, which, ls)
    grad = taps[0] * ext[:K]
    for j in range(1, KS):
        ext = pltpu.roll(ext * after, K + RIM - 1, 0)
        grad = grad + taps[j] * ext[:K]
    return grad.astype(BF16)


def mains_kernel(len_ref, taps_ref, tails_ref, gq_ref, gks_ref, gvs_ref, oq_ref, ok_ref, ov_ref):
    after = follows(len_ref, first_row(), K + RIM)

    def body(q):
        ls = lanes_of(q)
        oq_ref[:, ls] = back_short(0, after, ls, taps_ref, gq_ref, tails_ref)
        ok_ref[:, ls] = back_short(1, after, ls, taps_ref, gks_ref, tails_ref)
        ov_ref[:, ls] = back_short(2, after, ls, taps_ref, gvs_ref, tails_ref)

    each_chunk(gq_ref.shape[1], body)


def normed_kernel(total, summed_ref, gain_ref, sums_ref, normed_ref):
    inverse = inverse_of(sums_ref, total)

    def body(q):
        ls = lanes_of(q)
        normed_ref[:, ls] = (gain_ref[:, ls] * summed_ref[:, ls] * inverse).astype(BF16)

    each_chunk(summed_ref.shape[1], body)


def unpack_kernel(one_ref, two_ref, short_ref, long_ref, skip_ref, gain_ref):
    groups = long_ref.shape[0]
    rows = groups // PER
    total = one_ref[...] + two_ref[...]
    long_ref[...] = total[:groups]
    skip_ref[...] = total[groups : groups + rows]
    gain_ref[...] = total[groups + rows : groups + 2 * rows]
    for i in range(3):
        at = groups + 2 * rows + i * 8
        short_ref[i] = total[at : at + KS, :groups]


def shards(
    q_input, k_input, v_input, resid, lengths, short_filter, long_filter, skip, gain, cotangent
):
    length, channels = q_input.shape
    groups = channels // GS
    wide = channels * lax.axis_size("tp")
    rows = groups // PER
    packed_rows = groups + 2 * rows + 24

    def arr(shape, dtype):
        return jax.ShapeDtypeStruct(shape, dtype)

    smem = pl.BlockSpec(memory_space=pltpu.SMEM)
    vmem = pl.BlockSpec(memory_space=pltpu.VMEM)
    far_off = pl.BlockSpec(memory_space=pltpu.HBM)
    full_bf = arr((length, channels), BF16)
    full_f = arr((length, channels), F32)

    def call(name, kernel, outs, ins, scratch=(), flops=10**8, moved=10**6, grant=8, hbm=False):
        scalar = ins[0] is lengths
        return pl.pallas_call(
            kernel,
            out_shape=outs,
            in_specs=[far_off] * len(ins)
            if hbm
            else [smem if (i == 0 and scalar) else vmem for i in range(len(ins))],
            out_specs=[vmem] * len(outs),
            scratch_shapes=scratch,
            compiler_params=pltpu.CompilerParams(vmem_limit_bytes=grant * 1024 * 1024),
            cost_estimate=pl.CostEstimate(flops=flops, bytes_accessed=moved, transcendentals=0),
            name=name,
        )(*ins)

    skip2 = skip.reshape(1, channels)
    gain2 = gain.reshape(1, channels)
    taps, sent, far = call(
        "first", first_kernel,
        [arr((24, channels), F32), arr((SENT, channels), BF16), arr((2 * RIM, channels), BF16)],
        [lengths, jnp.transpose(short_filter, (0, 2, 1)), q_input, k_input, v_input],
        [
            pltpu.SMEM(lengths.shape, jnp.int32), pltpu.VMEM((3, KS, groups), BF16),
            pltpu.VMEM((PACK, channels), BF16), pltpu.VMEM((length, channels), BF16),
            pltpu.VMEM((length, channels), BF16), pltpu.SemaphoreType.DMA((5,)),
        ],
        grant=60,
        hbm=True,
    )
    came = shifted(sent, "ctx", 1)
    came_far = shifted(far, "ctx", 2)

    def circulants(filt, turned):
        return call(
            "circulants", functools.partial(circulant_kernel, turned),
            [arr((K, groups * K), BF16)], [filt], [pltpu.VMEM((groups, K), F32)],
            flops=10**9, moved=4 * 10**6,
        )[0]

    filt, filt2, sent = lax.optimization_barrier((long_filter, long_filter, sent))
    fwd = circulants(filt, True)
    bulk, part, top = call(
        "current", current_kernel, [full_f, full_f, full_bf],
        [lengths, q_input, taps, sent, fwd, skip2], flops=10**9, moved=5 * 10**6,
    )
    bwd = circulants(filt2, False)
    came, bwd = lax.optimization_barrier((came, bwd))
    q_short, gated, before, mixed, summed, sums = call(
        "summed", summed_kernel,
        [full_f, full_bf, full_bf, full_f, full_f, arr((2, K), F32)],
        [
            lengths, came, came_far, q_input, k_input, v_input, taps, sent, fwd, top,
            bulk, part, skip2, resid, cotangent, gain2,
        ],
        [pltpu.VMEM((2, K, LANES), F32)], flops=10**9, moved=5 * 10**6,
    )
    own_sums = sums
    step = 1
    while step < lax.axis_size("tp"):
        sums = sums + swapped(sums, "tp", step)
        step *= 2
    came, _ = lax.optimization_barrier((came, own_sums))
    k_short, v_short = call(
        "gates", gates_kernel, [full_f] * 2, [lengths, k_input, v_input, came, taps],
        flops=10**8, moved=2 * 10**6,
    )
    sums, k_short, v_short = lax.optimization_barrier((sums, k_short, v_short))
    grad_mixed, grad_qs = call(
        "grads", functools.partial(grads_kernel, wide), [full_bf, full_bf],
        [summed, mixed, q_short, cotangent, gain2, sums],
    )
    after = shifted(grad_mixed, "ctx", -1, wrap=False)
    stats, part, qcols = call(
        "beside", functools.partial(beside_kernel, wide),
        [
            arr((groups + 2 * rows, LANES), F32), full_f, arr((8, channels), F32),
        ],
        [
            lengths, summed, cotangent, sums, grad_mixed, grad_qs, gated, before, bwd,
            skip2, q_input, came,
        ],
        flops=4 * 10**9, moved=5 * 10**6,
    )
    grad_ks, grad_vs, tails, packed = call(
        "gate", gate_kernel,
        [
            full_bf, full_bf, arr((4 * RIM, channels), BF16),
            arr((packed_rows, LANES), F32),
        ],
        [
            lengths, part, after, bwd, k_short, v_short, grad_qs, k_input, v_input, came,
            stats, qcols,
        ],
        [pltpu.VMEM((24, channels), F32)], flops=10**9, moved=5 * 10**6,
    )
    count = lax.axis_size("ctx")
    packed, summed = lax.optimization_barrier((packed, summed))
    packed = packed + swapped(packed, "ctx", 1)
    (normed,) = call(
        "normed", functools.partial(normed_kernel, wide), [full_bf], [summed, gain2, sums],
        flops=10**9, moved=5 * 10**6,
    )
    normed, tails, packed = lax.optimization_barrier((normed, tails, packed))
    tails = shifted(tails, "ctx", -1)
    step = 2
    while 2 * step < count:
        packed = packed + swapped(packed, "ctx", step)
        step *= 2
    packed, grad_qs = lax.optimization_barrier((packed, grad_qs))
    other = swapped(packed, "ctx", step)
    grad_q, grad_k, grad_v = call(
        "mains", mains_kernel, [full_bf] * 3,
        [lengths, taps, tails, grad_qs, grad_ks, grad_vs], flops=10**9, moved=5 * 10**6,
    )
    grad_short, grad_long, grad_skip, grad_gain = call(
        "unpack", unpack_kernel,
        [
            arr((3, KS, groups), F32), arr((groups, K), F32),
            arr((rows, LANES), F32), arr((rows, LANES), F32),
        ],
        [packed, other],
    )
    return (
        normed, grad_q, grad_k, grad_v, jnp.transpose(grad_short, (0, 2, 1)), grad_long,
        grad_skip.reshape(channels), grad_gain.reshape(channels),
    )


def solution(mesh):
    tiled = P("ctx", "tp")
    return jax.shard_map(
        shards,
        mesh=mesh,
        in_specs=(
            tiled, tiled, tiled, tiled, P(), P(None, "tp", None), P("tp", None), P("tp"), P("tp"),
            tiled,
        ),
        out_specs=(
            tiled, tiled, tiled, tiled, P(None, "tp", None), P("tp", None), P("tp"), P("tp"),
        ),
        check_vma=False,
    )
```

```python
import functools

import jax
import jax.numpy as jnp
from jax import lax
from jax.experimental import pallas as pl
from jax.experimental.pallas import tpu as pltpu
from jax.sharding import PartitionSpec as P

GS = 16
K = 128
KS = 7
LANES = 128
PER = LANES // GS
RIM = 8
PACK = 16
EPS = 1e-06
F32 = jnp.float32
BF16 = jnp.bfloat16


def shifted(x, axis, by, wrap=True):
    count = lax.axis_size(axis)
    pairs = [(i, (i + by) % count) for i in range(count)]
    return lax.ppermute(x, axis, [p for p in pairs if wrap or p[1] - p[0] == by])


def swapped(x, axis, step):
    return lax.ppermute(x, axis, [(i, i ^ step) for i in range(lax.axis_size(axis))])


def iota(shape, dim):
    return lax.broadcasted_iota(jnp.int32, shape, dim)


def positions(len_ref, rows):
    begin = jnp.zeros_like(rows)
    start = jnp.int32(0)
    for n in range(len_ref.shape[0]):
        begin = jnp.where(rows >= start, start, begin)
        start = start + len_ref[n]
    return jnp.where(rows < start, rows - begin, -1)


def first_row():
    return lax.axis_index("ctx") * K


def lanes_of(q):
    return pl.ds(pl.multiple_of(q * LANES, LANES), LANES)


def each_chunk(channels, body, unroll=4):
    def step(q, carry):
        body(q)
        return carry

    lax.fori_loop(0, channels // LANES, step, 0, unroll=unroll)


def as_mask(cond):
    return jnp.where(cond, 1.0, 0.0).astype(BF16)


def join(*parts):
    return jnp.concatenate(parts, axis=0)


def tap_rows(taps_ref, which, ls):
    table = taps_ref[which * 8 : which * 8 + 8, ls]
    return [table[j : j + 1, :] for j in range(KS)]


def follows(len_ref, start, count):
    pos = positions(len_ref, start + iota((count, LANES), 0))
    return jnp.where(pos >= 1, 1.0, 0.0)


def moved_on(x, after):
    return pltpu.roll(x, 1, 0) * after


def causal(ext, taps, after):
    total = taps[0] * ext[RIM:]
    for j in range(1, KS):
        ext = moved_on(ext, after)
        total = total + taps[j] * ext[RIM:]
    return total


def tap_lines(grad, ext, after):
    lines = [jnp.sum(grad * ext[RIM:], axis=0, keepdims=True)]
    for j in range(1, KS):
        ext = moved_on(ext, after)
        lines.append(jnp.sum(grad * ext[RIM:], axis=0, keepdims=True))
    lines.append(jnp.zeros((8 - KS, LANES), F32))
    return join(*lines)


def owners():
    lane = iota((K, LANES), 1) // GS
    return [as_mask(lane == g) for g in range(PER)]


def per_group(right, own):
    return join(*[right * mask for mask in own])


def masked(table_ref, q, mask):
    table = table_ref[:, pl.ds(pl.multiple_of(q * PER * K, PER * K), PER * K)]
    return [table[:, g * K : (g + 1) * K] * mask for g in range(PER)]


def product(left, right):
    return jnp.dot(jnp.concatenate(left, axis=1), right, preferred_element_type=F32)


K_FIRST, Q_LAST, K_LAST, V_LAST, V_FIRST, SENT = 0, K, K + 8, K + 16, K + 24, K + 32


def rim_of(ref, at, ls):
    base = at // PACK * PACK
    return ref[base : base + PACK, ls].astype(F32)[at - base : at - base + RIM]


def first_kernel(
    len_hbm, short_hbm, q_hbm, k_hbm, v_hbm, taps_ref, sent_ref, far_ref,
    len_ref, short_ref, q_ref, k_ref, v_ref, sems,
):
    groups = short_ref.shape[2]
    channels = taps_ref.shape[1]
    pairs = (
        (short_hbm, short_ref), (len_hbm, len_ref), (k_hbm, k_ref), (v_hbm, v_ref),
        (q_hbm.at[K - PACK : K], q_ref),
    )
    copies = [pltpu.make_async_copy(a, b, sems.at[i]) for i, (a, b) in enumerate(pairs)]
    for copy in copies:
        copy.start()
    spread = as_mask(iota((groups, channels), 1) // GS == iota((groups, channels), 0))
    copies[0].wait()
    for i in range(3):
        taps_ref[i * 8 : i * 8 + KS] = jnp.dot(
            short_ref[i], spread, preferred_element_type=F32
        )
        taps_ref[i * 8 + KS : i * 8 + 8] = jnp.zeros((8 - KS, channels), F32)
    for copy in copies[1:]:
        copy.wait()
    after = follows(len_ref, first_row(), K)

    def body(q):
        ls = lanes_of(q)
        kx = k_ref[:, ls].astype(F32)
        vx = v_ref[:, ls].astype(F32)
        ks = causal(kx, tap_rows(taps_ref, 1, ls), after)
        vs = causal(vx, tap_rows(taps_ref, 2, ls), after)
        sent_ref[:K, ls] = join(kx[:RIM], ks * vs).astype(BF16)
        q_end = q_ref[:, ls].astype(F32)[PACK - RIM :]
        k_end = kx[K - RIM :]
        v_end = vx[K - RIM :]
        sent_ref[K:, ls] = join(q_end, k_end, v_end, vx[:RIM]).astype(BF16)
        far_ref[:, ls] = join(k_end, v_end).astype(BF16)

    each_chunk(channels, body)


def circulant_kernel(turned, long_ref, out_ref, line_ref):
    groups = long_ref.shape[0]
    filt = long_ref[...]
    if turned:
        flip = as_mask((iota((K, K), 0) + iota((K, K), 1)) % K == 0)
        line_ref[...] = jnp.dot(filt, flip, preferred_element_type=F32)
    else:
        line_ref[...] = filt.astype(F32)

    def step(g, carry):
        row = jnp.broadcast_to(line_ref[pl.ds(g, 1), :], (GS, K))
        block = pltpu.roll(row, 0, 1, stride=1, stride_axis=0)
        for i in range(K // GS):
            moved = block if i == 0 else pltpu.roll(block, i * GS, 1)
            at = pl.ds(pl.multiple_of(g * K, K), K)
            out_ref[i * GS : (i + 1) * GS, at] = moved.astype(BF16)
        return carry

    lax.fori_loop(0, groups, step, 0, unroll=8)


def current_kernel(
    len_ref, q_ref, taps_ref, sent_ref, fwd_ref, skip_ref, qs_ref, part_ref, top_ref
):
    row = iota((K, LANES), 0)
    col = iota((K, LANES), 1)
    pos = positions(len_ref, first_row() + row)
    near = (col <= row) & (pos >= row - col)
    mask = as_mask(near)
    mask_top = as_mask(near & (col < RIM))
    picks = join(*[as_mask((col == row + g * GS) & (row < GS)) for g in range(PER)])
    own = owners()
    top = jnp.zeros((RIM, LANES), F32)
    after = follows(len_ref, first_row(), K)

    def body(q):
        ls = lanes_of(q)
        qs_ref[RIM:, ls] = causal(q_ref[:, ls].astype(F32), tap_rows(taps_ref, 0, ls), after)
        qs_ref[:RIM, ls] = top
        gated = join(top, sent_ref[:K, ls].astype(F32)[RIM:])
        rest = product(masked(fwd_ref, q, mask), per_group(gated.astype(BF16), own))
        part_ref[:, ls] = rest + skip_ref[:, ls] * gated
        top_ref[:, ls] = product(masked(fwd_ref, q, mask_top), picks).astype(BF16)

    each_chunk(q_ref.shape[1], body)


def summed_kernel(
    len_ref, came_ref, far_ref, q_ref, k_ref, v_ref, taps_ref, sent_ref, fwd_ref, top_ref,
    bulk_ref, part_ref, skip_ref, resid_ref, cot_ref, gain_ref,
    qs_ref, gated_ref, before_ref, mixed_ref, summed_ref, sums_ref, acc_ref,
):
    row = iota((K, LANES), 0)
    col = iota((K, LANES), 1)
    pos = positions(len_ref, first_row() + row)
    mask = as_mask((col > row) & (pos >= row - col + K))
    after = follows(len_ref, first_row() - RIM, 2 * RIM)
    after_far = follows(len_ref, first_row() - K - RIM, 2 * RIM)
    own = owners()
    own_top = [
        as_mask((iota((PACK, LANES), 1) // GS == g) & (iota((PACK, LANES), 0) < RIM))
        for g in range(PER)
    ]
    acc_ref[...] = jnp.zeros_like(acc_ref)

    def body(q):
        ls = lanes_of(q)
        kt = tap_rows(taps_ref, 1, ls)
        vt = tap_rows(taps_ref, 2, ls)
        k_last = rim_of(came_ref, K_LAST, ls)
        v_last = rim_of(came_ref, V_LAST, ls)
        top = causal(join(k_last, rim_of(k_ref, 0, ls)), kt, after) * causal(
            join(v_last, rim_of(v_ref, 0, ls)), vt, after
        )
        far_top = causal(
            join(rim_of(far_ref, 0, ls), rim_of(came_ref, K_FIRST, ls)), kt, after_far
        ) * causal(join(rim_of(far_ref, RIM, ls), rim_of(came_ref, V_FIRST, ls)), vt, after_far)
        qs_top = causal(
            join(rim_of(came_ref, Q_LAST, ls), rim_of(q_ref, 0, ls)), tap_rows(taps_ref, 0, ls), after
        )
        before = join(far_top, came_ref[:K, ls].astype(F32)[RIM:]).astype(BF16)
        gated = join(top, sent_ref[:K, ls].astype(F32)[RIM:]).astype(BF16)
        before_ref[:, ls] = before
        gated_ref[:, ls] = gated
        qs = join(qs_top, bulk_ref[RIM:, ls])
        qs_ref[:, ls] = qs
        first = gated[:PACK]
        left = masked(fwd_ref, q, mask) + [top_ref[:, ls]]
        right = join(per_group(before, own), per_group(first, own_top))
        direct = skip_ref[:, ls] * first.astype(F32)[:RIM]
        mixed = part_ref[:, ls] + product(left, right)
        mixed = join(mixed[:RIM] + direct, mixed[RIM:])
        summed = resid_ref[:, ls].astype(F32) + qs * mixed
        mixed_ref[:, ls] = mixed
        summed_ref[:, ls] = summed
        acc_ref[0] += summed * summed
        acc_ref[1] += gain_ref[:, ls] * cot_ref[:, ls].astype(F32) * summed

    each_chunk(resid_ref.shape[1], body)
    for i in range(2):
        sums_ref[i : i + 1] = jnp.sum(acc_ref[i].T, axis=0, keepdims=True)


def group_sums(cols):
    count, channels = cols.shape
    gather = as_mask(iota((channels, LANES), 0) // GS == iota((channels, LANES), 1))
    high = cols.astype(BF16)
    rest = cols - high.astype(F32)
    mid = rest.astype(BF16)
    low = (rest - mid.astype(F32)).astype(BF16)
    parts = join(high.astype(F32), mid.astype(F32), low.astype(F32)).astype(BF16)
    sums = jnp.dot(parts, gather, preferred_element_type=F32)
    return sums[:count] + sums[count : 2 * count] + sums[2 * count :]


def by_row(line):
    return jnp.broadcast_to(line, (K, K)).T


def inverse_of(sums_ref, total):
    return by_row(lax.rsqrt(sums_ref[0:1] / total + EPS))


def gates_kernel(len_ref, k_ref, v_ref, came_ref, taps_ref, ks_ref, vs_ref):
    after = follows(len_ref, first_row() - RIM, K + RIM)

    def body(q):
        ls = lanes_of(q)
        k_ext = join(rim_of(came_ref, K_LAST, ls), k_ref[:, ls].astype(F32))
        v_ext = join(rim_of(came_ref, V_LAST, ls), v_ref[:, ls].astype(F32))
        ks_ref[:, ls] = causal(k_ext, tap_rows(taps_ref, 1, ls), after)
        vs_ref[:, ls] = causal(v_ext, tap_rows(taps_ref, 2, ls), after)

    each_chunk(k_ref.shape[1], body)


def grads_kernel(total, summed_ref, mixed_ref, qs_ref, cot_ref, gain_ref, sums_ref, gm_ref, gq_ref):
    inverse = inverse_of(sums_ref, total)
    scale = inverse * inverse * by_row(sums_ref[1:2] / total)

    def body(q):
        ls = lanes_of(q)
        scaled = gain_ref[:, ls] * cot_ref[:, ls].astype(F32)
        grad_sum = inverse * (scaled - summed_ref[:, ls] * scale)
        gm_ref[:, ls] = (grad_sum * qs_ref[:, ls]).astype(BF16)
        gq_ref[:, ls] = (grad_sum * mixed_ref[:, ls]).astype(BF16)

    each_chunk(cot_ref.shape[1], body)


def beside_kernel(
    total, len_ref, summed_ref, cot_ref, sums_ref, gm_ref, gq_ref, gated_ref, before_ref,
    bwd_ref, skip_ref, q_ref, came_ref, stats_ref, part_ref, cols_ref,
):
    groups = bwd_ref.shape[1] // K
    inverse = inverse_of(sums_ref, total)
    row = iota((K, LANES), 0)
    col = iota((K, LANES), 1)
    after = follows(len_ref, first_row() - RIM, K + RIM)
    pos = positions(len_ref, first_row() + col)
    mask = as_mask((col >= row) & (pos >= col - row))
    source = K - 1 - row
    near = (col >= source) & (pos >= col - source)
    far = (col < source) & (pos >= col - source + K)
    flip = as_mask(row + col == K - 1)
    own = owners()

    def body(q):
        ls = lanes_of(q)
        summed = summed_ref[:, ls]
        gm = gm_ref[:, ls]
        gmf = gm.astype(F32)
        gated = gated_ref[:, ls]
        stats_ref[pl.ds(groups + q, 1), :] = jnp.sum(gmf * gated.astype(F32), axis=0, keepdims=True)
        stats_ref[pl.ds(groups + groups // PER + q, 1), :] = jnp.sum(
            cot_ref[:, ls].astype(F32) * summed * inverse, axis=0, keepdims=True
        )
        right = per_group(gm, own)
        part_ref[:, ls] = skip_ref[:, ls] * gmf + product(masked(bwd_ref, q, mask), right)
        two = jnp.concatenate([before_ref[:, ls], gated], axis=1)
        flipped = jnp.dot(flip, two, preferred_element_type=F32).astype(BF16)
        left = join(flipped[:, :LANES], flipped[:, LANES:])
        turned = gmf.T.astype(BF16)
        spread = []
        for g in range(PER):
            pieces = [jnp.zeros((GS, K), BF16)] * PER
            pieces[g] = turned[g * GS : (g + 1) * GS]
            spread.append(join(*pieces))
        cross = jnp.dot(left, jnp.concatenate(spread, axis=1), preferred_element_type=F32)
        lines = []
        for g in range(PER):
            gs = slice(g * K, (g + 1) * K)
            square = jnp.where(near, cross[K:, gs], jnp.where(far, cross[:K, gs], 0.0))
            square = pltpu.roll(square, 1, 1, stride=1, stride_axis=0)
            lines.append(jnp.sum(square, axis=0, keepdims=True))
        stats_ref[pl.ds(pl.multiple_of(q * PER, PER), PER), :] = join(*lines)
        q_ext = join(rim_of(came_ref, Q_LAST, ls), q_ref[:, ls].astype(F32))
        cols_ref[:, ls] = tap_lines(gq_ref[:, ls].astype(F32), q_ext, after)

    each_chunk(cot_ref.shape[1], body, 4)


def gate_kernel(
    len_ref, part_ref, after_ref, bwd_ref, ks_ref, vs_ref, gq_ref, k_ref, v_ref, came_ref,
    stats_ref, qcols_ref, gks_ref, gvs_ref, tails_ref, packed_ref, cols_ref,
):
    channels = part_ref.shape[1]
    kept = stats_ref.shape[0]
    row = iota((K, LANES), 0)
    col = iota((K, LANES), 1)
    after = follows(len_ref, first_row() - RIM, K + RIM)
    pos = positions(len_ref, first_row() + K + col)
    mask = as_mask((col < row) & (pos >= col - row + K))
    own = owners()

    def body(q):
        ls = lanes_of(q)
        right = per_group(after_ref[:, ls], own)
        grad = part_ref[:, ls] + product(masked(bwd_ref, q, mask), right)
        gks = (grad * vs_ref[:, ls]).astype(BF16)
        gvs = (grad * ks_ref[:, ls]).astype(BF16)
        gks_ref[:, ls] = gks
        gvs_ref[:, ls] = gvs
        heads = (rim_of(gq_ref, 0, ls), gks.astype(F32)[:RIM], gvs.astype(F32)[:RIM])
        tails_ref[:, ls] = join(*heads, jnp.zeros((RIM, LANES), F32)).astype(BF16)
        k_ext = join(rim_of(came_ref, K_LAST, ls), k_ref[:, ls].astype(F32))
        v_ext = join(rim_of(came_ref, V_LAST, ls), v_ref[:, ls].astype(F32))
        cols_ref[0:8, ls] = qcols_ref[:, ls]
        cols_ref[8:16, ls] = tap_lines(gks.astype(F32), k_ext, after)
        cols_ref[16:24, ls] = tap_lines(gvs.astype(F32), v_ext, after)

    each_chunk(channels, body)
    packed_ref[0:kept] = stats_ref[...]
    sums = group_sums(cols_ref[...])
    packed_ref[kept : kept + 8] = sums[:8] + pltpu.roll(sums[8:16], LANES // 2, 1)
    packed_ref[kept + 8 :] = sums[16:]


def back_short(which, after, ls, taps_ref, grad_ref, tails_ref):
    ext = join(grad_ref[:, ls].astype(F32), rim_of(tails_ref, which * RIM, ls))
    taps = tap_rows(taps_ref, which, ls)
    grad = taps[0] * ext[:K]
    for j in range(1, KS):
        ext = pltpu.roll(ext * after, K + RIM - 1, 0)
        grad = grad + taps[j] * ext[:K]
    return grad.astype(BF16)


def main_qk_kernel(len_ref, taps_ref, tails_ref, gq_ref, gks_ref, oq_ref, ok_ref):
    after = follows(len_ref, first_row(), K + RIM)

    def body(q):
        ls = lanes_of(q)
        oq_ref[:, ls] = back_short(0, after, ls, taps_ref, gq_ref, tails_ref)
        ok_ref[:, ls] = back_short(1, after, ls, taps_ref, gks_ref, tails_ref)

    each_chunk(gq_ref.shape[1], body)


def main_v_kernel(
    total, len_ref, taps_ref, tails_ref, gvs_ref, summed_ref, gain_ref, sums_ref, ov_ref, normed_ref
):
    after = follows(len_ref, first_row(), K + RIM)
    inverse = inverse_of(sums_ref, total)

    def body(q):
        ls = lanes_of(q)
        normed_ref[:, ls] = (gain_ref[:, ls] * summed_ref[:, ls] * inverse).astype(BF16)
        ov_ref[:, ls] = back_short(2, after, ls, taps_ref, gvs_ref, tails_ref)

    each_chunk(gvs_ref.shape[1], body)


def unpack_kernel(one_ref, two_ref, short_ref, long_ref, skip_ref, gain_ref):
    groups = long_ref.shape[0]
    rows = groups // PER
    total = one_ref[...] + two_ref[...]
    long_ref[...] = total[:groups]
    skip_ref[...] = total[groups : groups + rows]
    gain_ref[...] = total[groups + rows : groups + 2 * rows]
    taps = total[groups + 2 * rows :]
    short_ref[0] = taps[:KS, :groups]
    short_ref[1] = pltpu.roll(taps[:8], LANES // 2, 1)[:KS, :groups]
    short_ref[2] = taps[8 : 8 + KS, :groups]


def shards(
    q_input, k_input, v_input, resid, lengths, short_filter, long_filter, skip, gain, cotangent
):
    length, channels = q_input.shape
    groups = channels // GS
    wide = channels * lax.axis_size("tp")
    rows = groups // PER
    packed_rows = groups + 2 * rows + 16

    def arr(shape, dtype):
        return jax.ShapeDtypeStruct(shape, dtype)

    smem = pl.BlockSpec(memory_space=pltpu.SMEM)
    vmem = pl.BlockSpec(memory_space=pltpu.VMEM)
    far_off = pl.BlockSpec(memory_space=pltpu.HBM)
    full_bf = arr((length, channels), BF16)
    full_f = arr((length, channels), F32)

    def call(name, kernel, outs, ins, scratch=(), flops=10**8, moved=10**6, grant=8, hbm=False):
        scalar = ins[0] is lengths
        return pl.pallas_call(
            kernel,
            out_shape=outs,
            in_specs=[far_off] * len(ins)
            if hbm
            else [smem if (i == 0 and scalar) else vmem for i in range(len(ins))],
            out_specs=[vmem] * len(outs),
            scratch_shapes=scratch,
            compiler_params=pltpu.CompilerParams(vmem_limit_bytes=grant * 1024 * 1024),
            cost_estimate=pl.CostEstimate(flops=flops, bytes_accessed=moved, transcendentals=0),
            name=name,
        )(*ins)

    skip2 = skip.reshape(1, channels)
    gain2 = gain.reshape(1, channels)
    taps, sent, far = call(
        "first", first_kernel,
        [arr((24, channels), F32), arr((SENT, channels), BF16), arr((2 * RIM, channels), BF16)],
        [lengths, jnp.transpose(short_filter, (0, 2, 1)), q_input, k_input, v_input],
        [
            pltpu.SMEM(lengths.shape, jnp.int32), pltpu.VMEM((3, KS, groups), BF16),
            pltpu.VMEM((PACK, channels), BF16), pltpu.VMEM((length, channels), BF16),
            pltpu.VMEM((length, channels), BF16), pltpu.SemaphoreType.DMA((5,)),
        ],
        grant=60,
        hbm=True,
    )
    came = shifted(sent, "ctx", 1)
    came_far = shifted(far, "ctx", 2)

    def circulants(filt, turned):
        return call(
            "circulants", functools.partial(circulant_kernel, turned),
            [arr((K, groups * K), BF16)], [filt], [pltpu.VMEM((groups, K), F32)],
            flops=10**9, moved=4 * 10**6,
        )[0]

    filt, filt2, sent = lax.optimization_barrier((long_filter, long_filter, sent))
    fwd = circulants(filt, True)
    bulk, part, top = call(
        "current", current_kernel, [full_f, full_f, full_bf],
        [lengths, q_input, taps, sent, fwd, skip2], flops=10**9, moved=5 * 10**6,
    )
    bwd = circulants(filt2, False)
    came, bwd = lax.optimization_barrier((came, bwd))
    q_short, gated, before, mixed, summed, sums = call(
        "summed", summed_kernel,
        [full_f, full_bf, full_bf, full_f, full_f, arr((2, K), F32)],
        [
            lengths, came, came_far, q_input, k_input, v_input, taps, sent, fwd, top,
            bulk, part, skip2, resid, cotangent, gain2,
        ],
        [pltpu.VMEM((2, K, LANES), F32)], flops=10**9, moved=5 * 10**6,
    )
    own_sums = sums
    step = 1
    while step < lax.axis_size("tp"):
        sums = sums + swapped(sums, "tp", step)
        step *= 2
    came, _ = lax.optimization_barrier((came, own_sums))
    k_short, v_short = call(
        "gates", gates_kernel, [full_f] * 2, [lengths, k_input, v_input, came, taps],
        flops=10**8, moved=2 * 10**6,
    )
    sums, k_short, v_short = lax.optimization_barrier((sums, k_short, v_short))
    grad_mixed, grad_qs = call(
        "grads", functools.partial(grads_kernel, wide), [full_bf, full_bf],
        [summed, mixed, q_short, cotangent, gain2, sums],
    )
    after = shifted(grad_mixed, "ctx", -1, wrap=False)
    stats, part, qcols = call(
        "beside", functools.partial(beside_kernel, wide),
        [
            arr((groups + 2 * rows, LANES), F32), full_f, arr((8, channels), F32),
        ],
        [
            lengths, summed, cotangent, sums, grad_mixed, grad_qs, gated, before, bwd,
            skip2, q_input, came,
        ],
        flops=4 * 10**9, moved=5 * 10**6,
    )
    grad_ks, grad_vs, tails, packed = call(
        "gate", gate_kernel,
        [
            full_bf, full_bf, arr((4 * RIM, channels), BF16),
            arr((packed_rows, LANES), F32),
        ],
        [
            lengths, part, after, bwd, k_short, v_short, grad_qs, k_input, v_input, came,
            stats, qcols,
        ],
        [pltpu.VMEM((24, channels), F32)], flops=10**9, moved=5 * 10**6,
    )
    tails = shifted(tails, "ctx", -1)
    grad_q, grad_k = call(
        "main_qk", main_qk_kernel, [full_bf] * 2, [lengths, taps, tails, grad_qs, grad_ks],
        flops=10**9, moved=5 * 10**6,
    )
    count = lax.axis_size("ctx")
    step = 1
    while 2 * step < count:
        packed = packed + swapped(packed, "ctx", step)
        step *= 2
    packed, grad_q, grad_k, grad_vs = lax.optimization_barrier((packed, grad_q, grad_k, grad_vs))
    grad_v, normed = call(
        "main_v", functools.partial(main_v_kernel, wide), [full_bf] * 2,
        [lengths, taps, tails, grad_vs, summed, gain2, sums], flops=10**9, moved=5 * 10**6,
    )
    other = swapped(packed, "ctx", step)
    grad_short, grad_long, grad_skip, grad_gain = call(
        "unpack", unpack_kernel,
        [
            arr((3, KS, groups), F32), arr((groups, K), F32),
            arr((rows, LANES), F32), arr((rows, LANES), F32),
        ],
        [packed, other],
    )
    return (
        normed, grad_q, grad_k, grad_v, jnp.transpose(grad_short, (0, 2, 1)), grad_long,
        grad_skip.reshape(channels), grad_gain.reshape(channels),
    )


def solution(mesh):
    tiled = P("ctx", "tp")
    return jax.shard_map(
        shards,
        mesh=mesh,
        in_specs=(
            tiled, tiled, tiled, tiled, P(), P(None, "tp", None), P("tp", None), P("tp"), P("tp"),
            tiled,
        ),
        out_specs=(
            tiled, tiled, tiled, tiled, P(None, "tp", None), P("tp", None), P("tp"), P("tp"),
        ),
        check_vma=False,
    )
```

```python
import functools

import jax
import jax.numpy as jnp
from jax import lax
from jax.experimental import pallas as pl
from jax.experimental.pallas import tpu as pltpu
from jax.sharding import PartitionSpec as P

GS = 16
K = 128
KS = 7
LANES = 128
PER = LANES // GS
RIM = 8
PACK = 16
EPS = 1e-06
F32 = jnp.float32
BF16 = jnp.bfloat16


def shifted(x, axis, by, wrap=True):
    count = lax.axis_size(axis)
    pairs = [(i, (i + by) % count) for i in range(count)]
    return lax.ppermute(x, axis, [p for p in pairs if wrap or p[1] - p[0] == by])


def swapped(x, axis, step):
    return lax.ppermute(x, axis, [(i, i ^ step) for i in range(lax.axis_size(axis))])


def iota(shape, dim):
    return lax.broadcasted_iota(jnp.int32, shape, dim)


def positions(len_ref, rows):
    begin = jnp.zeros_like(rows)
    start = jnp.int32(0)
    for n in range(len_ref.shape[0]):
        begin = jnp.where(rows >= start, start, begin)
        start = start + len_ref[n]
    return jnp.where(rows < start, rows - begin, -1)


def first_row():
    return lax.axis_index("ctx") * K


def lanes_of(q):
    return pl.ds(pl.multiple_of(q * LANES, LANES), LANES)


def each_chunk(channels, body, unroll=4):
    def step(q, carry):
        body(q)
        return carry

    lax.fori_loop(0, channels // LANES, step, 0, unroll=unroll)


def as_mask(cond):
    return jnp.where(cond, 1.0, 0.0).astype(BF16)


def join(*parts):
    return jnp.concatenate(parts, axis=0)


def tap_rows(taps_ref, which, ls):
    table = taps_ref[which * 8 : which * 8 + 8, ls]
    return [table[j : j + 1, :] for j in range(KS)]


def follows(len_ref, start, count):
    pos = positions(len_ref, start + iota((count, LANES), 0))
    return jnp.where(pos >= 1, 1.0, 0.0)


def moved_on(x, after):
    return pltpu.roll(x, 1, 0) * after


def causal(ext, taps, after):
    total = taps[0] * ext[RIM:]
    for j in range(1, KS):
        ext = moved_on(ext, after)
        total = total + taps[j] * ext[RIM:]
    return total


def tap_lines(grad, ext, after):
    lines = [jnp.sum(grad * ext[RIM:], axis=0, keepdims=True)]
    for j in range(1, KS):
        ext = moved_on(ext, after)
        lines.append(jnp.sum(grad * ext[RIM:], axis=0, keepdims=True))
    lines.append(jnp.zeros((8 - KS, LANES), F32))
    return join(*lines)


def owners():
    lane = iota((K, LANES), 1) // GS
    return [as_mask(lane == g) for g in range(PER)]


def per_group(right, own):
    return join(*[right * mask for mask in own])


def masked(table_ref, q, mask):
    table = table_ref[:, pl.ds(pl.multiple_of(q * PER * K, PER * K), PER * K)]
    return [table[:, g * K : (g + 1) * K] * mask for g in range(PER)]


def product(left, right):
    return jnp.dot(jnp.concatenate(left, axis=1), right, preferred_element_type=F32)


K_FIRST, Q_LAST, K_LAST, V_LAST, V_FIRST, SENT = 0, K, K + 8, K + 16, K + 24, K + 32


def rim_of(ref, at, ls):
    base = at // PACK * PACK
    return ref[base : base + PACK, ls].astype(F32)[at - base : at - base + RIM]


def first_kernel(
    len_hbm, short_hbm, q_hbm, k_hbm, v_hbm, taps_ref, sent_ref, far_ref,
    len_ref, short_ref, q_ref, k_ref, v_ref, sems,
):
    groups = short_ref.shape[2]
    channels = taps_ref.shape[1]
    pairs = (
        (short_hbm, short_ref), (len_hbm, len_ref), (k_hbm, k_ref), (v_hbm, v_ref),
        (q_hbm.at[K - PACK : K], q_ref),
    )
    copies = [pltpu.make_async_copy(a, b, sems.at[i]) for i, (a, b) in enumerate(pairs)]
    for copy in copies:
        copy.start()
    spread = as_mask(iota((groups, channels), 1) // GS == iota((groups, channels), 0))
    copies[0].wait()
    for i in range(3):
        taps_ref[i * 8 : i * 8 + KS] = jnp.dot(
            short_ref[i], spread, preferred_element_type=F32
        )
        taps_ref[i * 8 + KS : i * 8 + 8] = jnp.zeros((8 - KS, channels), F32)
    for copy in copies[1:]:
        copy.wait()
    after = follows(len_ref, first_row(), K)

    def body(q):
        ls = lanes_of(q)
        kx = k_ref[:, ls].astype(F32)
        vx = v_ref[:, ls].astype(F32)
        ks = causal(kx, tap_rows(taps_ref, 1, ls), after)
        vs = causal(vx, tap_rows(taps_ref, 2, ls), after)
        sent_ref[:K, ls] = join(kx[:RIM], ks * vs).astype(BF16)
        q_end = q_ref[:, ls].astype(F32)[PACK - RIM :]
        k_end = kx[K - RIM :]
        v_end = vx[K - RIM :]
        sent_ref[K:, ls] = join(q_end, k_end, v_end, vx[:RIM]).astype(BF16)
        far_ref[:, ls] = join(k_end, v_end).astype(BF16)

    each_chunk(channels, body)


def circulant_kernel(turned, long_ref, out_ref, line_ref):
    groups = long_ref.shape[0]
    filt = long_ref[...]
    if turned:
        flip = as_mask((iota((K, K), 0) + iota((K, K), 1)) % K == 0)
        line_ref[...] = jnp.dot(filt, flip, preferred_element_type=F32)
    else:
        line_ref[...] = filt.astype(F32)

    def step(g, carry):
        row = jnp.broadcast_to(line_ref[pl.ds(g, 1), :], (GS, K))
        block = pltpu.roll(row, 0, 1, stride=1, stride_axis=0)
        for i in range(K // GS):
            moved = block if i == 0 else pltpu.roll(block, i * GS, 1)
            at = pl.ds(pl.multiple_of(g * K, K), K)
            out_ref[i * GS : (i + 1) * GS, at] = moved.astype(BF16)
        return carry

    lax.fori_loop(0, groups, step, 0, unroll=8)


def current_kernel(
    len_ref, q_ref, taps_ref, sent_ref, fwd_ref, skip_ref, qs_ref, part_ref, top_ref
):
    row = iota((K, LANES), 0)
    col = iota((K, LANES), 1)
    pos = positions(len_ref, first_row() + row)
    near = (col <= row) & (pos >= row - col)
    mask = as_mask(near)
    mask_top = as_mask(near & (col < RIM))
    picks = join(*[as_mask((col == row + g * GS) & (row < GS)) for g in range(PER)])
    own = owners()
    top = jnp.zeros((RIM, LANES), F32)
    after = follows(len_ref, first_row(), K)

    def body(q):
        ls = lanes_of(q)
        qs_ref[RIM:, ls] = causal(q_ref[:, ls].astype(F32), tap_rows(taps_ref, 0, ls), after)
        qs_ref[:RIM, ls] = top
        gated = join(top, sent_ref[:K, ls].astype(F32)[RIM:])
        rest = product(masked(fwd_ref, q, mask), per_group(gated.astype(BF16), own))
        part_ref[:, ls] = rest + skip_ref[:, ls] * gated
        top_ref[:, ls] = product(masked(fwd_ref, q, mask_top), picks).astype(BF16)

    each_chunk(q_ref.shape[1], body)


def summed_kernel(
    len_ref, came_ref, far_ref, q_ref, k_ref, v_ref, taps_ref, sent_ref, fwd_ref, top_ref,
    bulk_ref, part_ref, skip_ref, resid_ref, cot_ref, gain_ref,
    qs_ref, gated_ref, before_ref, mixed_ref, summed_ref, sums_ref, acc_ref,
):
    row = iota((K, LANES), 0)
    col = iota((K, LANES), 1)
    pos = positions(len_ref, first_row() + row)
    mask = as_mask((col > row) & (pos >= row - col + K))
    after = follows(len_ref, first_row() - RIM, 2 * RIM)
    after_far = follows(len_ref, first_row() - K - RIM, 2 * RIM)
    own = owners()
    own_top = [
        as_mask((iota((PACK, LANES), 1) // GS == g) & (iota((PACK, LANES), 0) < RIM))
        for g in range(PER)
    ]
    acc_ref[...] = jnp.zeros_like(acc_ref)

    def body(q):
        ls = lanes_of(q)
        kt = tap_rows(taps_ref, 1, ls)
        vt = tap_rows(taps_ref, 2, ls)
        k_last = rim_of(came_ref, K_LAST, ls)
        v_last = rim_of(came_ref, V_LAST, ls)
        top = causal(join(k_last, rim_of(k_ref, 0, ls)), kt, after) * causal(
            join(v_last, rim_of(v_ref, 0, ls)), vt, after
        )
        far_top = causal(
            join(rim_of(far_ref, 0, ls), rim_of(came_ref, K_FIRST, ls)), kt, after_far
        ) * causal(join(rim_of(far_ref, RIM, ls), rim_of(came_ref, V_FIRST, ls)), vt, after_far)
        qs_top = causal(
            join(rim_of(came_ref, Q_LAST, ls), rim_of(q_ref, 0, ls)), tap_rows(taps_ref, 0, ls), after
        )
        before = join(far_top, came_ref[:K, ls].astype(F32)[RIM:]).astype(BF16)
        gated = join(top, sent_ref[:K, ls].astype(F32)[RIM:]).astype(BF16)
        before_ref[:, ls] = before
        gated_ref[:, ls] = gated
        qs = join(qs_top, bulk_ref[RIM:, ls])
        qs_ref[:, ls] = qs
        first = gated[:PACK]
        left = masked(fwd_ref, q, mask) + [top_ref[:, ls]]
        right = join(per_group(before, own), per_group(first, own_top))
        direct = skip_ref[:, ls] * first.astype(F32)[:RIM]
        mixed = part_ref[:, ls] + product(left, right)
        mixed = join(mixed[:RIM] + direct, mixed[RIM:])
        summed = resid_ref[:, ls].astype(F32) + qs * mixed
        mixed_ref[:, ls] = mixed
        summed_ref[:, ls] = summed
        acc_ref[0] += summed * summed
        acc_ref[1] += gain_ref[:, ls] * cot_ref[:, ls].astype(F32) * summed

    each_chunk(resid_ref.shape[1], body)
    for i in range(2):
        sums_ref[i : i + 1] = jnp.sum(acc_ref[i].T, axis=0, keepdims=True)


def group_sums(cols):
    count, channels = cols.shape
    gather = as_mask(iota((channels, LANES), 0) // GS == iota((channels, LANES), 1))
    high = cols.astype(BF16)
    rest = cols - high.astype(F32)
    mid = rest.astype(BF16)
    low = (rest - mid.astype(F32)).astype(BF16)
    parts = join(high.astype(F32), mid.astype(F32), low.astype(F32)).astype(BF16)
    sums = jnp.dot(parts, gather, preferred_element_type=F32)
    return sums[:count] + sums[count : 2 * count] + sums[2 * count :]


def by_row(line):
    return jnp.broadcast_to(line, (K, K)).T


def inverse_of(sums_ref, total):
    return by_row(lax.rsqrt(sums_ref[0:1] / total + EPS))


def gates_kernel(len_ref, k_ref, v_ref, came_ref, taps_ref, ks_ref, vs_ref):
    after = follows(len_ref, first_row() - RIM, K + RIM)

    def body(q):
        ls = lanes_of(q)
        k_ext = join(rim_of(came_ref, K_LAST, ls), k_ref[:, ls].astype(F32))
        v_ext = join(rim_of(came_ref, V_LAST, ls), v_ref[:, ls].astype(F32))
        ks_ref[:, ls] = causal(k_ext, tap_rows(taps_ref, 1, ls), after)
        vs_ref[:, ls] = causal(v_ext, tap_rows(taps_ref, 2, ls), after)

    each_chunk(k_ref.shape[1], body)


def grads_kernel(total, summed_ref, mixed_ref, qs_ref, cot_ref, gain_ref, sums_ref, gm_ref, gq_ref):
    inverse = inverse_of(sums_ref, total)
    scale = inverse * inverse * by_row(sums_ref[1:2] / total)

    def body(q):
        ls = lanes_of(q)
        scaled = gain_ref[:, ls] * cot_ref[:, ls].astype(F32)
        grad_sum = inverse * (scaled - summed_ref[:, ls] * scale)
        gm_ref[:, ls] = (grad_sum * qs_ref[:, ls]).astype(BF16)
        gq_ref[:, ls] = (grad_sum * mixed_ref[:, ls]).astype(BF16)

    each_chunk(cot_ref.shape[1], body)


def beside_kernel(
    total, len_ref, summed_ref, cot_ref, sums_ref, gm_ref, gq_ref, gated_ref, before_ref,
    bwd_ref, skip_ref, q_ref, came_ref, stats_ref, part_ref, cols_ref,
):
    groups = bwd_ref.shape[1] // K
    inverse = inverse_of(sums_ref, total)
    row = iota((K, LANES), 0)
    col = iota((K, LANES), 1)
    after = follows(len_ref, first_row() - RIM, K + RIM)
    pos = positions(len_ref, first_row() + col)
    mask = as_mask((col >= row) & (pos >= col - row))
    source = K - 1 - row
    near = (col >= source) & (pos >= col - source)
    far = (col < source) & (pos >= col - source + K)
    flip = as_mask(row + col == K - 1)
    own = owners()

    def body(q):
        ls = lanes_of(q)
        summed = summed_ref[:, ls]
        gm = gm_ref[:, ls]
        gmf = gm.astype(F32)
        gated = gated_ref[:, ls]
        stats_ref[pl.ds(groups + q, 1), :] = jnp.sum(gmf * gated.astype(F32), axis=0, keepdims=True)
        stats_ref[pl.ds(groups + groups // PER + q, 1), :] = jnp.sum(
            cot_ref[:, ls].astype(F32) * summed * inverse, axis=0, keepdims=True
        )
        right = per_group(gm, own)
        part_ref[:, ls] = skip_ref[:, ls] * gmf + product(masked(bwd_ref, q, mask), right)
        two = jnp.concatenate([before_ref[:, ls], gated], axis=1)
        flipped = jnp.dot(flip, two, preferred_element_type=F32).astype(BF16)
        left = join(flipped[:, :LANES], flipped[:, LANES:])
        turned = gmf.T.astype(BF16)
        spread = []
        for g in range(PER):
            pieces = [jnp.zeros((GS, K), BF16)] * PER
            pieces[g] = turned[g * GS : (g + 1) * GS]
            spread.append(join(*pieces))
        cross = jnp.dot(left, jnp.concatenate(spread, axis=1), preferred_element_type=F32)
        lines = []
        for g in range(PER):
            gs = slice(g * K, (g + 1) * K)
            square = jnp.where(near, cross[K:, gs], jnp.where(far, cross[:K, gs], 0.0))
            square = pltpu.roll(square, 1, 1, stride=1, stride_axis=0)
            lines.append(jnp.sum(square, axis=0, keepdims=True))
        stats_ref[pl.ds(pl.multiple_of(q * PER, PER), PER), :] = join(*lines)
        q_ext = join(rim_of(came_ref, Q_LAST, ls), q_ref[:, ls].astype(F32))
        cols_ref[:, ls] = tap_lines(gq_ref[:, ls].astype(F32), q_ext, after)

    each_chunk(cot_ref.shape[1], body, 2)


def gate_kernel(
    len_ref, part_ref, after_ref, bwd_ref, ks_ref, vs_ref, gq_ref, k_ref, v_ref, came_ref,
    stats_ref, qcols_ref, gks_ref, gvs_ref, tails_ref, packed_ref, cols_ref,
):
    channels = part_ref.shape[1]
    kept = stats_ref.shape[0]
    row = iota((K, LANES), 0)
    col = iota((K, LANES), 1)
    after = follows(len_ref, first_row() - RIM, K + RIM)
    pos = positions(len_ref, first_row() + K + col)
    mask = as_mask((col < row) & (pos >= col - row + K))
    own = owners()

    def body(q):
        ls = lanes_of(q)
        right = per_group(after_ref[:, ls], own)
        grad = part_ref[:, ls] + product(masked(bwd_ref, q, mask), right)
        gks = (grad * vs_ref[:, ls]).astype(BF16)
        gvs = (grad * ks_ref[:, ls]).astype(BF16)
        gks_ref[:, ls] = gks
        gvs_ref[:, ls] = gvs
        heads = (rim_of(gq_ref, 0, ls), gks.astype(F32)[:RIM], gvs.astype(F32)[:RIM])
        tails_ref[:, ls] = join(*heads, jnp.zeros((RIM, LANES), F32)).astype(BF16)
        k_ext = join(rim_of(came_ref, K_LAST, ls), k_ref[:, ls].astype(F32))
        v_ext = join(rim_of(came_ref, V_LAST, ls), v_ref[:, ls].astype(F32))
        cols_ref[0:8, ls] = qcols_ref[:, ls]
        cols_ref[8:16, ls] = tap_lines(gks.astype(F32), k_ext, after)
        cols_ref[16:24, ls] = tap_lines(gvs.astype(F32), v_ext, after)

    each_chunk(channels, body)
    packed_ref[0:kept] = stats_ref[...]
    packed_ref[kept:] = group_sums(cols_ref[...])


def back_short(which, after, ls, taps_ref, grad_ref, tails_ref):
    ext = join(grad_ref[:, ls].astype(F32), rim_of(tails_ref, which * RIM, ls))
    taps = tap_rows(taps_ref, which, ls)
    grad = taps[0] * ext[:K]
    for j in range(1, KS):
        ext = pltpu.roll(ext * after, K + RIM - 1, 0)
        grad = grad + taps[j] * ext[:K]
    return grad.astype(BF16)


def main_qk_kernel(len_ref, taps_ref, tails_ref, gq_ref, gks_ref, oq_ref, ok_ref):
    after = follows(len_ref, first_row(), K + RIM)

    def body(q):
        ls = lanes_of(q)
        oq_ref[:, ls] = back_short(0, after, ls, taps_ref, gq_ref, tails_ref)
        ok_ref[:, ls] = back_short(1, after, ls, taps_ref, gks_ref, tails_ref)

    each_chunk(gq_ref.shape[1], body)


def main_v_kernel(
    total, len_ref, taps_ref, tails_ref, gvs_ref, summed_ref, gain_ref, sums_ref, ov_ref, normed_ref
):
    after = follows(len_ref, first_row(), K + RIM)
    inverse = inverse_of(sums_ref, total)

    def body(q):
        ls = lanes_of(q)
        normed_ref[:, ls] = (gain_ref[:, ls] * summed_ref[:, ls] * inverse).astype(BF16)
        ov_ref[:, ls] = back_short(2, after, ls, taps_ref, gvs_ref, tails_ref)

    each_chunk(gvs_ref.shape[1], body)


def unpack_kernel(one_ref, two_ref, short_ref, long_ref, skip_ref, gain_ref):
    groups = long_ref.shape[0]
    rows = groups // PER
    total = one_ref[...] + two_ref[...]
    long_ref[...] = total[:groups]
    skip_ref[...] = total[groups : groups + rows]
    gain_ref[...] = total[groups + rows : groups + 2 * rows]
    for i in range(3):
        at = groups + 2 * rows + i * 8
        short_ref[i] = total[at : at + KS, :groups]


def shards(
    q_input, k_input, v_input, resid, lengths, short_filter, long_filter, skip, gain, cotangent
):
    length, channels = q_input.shape
    groups = channels // GS
    wide = channels * lax.axis_size("tp")
    rows = groups // PER
    packed_rows = groups + 2 * rows + 24

    def arr(shape, dtype):
        return jax.ShapeDtypeStruct(shape, dtype)

    smem = pl.BlockSpec(memory_space=pltpu.SMEM)
    vmem = pl.BlockSpec(memory_space=pltpu.VMEM)
    far_off = pl.BlockSpec(memory_space=pltpu.HBM)
    full_bf = arr((length, channels), BF16)
    full_f = arr((length, channels), F32)

    def call(name, kernel, outs, ins, scratch=(), flops=10**8, moved=10**6, grant=8, hbm=False):
        scalar = ins[0] is lengths
        return pl.pallas_call(
            kernel,
            out_shape=outs,
            in_specs=[far_off] * len(ins)
            if hbm
            else [smem if (i == 0 and scalar) else vmem for i in range(len(ins))],
            out_specs=[vmem] * len(outs),
            scratch_shapes=scratch,
            compiler_params=pltpu.CompilerParams(vmem_limit_bytes=grant * 1024 * 1024),
            cost_estimate=pl.CostEstimate(flops=flops, bytes_accessed=moved, transcendentals=0),
            name=name,
        )(*ins)

    skip2 = skip.reshape(1, channels)
    gain2 = gain.reshape(1, channels)
    taps, sent, far = call(
        "first", first_kernel,
        [arr((24, channels), F32), arr((SENT, channels), BF16), arr((2 * RIM, channels), BF16)],
        [lengths, jnp.transpose(short_filter, (0, 2, 1)), q_input, k_input, v_input],
        [
            pltpu.SMEM(lengths.shape, jnp.int32), pltpu.VMEM((3, KS, groups), BF16),
            pltpu.VMEM((PACK, channels), BF16), pltpu.VMEM((length, channels), BF16),
            pltpu.VMEM((length, channels), BF16), pltpu.SemaphoreType.DMA((5,)),
        ],
        grant=60,
        hbm=True,
    )
    came = shifted(sent, "ctx", 1)
    came_far = shifted(far, "ctx", 2)

    def circulants(filt, turned):
        return call(
            "circulants", functools.partial(circulant_kernel, turned),
            [arr((K, groups * K), BF16)], [filt], [pltpu.VMEM((groups, K), F32)],
            flops=10**9, moved=4 * 10**6,
        )[0]

    filt, filt2, sent = lax.optimization_barrier((long_filter, long_filter, sent))
    fwd = circulants(filt, True)
    bulk, part, top = call(
        "current", current_kernel, [full_f, full_f, full_bf],
        [lengths, q_input, taps, sent, fwd, skip2], flops=10**9, moved=5 * 10**6,
    )
    bwd = circulants(filt2, False)
    came, bwd = lax.optimization_barrier((came, bwd))
    q_short, gated, before, mixed, summed, sums = call(
        "summed", summed_kernel,
        [full_f, full_bf, full_bf, full_f, full_f, arr((2, K), F32)],
        [
            lengths, came, came_far, q_input, k_input, v_input, taps, sent, fwd, top,
            bulk, part, skip2, resid, cotangent, gain2,
        ],
        [pltpu.VMEM((2, K, LANES), F32)], flops=10**9, moved=5 * 10**6,
    )
    own_sums = sums
    step = 1
    while step < lax.axis_size("tp"):
        sums = sums + swapped(sums, "tp", step)
        step *= 2
    came, _ = lax.optimization_barrier((came, own_sums))
    k_short, v_short = call(
        "gates", gates_kernel, [full_f] * 2, [lengths, k_input, v_input, came, taps],
        flops=10**8, moved=2 * 10**6,
    )
    sums, k_short, v_short = lax.optimization_barrier((sums, k_short, v_short))
    grad_mixed, grad_qs = call(
        "grads", functools.partial(grads_kernel, wide), [full_bf, full_bf],
        [summed, mixed, q_short, cotangent, gain2, sums],
    )
    after = shifted(grad_mixed, "ctx", -1)
    stats, part, qcols = call(
        "beside", functools.partial(beside_kernel, wide),
        [
            arr((groups + 2 * rows, LANES), F32), full_f, arr((8, channels), F32),
        ],
        [
            lengths, summed, cotangent, sums, grad_mixed, grad_qs, gated, before, bwd,
            skip2, q_input, came,
        ],
        flops=4 * 10**9, moved=5 * 10**6,
    )
    grad_ks, grad_vs, tails, packed = call(
        "gate", gate_kernel,
        [
            full_bf, full_bf, arr((4 * RIM, channels), BF16),
            arr((packed_rows, LANES), F32),
        ],
        [
            lengths, part, after, bwd, k_short, v_short, grad_qs, k_input, v_input, came,
            stats, qcols,
        ],
        [pltpu.VMEM((24, channels), F32)], flops=10**9, moved=5 * 10**6,
    )
    tails = shifted(tails, "ctx", -1)
    grad_q, grad_k = call(
        "main_qk", main_qk_kernel, [full_bf] * 2, [lengths, taps, tails, grad_qs, grad_ks],
        flops=10**9, moved=5 * 10**6,
    )
    count = lax.axis_size("ctx")
    step = 1
    while 2 * step < count:
        packed = packed + swapped(packed, "ctx", step)
        step *= 2
    packed, grad_q, grad_k, grad_vs = lax.optimization_barrier((packed, grad_q, grad_k, grad_vs))
    grad_v, normed = call(
        "main_v", functools.partial(main_v_kernel, wide), [full_bf] * 2,
        [lengths, taps, tails, grad_vs, summed, gain2, sums], flops=10**9, moved=5 * 10**6,
    )
    other = swapped(packed, "ctx", step)
    grad_short, grad_long, grad_skip, grad_gain = call(
        "unpack", unpack_kernel,
        [
            arr((3, KS, groups), F32), arr((groups, K), F32),
            arr((rows, LANES), F32), arr((rows, LANES), F32),
        ],
        [packed, other],
    )
    return (
        normed, grad_q, grad_k, grad_v, jnp.transpose(grad_short, (0, 2, 1)), grad_long,
        grad_skip.reshape(channels), grad_gain.reshape(channels),
    )


def solution(mesh):
    tiled = P("ctx", "tp")
    return jax.shard_map(
        shards,
        mesh=mesh,
        in_specs=(
            tiled, tiled, tiled, tiled, P(), P(None, "tp", None), P("tp", None), P("tp"), P("tp"),
            tiled,
        ),
        out_specs=(
            tiled, tiled, tiled, tiled, P(None, "tp", None), P("tp", None), P("tp"), P("tp"),
        ),
        check_vma=False,
    )
```
